32 devices in a mesh: dp: 8 (over y, x, core), outer: 4 (over z).
Axes of the slice: x: 2, y: 2, z: 4, core: 2. Of those that a mesh axis runs over, the one named last changes fastest.
Arguments:
- images: bfloat16 [64, 144, 2048], P(('dp', 'outer')), may hold values from -27 to 27
- counts: int32 [32], replicated, may hold values from 1 to 2, as said below
- orientation: int32 [64], P(('dp', 'outer')), may hold values 0 or 1
- cotangent: bfloat16 [64, 144, 2048], P(('dp', 'outer')), may hold values from -6 to 6
- reducer: bfloat16 [2048, 512], replicated, may hold values from -0.125 to 0.125
- offseter: bfloat16 [4608, 18], replicated, may hold values from -0.125 to 0.125
- deformer: bfloat16 [4608, 512], replicated, may hold values from -0.09375 to 0.09375
- expander: bfloat16 [2048, 512], replicated, may hold values from -0.25 to 0.25
- narrower: bfloat16 [2048, 512], replicated, may hold values from -0.125 to 0.125
- convolver: bfloat16 [4608, 512], replicated, may hold values from -0.09375 to 0.09375
- widener: bfloat16 [2048, 512], replicated, may hold values from -0.25 to 0.25
- inner_gains: float32 [4, 512], replicated, may hold values from 0.5 to 1.5
- inner_biases: float32 [4, 512], replicated, may hold values from -2 to 2
- broad_gains: float32 [2, 2048], replicated, may hold values from 0.5 to 1.5
- broad_biases: float32 [2, 2048], replicated, may hold values from -2 to 2
Outputs:
- block_out: bfloat16 [64, 144, 2048], P(('dp', 'outer'))
- images_grad: bfloat16 [64, 144, 2048], P(('dp', 'outer'))
- reducer_grad: float32 [2048, 512], P('dp')
- offseter_grad: float32 [4608, 18], P('dp')
- deformer_grad: float32 [4608, 512], P('dp')
- expander_grad: float32 [2048, 512], P('dp')
- narrower_grad: float32 [2048, 512], P('dp')
- convolver_grad: float32 [4608, 512], P('dp')
- widener_grad: float32 [2048, 512], P('dp')
- inner_gains_grad: float32 [4, 512], P(None, 'dp')
- inner_biases_grad: float32 [4, 512], P(None, 'dp')
- broad_gains_grad: float32 [2, 2048], P(None, 'dp')
- broad_biases_grad: float32 [2, 2048], P(None, 'dp')
The draws below stay inside these ranges and needn't reach their ends.
Inputs may be any that keep to these rules, and one draw needn't show every extreme that they name: `counts`: some device holds 2 live images and some holds 1; a device's live images fill its first slots. `orientation`: 0 marks a map of 4 rows and 36 columns, 1 one of 36 rows and 4 columns.
All inputs are finite; a program needn't handle non-finite values. No bound on the sum of `orientation` on one device may be relied on, other than what follows from the above.
Results may differ from the reference program's by a relative error of at most 0.018.
Values sent between devices are 32-bit elements; how exact they have to be, the bound alone decides.
A program may use at most 256 MiB of HBM per device.

```python
import jax
import jax.numpy as jnp
from jax import lax

CHANNELS = 2048
INNER = 512
TAPS = 9
OFFSETS = 18
SLOTS = 2
SHORT = 4
LONG = 36
PIXELS = 144
IMAGES = 64
DEVICES = 32


def draw_images(key, part):
    first, second = jax.random.split(key, 2)
    order = jnp.arange(IMAGES, dtype=jnp.float32) / max(IMAGES - 1, 1)
    rise = jnp.exp(order * jnp.log(4.0))[:, None, None]
    level = order[:, None, None]
    pattern = jnp.clip(jax.random.normal(second, (1, 1, CHANNELS), jnp.float32), -3.0, 3.0)
    noise = jnp.clip(jax.random.normal(first, (IMAGES, PIXELS, CHANNELS), jnp.float32), -6.0, 6.0)
    return (rise * noise + level * pattern).astype(jnp.bfloat16)


def draw_counts(key, part):
    first, second = jax.random.split(jax.random.fold_in(key, 7))
    base = jax.random.randint(first, (DEVICES,), 1, SLOTS + 1)
    picks = jax.random.permutation(second, DEVICES)
    base = base.at[picks[0]].set(SLOTS)
    base = base.at[picks[1]].set(1)
    return base.astype(jnp.int32)


def set_ends(entries, stream_key, least, largest):
    dims = entries.shape
    place = [jax.random.randint(jax.random.fold_in(stream_key, axis), (), 0, dims[axis]) for axis in range(len(dims))]
    entries = entries.at[tuple(place)].set(least)
    longest = dims.index(max(dims))
    place[longest] = (place[longest] + 1) % dims[longest]
    return entries.at[tuple(place)].set(largest)


def block_levels(rng, extent, cuts, least, high):
    def one(axis_at, shards_of):
        steps = jax.random.uniform(jax.random.fold_in(jax.random.fold_in(rng, 6), axis_at), (shards_of,), jnp.float32, least / len(cuts), high / len(cuts))
        return jnp.repeat(jnp.exp(steps), extent[axis_at] // shards_of).reshape((-1,) + (1,) * (len(extent) - axis_at - 1))

    factor_of = one(*cuts[0])
    for cut in cuts[1:]:
        factor_of = factor_of * one(*cut)
    return factor_of


def scatter_about(own_key, dims, scale, reach, shards=(), kind=jnp.bfloat16):
    entries = scale * jax.random.normal(own_key, dims, jnp.float32)
    if shards:
        entries = entries * block_levels(own_key, dims, shards, -0.22, 0.18)
    return jnp.clip(entries, -reach, reach).astype(kind)


def setup_inputs(seed: int = 0) -> dict:
    streams_of = jax.random.split(jax.random.key(seed), 16)
    return {
        "images": draw_images(jax.random.fold_in(streams_of[15], 71), 0),
        "counts": draw_counts(jax.random.fold_in(streams_of[15], 71), 0),
        "orientation": set_ends((jax.random.randint(streams_of[2], (IMAGES,), 0, 2) < 1).astype(jnp.int32), jax.random.fold_in(streams_of[2], 1), 0, 1),
        "cotangent": scatter_about(streams_of[3], (IMAGES, PIXELS, CHANNELS), 1.0, 6.0, ((0, 32),)),
        "reducer": scatter_about(streams_of[4], (CHANNELS, INNER), CHANNELS ** -0.5, 0.125),
        "offseter": scatter_about(streams_of[5], (TAPS * INNER, OFFSETS), (TAPS * INNER // 2) ** -0.5, 0.125),
        "deformer": scatter_about(streams_of[6], (TAPS * INNER, INNER), (TAPS * INNER) ** -0.5, 0.09375),
        "expander": scatter_about(streams_of[7], (CHANNELS, INNER), INNER ** -0.5, 0.25),
        "narrower": scatter_about(streams_of[8], (CHANNELS, INNER), CHANNELS ** -0.5, 0.125),
        "convolver": scatter_about(streams_of[9], (TAPS * INNER, INNER), (TAPS * INNER) ** -0.5, 0.09375),
        "widener": scatter_about(streams_of[10], (CHANNELS, INNER), INNER ** -0.5, 0.25),
        "inner_gains": jnp.clip(1.0 + 0.1 * jax.random.normal(streams_of[11], (4, INNER), jnp.float32), 0.5, 1.5),
        "inner_biases": scatter_about(streams_of[12], (4, INNER), 0.3, 2.0, (), jnp.float32),
        "broad_gains": jnp.clip(1.0 + 0.1 * jax.random.normal(streams_of[13], (2, CHANNELS), jnp.float32), 0.5, 1.5),
        "broad_biases": scatter_about(streams_of[14], (2, CHANNELS), 0.3, 2.0, (), jnp.float32),
    }


EPS = 1e-05
HIGH = lax.Precision.HIGHEST

@jax.custom_vjp
def low(v):
    return lax.optimization_barrier(v.astype(jnp.bfloat16)).astype(jnp.float32)

@jax.custom_vjp
def low_back(v):
    return v

def low_keep(v):
    return (low(v), None)

def low_pass(kept, grad):
    return (grad,)

def back_keep(v):
    return (v, None)

def back_low(kept, grad):
    return (low(grad),)
low.defvjp(low_keep, low_pass)
low_back.defvjp(back_keep, back_low)

def geometry(orientation):
    flip = orientation.astype(jnp.int32)
    heights = SHORT + flip * (LONG - SHORT)
    widths = LONG - flip * (LONG - SHORT)
    return (heights, widths)

def positions(width):
    pixel = jnp.arange(PIXELS, dtype=jnp.int32)
    return (pixel // width, pixel % width)

def tap_steps():
    tap = jnp.arange(TAPS, dtype=jnp.int32)
    return (2 * (tap // 3 - 1), 2 * (tap % 3 - 1))

def gather_taps(field, height, width):
    row, col = positions(width)
    step_y, step_x = tap_steps()
    near_y = row[:, None] + step_y[None, :]
    near_x = col[:, None] + step_x[None, :]
    inside = (near_y >= 0) & (near_y < height) & (near_x >= 0) & (near_x < width)
    index = jnp.clip(near_y, 0, height - 1) * width + jnp.clip(near_x, 0, width - 1)
    taken = field[index] * inside[:, :, None].astype(field.dtype)
    return taken.reshape(PIXELS, TAPS * field.shape[1])

def sample(field, offsets, height, width):
    row, col = positions(width)
    step_y, step_x = tap_steps()
    pairs = offsets.reshape(PIXELS, TAPS, 2)
    frac_y = jax.nn.sigmoid(pairs[:, :, 0])
    frac_x = jax.nn.sigmoid(pairs[:, :, 1])
    corner_y = row[:, None] + step_y[None, :]
    corner_x = col[:, None] + step_x[None, :]
    total = jnp.zeros((PIXELS, TAPS, field.shape[1]), field.dtype)
    for shift_y in (0, 1):
        for shift_x in (0, 1):
            near_y = corner_y + shift_y
            near_x = corner_x + shift_x
            weight_y = frac_y if shift_y == 1 else 1.0 - frac_y
            weight_x = frac_x if shift_x == 1 else 1.0 - frac_x
            inside = (near_y >= 0) & (near_y < height) & (near_x >= 0) & (near_x < width)
            index = jnp.clip(near_y, 0, height - 1) * width + jnp.clip(near_x, 0, width - 1)
            weight = weight_y * weight_x * inside.astype(field.dtype)
            total = total + weight[:, :, None] * field[index]
    return total.reshape(PIXELS, TAPS * field.shape[1])

def inward(value, matrix):
    return jnp.einsum('ipc,cm->ipm', value, matrix, precision=HIGH)

def outward(value, matrix):
    return jnp.einsum('ipm,cm->ipc', value, matrix, precision=HIGH)

def reference(images, counts, orientation, cotangent, reducer, offseter, deformer, expander, narrower, convolver, widener, inner_gains, inner_biases, broad_gains, broad_biases):
    image = jnp.arange(IMAGES, dtype=jnp.int32)
    live = (image % SLOTS < counts[image // SLOTS]).astype(jnp.float32)
    total = (jnp.sum(counts) * PIXELS).astype(jnp.float32)
    heights, widths = geometry(orientation)
    mask = live[:, None, None]

    def normalize(value, gain, bias):
        mean = lax.optimization_barrier(jnp.sum(mask * value, axis=(0, 1))) / total
        centered = value - mean
        spread = lax.optimization_barrier(jnp.sum(mask * centered * centered, axis=(0, 1))) / total
        return centered * lax.rsqrt(spread + EPS) * gain + bias

    def forward(source, reducer, offseter, deformer, expander, narrower, convolver, widener, inner_gains, inner_biases, broad_gains, broad_biases):

        def deform_section(item):
            field, height, width = item
            columns = gather_taps(field, height, width)
            offsets = low_back(jnp.dot(columns, offseter, precision=HIGH))
            sampled = low_back(low(sample(field, offsets, height, width)))
            return low_back(jnp.dot(sampled, deformer, precision=HIGH))

        def plain_section(item):
            field, height, width = item
            columns = gather_taps(field, height, width)
            return low_back(jnp.dot(columns, convolver, precision=HIGH))
        first = low_back(inward(source, reducer))
        inner = low(jax.nn.silu(normalize(first, inner_gains[0], inner_biases[0])))
        middle = lax.map(jax.checkpoint(deform_section), (inner, heights, widths))
        hidden = low(jax.nn.silu(normalize(middle, inner_gains[1], inner_biases[1])))
        widened = low_back(outward(hidden, expander))
        between = low(jax.nn.silu(normalize(widened, broad_gains[0], broad_biases[0]) + source))
        second = low_back(inward(between, narrower))
        narrow = low(jax.nn.silu(normalize(second, inner_gains[2], inner_biases[2])))
        spatial = lax.map(jax.checkpoint(plain_section), (narrow, heights, widths))
        mixed = low(jax.nn.silu(normalize(spatial, inner_gains[3], inner_biases[3])))
        final = low_back(outward(mixed, widener))
        return mask * jax.nn.silu(normalize(final, broad_gains[1], broad_biases[1]) + between)
    primals = (images.astype(jnp.float32), reducer.astype(jnp.float32), offseter.astype(jnp.float32), deformer.astype(jnp.float32), expander.astype(jnp.float32), narrower.astype(jnp.float32), convolver.astype(jnp.float32), widener.astype(jnp.float32), inner_gains, inner_biases, broad_gains, broad_biases)
    result, pullback = jax.vjp(forward, *primals)
    grads = pullback(cotangent.astype(jnp.float32))
    return (result.astype(jnp.bfloat16), grads[0].astype(jnp.bfloat16), grads[1], grads[2], grads[3], grads[4], grads[5], grads[6], grads[7], grads[8], grads[9], grads[10], grads[11])
```

```python
import functools

import jax
import jax.numpy as jnp
from jax import lax
from jax.experimental import pallas as pl
from jax.experimental.pallas import tpu as pltpu
from jax.sharding import PartitionSpec as P

CHANNELS = 2048
INNER = 512
TAPS = 9
SLOTS = 2
SHORT = 4
LONG = 36
PIXELS = 144
ROWS = SLOTS * PIXELS
OFFSETS = 2 * TAPS
EPS = 1e-05
BF = jnp.bfloat16
F32 = jnp.float32
MESH = pl.DeviceIdType.MESH
NN = (((1,), (0,)), ((), ()))
NT = (((1,), (1,)), ((), ()))
TN = (((0,), (0,)), ((), ()))
INPUTS = [
    "counts",
    "orient",
    "ig",
    "ib",
    "bg",
    "bb",
    "images_h",
    "cot_h",
    "red_h",
    "off_h",
    "def_h",
    "exp_h",
    "nar_h",
    "con_h",
    "wid_h",
]
OUTPUTS = [
    "out_h",
    "grad_h",
    "g_red",
    "g_off",
    "g_def",
    "g_exp",
    "g_nar",
    "g_con",
    "g_wid",
    "g_ig",
    "g_ib",
    "g_bg",
    "g_bb",
]


def mm(left, right, dims):
    return lax.dot_general(left, right, dims, preferred_element_type=F32)


def sigmoid(value):
    return 0.5 * jnp.tanh(0.5 * value) + 0.5


def fold(value):
    return jnp.sum(value.reshape(value.shape[0] // 8, 8, value.shape[1]), axis=0)


def total_row(value):
    return jnp.sum(value, axis=0, keepdims=True)


def scratch(dp, outer):
    vmem = pltpu.VMEM
    dma = pltpu.SemaphoreType.DMA
    return dict(
        images=vmem((ROWS, CHANNELS), BF),
        cot=vmem((ROWS, CHANNELS), BF),
        red=vmem((CHANNELS, INNER), BF),
        off=vmem((TAPS * INNER, OFFSETS), BF),
        dfm=vmem((TAPS * INNER, INNER), BF),
        exp=vmem((CHANNELS, INNER), BF),
        nar=vmem((CHANNELS, INNER), BF),
        con=vmem((TAPS * INNER, INNER), BF),
        wid=vmem((CHANNELS, INNER), BF),
        a1=vmem((ROWS, INNER), F32),
        a2=vmem((ROWS, INNER), F32),
        b1=vmem((ROWS, INNER), F32),
        b2=vmem((ROWS, INNER), F32),
        acc=vmem((ROWS, INNER), F32),
        a3=vmem((ROWS, CHANNELS), F32),
        b3=vmem((ROWS, CHANNELS), F32),
        up=vmem((ROWS, CHANNELS), F32),
        inner=vmem((ROWS, INNER), BF),
        hidden=vmem((ROWS, INNER), BF),
        narrow=vmem((ROWS, INNER), BF),
        mixed=vmem((ROWS, INNER), BF),
        dn=vmem((ROWS, INNER), BF),
        turned=vmem((ROWS, INNER), BF),
        between=vmem((ROWS, CHANNELS), BF),
        dwide=vmem((ROWS, CHANNELS), BF),
        obuf=vmem((ROWS, CHANNELS), BF),
        samp=vmem((TAPS, ROWS, INNER), BF),
        cols=vmem((TAPS, ROWS, INNER), BF),
        wmat=vmem((SLOTS, TAPS, PIXELS, PIXELS), BF),
        tmat=vmem((SLOTS, TAPS, PIXELS, PIXELS), BF),
        geo=vmem((SLOTS, 2, PIXELS, PIXELS), jnp.int32),
        frac=vmem((ROWS, OFFSETS), F32),
        doff=vmem((ROWS, OFFSETS), F32),
        ogt=vmem((OFFSETS, TAPS * INNER), F32),
        stage=vmem((2, 512, 512), F32),
        stn=vmem((4, 2, INNER), F32),
        stw=vmem((2, 2, CHANNELS), F32),
        rxn1=vmem((8, dp, 2, INNER), F32),
        rxn2=vmem((8, outer, 2, INNER), F32),
        rxw1=vmem((4, dp, 2, CHANNELS), F32),
        rxw2=vmem((4, outer, 2, CHANNELS), F32),
        load_sem=dma((9,)),
        stage_sem=dma((2,)),
        out_sem=dma((3,)),
        send1=dma((12,)),
        recv1=dma((12,)),
        send2=dma((12,)),
        recv2=dma((12,)),
    )


def kernel(dp, outer, names, *refs):
    r = dict(zip(names, refs))
    me = lax.axis_index("dp")
    mine = lax.axis_index("outer")
    counts, orient = r["counts"], r["orient"]

    loads = {}
    for place, (source, target) in enumerate(
        (
            ("images_h", "images"),
            ("red_h", "red"),
            ("off_h", "off"),
            ("def_h", "dfm"),
            ("exp_h", "exp"),
            ("nar_h", "nar"),
            ("con_h", "con"),
            ("wid_h", "wid"),
            ("cot_h", "cot"),
        )
    ):
        loads[target] = pltpu.make_async_copy(r[source], r[target], r["load_sem"].at[place])
        loads[target].start()

    barrier = pltpu.get_barrier_semaphore()
    for step in range(1, dp):
        pl.semaphore_signal(
            barrier, inc=1, device_id=(lax.rem(me + step, dp), mine), device_id_type=MESH
        )
    for step in range(1, outer):
        pl.semaphore_signal(
            barrier, inc=1, device_id=(me, lax.rem(mine + step, outer)), device_id_type=MESH
        )

    def images_of(first, second):
        return counts[first * outer + second].astype(F32)

    near = jnp.zeros((dp, 1), F32)
    line = lax.broadcasted_iota(jnp.int32, (dp, 1), 0)
    for place in range(dp):
        near = near + jnp.where(line == place, images_of(place, mine), 0.0)
    near = near * float(PIXELS)
    far = jnp.zeros((outer, 1), F32)
    line = lax.broadcasted_iota(jnp.int32, (outer, 1), 0)
    for place in range(outer):
        group = images_of(0, place)
        for other in range(1, dp):
            group = group + images_of(other, place)
        far = far + jnp.where(line == place, group, 0.0)
    far = far * float(PIXELS)
    near_total = total_row(near)
    total = total_row(far)
    held = images_of(me, mine)
    live1 = held - 1.0
    local = held * float(PIXELS)

    def sweep(body, init):
        def step(i, carry):
            lv = jnp.where(i < 3, 1.0, live1)
            for j in range(3):
                carry = body(pl.ds(pl.multiple_of(i * 48 + j * 16, 16), 16), lv, carry)
            return carry

        return lax.fori_loop(0, 6, step, init)

    def several(count, count_bytes_of, sem):
        view = count_bytes_of.at[pl.ds(0, count)]
        return pltpu.make_async_copy(view, view, sem)

    pending = []

    def exchange(number, rx1, rx2, forward):
        for step in range(1, dp):
            pltpu.make_async_remote_copy(
                src_ref=rx1.at[me],
                dst_ref=rx1.at[me],
                send_sem=r["send1"].at[number],
                recv_sem=r["recv1"].at[number],
                device_id=(lax.rem(me + step, dp), mine),
                device_id_type=MESH,
            ).start()
        pending.append((dp - 1, rx1, r["send1"].at[number]))
        several(dp - 1, rx1, r["recv1"].at[number]).wait()
        rx2[mine] = merge(rx1, near, near_total, forward)
        for step in range(1, outer):
            pltpu.make_async_remote_copy(
                src_ref=rx2.at[mine],
                dst_ref=rx2.at[mine],
                send_sem=r["send2"].at[number],
                recv_sem=r["recv2"].at[number],
                device_id=(me, lax.rem(mine + step, outer)),
                device_id_type=MESH,
            ).start()
        pending.append((outer - 1, rx2, r["send2"].at[number]))
        several(outer - 1, rx2, r["recv2"].at[number]).wait()
        return merge(rx2, far, total, forward)

    def merge(rx, sizes, size, forward):
        first = rx[:, 0, :]
        second = rx[:, 1, :]
        if forward:
            summed = total_row(first)
            apart = first / sizes - summed / size
            spread = total_row(second + sizes * apart * apart)
            return jnp.concatenate([summed, spread], axis=0)
        return jnp.concatenate([total_row(first), total_row(second)], axis=0)

    def norm_stats(ref, width, number, rx1, rx2, st):
        for start in range(0, width, 512):
            cs = pl.ds(start, 512)
            zero = jnp.zeros((8, 512), F32)
            summed = total_row(sweep(lambda rs, lv, c: c + lv * fold(ref[rs, cs]), zero))
            mean = summed / local

            def squares(rs, lv, carry):
                apart = ref[rs, cs] - mean
                return carry + lv * fold(apart * apart)

            spread = total_row(sweep(squares, zero))
            rx1[me, 0:1, cs] = summed
            rx1[me, 1:2, cs] = spread
        both = exchange(number, rx1, rx2, True)
        st[0:1, :] = both[0:1] / total
        st[1:2, :] = lax.rsqrt(both[1:2] / total + EPS)

    def norm_silu(ref, st, gain, bias, out):
        mean, scale = st[0:1, :], st[1:2, :]
        steep = scale * gain

        def body(rs, lv, carry):
            z = (ref[rs, :] - mean) * steep + bias
            out[rs, :] = (z * sigmoid(z)).astype(BF)
            return carry

        sweep(body, 0)

    def narrow_cotangent(ref, st, gain, bias, number, place):
        acc = r["acc"]
        mean, scale = st[0:1, :], st[1:2, :]

        def body(rs, lv, carry):
            xhat = (ref[rs, :] - mean) * scale
            z = xhat * gain + bias
            sg = sigmoid(z)
            g = acc[rs, :] * (sg * (1.0 + z * (1.0 - sg)))
            acc[rs, :] = g
            return carry[0] + fold(g), carry[1] + fold(g * xhat)

        zero = jnp.zeros((8, INNER), F32)
        summed, paired = sweep(body, (zero, zero))
        rx1, rx2 = r["rxn1"].at[number], r["rxn2"].at[number]
        rx1[me, 0:1, :] = total_row(summed)
        rx1[me, 1:2, :] = total_row(paired)
        both = exchange(number, rx1, rx2, False)
        r["g_ib"][place : place + 1, :] = both[0:1]
        r["g_ig"][place : place + 1, :] = both[1:2]
        steep = scale * gain
        lift, tilt = both[0:1] / total, both[1:2] / total

        def back(rs, lv, carry):
            xhat = (ref[rs, :] - mean) * scale
            r["dn"][rs, :] = (steep * (acc[rs, :] - lv * (lift + xhat * tilt))).astype(BF)
            return carry

        sweep(back, 0)

    def wide_back(ref, st, gain, both):
        for start in range(0, CHANNELS, 512):
            cs = pl.ds(start, 512)
            mean, scale = st[0:1, cs], st[1:2, cs]
            steep = scale * gain[:, start : start + 512]
            lift = both[0:1, start : start + 512] / total
            tilt = both[1:2, start : start + 512] / total

            def back(rs, lv, carry):
                xhat = (ref[rs, cs] - mean) * scale
                r["dwide"][rs, cs] = (steep * (r["up"][rs, cs] - lv * (lift + xhat * tilt))).astype(BF)
                return carry

            sweep(back, 0)

    def partial_tiles(count, left_of, right, target):
        def step(t, carry):
            slot = lax.rem(t, 2)

            @pl.when(t >= 2)
            def _():
                pltpu.make_async_copy(
                    r["stage"].at[slot], target.at[pl.ds(0, 512)], r["stage_sem"].at[slot]
                ).wait()

            r["stage"][slot] = mm(left_of(t), right[...], TN)
            pltpu.make_async_copy(
                r["stage"].at[slot],
                target.at[pl.ds(pl.multiple_of(t * 512, 512), 512)],
                r["stage_sem"].at[slot],
            ).start()
            return carry

        lax.fori_loop(0, count, step, 0)
        for slot in range(2):
            pltpu.make_async_copy(
                r["stage"].at[slot], target.at[pl.ds(0, 512)], r["stage_sem"].at[slot]
            ).wait()

    def column(ref):
        return lambda t: ref[:, pl.ds(pl.multiple_of(t * 512, 512), 512)]

    def tap(ref, k):
        return ref[pl.ds(pl.multiple_of(k * INNER, INNER), INNER), :]

    def slot_rows(s):
        return pl.ds(s * PIXELS, PIXELS)

    images, between, acc, up = r["images"], r["between"], r["acc"], r["up"]
    stn, stw = r["stn"], r["stw"]
    ig = [r["ig"][i : i + 1, :] for i in range(4)]
    ib = [r["ib"][i : i + 1, :] for i in range(4)]
    bg = [r["bg"][i : i + 1, :] for i in range(2)]
    bb = [r["bb"][i : i + 1, :] for i in range(2)]

    def narrow_stats(ref, number):
        norm_stats(
            ref, INNER, number, r["rxn1"].at[number], r["rxn2"].at[number], stn.at[number]
        )

    def wide_stats(ref, number):
        norm_stats(
            ref, CHANNELS, 8 + number, r["rxw1"].at[number], r["rxw2"].at[number], stw.at[number]
        )

    for s in range(SLOTS):
        level = orient[s]
        q = lax.broadcasted_iota(jnp.int32, (PIXELS, PIXELS), 1)
        p = lax.broadcasted_iota(jnp.int32, (PIXELS, PIXELS), 0)

        def place_of(at):
            long_row = (at >= 36).astype(jnp.int32)
            long_row = long_row + (at >= 72).astype(jnp.int32) + (at >= 108).astype(jnp.int32)
            row = jnp.where(level == 0, long_row, lax.shift_right_logical(at, 2))
            return row, at - row * (LONG - level * (LONG - SHORT))

        row_q, col_q = place_of(q)
        row_p, col_p = place_of(p)
        r["geo"][s, 0] = row_q - row_p
        r["geo"][s, 1] = col_q - col_p

        def hot(k, carry, s=s):
            down = 2 * (k // 3) - 2
            across = 2 * lax.rem(k, 3) - 2
            hit = (r["geo"][s, 0] == down) & (r["geo"][s, 1] == across)
            r["tmat"][s, k] = jnp.where(hit, 1.0, 0.0).astype(BF)
            return carry

        lax.fori_loop(0, TAPS, hot, 0)

    loads["images"].wait()
    loads["red"].wait()
    r["a1"][...] = mm(images[...], r["red"][...], NN)
    pl.semaphore_wait(barrier, dp - 1 + outer - 1)
    narrow_stats(r["a1"], 0)
    norm_silu(r["a1"], stn.at[0], ig[0], ib[0], r["inner"])

    loads["off"].wait()
    inner = r["inner"]
    lane = lax.broadcasted_iota(jnp.int32, (PIXELS, OFFSETS), 1)
    for s in range(SLOTS):
        def gather(k, carry, s=s):
            col = mm(r["tmat"][s, k], inner[slot_rows(s), :], NN).astype(BF)
            return carry + mm(col, tap(r["off"], k), NN)

        offsets = lax.fori_loop(0, TAPS, gather, jnp.zeros((PIXELS, OFFSETS), F32))
        r["frac"][slot_rows(s), :] = sigmoid(offsets)

    def bilinear(s, k):
        down = 2 * (k // 3) - 2
        across = 2 * lax.rem(k, 3) - 2
        frac = r["frac"][slot_rows(s), :]
        fy = jnp.sum(jnp.where(lane == 2 * k, frac, 0.0), axis=1, keepdims=True)
        fx = jnp.sum(jnp.where(lane == 2 * k + 1, frac, 0.0), axis=1, keepdims=True)
        dr, dc = r["geo"][s, 0], r["geo"][s, 1]
        in_y = (dr == down, dr == down + 1)
        in_x = (dc == across, dc == across + 1)
        ay = jnp.where(in_y[0], 1.0 - fy, jnp.where(in_y[1], fy, 0.0))
        ax = jnp.where(in_x[0], 1.0 - fx, jnp.where(in_x[1], fx, 0.0))
        return fy, fx, ay, ax, in_y, in_x

    loads["dfm"].wait()
    acc[...] = jnp.zeros((ROWS, INNER), F32)

    def sample(k, carry):
        for s in range(SLOTS):
            _, _, ay, ax, _, _ = bilinear(s, k)
            weight = (ay * ax).astype(BF)
            r["wmat"][s, k] = weight
            r["samp"][k, slot_rows(s), :] = mm(weight, inner[slot_rows(s), :], NN).astype(BF)
        acc[...] += mm(r["samp"][k], tap(r["dfm"], k), NN)
        return carry

    lax.fori_loop(0, TAPS, sample, 0)
    r["a2"][...] = acc[...]
    narrow_stats(r["a2"], 1)
    norm_silu(r["a2"], stn.at[1], ig[1], ib[1], r["hidden"])

    def widen(source, weight, target):
        def step(n, carry):
            rows = pl.ds(pl.multiple_of(n * 512, 512), 512)
            target[:, rows] = mm(source[...], weight[rows, :], NT)
            return carry

        lax.fori_loop(0, CHANNELS // 512, step, 0)

    loads["exp"].wait()
    widen(r["hidden"], r["exp"], r["a3"])
    wide_stats(r["a3"], 0)
    for start in range(0, CHANNELS, 512):
        cs = pl.ds(start, 512)
        mean = stw[0, 0:1, cs]
        steep = stw[0, 1:2, cs] * bg[0][:, start : start + 512]
        bias = bb[0][:, start : start + 512]

        def join(rs, lv, carry):
            z = (r["a3"][rs, cs] - mean) * steep + bias + images[rs, cs].astype(F32)
            between[rs, cs] = (z * sigmoid(z)).astype(BF)
            return carry

        sweep(join, 0)

    loads["nar"].wait()
    r["b1"][...] = mm(between[...], r["nar"][...], NN)
    narrow_stats(r["b1"], 2)
    norm_silu(r["b1"], stn.at[2], ig[2], ib[2], r["narrow"])

    loads["con"].wait()
    acc[...] = jnp.zeros((ROWS, INNER), F32)

    def convolve(k, carry):
        for s in range(SLOTS):
            r["cols"][k, slot_rows(s), :] = mm(
                r["tmat"][s, k], r["narrow"][slot_rows(s), :], NN
            ).astype(BF)
        acc[...] += mm(r["cols"][k], tap(r["con"], k), NN)
        return carry

    lax.fori_loop(0, TAPS, convolve, 0)
    r["b2"][...] = acc[...]
    narrow_stats(r["b2"], 3)
    norm_silu(r["b2"], stn.at[3], ig[3], ib[3], r["mixed"])

    loads["wid"].wait()
    widen(r["mixed"], r["wid"], r["b3"])
    wide_stats(r["b3"], 1)

    def wide_cotangent(number, ref, st, gain, bias, cotangent):
        rx1, rx2 = r["rxw1"].at[number], r["rxw2"].at[number]
        for start in range(0, CHANNELS, 512):
            cs = pl.ds(start, 512)
            mean, scale = st[0:1, cs], st[1:2, cs]
            gn, bs = gain[:, start : start + 512], bias[:, start : start + 512]

            def body(rs, lv, carry):
                xhat = (ref[rs, cs] - mean) * scale
                g = cotangent(rs, cs, lv, xhat * gn + bs)
                up[rs, cs] = g
                return carry[0] + fold(g), carry[1] + fold(g * xhat)

            zero = jnp.zeros((8, 512), F32)
            summed, paired = sweep(body, (zero, zero))
            rx1[me, 0:1, cs] = total_row(summed)
            rx1[me, 1:2, cs] = total_row(paired)
        return exchange(8 + number, rx1, rx2, False)

    loads["cot"].wait()

    def last(rs, cs, lv, pre):
        z = pre + between[rs, cs].astype(F32)
        sg = sigmoid(z)
        r["obuf"][rs, cs] = (lv * (z * sg)).astype(BF)
        return r["cot"][rs, cs].astype(F32) * (lv * (sg * (1.0 + z * (1.0 - sg))))

    both = wide_cotangent(2, r["b3"], stw.at[1], bg[1], bb[1], last)
    out_copy = pltpu.make_async_copy(r["obuf"], r["out_h"], r["out_sem"].at[0])
    out_copy.start()
    r["g_bb"][1:2, :] = both[0:1]
    r["g_bg"][1:2, :] = both[1:2]
    wide_back(r["b3"], stw.at[1], bg[1], both)

    acc[...] = mm(r["dwide"][...], r["wid"][...], NN)
    narrow_cotangent(r["b2"], stn.at[3], ig[3], ib[3], 4, 3)
    partial_tiles(CHANNELS // 512, column(r["dwide"]), r["mixed"], r["g_wid"])

    acc[...] = jnp.zeros((ROWS, INNER), F32)

    def spread(k, carry):
        for s in range(SLOTS):
            r["turned"][slot_rows(s), :] = mm(
                r["tmat"][s, TAPS - 1 - k], r["dn"][slot_rows(s), :], NN
            ).astype(BF)
        acc[...] += mm(r["turned"][...], tap(r["con"], k), NT)
        return carry

    lax.fori_loop(0, TAPS, spread, 0)
    partial_tiles(TAPS, lambda t: r["cols"][t], r["dn"], r["g_con"])
    narrow_cotangent(r["b1"], stn.at[2], ig[2], ib[2], 5, 2)

    def add_back(n, carry):
        rows = pl.ds(pl.multiple_of(n * 512, 512), 512)
        up[:, rows] += mm(r["dn"][...], r["nar"][rows, :], NT)
        return carry

    lax.fori_loop(0, CHANNELS // 512, add_back, 0)
    partial_tiles(CHANNELS // 512, column(between), r["dn"], r["g_nar"])

    def first(rs, cs, lv, pre):
        z = pre + images[rs, cs].astype(F32)
        sg = sigmoid(z)
        return up[rs, cs] * (sg * (1.0 + z * (1.0 - sg)))

    both = wide_cotangent(3, r["a3"], stw.at[0], bg[0], bb[0], first)
    r["g_bb"][0:1, :] = both[0:1]
    r["g_bg"][0:1, :] = both[1:2]
    wide_back(r["a3"], stw.at[0], bg[0], both)

    acc[...] = mm(r["dwide"][...], r["exp"][...], NN)
    narrow_cotangent(r["a2"], stn.at[1], ig[1], ib[1], 6, 1)
    partial_tiles(CHANNELS // 512, column(r["dwide"]), r["hidden"], r["g_exp"])

    acc[...] = jnp.zeros((ROWS, INNER), F32)
    r["doff"][...] = jnp.zeros((ROWS, OFFSETS), F32)

    def unsample(k, carry):
        r["turned"][...] = mm(r["dn"][...], tap(r["dfm"], k), NT).astype(BF)
        for s in range(SLOTS):
            rs = slot_rows(s)
            grad = r["turned"][rs, :]
            pairs = mm(grad, inner[rs, :], NT)
            fy, fx, ay, ax, in_y, in_x = bilinear(s, k)
            slope_y = jnp.where(in_y[1], ax, 0.0) - jnp.where(in_y[0], ax, 0.0)
            slope_x = jnp.where(in_x[1], ay, 0.0) - jnp.where(in_x[0], ay, 0.0)
            to_y = jnp.sum(pairs * slope_y, axis=1, keepdims=True) * (fy * (1.0 - fy))
            to_x = jnp.sum(pairs * slope_x, axis=1, keepdims=True) * (fx * (1.0 - fx))
            r["doff"][rs, :] += jnp.where(lane == 2 * k, to_y, 0.0) + jnp.where(
                lane == 2 * k + 1, to_x, 0.0
            )
            acc[rs, :] += mm(r["wmat"][s, k], grad, TN)
        return carry

    lax.fori_loop(0, TAPS, unsample, 0)
    partial_tiles(TAPS, lambda t: r["samp"][t], r["dn"], r["g_def"])

    def untap(k, carry):
        columns = pl.ds(pl.multiple_of(k * INNER, INNER), INNER)
        share = jnp.zeros((OFFSETS, INNER), F32)
        for s in range(SLOTS):
            rs = slot_rows(s)
            moved = mm(r["tmat"][s, TAPS - 1 - k], r["doff"][rs, :].astype(BF), NN).astype(BF)
            acc[rs, :] += mm(moved, tap(r["off"], k), NT)
            share = share + mm(moved, inner[rs, :], TN)
        r["ogt"][:, columns] = share
        return carry

    lax.fori_loop(0, TAPS, untap, 0)
    off_copy = pltpu.make_async_copy(r["ogt"], r["g_off"], r["out_sem"].at[1])
    off_copy.start()
    narrow_cotangent(r["a1"], stn.at[0], ig[0], ib[0], 7, 0)

    out_copy.wait()

    def finish(n, carry):
        rows = pl.ds(pl.multiple_of(n * 512, 512), 512)
        r["obuf"][:, rows] = (up[:, rows] + mm(r["dn"][...], r["red"][rows, :], NT)).astype(BF)
        return carry

    lax.fori_loop(0, CHANNELS // 512, finish, 0)
    grad_copy = pltpu.make_async_copy(r["obuf"], r["grad_h"], r["out_sem"].at[2])
    grad_copy.start()
    partial_tiles(CHANNELS // 512, column(images), r["dn"], r["g_red"])
    off_copy.wait()
    grad_copy.wait()
    for count, ref, sem in pending:
        several(count, ref, sem).wait()


def per_device(
    images,
    counts,
    orientation,
    cotangent,
    reducer,
    offseter,
    deformer,
    expander,
    narrower,
    convolver,
    widener,
    inner_gains,
    inner_biases,
    broad_gains,
    broad_biases,
):
    dp, outer = lax.axis_size("dp"), lax.axis_size("outer")
    buffers = scratch(dp, outer)
    names = INPUTS + OUTPUTS + list(buffers)
    smem = pl.BlockSpec(memory_space=pltpu.SMEM)
    vmem = pl.BlockSpec(memory_space=pltpu.VMEM)
    far = pl.BlockSpec(memory_space=pl.ANY)
    shape = jax.ShapeDtypeStruct
    outs = pl.pallas_call(
        functools.partial(kernel, dp, outer, names),
        out_shape=[
            shape((ROWS, CHANNELS), BF),
            shape((ROWS, CHANNELS), BF),
            shape((CHANNELS, INNER), F32),
            shape((OFFSETS, TAPS * INNER), F32),
            shape((TAPS * INNER, INNER), F32),
            shape((CHANNELS, INNER), F32),
            shape((CHANNELS, INNER), F32),
            shape((TAPS * INNER, INNER), F32),
            shape((CHANNELS, INNER), F32),
            shape((4, INNER), F32),
            shape((4, INNER), F32),
            shape((2, CHANNELS), F32),
            shape((2, CHANNELS), F32),
        ],
        in_specs=[smem] * 2 + [vmem] * 4 + [far] * 9,
        out_specs=[far] * 9 + [vmem] * 4,
        scratch_shapes=list(buffers.values()),
        compiler_params=pltpu.CompilerParams(
            collective_id=0, has_side_effects=True, vmem_limit_bytes=60 * 1024 * 1024
        ),
        name="chain",
    )(
        counts,
        orientation,
        inner_gains,
        inner_biases,
        broad_gains,
        broad_biases,
        images.reshape(ROWS, CHANNELS),
        cotangent.reshape(ROWS, CHANNELS),
        reducer,
        offseter,
        deformer,
        expander,
        narrower,
        convolver,
        widener,
    )
    out, grad, g_red, g_off, g_def, g_exp, g_nar, g_con, g_wid, g_ig, g_ib, g_bg, g_bb = outs
    parts = [
        lax.psum_scatter(part, "dp", scatter_dimension=0, tiled=True)
        for part in (g_red, g_off.T, g_def, g_exp, g_nar, g_con, g_wid)
    ]
    parts = lax.psum(parts, "outer")
    place = lax.axis_index("dp")
    inner_share, broad_share = INNER // dp, CHANNELS // dp
    return (
        out.reshape(SLOTS, PIXELS, CHANNELS),
        grad.reshape(SLOTS, PIXELS, CHANNELS),
        *parts,
        lax.dynamic_slice_in_dim(g_ig, place * inner_share, inner_share, 1),
        lax.dynamic_slice_in_dim(g_ib, place * inner_share, inner_share, 1),
        lax.dynamic_slice_in_dim(g_bg, place * broad_share, broad_share, 1),
        lax.dynamic_slice_in_dim(g_bb, place * broad_share, broad_share, 1),
    )


def solution(mesh):
    spread = P(("dp", "outer"), None, None)
    in_specs = (spread, P(), P(("dp", "outer")), spread) + (P(),) * 11
    out_specs = (spread, spread) + (P("dp", None),) * 7 + (P(None, "dp"),) * 4
    return jax.shard_map(
        per_device, mesh=mesh, in_specs=in_specs, out_specs=out_specs, check_vma=False
    )
```

```python
import functools
import math
import types

import jax
import jax.numpy as jnp
from jax import lax
from jax.experimental import pallas as pl
from jax.experimental.pallas import tpu as pltpu
from jax.sharding import PartitionSpec as P

CHANNELS = 2048
INNER = 512
TAPS = 9
SLOTS = 2
SHORT = 4
LONG = 36
PIXELS = 144
ROWS = SLOTS * PIXELS
OFFSETS = 2 * TAPS
EPS = 1e-05
BF = jnp.bfloat16
F32 = jnp.float32
MESH = pl.DeviceIdType.MESH
NN = (((1,), (0,)), ((), ()))
NT = (((1,), (1,)), ((), ()))
TN = (((0,), (0,)), ((), ()))


def mm(left, right, dims):
    return lax.dot_general(left, right, dims, preferred_element_type=F32)


def sigmoid(value):
    return 0.5 * jnp.tanh(0.5 * value) + 0.5


def fold(value):
    return jnp.sum(value.reshape(value.shape[0] // 8, 8, value.shape[1]), axis=0)


def total_row(value):
    return jnp.sum(value, axis=0, keepdims=True)


def layout(dp):
    chips = dp // 2
    bits = chips.bit_length() - 1
    wide = CHANNELS // dp
    deep = TAPS * INNER // dp
    taps = max(
        -(-(2 * deep * chip % INNER + 2 * deep) // INNER) for chip in range(chips)
    )
    return chips, bits, wide, deep, taps


def scratch(dp, outer):
    vmem = pltpu.VMEM
    dma = pltpu.SemaphoreType.DMA
    chips, bits, wide, deep, taps = layout(dp)
    everyone = dp * outer
    group = min(chips, 4)
    return dict(
        images=vmem((ROWS, CHANNELS), BF),
        between=vmem((ROWS, CHANNELS), BF),
        dwide=vmem((ROWS, CHANNELS), BF),
        obuf=vmem((ROWS, CHANNELS), BF),
        redwid=vmem((CHANNELS, INNER), BF),
        exp=vmem((CHANNELS, INNER), BF),
        nar=vmem((CHANNELS, INNER), BF),
        dfmcon=vmem((TAPS * INNER, INNER), BF),
        off=vmem((TAPS * INNER, OFFSETS), BF),
        a1=vmem((ROWS, INNER), F32),
        a2=vmem((ROWS, INNER), F32),
        b1=vmem((ROWS, INNER), F32),
        b2=vmem((ROWS, INNER), F32),
        acc=vmem((ROWS, INNER), F32),
        a3=vmem((CHANNELS // 512, ROWS, 512), F32),
        b3=vmem((CHANNELS // 512, ROWS, 512), F32),
        up=vmem((CHANNELS // 512, ROWS, 512), F32),
        inner=vmem((ROWS, INNER), BF),
        hidden=vmem((ROWS, INNER), BF),
        narrow=vmem((ROWS, INNER), BF),
        mixed=vmem((ROWS, INNER), BF),
        dn=vmem((ROWS, INNER), BF),
        turned=vmem((ROWS, INNER), BF),
        wmat=vmem((SLOTS, TAPS, PIXELS, PIXELS), BF),
        tmat=vmem((2, TAPS, PIXELS, PIXELS), BF),
        geo=vmem((2, 2, PIXELS, PIXELS), jnp.int32),
        frac=vmem((ROWS, OFFSETS), F32),
        doff=vmem((ROWS, OFFSETS), F32),
        stn=vmem((4, 2, INNER), F32),
        stw=vmem((2, 2, CHANNELS), F32),
        rxn=vmem((8, everyone, 2, INNER), F32),
        rxw1=vmem((4, dp, 2, CHANNELS), F32),
        rxw2=vmem((4, outer, 2, CHANNELS), F32),
        pool=vmem((3, chips, wide, INNER), F32),
        corel=vmem((chips, wide, INNER), F32),
        land=vmem((2, 2, chips - 1, wide, INNER // 2), F32),
        zwide=vmem((2, 3, wide, INNER), F32),
        tiny=vmem((2, chips, SLOTS, 24, PIXELS), F32),
        give=vmem((ROWS, INNER), F32),
        taken=vmem((group, ROWS, INNER), F32),
        drawn=vmem((2, ROWS, INNER), F32),
        yall=vmem((group * ROWS, INNER), BF),
        xall=vmem((group * ROWS, INNER), BF),
        grad=vmem((taps * INNER, INNER), F32),
        cored=vmem((deep, INNER), F32),
        zdeep=vmem((2, 2, deep // 2, INNER), F32),
        goff=vmem((24, taps * INNER), F32),
        coreo=vmem((24, taps * INNER), F32),
        zoff=vmem((2, 24, taps * INNER), F32),
        free=pltpu.SemaphoreType.REGULAR,
        load_sem=dma((11,)),
        out_sem=dma((2,)),
        res_sem=dma((7, 2)),
        xn_s=dma((8,)),
        xn_r=dma((8,)),
        xw_s=dma((4, 2)),
        xw_r=dma((4, 2)),
        core_s=dma((7,)),
        core_r=dma((7,)),
        step_s=dma((4, 2, bits)),
        step_r=dma((4, 2, bits)),
        give_sem=dma((4,)),
        take_sem=dma((3,)),
        ag_s=dma((4, 2, bits)),
        ag_r=dma((4, 2, bits)),
        tiny_s=dma((2,)),
        tiny_r=dma((2,)),
        z_s=dma((7, 2, 3)),
        z_r=dma((7, 2, 3)),
    )


def kernel(dp, outer, names, *refs):
    assert outer == 4
    r = types.SimpleNamespace(**dict(zip(names, refs)))
    chips, bits, wide, deep, taps = layout(dp)
    everyone = dp * outer
    me = lax.axis_index("dp")
    mine = lax.axis_index("outer")
    own = me * outer + mine
    core = lax.rem(me, 2)
    chip = lax.div(me, 2)
    sibling = (me + 1 - 2 * core, mine)
    inside = (mine == 1) | (mine == 2)
    outside = (mine == 0) | (mine == 3)
    counts, orient = r.counts, r.orient
    dma = pltpu.make_async_copy

    loads = types.SimpleNamespace()

    def load(place, source, target):
        copy = dma(source, target, r.load_sem.at[place])
        copy.start()
        return copy

    loads.images_h = load(0, r.images_h, r.images)
    loads.red_h = load(1, r.red_h, r.redwid)
    loads.off_h = load(2, r.off_h, r.off)
    loads.def_h = load(3, r.def_h, r.dfmcon)
    loads.exp_h = load(4, r.exp_h, r.exp)
    loads.nar_h = load(5, r.nar_h, r.nar)
    loads.cot_h = load(6, r.cot_h, r.dwide)

    def other(step):
        target = lax.rem(own + step, everyone)
        return lax.div(target, outer), lax.rem(target, outer)

    barrier = pltpu.get_barrier_semaphore()

    def greet(step, carry):
        pl.semaphore_signal(barrier, inc=1, device_id=other(step), device_id_type=MESH)
        return carry

    lax.fori_loop(1, everyone, greet, 0)

    def size(i, carry):
        sizes, near, far = carry
        row, place = lax.div(i, outer), lax.rem(i, outer)
        held = counts[i].astype(F32)
        here = jnp.where(place == mine, held, 0.0)

        def mark(count, at, value):
            line = lax.broadcasted_iota(jnp.int32, (count, 1), 0)
            return jnp.where(line == at, value, 0.0)

        return (
            sizes + mark(everyone, i, held),
            near + mark(dp, row, here),
            far + mark(outer, place, held),
        )

    zeros = tuple(jnp.zeros((count, 1), F32) for count in (everyone, dp, outer))
    sizes, near, far = (
        value * float(PIXELS) for value in lax.fori_loop(0, everyone, size, zeros)
    )
    near_total = total_row(near)
    total = total_row(far)
    held = counts[own].astype(F32)
    live1 = held - 1.0
    local = held * float(PIXELS)

    def sweep(body, init):
        def step(i, carry):
            lv = jnp.where(i < 3, 1.0, live1)
            for j in range(3):
                carry = body(pl.ds(pl.multiple_of(i * 48 + j * 16, 16), 16), lv, carry)
            return carry

        return lax.fori_loop(0, 6, step, init)

    def send(source, target, sent, received, device):
        pltpu.make_async_remote_copy(
            src_ref=source,
            dst_ref=target,
            send_sem=sent,
            recv_sem=received,
            device_id=device,
            device_id_type=MESH,
        ).start()

    def settle(view, sem):
        dma(view, view, sem).wait()

    waiting = {}

    def later(tag, view, sem, when=None):
        waiting.setdefault(tag, []).append((when, view, sem))

    def flush(tag):
        for when, view, sem in waiting.pop(tag, []):
            if when is None:
                settle(view, sem)
            else:
                pl.when(when)(functools.partial(settle, view, sem))

    def accumulate(target, source):
        rows = target.shape[0]
        step = math.gcd(rows, 32)

        def body(i, carry):
            rs = pl.ds(pl.multiple_of(i * step, 8), step)
            target[rs, :] += source[rs, :]
            return carry

        lax.fori_loop(0, rows // step, body, 0)

    def mix(target, one, two):
        rows = target.shape[0]
        step = math.gcd(rows, 32)

        def body(i, carry):
            rs = pl.ds(pl.multiple_of(i * step, 8), step)
            target[rs, :] = one[rs, :] + two[rs, :]
            return carry

        lax.fori_loop(0, rows // step, body, 0)

    def flip(value, bit):
        weight = 1 << bit
        return value + weight - 2 * weight * lax.rem(lax.div(value, weight), 2)

    def bit_of(value, bit):
        return lax.rem(lax.div(value, 1 << bit), 2)

    orders = [
        list(range(bits)),
        list(range(bits // 2, bits)) + list(range(bits // 2)),
    ]
    halves = [pl.ds(0, INNER // 2), pl.ds(INNER // 2, INNER // 2)]

    def merge(rx, counted, size, forward):
        first = rx[:, 0, :]
        second = rx[:, 1, :]
        if forward:
            summed = total_row(first)
            apart = first / counted - summed / size
            spread = total_row(second + counted * apart * apart)
            return jnp.concatenate([summed, spread], axis=0)
        return jnp.concatenate([total_row(first), total_row(second)], axis=0)

    def nothing():
        pass

    def share_narrow(number, forward, work):
        rx = r.rxn.at[number]

        def step(i, carry):
            send(rx.at[own], rx.at[own], r.xn_s.at[number], r.xn_r.at[number], other(i))
            return carry

        lax.fori_loop(1, everyone, step, 0)
        rest = rx.at[pl.ds(0, everyone - 1)]
        later("end", rest, r.xn_s.at[number])
        work()
        settle(rest, r.xn_r.at[number])
        return merge(rx, sizes, total, forward)

    def share_wide(number, forward, work, work_more):
        rx1, rx2 = r.rxw1.at[number], r.rxw2.at[number]
        for step in range(1, dp):
            send(
                rx1.at[me],
                rx1.at[me],
                r.xw_s.at[number, 0],
                r.xw_r.at[number, 0],
                (lax.rem(me + step, dp), mine),
            )
        rest = rx1.at[pl.ds(0, dp - 1)]
        later("end", rest, r.xw_s.at[number, 0])
        work()
        settle(rest, r.xw_r.at[number, 0])
        rx2[mine] = merge(rx1, near, near_total, forward)
        for step in range(1, outer):
            send(
                rx2.at[mine],
                rx2.at[mine],
                r.xw_s.at[number, 1],
                r.xw_r.at[number, 1],
                (me, lax.rem(mine + step, outer)),
            )
        rest = rx2.at[pl.ds(0, outer - 1)]
        later("end", rest, r.xw_s.at[number, 1])
        work_more()
        settle(rest, r.xw_r.at[number, 1])
        return merge(rx2, far, total, forward)

    def local_stats(ref, put, cs):
        zero = jnp.zeros((8, 512), F32)
        summed = total_row(sweep(lambda rs, lv, c: c + lv * fold(ref[rs, :]), zero))
        mean = summed / local

        def squares(rs, lv, carry):
            apart = ref[rs, :] - mean
            return carry + lv * fold(apart * apart)

        put[0:1, cs] = summed
        put[1:2, cs] = total_row(sweep(squares, zero))

    def keep_stats(both, st):
        st[0:1, :] = both[0:1] / total
        st[1:2, :] = lax.rsqrt(both[1:2] / total + EPS)

    def narrow_stats(ref, number, work=nothing):
        local_stats(ref, r.rxn.at[number, own], pl.ds(0, INNER))
        keep_stats(share_narrow(number, True, work), r.stn.at[number])

    blocks = [pl.ds(start, 512) for start in range(0, CHANNELS, 512)]

    def wide_stats(ref, number, work=nothing, work_more=nothing):
        for n, cs in enumerate(blocks):
            local_stats(ref.at[n], r.rxw1.at[number, me], cs)
        keep_stats(share_wide(number, True, work, work_more), r.stw.at[number])

    def norm_silu(ref, number, gain, bias, out, spread):
        st = r.stn.at[number]
        mean, scale = st[0:1, :], st[1:2, :]
        steep = scale * gain

        def body(rs, lv, carry):
            z = (ref[rs, :] - mean) * steep + bias
            value = (z * sigmoid(z)).astype(BF)
            out[rs, :] = value
            if spread:
                r.give[rs, :] = value.astype(F32)
            return carry

        sweep(body, 0)

    def narrow_cotangent(ref, place, gain, bias, number, spread, work=nothing):
        acc = r.acc
        st = r.stn.at[place]
        mean, scale = st[0:1, :], st[1:2, :]

        def body(rs, lv, carry):
            xhat = (ref[rs, :] - mean) * scale
            z = xhat * gain + bias
            sg = sigmoid(z)
            g = acc[rs, :] * (sg * (1.0 + z * (1.0 - sg)))
            acc[rs, :] = g
            return carry[0] + fold(g), carry[1] + fold(g * xhat)

        zero = jnp.zeros((8, INNER), F32)
        summed, paired = sweep(body, (zero, zero))
        put = r.rxn.at[number, own]
        put[0:1, :] = total_row(summed)
        put[1:2, :] = total_row(paired)
        both = share_narrow(number, False, work)
        r.g_ib[place : place + 1, :] = both[0:1]
        r.g_ig[place : place + 1, :] = both[1:2]
        steep = scale * gain
        lift, tilt = both[0:1] / total, both[1:2] / total

        def back(rs, lv, carry):
            xhat = (ref[rs, :] - mean) * scale
            value = (steep * (acc[rs, :] - lv * (lift + xhat * tilt))).astype(BF)
            r.dn[rs, :] = value
            if spread:
                r.give[rs, :] = value.astype(F32)
            return carry

        sweep(back, 0)

    def wide_cotangent(number, ref, place, gain, bias, cotangent, work=nothing, work_more=nothing):
        put = r.rxw1.at[number, me]
        st = r.stw.at[place]
        for n, cs in enumerate(blocks):
            mean, scale = st[0:1, cs], st[1:2, cs]
            gn, bs = gain[:, 512 * n : 512 * n + 512], bias[:, 512 * n : 512 * n + 512]

            def body(rs, lv, carry):
                xhat = (ref[n, rs, :] - mean) * scale
                g = cotangent(n, rs, cs, lv, xhat * gn + bs)
                r.up[n, rs, :] = g
                return carry[0] + fold(g), carry[1] + fold(g * xhat)

            zero = jnp.zeros((8, 512), F32)
            summed, paired = sweep(body, (zero, zero))
            put[0:1, cs] = total_row(summed)
            put[1:2, cs] = total_row(paired)
        both = share_wide(number, False, work, work_more)
        r.g_bb[place : place + 1, :] = both[0:1]
        r.g_bg[place : place + 1, :] = both[1:2]
        for n, cs in enumerate(blocks):
            mean, scale = st[0:1, cs], st[1:2, cs]
            span = slice(512 * n, 512 * n + 512)
            steep = scale * gain[:, span]
            lift, tilt = both[0:1, span] / total, both[1:2, span] / total

            def back(rs, lv, carry):
                xhat = (ref[n, rs, :] - mean) * scale
                value = steep * (r.up[n, rs, :] - lv * (lift + xhat * tilt))
                r.dwide[rs, cs] = value.astype(BF)
                return carry

            sweep(back, 0)

    def tap(ref, k):
        return ref[pl.ds(pl.multiple_of(k * INNER, INNER), INNER), :]

    def slot_rows(s):
        return pl.ds(s * PIXELS, PIXELS)

    def steps_of(k):
        return 2 * lax.div(k, 3) - 2, 2 * lax.rem(k, 3) - 2

    WID, CON, NAR, EXP, DEF, RED, OFF = range(7)
    nth = {WID: 0, NAR: 1, EXP: 2, RED: 3}
    result = {
        WID: r.g_wid,
        CON: r.g_con,
        NAR: r.g_nar,
        EXP: r.g_exp,
        DEF: r.g_def,
        RED: r.g_red,
        OFF: r.g_off,
    }
    pool, land, grad, far_blocks = r.pool, r.land, r.grad, r.far_blocks

    def z_parts(u):
        if u in nth:
            if u == RED:
                hold = [r.a3.at[i, pl.ds(0, wide)] for i in range(3)]
            else:
                hold = [r.zwide.at[nth[u] % 2, i] for i in range(3)]
            for hs in halves:
                yield tuple(ref.at[:, hs] for ref in hold) + (result[u].at[:, hs],)
        elif u == OFF:
            yield r.goff, r.zoff.at[0], r.zoff.at[1], result[u]
        else:
            for q in range(2):
                source = r.b3.at[(2 if u == DEF else 0) + q]
                if u == DEF:
                    first, second = (r.b1, r.a2) if q == 0 else (r.b2, r.a3.at[3])
                else:
                    first, second = r.zdeep.at[0, q], r.zdeep.at[1, q]
                rows = pl.ds(0, deep // 2)
                out = result[u].at[pl.ds(q * (deep // 2), deep // 2)]
                yield source.at[rows], first.at[rows], second.at[rows], out

    def z_sems(u, q, step):
        return r.z_s.at[u, q, step], r.z_r.at[u, q, step]

    def z1(u):
        for q, (source, first, second, out) in enumerate(z_parts(u)):
            sent, received = z_sems(u, q, 0)

            @pl.when(outside)
            def _():
                send(source, first, sent, received, (me, flip(mine, 0)))

            later(("z", u), source, sent, outside)

    def z2(u):
        for q, (source, first, second, out) in enumerate(z_parts(u)):
            sent, received = z_sems(u, q, 1)

            @pl.when(inside)
            def _():
                settle(first, z_sems(u, q, 0)[1])
                accumulate(source, first)
                send(source, second, sent, received, (me, 3 - mine))

            later(("z", u), source, sent, inside)

    def z3(u):
        for q, (source, first, second, out) in enumerate(z_parts(u)):
            sent, received = z_sems(u, q, 2)

            @pl.when(inside)
            def _():
                settle(second, z_sems(u, q, 1)[1])
                accumulate(second, source)
                send(second, first, sent, received, (me, flip(mine, 0)))
                dma(second, out, r.res_sem.at[u, q]).start()

            later(("zl", u), second, sent, inside)

    def z4(u):
        for q, (source, first, second, out) in enumerate(z_parts(u)):

            @pl.when(outside)
            def _():
                settle(first, z_sems(u, q, 2)[1])
                dma(first, out, r.res_sem.at[u, q]).start()

    def z_clear(u):
        flush(("z", u))
        flush(("zl", u))
        for q, (source, first, second, out) in enumerate(z_parts(u)):
            dma(first, out, r.res_sem.at[u, q]).wait()

    def wide_begin(u, left, right):
        p = nth[u] % 2
        flush("sib")
        flush(("keep", p))
        low = p + (2 - p) * core
        high = p + (2 - p) * (1 - core)

        def step(m, carry):
            block = left[:, pl.ds(pl.multiple_of(m * (2 * wide), 2 * wide), 2 * wide)]
            pool[low, m] = mm(block[:, :wide], right[...], TN)
            pool[high, m] = mm(block[:, wide:], right[...], TN)
            send(
                pool.at[2, m], r.corel.at[m], r.core_s.at[u], r.core_r.at[u], sibling
            )
            return carry

        lax.fori_loop(0, chips, step, 0)
        later("sib", r.corel, r.core_s.at[u])

    def piece(h, t, j, toward):
        value = 0
        for i, bit in enumerate(orders[h]):
            if i < t:
                part = bit_of(chip, bit)
            elif i == t:
                part = bit_of(toward, bit)
            else:
                part = (j >> (i - t - 1)) & 1
            value = value + part * (1 << bit)
        return value

    def step_place(u, h, t):
        first, count = chips - (chips >> t), chips >> (t + 1)
        p = nth[u] % 2
        sems = r.step_s.at[nth[u], h, t], r.step_r.at[nth[u], h, t]
        return p, first, count, sems, land.at[p, h, pl.ds(first, count)]

    def wide_send(u, t):
        for h in range(2):
            p, first, count, (sent, received), region = step_place(u, h, t)
            toward = flip(chip, orders[h][t])
            for j in range(count):
                send(
                    pool.at[p, piece(h, t, j, toward), :, halves[h]],
                    land.at[p, h, first + j],
                    sent,
                    received,
                    (2 * toward + core, mine),
                )
            later(("keep", p), region, sent)

    def wide_add(u, t):
        for h in range(2):
            p, first, count, (sent, received), region = step_place(u, h, t)
            settle(region, received)
            if t == bits - 1:
                mix(list(z_parts(u))[h][0], pool.at[p, chip, :, halves[h]], land.at[p, h, first])
                continue
            for j in range(count):
                accumulate(
                    pool.at[p, piece(h, t, j, chip), :, halves[h]], land.at[p, h, first + j]
                )

    def wide_core(u):
        p = nth[u] % 2
        settle(r.corel, r.core_r.at[u])

        def step(m, carry):
            accumulate(pool.at[p, m], r.corel.at[m])
            return carry

        lax.fori_loop(0, chips, step, 0)
        wide_send(u, 0)

    def wide_step(u, t):
        wide_add(u, t - 1)
        if t < bits:
            wide_send(u, t)
        else:
            z1(u)

    def held_at(h, j):
        value = chip
        for i in range(bits):
            if (j >> i) & 1:
                value = flip(value, orders[h][i])
        return value

    def gather_send(a, t):
        for h in range(2):
            partner = flip(chip, orders[h][t])
            sent, received = r.ag_s.at[a, h, t], r.ag_r.at[a, h, t]
            for j in range(1 << t):
                block = far_blocks.at[a, held_at(h, j), :, halves[h]]
                source = r.give.at[:, halves[h]] if j == 0 else block
                send(source, block, sent, received, (2 * partner + core, mine))
            later(("ag", a), far_blocks.at[a, pl.ds(0, 1 << t), :, halves[h]], sent)

    def gather_start(a):
        block = far_blocks.at[a, chip]
        dma(r.give, block, r.give_sem.at[a]).start()
        later(("ag", a), block, r.give_sem.at[a])
        gather_send(a, 0)

    def gather_wait(a, t):
        for h in range(2):
            settle(far_blocks.at[a, pl.ds(0, 1 << t), :, halves[h]], r.ag_r.at[a, h, t])

    def gather_step(a, t):
        gather_wait(a, t - 1)
        gather_send(a, t)

    def gather_end(a):
        gather_wait(a, bits - 1)
        flush(("ag", a))

    def tiny_send(a):
        for step in range(1, chips):
            block = r.tiny.at[a, chip]
            peer = lax.rem(chip + step, chips)
            send(block, block, r.tiny_s.at[a], r.tiny_r.at[a], (2 * peer + core, mine))
        later("end", r.tiny.at[a, pl.ds(0, chips - 1)], r.tiny_s.at[a])

    def tiny_wait(a):
        settle(r.tiny.at[a, pl.ds(0, chips - 1)], r.tiny_r.at[a])

    group = min(chips, 4)
    first_tap = lax.div(2 * deep * chip, INNER)
    margin = 2 * deep * chip - first_tap * INNER

    def deep_make(u):
        flush("deep")
        field_of, back_of = (0, 3) if u == DEF else (1, 2)
        for g in range(chips // group):
            fields = dma(
                far_blocks.at[field_of, pl.ds(g * group, group)], r.taken, r.take_sem.at[2]
            )
            fields.start()

            def fetch(m):
                return dma(
                    far_blocks.at[back_of, g * group + m], r.drawn.at[m % 2], r.take_sem.at[m % 2]
                )

            for m in range(min(2, group)):
                fetch(m).start()
            for m in range(group):
                fetch(m).wait()

                def lower(i, carry):
                    rows = pl.ds(pl.multiple_of(m * ROWS + i * 32, 32), 32)
                    there = pl.ds(pl.multiple_of(i * 32, 32), 32)
                    r.yall[rows, :] = r.drawn[m % 2, there, :].astype(BF)
                    return carry

                lax.fori_loop(0, ROWS // 32, lower, 0)
                if m + 2 < group:
                    fetch(m + 2).start()
            fields.wait()

            def one(kk, carry):
                k = jnp.minimum(first_tap + kk, TAPS - 1)
                down, across = steps_of(k)

                def image(i, share):
                    m, s = lax.div(i, SLOTS), lax.rem(i, SLOTS)
                    rows = pl.ds(pl.multiple_of(i * PIXELS, PIXELS), PIXELS)
                    there = pl.ds(pl.multiple_of(s * PIXELS, PIXELS), PIXELS)
                    field = r.taken[m, there, :].astype(BF)
                    tiny = r.tiny.at[0, g * group + m, s]
                    flat = tiny[18:19, :] == 0.0
                    dr = jnp.where(flat, r.geo[0, 0], r.geo[1, 0])
                    dc = jnp.where(flat, r.geo[0, 1], r.geo[1, 1])
                    hit = jnp.where((dr == down) & (dc == across), 1.0, 0.0).astype(BF)
                    if u == CON:
                        r.xall[rows, :] = mm(hit, field, NN).astype(BF)
                        return share
                    fy, fx = tiny[pl.ds(2 * k, 1), :], tiny[pl.ds(2 * k + 1, 1), :]
                    ay = jnp.where(dr == -down, 1.0 - fy, jnp.where(dr == -down - 1, fy, 0.0))
                    ax = jnp.where(
                        dc == -across, 1.0 - fx, jnp.where(dc == -across - 1, fx, 0.0)
                    )
                    r.xall[rows, :] = mm((ay * ax).astype(BF), field, TN).astype(BF)
                    shift = r.tiny[1, g * group + m, s].astype(BF)
                    moved = mm(shift, hit, NN).astype(BF)
                    return share + mm(moved, field, NN)

                at = pl.ds(pl.multiple_of(kk * INNER, INNER), INNER)
                zero = jnp.zeros((24, INNER) if u == DEF else (8, 128), F32)
                share = lax.fori_loop(0, group * SLOTS, image, zero)
                part = mm(r.xall[...], r.yall[...], TN)
                if g == 0:
                    grad[at, :] = part
                else:
                    grad[at, :] += part
                if u == DEF:
                    if g == 0:
                        r.goff[:, at] = share
                    else:
                        r.goff[:, at] += share
                return carry

            lax.fori_loop(0, taps, one, 0)
        away = pl.ds(pl.multiple_of(margin + (1 - core) * deep, 8), deep)
        send(grad.at[away], r.cored, r.core_s.at[u], r.core_r.at[u], sibling)
        later("deep", r.cored, r.core_s.at[u])
        if u == DEF:
            send(r.goff, r.coreo, r.core_s.at[OFF], r.core_r.at[OFF], sibling)

    def deep_core(u):
        settle(r.cored, r.core_r.at[u])
        half = deep // 2
        step = math.gcd(half, 32)
        for q in range(2):
            target = r.b3.at[(2 if u == DEF else 0) + q]

            def body(i, carry):
                at = pl.multiple_of(i * step, 8)
                here = grad[pl.ds(pl.multiple_of(margin + core * deep + q * half + at, 8), step), :]
                target[pl.ds(at, step), :] = here + r.cored[pl.ds(q * half + at, step), :]
                return carry

            lax.fori_loop(0, half // step, body, 0)
        if u == DEF:
            settle(r.goff, r.core_s.at[OFF])
            settle(r.coreo, r.core_r.at[OFF])
            accumulate(r.goff, r.coreo)
            z1(OFF)
        z1(u)

    images, between, acc, up = r.images, r.between, r.acc, r.up
    ig = [r.ig[i : i + 1, :] for i in range(4)]
    ib = [r.ib[i : i + 1, :] for i in range(4)]
    bg = [r.bg[i : i + 1, :] for i in range(2)]
    bb = [r.bb[i : i + 1, :] for i in range(2)]

    def geometry():
        q = lax.broadcasted_iota(jnp.int32, (PIXELS, PIXELS), 1)
        p = lax.broadcasted_iota(jnp.int32, (PIXELS, PIXELS), 0)

        def place_of(at, kind):
            if kind:
                row = lax.shift_right_logical(at, 2)
                return row, at - row * SHORT
            row = (at >= LONG).astype(jnp.int32) + (at >= 2 * LONG).astype(jnp.int32)
            row = row + (at >= 3 * LONG).astype(jnp.int32)
            return row, at - row * LONG

        for kind in range(2):
            row_q, col_q = place_of(q, kind)
            row_p, col_p = place_of(p, kind)
            r.geo[kind, 0] = row_q - row_p
            r.geo[kind, 1] = col_q - col_p

            def hot(k, carry):
                down, across = steps_of(k)
                hit = (r.geo[kind, 0] == down) & (r.geo[kind, 1] == across)
                r.tmat[kind, k] = jnp.where(hit, 1.0, 0.0).astype(BF)
                return carry

            lax.fori_loop(0, TAPS, hot, 0)

    def shifted(s, k):
        return r.tmat[orient[s], k]

    loads.images_h.wait()
    loads.red_h.wait()
    r.a1[...] = mm(images[...], r.redwid[...], NN)
    loads.wid_h = load(7, r.wid_h, r.redwid)
    pl.semaphore_wait(barrier, everyone - 1)
    narrow_stats(r.a1, 0, geometry)
    norm_silu(r.a1, 0, ig[0], ib[0], r.inner, True)
    gather_start(0)

    loads.off_h.wait()
    inner = r.inner
    lane = lax.broadcasted_iota(jnp.int32, (PIXELS, OFFSETS), 1)
    for s in range(SLOTS):

        def gather(k, carry):
            col = mm(shifted(s, k), inner[slot_rows(s), :], NN).astype(BF)
            return carry + mm(col, tap(r.off, k), NN)

        offsets = lax.fori_loop(0, TAPS, gather, jnp.zeros((PIXELS, OFFSETS), F32))
        frac = sigmoid(offsets)
        r.frac[slot_rows(s), :] = frac
        coarse = frac.astype(BF)
        fine = (frac - coarse.astype(F32)).astype(BF)
        unit = r.tmat[0, TAPS // 2]
        put = r.tiny.at[0, chip, s]
        put[...] = jnp.zeros((24, PIXELS), F32) + orient[s].astype(F32)
        put[0:OFFSETS, :] = mm(coarse, unit, TN) + mm(fine, unit, TN)
    tiny_send(0)

    def bilinear(s, k):
        down, across = steps_of(k)
        frac = r.frac[slot_rows(s), :]
        fy = jnp.sum(jnp.where(lane == 2 * k, frac, 0.0), axis=1, keepdims=True)
        fx = jnp.sum(jnp.where(lane == 2 * k + 1, frac, 0.0), axis=1, keepdims=True)
        dr, dc = r.geo[orient[s], 0], r.geo[orient[s], 1]
        in_y = (dr == down, dr == down + 1)
        in_x = (dc == across, dc == across + 1)
        ay = jnp.where(in_y[0], 1.0 - fy, jnp.where(in_y[1], fy, 0.0))
        ax = jnp.where(in_x[0], 1.0 - fx, jnp.where(in_x[1], fx, 0.0))
        return fy, fx, ay, ax, in_y, in_x

    loads.def_h.wait()
    acc[...] = jnp.zeros((ROWS, INNER), F32)

    def sample(k, carry):
        for s in range(SLOTS):
            _, _, ay, ax, _, _ = bilinear(s, k)
            weight = (ay * ax).astype(BF)
            r.wmat[s, k] = weight
            r.turned[slot_rows(s), :] = mm(weight, inner[slot_rows(s), :], NN).astype(BF)
        acc[...] += mm(r.turned[...], tap(r.dfmcon, k), NN)
        return carry

    lax.fori_loop(0, TAPS, sample, 0)
    loads.con_h = load(8, r.con_h, r.dfmcon)
    r.a2[...] = acc[...]
    narrow_stats(r.a2, 1, lambda: gather_step(0, 1))
    norm_silu(r.a2, 1, ig[1], ib[1], r.hidden, False)

    def widen(source, weight, target):
        def step(n, carry):
            rows = pl.ds(pl.multiple_of(n * 512, 512), 512)
            target[n] = mm(source[...], weight[rows, :], NT)
            return carry

        lax.fori_loop(0, CHANNELS // 512, step, 0)

    loads.exp_h.wait()
    widen(r.hidden, r.exp, r.a3)
    wide_stats(r.a3, 0)
    for n, cs in enumerate(blocks):
        mean = r.stw[0, 0:1, cs]
        steep = r.stw[0, 1:2, cs] * bg[0][:, 512 * n : 512 * n + 512]
        bias = bb[0][:, 512 * n : 512 * n + 512]

        def join(rs, lv, carry):
            z = (r.a3[n, rs, :] - mean) * steep + bias + images[rs, cs].astype(F32)
            between[rs, cs] = (z * sigmoid(z)).astype(BF)
            return carry

        sweep(join, 0)

    loads.nar_h.wait()
    r.b1[...] = mm(between[...], r.nar[...], NN)

    def work_b1():
        gather_end(0)
        tiny_wait(0)

    narrow_stats(r.b1, 2, work_b1)
    norm_silu(r.b1, 2, ig[2], ib[2], r.narrow, True)
    gather_start(1)

    loads.con_h.wait()
    acc[...] = jnp.zeros((ROWS, INNER), F32)

    def convolve(k, carry):
        for s in range(SLOTS):
            r.turned[slot_rows(s), :] = mm(
                shifted(s, k), r.narrow[slot_rows(s), :], NN
            ).astype(BF)
        acc[...] += mm(r.turned[...], tap(r.dfmcon, k), NN)
        return carry

    lax.fori_loop(0, TAPS, convolve, 0)
    r.b2[...] = acc[...]
    narrow_stats(r.b2, 3, lambda: gather_step(1, 1))
    norm_silu(r.b2, 3, ig[3], ib[3], r.mixed, False)

    loads.wid_h.wait()
    widen(r.mixed, r.redwid, r.b3)
    wide_stats(r.b3, 1)

    loads.cot_h.wait()

    def last(n, rs, cs, lv, pre):
        z = pre + between[rs, cs].astype(F32)
        sg = sigmoid(z)
        r.obuf[rs, cs] = (lv * (z * sg)).astype(BF)
        return r.dwide[rs, cs].astype(F32) * (lv * (sg * (1.0 + z * (1.0 - sg))))

    wide_cotangent(
        2, r.b3, 1, bg[1], bb[1], last, nothing, lambda: gather_end(1)
    )
    out_copy = dma(r.obuf, r.out_h, r.out_sem.at[0])
    out_copy.start()
    wide_begin(WID, r.dwide, r.mixed)
    acc[...] = mm(r.dwide[...], r.redwid[...], NN)
    loads.red_h = load(9, r.red_h, r.redwid)
    wide_core(WID)
    narrow_cotangent(r.b2, 3, ig[3], ib[3], 4, True)
    gather_start(2)

    acc[...] = jnp.zeros((ROWS, INNER), F32)

    def spread(k, carry):
        for s in range(SLOTS):
            r.turned[slot_rows(s), :] = mm(
                shifted(s, TAPS - 1 - k), r.dn[slot_rows(s), :], NN
            ).astype(BF)
        acc[...] += mm(r.turned[...], tap(r.dfmcon, k), NT)
        return carry

    lax.fori_loop(0, TAPS, spread, 0)
    loads.def_h = load(10, r.def_h, r.dfmcon)
    wide_step(WID, 1)
    narrow_cotangent(r.b1, 2, ig[2], ib[2], 5, False, lambda: gather_step(2, 1))
    wide_begin(NAR, between, r.dn)

    def add_back(n, carry):
        rows = pl.ds(pl.multiple_of(n * 512, 512), 512)
        up[n] += mm(r.dn[...], r.nar[rows, :], NT)
        return carry

    lax.fori_loop(0, CHANNELS // 512, add_back, 0)
    wide_step(WID, 2)
    wide_core(NAR)

    def first(n, rs, cs, lv, pre):
        z = pre + images[rs, cs].astype(F32)
        sg = sigmoid(z)
        return up[n, rs, :] * (sg * (1.0 + z * (1.0 - sg)))

    wide_cotangent(3, r.a3, 0, bg[0], bb[0], first, nothing, nothing)
    wide_begin(EXP, r.dwide, r.hidden)
    acc[...] = mm(r.dwide[...], r.exp[...], NN)
    wide_step(NAR, 1)
    wide_core(EXP)
    z2(WID)

    def work_b():
        gather_end(2)
        deep_make(CON)

    narrow_cotangent(r.a2, 1, ig[1], ib[1], 6, True, work_b)
    gather_start(3)
    deep_core(CON)
    wide_step(NAR, 2)
    z3(WID)

    loads.def_h.wait()
    acc[...] = jnp.zeros((ROWS, INNER), F32)
    r.doff[...] = jnp.zeros((ROWS, OFFSETS), F32)

    def unsample(k, carry):
        r.turned[...] = mm(r.dn[...], tap(r.dfmcon, k), NT).astype(BF)
        for s in range(SLOTS):
            rs = slot_rows(s)
            back = r.turned[rs, :]
            pairs = mm(back, inner[rs, :], NT)
            fy, fx, ay, ax, in_y, in_x = bilinear(s, k)
            slope_y = jnp.where(in_y[1], ax, 0.0) - jnp.where(in_y[0], ax, 0.0)
            slope_x = jnp.where(in_x[1], ay, 0.0) - jnp.where(in_x[0], ay, 0.0)
            to_y = jnp.sum(pairs * slope_y, axis=1, keepdims=True) * (fy * (1.0 - fy))
            to_x = jnp.sum(pairs * slope_x, axis=1, keepdims=True) * (fx * (1.0 - fx))
            r.doff[rs, :] += jnp.where(lane == 2 * k, to_y, 0.0) + jnp.where(
                lane == 2 * k + 1, to_x, 0.0
            )
            acc[rs, :] += mm(r.wmat[s, k], back, TN)
        return carry

    lax.fori_loop(0, TAPS, unsample, 0)
    for s in range(SLOTS):
        put = r.tiny.at[1, chip, s]
        put[...] = jnp.zeros((24, PIXELS), F32)
        put[0:OFFSETS, :] = mm(
            r.doff[slot_rows(s), :].astype(BF), r.tmat[0, TAPS // 2], TN
        )
    tiny_send(1)
    gather_step(3, 1)

    def untap(k, carry):
        for s in range(SLOTS):
            rs = slot_rows(s)
            moved = mm(shifted(s, TAPS - 1 - k), r.doff[rs, :].astype(BF), NN).astype(BF)
            acc[rs, :] += mm(moved, tap(r.off, k), NT)
        return carry

    lax.fori_loop(0, TAPS, untap, 0)
    z4(WID)
    wide_step(EXP, 1)
    z2(CON)
    z_clear(WID)
    narrow_cotangent(r.a1, 0, ig[0], ib[0], 7, False, lambda: z2(NAR))
    wide_begin(RED, images, r.dn)

    out_copy.wait()
    loads.red_h.wait()

    def finish(n, carry):
        rows = pl.ds(pl.multiple_of(n * 512, 512), 512)
        r.obuf[:, rows] = (up[n] + mm(r.dn[...], r.redwid[rows, :], NT)).astype(BF)
        return carry

    lax.fori_loop(0, CHANNELS // 512, finish, 0)
    grad_copy = dma(r.obuf, r.grad_h, r.out_sem.at[1])
    grad_copy.start()
    wide_step(EXP, 2)
    wide_core(RED)
    z3(CON)
    z3(NAR)
    gather_end(3)
    tiny_wait(1)
    z4(CON)
    z_clear(CON)
    deep_make(DEF)
    wide_step(RED, 1)
    z2(EXP)
    deep_core(DEF)
    z4(NAR)
    z_clear(NAR)
    wide_step(RED, 2)
    z3(EXP)
    z4(EXP)
    z2(OFF)
    z2(DEF)
    z2(RED)
    z3(OFF)
    z3(DEF)
    z3(RED)
    z4(OFF)
    z4(DEF)
    z4(RED)
    for u in (EXP, OFF, DEF, RED):
        z_clear(u)
    grad_copy.wait()
    for tag in list(waiting):
        flush(tag)


def per_device(
    images,
    counts,
    orientation,
    cotangent,
    reducer,
    offseter,
    deformer,
    expander,
    narrower,
    convolver,
    widener,
    inner_gains,
    inner_biases,
    broad_gains,
    broad_biases,
):
    dp, outer = lax.axis_size("dp"), lax.axis_size("outer")
    chips, bits, wide, deep, taps = layout(dp)
    buffers = scratch(dp, outer)
    smem = pl.BlockSpec(memory_space=pltpu.SMEM)
    vmem = pl.BlockSpec(memory_space=pltpu.VMEM)
    far = pl.BlockSpec(memory_space=pl.ANY)
    shape = jax.ShapeDtypeStruct
    inputs = dict(
        counts=(smem, counts),
        orient=(smem, orientation),
        ig=(vmem, inner_gains),
        ib=(vmem, inner_biases),
        bg=(vmem, broad_gains),
        bb=(vmem, broad_biases),
        images_h=(far, images.reshape(ROWS, CHANNELS)),
        cot_h=(far, cotangent.reshape(ROWS, CHANNELS)),
        red_h=(far, reducer),
        off_h=(far, offseter),
        def_h=(far, deformer),
        exp_h=(far, expander),
        nar_h=(far, narrower),
        con_h=(far, convolver),
        wid_h=(far, widener),
    )
    outputs = dict(
        out_h=(far, shape((ROWS, CHANNELS), BF)),
        grad_h=(far, shape((ROWS, CHANNELS), BF)),
        g_red=(far, shape((wide, INNER), F32)),
        g_off=(far, shape((24, taps * INNER), F32)),
        g_def=(far, shape((deep, INNER), F32)),
        g_exp=(far, shape((wide, INNER), F32)),
        g_nar=(far, shape((wide, INNER), F32)),
        g_con=(far, shape((deep, INNER), F32)),
        g_wid=(far, shape((wide, INNER), F32)),
        g_ig=(vmem, shape((4, INNER), F32)),
        g_ib=(vmem, shape((4, INNER), F32)),
        g_bg=(vmem, shape((2, CHANNELS), F32)),
        g_bb=(vmem, shape((2, CHANNELS), F32)),
        far_blocks=(far, shape((4, chips, ROWS, INNER), F32)),
    )
    names = list(inputs) + list(outputs) + list(buffers)
    outs = pl.pallas_call(
        functools.partial(kernel, dp, outer, names),
        out_shape=[spec for _, spec in outputs.values()],
        in_specs=[space for space, _ in inputs.values()],
        out_specs=[space for space, _ in outputs.values()],
        scratch_shapes=list(buffers.values()),
        compiler_params=pltpu.CompilerParams(
            collective_id=0, has_side_effects=True, vmem_limit_bytes=62 * 1024 * 1024
        ),
        name="chain",
    )(*[value for _, value in inputs.values()])
    out, grad, g_red, g_off, g_def, g_exp, g_nar, g_con, g_wid, g_ig, g_ib, g_bg, g_bb, _ = outs
    place = lax.axis_index("dp")
    inner_share, broad_share = INNER // dp, CHANNELS // dp
    begin = 2 * deep * (place // 2) % INNER + deep * (place % 2)
    g_off = lax.dynamic_slice_in_dim(g_off.T, begin, deep, 0)[:, :OFFSETS]
    return (
        out.reshape(SLOTS, PIXELS, CHANNELS),
        grad.reshape(SLOTS, PIXELS, CHANNELS),
        g_red,
        g_off,
        g_def,
        g_exp,
        g_nar,
        g_con,
        g_wid,
        lax.dynamic_slice_in_dim(g_ig, place * inner_share, inner_share, 1),
        lax.dynamic_slice_in_dim(g_ib, place * inner_share, inner_share, 1),
        lax.dynamic_slice_in_dim(g_bg, place * broad_share, broad_share, 1),
        lax.dynamic_slice_in_dim(g_bb, place * broad_share, broad_share, 1),
    )


def solution(mesh):
    spread = P(("dp", "outer"), None, None)
    in_specs = (spread, P(), P(("dp", "outer")), spread) + (P(),) * 11
    out_specs = (spread, spread) + (P("dp", None),) * 7 + (P(None, "dp"),) * 4
    return jax.shard_map(
        per_device, mesh=mesh, in_specs=in_specs, out_specs=out_specs, check_vma=False
    )
```

```python
import functools
import math
import types

import jax
import jax.numpy as jnp
from jax import lax
from jax.experimental import pallas as pl
from jax.experimental.pallas import tpu as pltpu
from jax.sharding import PartitionSpec as P

CHANNELS = 2048
INNER = 512
TAPS = 9
SLOTS = 2
SHORT = 4
LONG = 36
PIXELS = 144
ROWS = SLOTS * PIXELS
OFFSETS = 2 * TAPS
EPS = 1e-05
BF = jnp.bfloat16
F32 = jnp.float32
MESH = pl.DeviceIdType.MESH
NN = (((1,), (0,)), ((), ()))
NT = (((1,), (1,)), ((), ()))
TN = (((0,), (0,)), ((), ()))


def mm(left, right, dims):
    return lax.dot_general(left, right, dims, preferred_element_type=F32)


def sigmoid(value):
    return 0.5 * jnp.tanh(0.5 * value) + 0.5


def fold(value):
    return jnp.sum(value.reshape(value.shape[0] // 8, 8, value.shape[1]), axis=0)


def total_row(value):
    return jnp.sum(value, axis=0, keepdims=True)


def layout(dp):
    chips = dp // 2
    bits = chips.bit_length() - 1
    wide = CHANNELS // dp
    deep = TAPS * INNER // dp
    taps = max(
        -(-(2 * deep * chip % INNER + 2 * deep) // INNER) for chip in range(chips)
    )
    return chips, bits, wide, deep, taps


def scratch(dp, outer):
    vmem = pltpu.VMEM
    dma = pltpu.SemaphoreType.DMA
    chips, bits, wide, deep, taps = layout(dp)
    everyone = dp * outer
    group = min(chips, 4)
    return dict(
        images=vmem((ROWS, CHANNELS), BF),
        between=vmem((ROWS, CHANNELS), BF),
        dwide=vmem((ROWS, CHANNELS), BF),
        obuf=vmem((ROWS, CHANNELS), BF),
        redwid=vmem((CHANNELS, INNER), BF),
        exp=vmem((CHANNELS, INNER), BF),
        nar=vmem((CHANNELS, INNER), BF),
        dfmcon=vmem((TAPS * INNER, INNER), BF),
        off=vmem((OFFSETS, TAPS * INNER), BF),
        a1=vmem((ROWS, INNER), F32),
        a2=vmem((ROWS, INNER), F32),
        b1=vmem((ROWS, INNER), F32),
        b2=vmem((ROWS, INNER), F32),
        acc=vmem((ROWS, INNER), F32),
        a3=vmem((CHANNELS // 512, ROWS, 512), F32),
        b3=vmem((CHANNELS // 512, ROWS, 512), F32),
        up=vmem((CHANNELS // 512, ROWS, 512), F32),
        inner=vmem((ROWS, INNER), BF),
        hidden=vmem((ROWS, INNER), BF),
        narrow=vmem((ROWS, INNER), BF),
        mixed=vmem((ROWS, INNER), BF),
        dn=vmem((ROWS, INNER), BF),
        turned=vmem((ROWS, INNER), BF),
        wmat=vmem((SLOTS, TAPS, PIXELS, PIXELS), BF),
        tmat=vmem((2, TAPS, PIXELS, PIXELS), BF),
        geo=vmem((2, 2, PIXELS, PIXELS), jnp.int32),
        frac=vmem((ROWS, OFFSETS), F32),
        doff=vmem((ROWS, OFFSETS), F32),
        stn=vmem((4, 2, INNER), F32),
        stw=vmem((2, 2, CHANNELS), F32),
        rxn=vmem((8, everyone, 2, INNER), F32),
        rxw1=vmem((4, dp, 2, CHANNELS), F32),
        rxw2=vmem((4, outer, 2, CHANNELS), F32),
        pool=vmem((3, chips, wide, INNER), F32),
        corel=vmem((chips, wide, INNER), F32),
        land=vmem((2, 2, chips - 1, wide, INNER // 2), F32),
        zwide=vmem((3, 3, wide, INNER), F32),
        tiny=vmem((2, chips, SLOTS, 24, PIXELS), F32),
        give=vmem((ROWS, INNER), F32),
        taken=vmem((group, ROWS, INNER), F32),
        drawn=vmem((2, ROWS, INNER), F32),
        yall=vmem((group * ROWS, INNER), BF),
        xall=vmem((group * ROWS, INNER), BF),
        grad=vmem((taps * INNER, INNER), F32),
        cored=vmem((deep, INNER), F32),
        zdeep=vmem((2, 2, deep // 2, INNER), F32),
        goff=vmem((24, taps * INNER), F32),
        coreo=vmem((24, taps * INNER), F32),
        zoff=vmem((2, 24, taps * INNER), F32),
        free=pltpu.SemaphoreType.REGULAR,
        credit=pltpu.SemaphoreType.REGULAR((2, bits)),
        load_sem=dma((11,)),
        out_sem=dma((2,)),
        res_sem=dma((7, 4)),
        xn_s=dma((8,)),
        xn_r=dma((8,)),
        xw_s=dma((4, 2)),
        xw_r=dma((4, 2)),
        core_s=dma((7,)),
        core_r=dma((7,)),
        step_s=dma((4, 2, bits)),
        step_r=dma((4, 2, bits)),
        give_sem=dma((4,)),
        take_sem=dma((3,)),
        ag_s=dma((4, 2, bits)),
        ag_r=dma((4, 2, bits)),
        tiny_s=dma((2,)),
        tiny_r=dma((2,)),
        z_s=dma((7, 4, 3)),
        z_r=dma((7, 4, 3)),
    )


def kernel(dp, outer, names, *refs):
    assert outer == 4
    r = types.SimpleNamespace(**dict(zip(names, refs)))
    chips, bits, wide, deep, taps = layout(dp)
    everyone = dp * outer
    me = lax.axis_index("dp")
    mine = lax.axis_index("outer")
    own = me * outer + mine
    core = lax.rem(me, 2)
    chip = lax.div(me, 2)
    sibling = (me + 1 - 2 * core, mine)
    inside = (mine == 1) | (mine == 2)
    outside = (mine == 0) | (mine == 3)
    counts, orient = r.counts, r.orient
    dma = pltpu.make_async_copy

    loads = types.SimpleNamespace()

    def load(place, source, target):
        copy = dma(source, target, r.load_sem.at[place])
        copy.start()
        return copy

    loads.images_h = load(0, r.images_h, r.images)
    loads.red_h = load(1, r.red_h, r.redwid)
    loads.off_h = load(2, r.off_h, r.off)
    loads.def_h = load(3, r.def_h, r.dfmcon)
    loads.exp_h = load(4, r.exp_h, r.exp)
    loads.nar_h = load(5, r.nar_h, r.nar)
    loads.cot_h = load(6, r.cot_h, r.dwide)

    def other(step):
        target = lax.rem(own + step, everyone)
        return lax.div(target, outer), lax.rem(target, outer)

    barrier = pltpu.get_barrier_semaphore()

    def greet(step, carry):
        pl.semaphore_signal(barrier, inc=1, device_id=other(step), device_id_type=MESH)
        return carry

    lax.fori_loop(1, everyone, greet, 0)

    def size(i, carry):
        sizes, near, far = carry
        row, place = lax.div(i, outer), lax.rem(i, outer)
        held = counts[i].astype(F32)
        here = jnp.where(place == mine, held, 0.0)

        def mark(count, at, value):
            line = lax.broadcasted_iota(jnp.int32, (count, 1), 0)
            return jnp.where(line == at, value, 0.0)

        return (
            sizes + mark(everyone, i, held),
            near + mark(dp, row, here),
            far + mark(outer, place, held),
        )

    zeros = tuple(jnp.zeros((count, 1), F32) for count in (everyone, dp, outer))
    sizes, near, far = (
        value * float(PIXELS) for value in lax.fori_loop(0, everyone, size, zeros)
    )
    near_total = total_row(near)
    total = total_row(far)
    held = counts[own].astype(F32)
    live1 = held - 1.0
    local = held * float(PIXELS)

    def sweep(body, init):
        def step(i, carry):
            lv = jnp.where(i < 3, 1.0, live1)
            for j in range(3):
                carry = body(pl.ds(pl.multiple_of(i * 48 + j * 16, 16), 16), lv, carry)
            return carry

        return lax.fori_loop(0, 6, step, init)

    def send(source, target, sent, received, device):
        pltpu.make_async_remote_copy(
            src_ref=source,
            dst_ref=target,
            send_sem=sent,
            recv_sem=received,
            device_id=device,
            device_id_type=MESH,
        ).start()

    def settle(view, sem):
        dma(view, view, sem).wait()

    waiting = {}

    def later(tag, view, sem, when=None):
        waiting.setdefault(tag, []).append((when, view, sem))

    def flush(tag):
        for when, view, sem in waiting.pop(tag, []):
            if when is None:
                settle(view, sem)
            else:
                pl.when(when)(functools.partial(settle, view, sem))

    def accumulate(target, source):
        rows = target.shape[0]
        step = math.gcd(rows, 32)

        def body(i, carry):
            rs = pl.ds(pl.multiple_of(i * step, 8), step)
            target[rs, :] += source[rs, :]
            return carry

        lax.fori_loop(0, rows // step, body, 0)

    def mix(target, one, two):
        rows = target.shape[0]
        step = math.gcd(rows, 32)

        def body(i, carry):
            rs = pl.ds(pl.multiple_of(i * step, 8), step)
            target[rs, :] = one[rs, :] + two[rs, :]
            return carry

        lax.fori_loop(0, rows // step, body, 0)

    def flip(value, bit):
        weight = 1 << bit
        return value + weight - 2 * weight * lax.rem(lax.div(value, weight), 2)

    def bit_of(value, bit):
        return lax.rem(lax.div(value, 1 << bit), 2)

    orders = [
        list(range(bits)),
        list(range(bits // 2, bits)) + list(range(bits // 2)),
    ]
    halves = [pl.ds(0, INNER // 2), pl.ds(INNER // 2, INNER // 2)]

    def merge(rx, counted, size, forward):
        first = rx[:, 0, :]
        second = rx[:, 1, :]
        if forward:
            summed = total_row(first)
            apart = first / counted - summed / size
            spread = total_row(second + counted * apart * apart)
            return jnp.concatenate([summed, spread], axis=0)
        return jnp.concatenate([total_row(first), total_row(second)], axis=0)

    def nothing():
        pass

    def share_narrow(number, forward, work):
        rx = r.rxn.at[number]

        def step(i, carry):
            send(rx.at[own], rx.at[own], r.xn_s.at[number], r.xn_r.at[number], other(i))
            return carry

        lax.fori_loop(1, everyone, step, 0)
        rest = rx.at[pl.ds(0, everyone - 1)]
        later("end", rest, r.xn_s.at[number])
        work()
        settle(rest, r.xn_r.at[number])
        return merge(rx, sizes, total, forward)

    def share_wide(number, forward, work, work_more):
        rx1, rx2 = r.rxw1.at[number], r.rxw2.at[number]
        for step in range(1, dp):
            send(
                rx1.at[me],
                rx1.at[me],
                r.xw_s.at[number, 0],
                r.xw_r.at[number, 0],
                (lax.rem(me + step, dp), mine),
            )
        rest = rx1.at[pl.ds(0, dp - 1)]
        later("end", rest, r.xw_s.at[number, 0])
        work()
        settle(rest, r.xw_r.at[number, 0])
        rx2[mine] = merge(rx1, near, near_total, forward)
        for step in range(1, outer):
            send(
                rx2.at[mine],
                rx2.at[mine],
                r.xw_s.at[number, 1],
                r.xw_r.at[number, 1],
                (me, lax.rem(mine + step, outer)),
            )
        rest = rx2.at[pl.ds(0, outer - 1)]
        later("end", rest, r.xw_s.at[number, 1])
        work_more()
        settle(rest, r.xw_r.at[number, 1])
        return merge(rx2, far, total, forward)

    def local_stats(ref, put, cs):
        zero = jnp.zeros((8, 512), F32)
        summed = total_row(sweep(lambda rs, lv, c: c + lv * fold(ref[rs, :]), zero))
        mean = summed / local

        def squares(rs, lv, carry):
            apart = ref[rs, :] - mean
            return carry + lv * fold(apart * apart)

        put[0:1, cs] = summed
        put[1:2, cs] = total_row(sweep(squares, zero))

    def keep_stats(both, st):
        st[0:1, :] = both[0:1] / total
        st[1:2, :] = lax.rsqrt(both[1:2] / total + EPS)

    def narrow_stats(ref, number, work=nothing):
        local_stats(ref, r.rxn.at[number, own], pl.ds(0, INNER))
        keep_stats(share_narrow(number, True, work), r.stn.at[number])

    blocks = [pl.ds(start, 512) for start in range(0, CHANNELS, 512)]

    def wide_stats(ref, number, work=nothing, work_more=nothing):
        for n, cs in enumerate(blocks):
            local_stats(ref.at[n], r.rxw1.at[number, me], cs)
        keep_stats(share_wide(number, True, work, work_more), r.stw.at[number])

    def norm_silu(ref, number, gain, bias, out, spread):
        st = r.stn.at[number]
        mean, scale = st[0:1, :], st[1:2, :]
        steep = scale * gain

        def body(rs, lv, carry):
            z = (ref[rs, :] - mean) * steep + bias
            value = (z * sigmoid(z)).astype(BF)
            out[rs, :] = value
            if spread:
                r.give[rs, :] = value.astype(F32)
            return carry

        sweep(body, 0)

    def narrow_cotangent(ref, place, gain, bias, number, spread, work=nothing):
        acc = r.acc
        st = r.stn.at[place]
        mean, scale = st[0:1, :], st[1:2, :]

        def body(rs, lv, carry):
            xhat = (ref[rs, :] - mean) * scale
            z = xhat * gain + bias
            sg = sigmoid(z)
            g = acc[rs, :] * (sg * (1.0 + z * (1.0 - sg)))
            acc[rs, :] = g
            return carry[0] + fold(g), carry[1] + fold(g * xhat)

        zero = jnp.zeros((8, INNER), F32)
        summed, paired = sweep(body, (zero, zero))
        put = r.rxn.at[number, own]
        put[0:1, :] = total_row(summed)
        put[1:2, :] = total_row(paired)
        both = share_narrow(number, False, work)
        r.g_ib[place : place + 1, :] = both[0:1]
        r.g_ig[place : place + 1, :] = both[1:2]
        steep = scale * gain
        lift, tilt = both[0:1] / total, both[1:2] / total

        def back(rs, lv, carry):
            xhat = (ref[rs, :] - mean) * scale
            value = (steep * (acc[rs, :] - lv * (lift + xhat * tilt))).astype(BF)
            r.dn[rs, :] = value
            if spread:
                r.give[rs, :] = value.astype(F32)
            return carry

        sweep(back, 0)

    def wide_cotangent(number, ref, place, gain, bias, cotangent, work=nothing, work_more=nothing):
        put = r.rxw1.at[number, me]
        st = r.stw.at[place]
        for n, cs in enumerate(blocks):
            mean, scale = st[0:1, cs], st[1:2, cs]
            gn, bs = gain[:, 512 * n : 512 * n + 512], bias[:, 512 * n : 512 * n + 512]

            def body(rs, lv, carry):
                xhat = (ref[n, rs, :] - mean) * scale
                g = cotangent(n, rs, cs, lv, xhat * gn + bs)
                r.up[n, rs, :] = g
                return carry[0] + fold(g), carry[1] + fold(g * xhat)

            zero = jnp.zeros((8, 512), F32)
            summed, paired = sweep(body, (zero, zero))
            put[0:1, cs] = total_row(summed)
            put[1:2, cs] = total_row(paired)
        both = share_wide(number, False, work, work_more)
        r.g_bb[place : place + 1, :] = both[0:1]
        r.g_bg[place : place + 1, :] = both[1:2]
        for n, cs in enumerate(blocks):
            mean, scale = st[0:1, cs], st[1:2, cs]
            span = slice(512 * n, 512 * n + 512)
            steep = scale * gain[:, span]
            lift, tilt = both[0:1, span] / total, both[1:2, span] / total

            def back(rs, lv, carry):
                xhat = (ref[n, rs, :] - mean) * scale
                value = steep * (r.up[n, rs, :] - lv * (lift + xhat * tilt))
                r.dwide[rs, cs] = value.astype(BF)
                return carry

            sweep(back, 0)

    def tap(ref, k):
        return ref[pl.ds(pl.multiple_of(k * INNER, INNER), INNER), :]

    def offset_tap(k):
        return r.off[:, pl.ds(pl.multiple_of(k * INNER, INNER), INNER)]

    def slot_rows(s):
        return pl.ds(s * PIXELS, PIXELS)

    def steps_of(k):
        return 2 * lax.div(k, 3) - 2, 2 * lax.rem(k, 3) - 2

    WID, CON, NAR, EXP, DEF, RED, OFF = range(7)
    nth = {WID: 0, NAR: 1, EXP: 2, RED: 3}
    result = {
        WID: r.g_wid,
        CON: r.g_con,
        NAR: r.g_nar,
        EXP: r.g_exp,
        DEF: r.g_def,
        RED: r.g_red,
        OFF: r.g_off,
    }
    pool, land, grad, far_blocks = r.pool, r.land, r.grad, r.far_blocks

    deep_parts = 4 if deep % 32 == 0 else 2

    def z_parts(u):
        if u in nth:
            if u == RED:
                hold = [r.a3.at[i, pl.ds(0, wide)] for i in range(3)]
            else:
                hold = [r.zwide.at[nth[u], i] for i in range(3)]
            for hs in halves:
                yield tuple(ref.at[:, hs] for ref in hold) + (result[u].at[:, hs],)
        elif u == OFF:
            yield r.goff, r.zoff.at[0], r.zoff.at[1], result[u]
        else:
            for q in range(deep_parts):
                back, at = divmod(q, deep_parts // 2)
                source = r.b3.at[(2 if u == DEF else 0) + back]
                if u == DEF:
                    first, second = (r.b1, r.a2) if back == 0 else (r.b2, r.a3.at[3])
                else:
                    first, second = r.zdeep.at[0, back], r.zdeep.at[1, back]
                size = deep // deep_parts
                rows = pl.ds(at * size, size)
                out = result[u].at[pl.ds(q * size, size)]
                yield source.at[rows], first.at[rows], second.at[rows], out

    def z_sems(u, q, step):
        return r.z_s.at[u, q, step], r.z_r.at[u, q, step]

    def z1(u, some=None):
        for q, (source, first, second, out) in enumerate(z_parts(u)):
            if some is not None and q not in some:
                continue
            sent, received = z_sems(u, q, 0)

            @pl.when(outside)
            def _():
                send(source, first, sent, received, (me, flip(mine, 0)))

            later(("z", u), source, sent, outside)

    def z2(u, some=None):
        for q, (source, first, second, out) in enumerate(z_parts(u)):
            if some is not None and q not in some:
                continue
            sent, received = z_sems(u, q, 1)

            @pl.when(inside)
            def _():
                settle(first, z_sems(u, q, 0)[1])
                accumulate(source, first)
                send(source, second, sent, received, (me, 3 - mine))

            later(("z", u), source, sent, inside)

    def z3(u, some=None):
        for q, (source, first, second, out) in enumerate(z_parts(u)):
            if some is not None and q not in some:
                continue
            sent, received = z_sems(u, q, 2)

            @pl.when(inside)
            def _():
                settle(second, z_sems(u, q, 1)[1])
                accumulate(second, source)
                send(second, first, sent, received, (me, flip(mine, 0)))
                dma(second, out, r.res_sem.at[u, q]).start()

            later(("zl", u), second, sent, inside)

    def z4(u, some=None):
        for q, (source, first, second, out) in enumerate(z_parts(u)):
            if some is not None and q not in some:
                continue

            @pl.when(outside)
            def _():
                settle(first, z_sems(u, q, 2)[1])
                dma(first, out, r.res_sem.at[u, q]).start()

    def z_clear(u):
        flush(("z", u))
        flush(("zl", u))
        for q, (source, first, second, out) in enumerate(z_parts(u)):
            dma(first, out, r.res_sem.at[u, q]).wait()

    def wide_begin(u, left, right):
        p = nth[u] % 2
        flush("sib")
        flush(("keep", p))
        low = p + (2 - p) * core
        high = p + (2 - p) * (1 - core)

        def step(m, carry):
            block = left[:, pl.ds(pl.multiple_of(m * (2 * wide), 2 * wide), 2 * wide)]
            pool[low, m] = mm(block[:, :wide], right[...], TN)
            pool[high, m] = mm(block[:, wide:], right[...], TN)
            send(
                pool.at[2, m], r.corel.at[m], r.core_s.at[u], r.core_r.at[u], sibling
            )
            return carry

        lax.fori_loop(0, chips, step, 0)
        later("sib", r.corel, r.core_s.at[u])

    def piece(h, t, j, toward):
        value = 0
        for i, bit in enumerate(orders[h]):
            if i < t:
                part = bit_of(chip, bit)
            elif i == t:
                part = bit_of(toward, bit)
            else:
                part = (j >> (i - t - 1)) & 1
            value = value + part * (1 << bit)
        return value

    def step_place(u, h, t):
        first, count = chips - (chips >> t), chips >> (t + 1)
        p = nth[u] % 2
        sems = r.step_s.at[nth[u], h, t], r.step_r.at[nth[u], h, t]
        return p, first, count, sems, land.at[p, h, pl.ds(first, count)]

    def wide_send(u, t):
        for h in range(2):
            p, first, count, (sent, received), region = step_place(u, h, t)
            toward = flip(chip, orders[h][t])
            if u == RED:
                pl.semaphore_wait(r.credit.at[h, t], 1)
            for j in range(count):
                send(
                    pool.at[p, piece(h, t, j, toward), :, halves[h]],
                    land.at[p, h, first + j],
                    sent,
                    received,
                    (2 * toward + core, mine),
                )
            later(("keep", p), region, sent)

    def wide_add(u, t):
        for h in range(2):
            p, first, count, (sent, received), region = step_place(u, h, t)
            settle(region, received)
            if t == bits - 1:
                mix(list(z_parts(u))[h][0], pool.at[p, chip, :, halves[h]], land.at[p, h, first])
            else:
                for j in range(count):
                    accumulate(
                        pool.at[p, piece(h, t, j, chip), :, halves[h]], land.at[p, h, first + j]
                    )
            if u == NAR:
                pl.semaphore_signal(
                    r.credit.at[h, t],
                    inc=1,
                    device_id=(2 * flip(chip, orders[h][t]) + core, mine),
                    device_id_type=MESH,
                )

    def wide_core(u):
        p = nth[u] % 2
        settle(r.corel, r.core_r.at[u])

        def step(m, carry):
            accumulate(pool.at[p, m], r.corel.at[m])
            return carry

        lax.fori_loop(0, chips, step, 0)

    def wide_step(u, t):
        wide_add(u, t - 1)
        if t < bits:
            wide_send(u, t)
        else:
            z1(u)

    def held_at(h, j):
        value = chip
        for i in range(bits):
            if (j >> i) & 1:
                value = flip(value, orders[h][i])
        return value

    def gather_send(a, t, some=None):
        for h in range(2):
            partner = flip(chip, orders[h][t])
            sent, received = r.ag_s.at[a, h, t], r.ag_r.at[a, h, t]
            for j in range(1 << t) if some is None else some:
                block = far_blocks.at[a, held_at(h, j), :, halves[h]]
                source = r.give.at[:, halves[h]] if j == 0 else block
                send(source, block, sent, received, (2 * partner + core, mine))
            if some is None or 0 in some:
                later(("ag", a), far_blocks.at[a, pl.ds(0, 1 << t), :, halves[h]], sent)

    def gather_start(a):
        block = far_blocks.at[a, chip]
        dma(r.give, block, r.give_sem.at[a]).start()
        later(("ag", a), block, r.give_sem.at[a])
        gather_send(a, 0)

    def gather_wait(a, t):
        for h in range(2):
            settle(far_blocks.at[a, pl.ds(0, 1 << t), :, halves[h]], r.ag_r.at[a, h, t])

    def gather_step(a, t, some=None):
        gather_wait(a, t - 1)
        gather_send(a, t, some)

    def gather_first(a, t):
        if t < bits:
            gather_send(a, t, [0])

    def gather_rest(a):
        for t in range(1, bits):
            gather_wait(a, t - 1)
            gather_send(a, t, range(1 if t == 1 else 0, 1 << t))

    def gather_end(a):
        gather_wait(a, bits - 1)
        flush(("ag", a))

    def tiny_send(a):
        for step in range(1, chips):
            block = r.tiny.at[a, chip]
            peer = lax.rem(chip + step, chips)
            send(block, block, r.tiny_s.at[a], r.tiny_r.at[a], (2 * peer + core, mine))
        later("end", r.tiny.at[a, pl.ds(0, chips - 1)], r.tiny_s.at[a])

    def tiny_wait(a):
        settle(r.tiny.at[a, pl.ds(0, chips - 1)], r.tiny_r.at[a])

    group = min(chips, 4)
    first_tap = lax.div(2 * deep * chip, INNER)
    margin = 2 * deep * chip - first_tap * INNER

    def deep_make(u):
        flush("deep")
        field_of, back_of = (0, 3) if u == DEF else (1, 2)
        for g in range(chips // group):
            fields = dma(
                far_blocks.at[field_of, pl.ds(g * group, group)], r.taken, r.take_sem.at[2]
            )
            fields.start()

            def fetch(m):
                return dma(
                    far_blocks.at[back_of, g * group + m], r.drawn.at[m % 2], r.take_sem.at[m % 2]
                )

            for m in range(min(2, group)):
                fetch(m).start()
            for m in range(group):
                fetch(m).wait()

                def lower(i, carry):
                    rows = pl.ds(pl.multiple_of(m * ROWS + i * 32, 32), 32)
                    there = pl.ds(pl.multiple_of(i * 32, 32), 32)
                    r.yall[rows, :] = r.drawn[m % 2, there, :].astype(BF)
                    return carry

                lax.fori_loop(0, ROWS // 32, lower, 0)
                if m + 2 < group:
                    fetch(m + 2).start()
            fields.wait()

            def one(kk, carry):
                k = jnp.minimum(first_tap + kk, TAPS - 1)
                down, across = steps_of(k)

                def image(i, share):
                    m, s = lax.div(i, SLOTS), lax.rem(i, SLOTS)
                    rows = pl.ds(pl.multiple_of(i * PIXELS, PIXELS), PIXELS)
                    there = pl.ds(pl.multiple_of(s * PIXELS, PIXELS), PIXELS)
                    field = r.taken[m, there, :].astype(BF)
                    tiny = r.tiny.at[0, g * group + m, s]
                    flat = tiny[18:19, :] == 0.0
                    dr = jnp.where(flat, r.geo[0, 0], r.geo[1, 0])
                    dc = jnp.where(flat, r.geo[0, 1], r.geo[1, 1])
                    hit = jnp.where((dr == down) & (dc == across), 1.0, 0.0).astype(BF)
                    if u == CON:
                        r.xall[rows, :] = mm(hit, field, NN).astype(BF)
                        return share
                    fy, fx = tiny[pl.ds(2 * k, 1), :], tiny[pl.ds(2 * k + 1, 1), :]
                    ay = jnp.where(dr == -down, 1.0 - fy, jnp.where(dr == -down - 1, fy, 0.0))
                    ax = jnp.where(
                        dc == -across, 1.0 - fx, jnp.where(dc == -across - 1, fx, 0.0)
                    )
                    r.xall[rows, :] = mm((ay * ax).astype(BF), field, TN).astype(BF)
                    shift = r.tiny[1, g * group + m, s].astype(BF)
                    moved = mm(shift, hit, NN).astype(BF)
                    return share + mm(moved, field, NN)

                at = pl.ds(pl.multiple_of(kk * INNER, INNER), INNER)
                zero = jnp.zeros((24, INNER) if u == DEF else (8, 128), F32)
                share = lax.fori_loop(0, group * SLOTS, image, zero)
                part = mm(r.xall[...], r.yall[...], TN)
                if g == 0:
                    grad[at, :] = part
                else:
                    grad[at, :] += part
                if u == DEF:
                    if g == 0:
                        r.goff[:, at] = share
                    else:
                        r.goff[:, at] += share
                return carry

            lax.fori_loop(0, taps, one, 0)
        away = pl.ds(pl.multiple_of(margin + (1 - core) * deep, 8), deep)
        send(grad.at[away], r.cored, r.core_s.at[u], r.core_r.at[u], sibling)
        later("deep", r.cored, r.core_s.at[u])
        if u == DEF:
            send(r.goff, r.coreo, r.core_s.at[OFF], r.core_r.at[OFF], sibling)

    def deep_core(u):
        settle(r.cored, r.core_r.at[u])
        half = deep // 2
        step = math.gcd(half, 32)
        for q in range(2):
            target = r.b3.at[(2 if u == DEF else 0) + q]

            def body(i, carry):
                at = pl.multiple_of(i * step, 8)
                here = grad[pl.ds(pl.multiple_of(margin + core * deep + q * half + at, 8), step), :]
                target[pl.ds(at, step), :] = here + r.cored[pl.ds(q * half + at, step), :]
                return carry

            lax.fori_loop(0, half // step, body, 0)
        if u == DEF:
            settle(r.goff, r.core_s.at[OFF])
            settle(r.coreo, r.core_r.at[OFF])
            accumulate(r.goff, r.coreo)

    images, between, acc, up = r.images, r.between, r.acc, r.up
    ig = [r.ig[i : i + 1, :] for i in range(4)]
    ib = [r.ib[i : i + 1, :] for i in range(4)]
    bg = [r.bg[i : i + 1, :] for i in range(2)]
    bb = [r.bb[i : i + 1, :] for i in range(2)]

    def geometry():
        q = lax.broadcasted_iota(jnp.int32, (PIXELS, PIXELS), 1)
        p = lax.broadcasted_iota(jnp.int32, (PIXELS, PIXELS), 0)

        def place_of(at, kind):
            if kind:
                row = lax.shift_right_logical(at, 2)
                return row, at - row * SHORT
            row = (at >= LONG).astype(jnp.int32) + (at >= 2 * LONG).astype(jnp.int32)
            row = row + (at >= 3 * LONG).astype(jnp.int32)
            return row, at - row * LONG

        for kind in range(2):
            row_q, col_q = place_of(q, kind)
            row_p, col_p = place_of(p, kind)
            r.geo[kind, 0] = row_q - row_p
            r.geo[kind, 1] = col_q - col_p

            def hot(k, carry):
                down, across = steps_of(k)
                hit = (r.geo[kind, 0] == down) & (r.geo[kind, 1] == across)
                r.tmat[kind, k] = jnp.where(hit, 1.0, 0.0).astype(BF)
                return carry

            lax.fori_loop(0, TAPS, hot, 0)

    def shifted(s, k):
        return r.tmat[orient[s], k]

    loads.images_h.wait()
    loads.red_h.wait()
    r.a1[...] = mm(images[...], r.redwid[...], NN)
    loads.wid_h = load(7, r.wid_h, r.redwid)
    pl.semaphore_wait(barrier, everyone - 1)
    narrow_stats(r.a1, 0, geometry)
    norm_silu(r.a1, 0, ig[0], ib[0], r.inner, True)
    gather_start(0)

    loads.off_h.wait()
    inner = r.inner
    lane = lax.broadcasted_iota(jnp.int32, (PIXELS, OFFSETS), 1)
    for s in range(SLOTS):

        def gather(k, carry):
            col = mm(shifted(s, k), inner[slot_rows(s), :], NN).astype(BF)
            return carry + mm(col, offset_tap(k), NT)

        offsets = lax.fori_loop(0, TAPS, gather, jnp.zeros((PIXELS, OFFSETS), F32))
        frac = sigmoid(offsets)
        r.frac[slot_rows(s), :] = frac
        coarse = frac.astype(BF)
        fine = (frac - coarse.astype(F32)).astype(BF)
        unit = r.tmat[0, TAPS // 2]
        put = r.tiny.at[0, chip, s]
        put[...] = jnp.zeros((24, PIXELS), F32) + orient[s].astype(F32)
        put[0:OFFSETS, :] = mm(coarse, unit, TN) + mm(fine, unit, TN)
    tiny_send(0)

    def bilinear(s, k):
        down, across = steps_of(k)
        frac = r.frac[slot_rows(s), :]
        fy = jnp.sum(jnp.where(lane == 2 * k, frac, 0.0), axis=1, keepdims=True)
        fx = jnp.sum(jnp.where(lane == 2 * k + 1, frac, 0.0), axis=1, keepdims=True)
        dr, dc = r.geo[orient[s], 0], r.geo[orient[s], 1]
        in_y = (dr == down, dr == down + 1)
        in_x = (dc == across, dc == across + 1)
        ay = jnp.where(in_y[0], 1.0 - fy, jnp.where(in_y[1], fy, 0.0))
        ax = jnp.where(in_x[0], 1.0 - fx, jnp.where(in_x[1], fx, 0.0))
        return fy, fx, ay, ax, in_y, in_x

    loads.def_h.wait()
    acc[...] = jnp.zeros((ROWS, INNER), F32)

    def sample(k, carry):
        for s in range(SLOTS):
            _, _, ay, ax, _, _ = bilinear(s, k)
            weight = (ay * ax).astype(BF)
            r.wmat[s, k] = weight
            r.turned[slot_rows(s), :] = mm(weight, inner[slot_rows(s), :], NN).astype(BF)
        acc[...] += mm(r.turned[...], tap(r.dfmcon, k), NN)
        return carry

    lax.fori_loop(0, TAPS, sample, 0)
    loads.con_h = load(8, r.con_h, r.dfmcon)
    r.a2[...] = acc[...]
    narrow_stats(r.a2, 1, lambda: gather_first(0, 1))
    norm_silu(r.a2, 1, ig[1], ib[1], r.hidden, False)

    def widen(source, weight, target):
        def step(n, carry):
            rows = pl.ds(pl.multiple_of(n * 512, 512), 512)
            target[n] = mm(source[...], weight[rows, :], NT)
            return carry

        lax.fori_loop(0, CHANNELS // 512, step, 0)

    loads.exp_h.wait()
    widen(r.hidden, r.exp, r.a3)
    wide_stats(r.a3, 0, lambda: gather_rest(0))
    for n, cs in enumerate(blocks):
        mean = r.stw[0, 0:1, cs]
        steep = r.stw[0, 1:2, cs] * bg[0][:, 512 * n : 512 * n + 512]
        bias = bb[0][:, 512 * n : 512 * n + 512]

        def join(rs, lv, carry):
            z = (r.a3[n, rs, :] - mean) * steep + bias + images[rs, cs].astype(F32)
            between[rs, cs] = (z * sigmoid(z)).astype(BF)
            return carry

        sweep(join, 0)

    loads.nar_h.wait()
    r.b1[...] = mm(between[...], r.nar[...], NN)

    def work_b1():
        gather_end(0)
        tiny_wait(0)

    narrow_stats(r.b1, 2, work_b1)
    norm_silu(r.b1, 2, ig[2], ib[2], r.narrow, True)
    gather_start(1)

    loads.con_h.wait()
    acc[...] = jnp.zeros((ROWS, INNER), F32)

    def convolve(k, carry):
        for s in range(SLOTS):
            r.turned[slot_rows(s), :] = mm(
                shifted(s, k), r.narrow[slot_rows(s), :], NN
            ).astype(BF)
        acc[...] += mm(r.turned[...], tap(r.dfmcon, k), NN)
        return carry

    lax.fori_loop(0, TAPS, convolve, 0)
    r.b2[...] = acc[...]
    narrow_stats(r.b2, 3, lambda: gather_first(1, 1))
    norm_silu(r.b2, 3, ig[3], ib[3], r.mixed, False)

    loads.wid_h.wait()
    widen(r.mixed, r.redwid, r.b3)
    wide_stats(r.b3, 1, lambda: gather_rest(1))

    loads.cot_h.wait()

    def last(n, rs, cs, lv, pre):
        z = pre + between[rs, cs].astype(F32)
        sg = sigmoid(z)
        r.obuf[rs, cs] = (lv * (z * sg)).astype(BF)
        return r.dwide[rs, cs].astype(F32) * (lv * (sg * (1.0 + z * (1.0 - sg))))

    wide_cotangent(
        2, r.b3, 1, bg[1], bb[1], last, nothing, lambda: gather_end(1)
    )
    out_copy = dma(r.obuf, r.out_h, r.out_sem.at[0])
    out_copy.start()
    wide_begin(WID, r.dwide, r.mixed)
    acc[...] = mm(r.dwide[...], r.redwid[...], NN)
    loads.red_h = load(9, r.red_h, r.redwid)
    wide_core(WID)
    narrow_cotangent(r.b2, 3, ig[3], ib[3], 4, True, lambda: wide_send(WID, 0))

    acc[...] = jnp.zeros((ROWS, INNER), F32)

    def spread(k, carry):
        for s in range(SLOTS):
            r.turned[slot_rows(s), :] = mm(
                shifted(s, TAPS - 1 - k), r.dn[slot_rows(s), :], NN
            ).astype(BF)
        acc[...] += mm(r.turned[...], tap(r.dfmcon, k), NT)
        return carry

    lax.fori_loop(0, TAPS, spread, 0)
    loads.def_h = load(10, r.def_h, r.dfmcon)

    def work_d():
        gather_start(2)
        wide_step(WID, 1)

    narrow_cotangent(r.b1, 2, ig[2], ib[2], 5, False, work_d)
    wide_begin(NAR, between, r.dn)

    def add_back(n, carry):
        rows = pl.ds(pl.multiple_of(n * 512, 512), 512)
        up[n] += mm(r.dn[...], r.nar[rows, :], NT)
        return carry

    lax.fori_loop(0, CHANNELS // 512, add_back, 0)
    wide_core(NAR)

    def first(n, rs, cs, lv, pre):
        z = pre + images[rs, cs].astype(F32)
        sg = sigmoid(z)
        return up[n, rs, :] * (sg * (1.0 + z * (1.0 - sg)))

    def work_c():
        for t in range(1, bits):
            gather_step(2, t)

    def work_more_c():
        for t in range(2, bits + 1):
            wide_step(WID, t)

    wide_cotangent(3, r.a3, 0, bg[0], bb[0], first, work_c, work_more_c)
    wide_begin(EXP, r.dwide, r.hidden)
    acc[...] = mm(r.dwide[...], r.exp[...], NN)
    wide_core(EXP)

    def work_b():
        wide_send(NAR, 0)
        z2(WID)
        gather_end(2)
        deep_make(CON)

    narrow_cotangent(r.a2, 1, ig[1], ib[1], 6, True, work_b)
    gather_start(3)
    deep_core(CON)
    early, late = range(deep_parts // 2), range(deep_parts // 2, deep_parts)
    z1(CON, early)

    loads.def_h.wait()
    acc[...] = jnp.zeros((ROWS, INNER), F32)
    r.doff[...] = jnp.zeros((ROWS, OFFSETS), F32)

    def unsample(k, carry):
        r.turned[...] = mm(r.dn[...], tap(r.dfmcon, k), NT).astype(BF)
        for s in range(SLOTS):
            rs = slot_rows(s)
            back = r.turned[rs, :]
            pairs = mm(back, inner[rs, :], NT)
            fy, fx, ay, ax, in_y, in_x = bilinear(s, k)
            slope_y = jnp.where(in_y[1], ax, 0.0) - jnp.where(in_y[0], ax, 0.0)
            slope_x = jnp.where(in_x[1], ay, 0.0) - jnp.where(in_x[0], ay, 0.0)
            to_y = jnp.sum(pairs * slope_y, axis=1, keepdims=True) * (fy * (1.0 - fy))
            to_x = jnp.sum(pairs * slope_x, axis=1, keepdims=True) * (fx * (1.0 - fx))
            r.doff[rs, :] += jnp.where(lane == 2 * k, to_y, 0.0) + jnp.where(
                lane == 2 * k + 1, to_x, 0.0
            )
            acc[rs, :] += mm(r.wmat[s, k], back, TN)
        return carry

    lax.fori_loop(0, TAPS, unsample, 0)
    for s in range(SLOTS):
        put = r.tiny.at[1, chip, s]
        put[...] = jnp.zeros((24, PIXELS), F32)
        put[0:OFFSETS, :] = mm(
            r.doff[slot_rows(s), :].astype(BF), r.tmat[0, TAPS // 2], TN
        )
    tiny_send(1)

    def untap(k, carry):
        for s in range(SLOTS):
            rs = slot_rows(s)
            moved = mm(shifted(s, TAPS - 1 - k), r.doff[rs, :].astype(BF), NN).astype(BF)
            acc[rs, :] += mm(moved, offset_tap(k), NN)
        return carry

    lax.fori_loop(0, TAPS, untap, 0)

    def work_a():
        wide_step(NAR, 1)
        for t in range(1, bits):
            gather_step(3, t)
        z1(CON, late)
        wide_send(EXP, 0)
        z3(WID)
        z2(CON, early)

    narrow_cotangent(r.a1, 0, ig[0], ib[0], 7, False, work_a)
    for t in range(2, bits + 1):
        wide_step(NAR, t)
    wide_begin(RED, images, r.dn)

    out_copy.wait()
    loads.red_h.wait()

    def finish(n, carry):
        rows = pl.ds(pl.multiple_of(n * 512, 512), 512)
        r.obuf[:, rows] = (up[n] + mm(r.dn[...], r.redwid[rows, :], NT)).astype(BF)
        return carry

    lax.fori_loop(0, CHANNELS // 512, finish, 0)
    grad_copy = dma(r.obuf, r.grad_h, r.out_sem.at[1])
    grad_copy.start()
    wide_core(RED)
    wide_send(RED, 0)
    z2(CON, late)
    z3(CON, early)
    z2(NAR)
    gather_end(3)
    tiny_wait(1)
    deep_make(DEF)
    z3(CON, late)
    z4(WID)
    z3(NAR)
    z4(CON)
    wide_step(EXP, 1)
    deep_core(DEF)
    z1(OFF)
    z1(DEF)
    wide_step(RED, 1)
    for t in range(2, bits + 1):
        wide_step(EXP, t)
    z4(NAR)
    z2(OFF)
    z2(DEF)
    for t in range(2, bits + 1):
        wide_step(RED, t)
    z2(EXP)
    z3(OFF)
    z3(DEF)
    z2(RED)
    z3(EXP)
    z3(RED)
    z4(OFF)
    z4(DEF)
    z4(EXP)
    z4(RED)
    for u in range(7):
        z_clear(u)
    grad_copy.wait()
    for tag in list(waiting):
        flush(tag)


MOVED = ["out", "grad", "con", "def", "wid", "nar", "exp", "red"]


def deliver(dp, names, *refs):
    r = types.SimpleNamespace(**dict(zip(names, refs)))
    _, _, _, deep, _ = layout(dp)
    place = lax.axis_index("dp")
    moves = []
    for i, name in enumerate(MOVED):
        source, target, hold = (getattr(r, kind + name) for kind in ("from_", "to_", "hold_"))
        taken = pltpu.make_async_copy(source, hold, r.sems.at[0, i])
        taken.start()
        moves.append((taken, pltpu.make_async_copy(hold, target, r.sems.at[1, i])))

    for taken, given in moves:
        taken.wait()
        given.start()

    def span(ref, start, target):
        rows, lanes = ref.shape
        moved = pltpu.roll(ref[...], lax.rem(lanes - start, lanes), 1)
        target[...] = moved[: target.shape[0], : target.shape[1]]

    span(r.g_ig, place * (INNER // dp), r.to_ig)
    span(r.g_ib, place * (INNER // dp), r.to_ib)
    span(r.g_bg, place * (CHANNELS // dp), r.to_bg)
    span(r.g_bb, place * (CHANNELS // dp), r.to_bb)
    chip, core = lax.div(place, 2), lax.rem(place, 2)
    span(r.g_off, lax.rem(2 * deep * chip, INNER) + deep * core, r.to_off)
    for taken, given in moves:
        given.wait()


def per_device(
    images,
    counts,
    orientation,
    cotangent,
    reducer,
    offseter,
    deformer,
    expander,
    narrower,
    convolver,
    widener,
    inner_gains,
    inner_biases,
    broad_gains,
    broad_biases,
):
    dp, outer = lax.axis_size("dp"), lax.axis_size("outer")
    chips, bits, wide, deep, taps = layout(dp)
    buffers = scratch(dp, outer)
    smem = pl.BlockSpec(memory_space=pltpu.SMEM)
    vmem = pl.BlockSpec(memory_space=pltpu.VMEM)
    far = pl.BlockSpec(memory_space=pl.ANY)
    shape = jax.ShapeDtypeStruct
    inputs = dict(
        counts=(smem, counts),
        orient=(smem, orientation),
        ig=(vmem, inner_gains),
        ib=(vmem, inner_biases),
        bg=(vmem, broad_gains),
        bb=(vmem, broad_biases),
        images_h=(far, images.reshape(ROWS, CHANNELS)),
        cot_h=(far, cotangent.reshape(ROWS, CHANNELS)),
        red_h=(far, reducer),
        off_h=(far, offseter.T),
        def_h=(far, deformer),
        exp_h=(far, expander),
        nar_h=(far, narrower),
        con_h=(far, convolver),
        wid_h=(far, widener),
    )
    outputs = dict(
        out_h=(far, shape((ROWS, CHANNELS), BF)),
        grad_h=(far, shape((ROWS, CHANNELS), BF)),
        g_red=(far, shape((wide, INNER), F32)),
        g_off=(far, shape((24, taps * INNER), F32)),
        g_def=(far, shape((deep, INNER), F32)),
        g_exp=(far, shape((wide, INNER), F32)),
        g_nar=(far, shape((wide, INNER), F32)),
        g_con=(far, shape((deep, INNER), F32)),
        g_wid=(far, shape((wide, INNER), F32)),
        g_ig=(vmem, shape((4, INNER), F32)),
        g_ib=(vmem, shape((4, INNER), F32)),
        g_bg=(vmem, shape((2, CHANNELS), F32)),
        g_bb=(vmem, shape((2, CHANNELS), F32)),
        far_blocks=(far, shape((4, chips, ROWS, INNER), F32)),
    )
    names = list(inputs) + list(outputs) + list(buffers)
    outs = pl.pallas_call(
        functools.partial(kernel, dp, outer, names),
        out_shape=[spec for _, spec in outputs.values()],
        in_specs=[space for space, _ in inputs.values()],
        out_specs=[space for space, _ in outputs.values()],
        scratch_shapes=list(buffers.values()),
        compiler_params=pltpu.CompilerParams(
            collective_id=0, has_side_effects=True, vmem_limit_bytes=63 * 1024 * 1024
        ),
        name="chain",
    )(*[value for _, value in inputs.values()])
    held = dict(zip(outputs, outs))
    big = dict(
        out=held["out_h"],
        grad=held["grad_h"],
        red=held["g_red"],
        **{"def": held["g_def"]},
        exp=held["g_exp"],
        nar=held["g_nar"],
        con=held["g_con"],
        wid=held["g_wid"],
    )
    small = {name: held[name] for name in ("g_off", "g_ig", "g_ib", "g_bg", "g_bb")}
    firsts = {"from_" + name: value for name, value in big.items()}
    finals = {"to_" + name: shape(value.shape, value.dtype) for name, value in big.items()}
    holds = {"hold_" + name: pltpu.VMEM(value.shape, value.dtype) for name, value in big.items()}
    lasts = dict(
        to_off=shape((OFFSETS, deep), F32),
        to_ig=shape((4, INNER // dp), F32),
        to_ib=shape((4, INNER // dp), F32),
        to_bg=shape((2, CHANNELS // dp), F32),
        to_bb=shape((2, CHANNELS // dp), F32),
    )
    names = [*firsts, *small, *finals, *lasts, *holds, "sems"]
    got = pl.pallas_call(
        functools.partial(deliver, dp, names),
        out_shape=[*finals.values(), *lasts.values()],
        in_specs=[far] * len(firsts) + [vmem] * len(small),
        out_specs=[far] * len(finals) + [vmem] * len(lasts),
        scratch_shapes=[*holds.values(), pltpu.SemaphoreType.DMA((2, len(big)))],
        compiler_params=pltpu.CompilerParams(vmem_limit_bytes=60 * 1024 * 1024),
        name="deliver",
    )(*firsts.values(), *small.values())
    out, grad, g_red, g_def, g_exp, g_nar, g_con, g_wid, g_off, *others = got
    return (
        out.reshape(SLOTS, PIXELS, CHANNELS),
        grad.reshape(SLOTS, PIXELS, CHANNELS),
        g_red,
        g_off.T,
        g_def,
        g_exp,
        g_nar,
        g_con,
        g_wid,
        *others,
    )


def solution(mesh):
    spread = P(("dp", "outer"), None, None)
    in_specs = (spread, P(), P(("dp", "outer")), spread) + (P(),) * 11
    out_specs = (spread, spread) + (P("dp", None),) * 7 + (P(None, "dp"),) * 4
    return jax.shard_map(
        per_device, mesh=mesh, in_specs=in_specs, out_specs=out_specs, check_vma=False
    )
```

```python
import functools
import math
import types

import jax
import jax.numpy as jnp
from jax import lax
from jax.experimental import pallas as pl
from jax.experimental.pallas import tpu as pltpu
from jax.sharding import PartitionSpec as P

CHANNELS = 2048
INNER = 512
TAPS = 9
SLOTS = 2
SHORT = 4
LONG = 36
PIXELS = 144
ROWS = SLOTS * PIXELS
OFFSETS = 2 * TAPS
EPS = 1e-05
BF = jnp.bfloat16
F32 = jnp.float32
MESH = pl.DeviceIdType.MESH
NN = (((1,), (0,)), ((), ()))
NT = (((1,), (1,)), ((), ()))
TN = (((0,), (0,)), ((), ()))


def mm(left, right, dims):
    return lax.dot_general(left, right, dims, preferred_element_type=F32)


def sigmoid(value):
    return 0.5 * jnp.tanh(0.5 * value) + 0.5


def fold(value):
    return jnp.sum(value.reshape(value.shape[0] // 8, 8, value.shape[1]), axis=0)


def total_row(value):
    return jnp.sum(value, axis=0, keepdims=True)


def layout(dp):
    chips = dp // 2
    bits = chips.bit_length() - 1
    wide = CHANNELS // dp
    deep = TAPS * INNER // dp
    taps = max(
        -(-(2 * deep * chip % INNER + 2 * deep) // INNER) for chip in range(chips)
    )
    return chips, bits, wide, deep, taps


def scratch(dp, outer):
    vmem = pltpu.VMEM
    dma = pltpu.SemaphoreType.DMA
    chips, bits, wide, deep, taps = layout(dp)
    everyone = dp * outer
    group = min(chips, 4)
    return dict(
        images=vmem((ROWS, CHANNELS), BF),
        between=vmem((ROWS, CHANNELS), BF),
        dwide=vmem((ROWS, CHANNELS), BF),
        obuf=vmem((ROWS, CHANNELS), BF),
        redwid=vmem((CHANNELS, INNER), BF),
        exp=vmem((CHANNELS, INNER), BF),
        nar=vmem((CHANNELS, INNER), BF),
        dfmcon=vmem((TAPS * INNER, INNER), BF),
        off=vmem((OFFSETS, TAPS * INNER), BF),
        a1=vmem((ROWS, INNER), F32),
        a2=vmem((ROWS, INNER), F32),
        b1=vmem((ROWS, INNER), F32),
        b2=vmem((ROWS, INNER), F32),
        acc=vmem((ROWS, INNER), F32),
        a3=vmem((CHANNELS // 512, ROWS, 512), F32),
        b3=vmem((CHANNELS // 512, ROWS, 512), F32),
        up=vmem((CHANNELS // 512, ROWS, 512), F32),
        inner=vmem((ROWS, INNER), BF),
        hidden=vmem((ROWS, INNER), BF),
        narrow=vmem((ROWS, INNER), BF),
        mixed=vmem((ROWS, INNER), BF),
        dn=vmem((ROWS, INNER), BF),
        turned=vmem((ROWS, INNER), BF),
        wmat=vmem((SLOTS, TAPS, PIXELS, PIXELS), BF),
        tmat=vmem((2, TAPS, PIXELS, PIXELS), BF),
        geo=vmem((2, 2, PIXELS, PIXELS), jnp.int32),
        frac=vmem((ROWS, OFFSETS), F32),
        doff=vmem((ROWS, OFFSETS), F32),
        stn=vmem((4, 2, INNER), F32),
        stw=vmem((2, 2, CHANNELS), F32),
        rxn=vmem((8, everyone, 2, INNER), F32),
        rxw1=vmem((4, dp, 2, CHANNELS), F32),
        rxw2=vmem((4, outer, 2, CHANNELS), F32),
        pool=vmem((3, chips, wide, INNER), F32),
        corel=vmem((chips, wide, INNER), F32),
        land=vmem((2, 2, chips - 1, wide, INNER // 2), F32),
        zwide=vmem((3, 3, wide, INNER), F32),
        tiny=vmem((2, chips, SLOTS, 24, PIXELS), F32),
        give=vmem((ROWS, INNER), F32),
        taken=vmem((group, ROWS, INNER), F32),
        drawn=vmem((2, ROWS, INNER), F32),
        yall=vmem((group * ROWS, INNER), BF),
        xall=vmem((2, group * ROWS, INNER), BF),
        grad=vmem((taps * INNER, INNER), F32),
        cored=vmem((deep, INNER), F32),
        zdeep=vmem((2, 2, deep // 2, INNER), F32),
        goff=vmem((24, taps * INNER), F32),
        coreo=vmem((24, taps * INNER), F32),
        zoff=vmem((2, 24, taps * INNER), F32),
        free=pltpu.SemaphoreType.REGULAR,
        credit=pltpu.SemaphoreType.REGULAR((2, bits)),
        load_sem=dma((11,)),
        out_sem=dma((2,)),
        res_sem=dma((7, 4)),
        xn_s=dma((8,)),
        xn_r=dma((8,)),
        xw_s=dma((4, 2)),
        xw_r=dma((4, 2)),
        core_s=dma((7,)),
        core_r=dma((7,)),
        step_s=dma((4, 2, bits)),
        step_r=dma((4, 2, bits)),
        give_sem=dma((4,)),
        take_sem=dma((3,)),
        x_sem=dma((2,)),
        ag_s=dma((4, 2, bits)),
        ag_r=dma((4, 2, bits)),
        tiny_s=dma((2,)),
        tiny_r=dma((2,)),
        z_s=dma((7, 4, 3)),
        z_r=dma((7, 4, 3)),
    )


def kernel(dp, outer, names, *refs):
    assert outer == 4
    r = types.SimpleNamespace(**dict(zip(names, refs)))
    chips, bits, wide, deep, taps = layout(dp)
    everyone = dp * outer
    me = lax.axis_index("dp")
    mine = lax.axis_index("outer")
    own = me * outer + mine
    core = lax.rem(me, 2)
    chip = lax.div(me, 2)
    sibling = (me + 1 - 2 * core, mine)
    inside = (mine == 1) | (mine == 2)
    outside = (mine == 0) | (mine == 3)
    counts, orient = r.counts, r.orient
    dma = pltpu.make_async_copy

    loads = types.SimpleNamespace()

    def load(place, source, target):
        copy = dma(source, target, r.load_sem.at[place])
        copy.start()
        return copy

    loads.images_h = load(0, r.images_h, r.images)
    loads.red_h = load(1, r.red_h, r.redwid)
    loads.off_h = load(2, r.off_h, r.off)
    loads.def_h = load(3, r.def_h, r.dfmcon)
    loads.exp_h = load(4, r.exp_h, r.exp)
    loads.nar_h = load(5, r.nar_h, r.nar)
    loads.cot_h = load(6, r.cot_h, r.dwide)

    def other(step):
        target = lax.rem(own + step, everyone)
        return lax.div(target, outer), lax.rem(target, outer)

    barrier = pltpu.get_barrier_semaphore()

    def greet(step, carry):
        pl.semaphore_signal(barrier, inc=1, device_id=other(step), device_id_type=MESH)
        return carry

    lax.fori_loop(1, everyone, greet, 0)

    def size(i, carry):
        sizes, near, far = carry
        row, place = lax.div(i, outer), lax.rem(i, outer)
        held = counts[i].astype(F32)
        here = jnp.where(place == mine, held, 0.0)

        def mark(count, at, value):
            line = lax.broadcasted_iota(jnp.int32, (count, 1), 0)
            return jnp.where(line == at, value, 0.0)

        return (
            sizes + mark(everyone, i, held),
            near + mark(dp, row, here),
            far + mark(outer, place, held),
        )

    zeros = tuple(jnp.zeros((count, 1), F32) for count in (everyone, dp, outer))
    sizes, near, far = (
        value * float(PIXELS) for value in lax.fori_loop(0, everyone, size, zeros)
    )
    near_total = total_row(near)
    total = total_row(far)
    held = counts[own].astype(F32)
    live1 = held - 1.0
    local = held * float(PIXELS)

    def sweep(body, init):
        def step(i, carry):
            lv = jnp.where(i < 3, 1.0, live1)
            for j in range(3):
                carry = body(pl.ds(pl.multiple_of(i * 48 + j * 16, 16), 16), lv, carry)
            return carry

        return lax.fori_loop(0, 6, step, init)

    def send(source, target, sent, received, device):
        pltpu.make_async_remote_copy(
            src_ref=source,
            dst_ref=target,
            send_sem=sent,
            recv_sem=received,
            device_id=device,
            device_id_type=MESH,
        ).start()

    def settle(view, sem):
        dma(view, view, sem).wait()

    waiting = {}

    def later(tag, view, sem, when=None):
        waiting.setdefault(tag, []).append((when, view, sem))

    def flush(tag):
        for when, view, sem in waiting.pop(tag, []):
            if when is None:
                settle(view, sem)
            else:
                pl.when(when)(functools.partial(settle, view, sem))

    def accumulate(target, source):
        rows = target.shape[0]
        step = math.gcd(rows, 32)

        def body(i, carry):
            rs = pl.ds(pl.multiple_of(i * step, 8), step)
            target[rs, :] += source[rs, :]
            return carry

        lax.fori_loop(0, rows // step, body, 0)

    def mix(target, one, two):
        rows = target.shape[0]
        step = math.gcd(rows, 32)

        def body(i, carry):
            rs = pl.ds(pl.multiple_of(i * step, 8), step)
            target[rs, :] = one[rs, :] + two[rs, :]
            return carry

        lax.fori_loop(0, rows // step, body, 0)

    def flip(value, bit):
        weight = 1 << bit
        return value + weight - 2 * weight * lax.rem(lax.div(value, weight), 2)

    def bit_of(value, bit):
        return lax.rem(lax.div(value, 1 << bit), 2)

    orders = [
        list(range(bits)),
        list(range(bits // 2, bits)) + list(range(bits // 2)),
    ]
    halves = [pl.ds(0, INNER // 2), pl.ds(INNER // 2, INNER // 2)]

    def merge(rx, counted, size, forward):
        first = rx[:, 0, :]
        second = rx[:, 1, :]
        if forward:
            summed = total_row(first)
            apart = first / counted - summed / size
            spread = total_row(second + counted * apart * apart)
            return jnp.concatenate([summed, spread], axis=0)
        return jnp.concatenate([total_row(first), total_row(second)], axis=0)

    def nothing():
        pass

    def share_narrow(number, forward, work):
        rx = r.rxn.at[number]

        def step(i, carry):
            send(rx.at[own], rx.at[own], r.xn_s.at[number], r.xn_r.at[number], other(i))
            return carry

        lax.fori_loop(1, everyone, step, 0)
        rest = rx.at[pl.ds(0, everyone - 1)]
        later("end", rest, r.xn_s.at[number])
        work()
        settle(rest, r.xn_r.at[number])
        return merge(rx, sizes, total, forward)

    def share_wide(number, forward, work, work_more):
        rx1, rx2 = r.rxw1.at[number], r.rxw2.at[number]
        for step in range(1, dp):
            send(
                rx1.at[me],
                rx1.at[me],
                r.xw_s.at[number, 0],
                r.xw_r.at[number, 0],
                (lax.rem(me + step, dp), mine),
            )
        rest = rx1.at[pl.ds(0, dp - 1)]
        later("end", rest, r.xw_s.at[number, 0])
        work()
        settle(rest, r.xw_r.at[number, 0])
        rx2[mine] = merge(rx1, near, near_total, forward)
        for step in range(1, outer):
            send(
                rx2.at[mine],
                rx2.at[mine],
                r.xw_s.at[number, 1],
                r.xw_r.at[number, 1],
                (me, lax.rem(mine + step, outer)),
            )
        rest = rx2.at[pl.ds(0, outer - 1)]
        later("end", rest, r.xw_s.at[number, 1])
        work_more()
        settle(rest, r.xw_r.at[number, 1])
        return merge(rx2, far, total, forward)

    def local_stats(ref, put, cs):
        zero = jnp.zeros((8, 512), F32)
        summed = total_row(sweep(lambda rs, lv, c: c + lv * fold(ref[rs, :]), zero))
        mean = summed / local

        def squares(rs, lv, carry):
            apart = ref[rs, :] - mean
            return carry + lv * fold(apart * apart)

        put[0:1, cs] = summed
        put[1:2, cs] = total_row(sweep(squares, zero))

    def keep_stats(both, st):
        st[0:1, :] = both[0:1] / total
        st[1:2, :] = lax.rsqrt(both[1:2] / total + EPS)

    def narrow_stats(ref, number, work=nothing):
        local_stats(ref, r.rxn.at[number, own], pl.ds(0, INNER))
        keep_stats(share_narrow(number, True, work), r.stn.at[number])

    blocks = [pl.ds(start, 512) for start in range(0, CHANNELS, 512)]

    def wide_stats(ref, number, work=nothing, work_more=nothing):
        for n, cs in enumerate(blocks):
            local_stats(ref.at[n], r.rxw1.at[number, me], cs)
        keep_stats(share_wide(number, True, work, work_more), r.stw.at[number])

    def norm_silu(ref, number, gain, bias, out, spread):
        st = r.stn.at[number]
        mean, scale = st[0:1, :], st[1:2, :]
        steep = scale * gain

        def body(rs, lv, carry):
            z = (ref[rs, :] - mean) * steep + bias
            value = (z * sigmoid(z)).astype(BF)
            out[rs, :] = value
            if spread:
                r.give[rs, :] = value.astype(F32)
            return carry

        sweep(body, 0)

    def narrow_cotangent(ref, place, gain, bias, number, spread, work=nothing):
        acc = r.acc
        st = r.stn.at[place]
        mean, scale = st[0:1, :], st[1:2, :]

        def body(rs, lv, carry):
            xhat = (ref[rs, :] - mean) * scale
            z = xhat * gain + bias
            sg = sigmoid(z)
            g = acc[rs, :] * (sg * (1.0 + z * (1.0 - sg)))
            acc[rs, :] = g
            return carry[0] + fold(g), carry[1] + fold(g * xhat)

        zero = jnp.zeros((8, INNER), F32)
        summed, paired = sweep(body, (zero, zero))
        put = r.rxn.at[number, own]
        put[0:1, :] = total_row(summed)
        put[1:2, :] = total_row(paired)
        both = share_narrow(number, False, work)
        r.g_ib[place : place + 1, :] = both[0:1]
        r.g_ig[place : place + 1, :] = both[1:2]
        steep = scale * gain
        lift, tilt = both[0:1] / total, both[1:2] / total

        def back(rs, lv, carry):
            xhat = (ref[rs, :] - mean) * scale
            value = (steep * (acc[rs, :] - lv * (lift + xhat * tilt))).astype(BF)
            r.dn[rs, :] = value
            if spread:
                r.give[rs, :] = value.astype(F32)
            return carry

        sweep(back, 0)

    def wide_cotangent(number, ref, place, gain, bias, cotangent, work=nothing, work_more=nothing):
        put = r.rxw1.at[number, me]
        st = r.stw.at[place]
        for n, cs in enumerate(blocks):
            mean, scale = st[0:1, cs], st[1:2, cs]
            gn, bs = gain[:, 512 * n : 512 * n + 512], bias[:, 512 * n : 512 * n + 512]

            def body(rs, lv, carry):
                xhat = (ref[n, rs, :] - mean) * scale
                g = cotangent(n, rs, cs, lv, xhat * gn + bs)
                r.up[n, rs, :] = g
                return carry[0] + fold(g), carry[1] + fold(g * xhat)

            zero = jnp.zeros((8, 512), F32)
            summed, paired = sweep(body, (zero, zero))
            put[0:1, cs] = total_row(summed)
            put[1:2, cs] = total_row(paired)
        both = share_wide(number, False, work, work_more)
        r.g_bb[place : place + 1, :] = both[0:1]
        r.g_bg[place : place + 1, :] = both[1:2]
        for n, cs in enumerate(blocks):
            mean, scale = st[0:1, cs], st[1:2, cs]
            span = slice(512 * n, 512 * n + 512)
            steep = scale * gain[:, span]
            lift, tilt = both[0:1, span] / total, both[1:2, span] / total

            def back(rs, lv, carry):
                xhat = (ref[n, rs, :] - mean) * scale
                value = steep * (r.up[n, rs, :] - lv * (lift + xhat * tilt))
                r.dwide[rs, cs] = value.astype(BF)
                return carry

            sweep(back, 0)

    def tap(ref, k):
        return ref[pl.ds(pl.multiple_of(k * INNER, INNER), INNER), :]

    def offset_tap(k):
        return r.off[:, pl.ds(pl.multiple_of(k * INNER, INNER), INNER)]

    def slot_rows(s):
        return pl.ds(s * PIXELS, PIXELS)

    def steps_of(k):
        return 2 * lax.div(k, 3) - 2, 2 * lax.rem(k, 3) - 2

    WID, CON, NAR, EXP, DEF, RED, OFF = range(7)
    nth = {WID: 0, NAR: 1, EXP: 2, RED: 3}
    result = {
        WID: r.g_wid,
        CON: r.g_con,
        NAR: r.g_nar,
        EXP: r.g_exp,
        DEF: r.g_def,
        RED: r.g_red,
        OFF: r.g_off,
    }
    pool, land, grad, far_blocks = r.pool, r.land, r.grad, r.far_blocks

    deep_parts = 4 if deep % 32 == 0 else 2
    wide_parts = {WID: 2, NAR: 2, EXP: 2, RED: 4}

    def z_hold(u):
        if u == RED:
            return [r.a3.at[i, pl.ds(0, wide)] for i in range(3)]
        return [r.zwide.at[nth[u], i] for i in range(3)]

    def z_parts(u):
        if u in nth:
            hold = z_hold(u)
            for q in range(wide_parts[u]):
                rows = wide // (wide_parts[u] // 2)
                rs, hs = pl.ds(q // 2 * rows, rows), halves[q % 2]
                yield tuple(ref.at[rs, hs] for ref in hold) + (result[u].at[rs, hs],)
        elif u == OFF:
            yield r.goff, r.zoff.at[0], r.zoff.at[1], result[u]
        else:
            for q in range(deep_parts):
                back, at = divmod(q, deep_parts // 2)
                source = r.b3.at[(2 if u == DEF else 0) + back]
                if u == DEF:
                    first, second = (r.b1, r.a2) if back == 0 else (r.b2, r.a3.at[3])
                else:
                    first, second = r.zdeep.at[0, back], r.zdeep.at[1, back]
                size = deep // deep_parts
                rows = pl.ds(at * size, size)
                out = result[u].at[pl.ds(q * size, size)]
                yield source.at[rows], first.at[rows], second.at[rows], out

    def z_sems(u, q, step):
        return r.z_s.at[u, q, step], r.z_r.at[u, q, step]

    def z1(u, some=None):
        for q, (source, first, second, out) in enumerate(z_parts(u)):
            if some is not None and q not in some:
                continue
            sent, received = z_sems(u, q, 0)

            @pl.when(outside)
            def _():
                send(source, first, sent, received, (me, flip(mine, 0)))

            later(("z", u), source, sent, outside)

    def z2(u, some=None):
        for q, (source, first, second, out) in enumerate(z_parts(u)):
            if some is not None and q not in some:
                continue
            sent, received = z_sems(u, q, 1)

            @pl.when(inside)
            def _():
                settle(first, z_sems(u, q, 0)[1])
                accumulate(source, first)
                send(source, second, sent, received, (me, 3 - mine))

            later(("z", u), source, sent, inside)

    def z3(u, some=None):
        for q, (source, first, second, out) in enumerate(z_parts(u)):
            if some is not None and q not in some:
                continue
            sent, received = z_sems(u, q, 2)

            @pl.when(inside)
            def _():
                settle(second, z_sems(u, q, 1)[1])
                accumulate(second, source)
                send(second, first, sent, received, (me, flip(mine, 0)))
                dma(second, out, r.res_sem.at[u, q]).start()

            later(("zl", u), second, sent, inside)

    def z4(u, some=None):
        for q, (source, first, second, out) in enumerate(z_parts(u)):
            if some is not None and q not in some:
                continue

            @pl.when(outside)
            def _():
                settle(first, z_sems(u, q, 2)[1])
                dma(first, out, r.res_sem.at[u, q]).start()

    def z_clear(u):
        flush(("z", u))
        flush(("zl", u))
        for q, (source, first, second, out) in enumerate(z_parts(u)):
            dma(first, out, r.res_sem.at[u, q]).wait()

    def wide_begin(u, left, right):
        p = nth[u] % 2
        flush("sib")
        flush(("keep", p))
        low = p + (2 - p) * core
        high = p + (2 - p) * (1 - core)

        def step(m, carry):
            block = left[:, pl.ds(pl.multiple_of(m * (2 * wide), 2 * wide), 2 * wide)]
            pool[low, m] = mm(block[:, :wide], right[...], TN)
            pool[high, m] = mm(block[:, wide:], right[...], TN)
            send(
                pool.at[2, m], r.corel.at[m], r.core_s.at[u], r.core_r.at[u], sibling
            )
            return carry

        lax.fori_loop(0, chips, step, 0)
        later("sib", r.corel, r.core_s.at[u])

    def piece(h, t, j, toward):
        value = 0
        for i, bit in enumerate(orders[h]):
            if i < t:
                part = bit_of(chip, bit)
            elif i == t:
                part = bit_of(toward, bit)
            else:
                part = (j >> (i - t - 1)) & 1
            value = value + part * (1 << bit)
        return value

    def step_place(u, h, t):
        first, count = chips - (chips >> t), chips >> (t + 1)
        p = nth[u] % 2
        sems = r.step_s.at[nth[u], h, t], r.step_r.at[nth[u], h, t]
        return p, first, count, sems, land.at[p, h, pl.ds(first, count)]

    def wide_send(u, t):
        for h in range(2):
            p, first, count, (sent, received), region = step_place(u, h, t)
            toward = flip(chip, orders[h][t])
            if u == RED:
                pl.semaphore_wait(r.credit.at[h, t], 1)
            for j in range(count):
                send(
                    pool.at[p, piece(h, t, j, toward), :, halves[h]],
                    land.at[p, h, first + j],
                    sent,
                    received,
                    (2 * toward + core, mine),
                )
            later(("keep", p), region, sent)

    def wide_add(u, t):
        for h in range(2):
            p, first, count, (sent, received), region = step_place(u, h, t)
            settle(region, received)
            if t == bits - 1:
                mix(z_hold(u)[0].at[:, halves[h]], pool.at[p, chip, :, halves[h]], land.at[p, h, first])
            else:
                for j in range(count):
                    accumulate(
                        pool.at[p, piece(h, t, j, chip), :, halves[h]], land.at[p, h, first + j]
                    )
            if u == NAR:
                pl.semaphore_signal(
                    r.credit.at[h, t],
                    inc=1,
                    device_id=(2 * flip(chip, orders[h][t]) + core, mine),
                    device_id_type=MESH,
                )

    def wide_core(u):
        p = nth[u] % 2
        settle(r.corel, r.core_r.at[u])

        def step(m, carry):
            accumulate(pool.at[p, m], r.corel.at[m])
            return carry

        lax.fori_loop(0, chips, step, 0)

    def wide_step(u, t):
        wide_add(u, t - 1)
        if t < bits:
            wide_send(u, t)
        else:
            z1(u)

    def held_at(h, j):
        value = chip
        for i in range(bits):
            if (j >> i) & 1:
                value = flip(value, orders[h][i])
        return value

    def gather_send(a, t, some=None):
        for h in range(2):
            partner = flip(chip, orders[h][t])
            sent, received = r.ag_s.at[a, h, t], r.ag_r.at[a, h, t]
            for j in range(1 << t) if some is None else some:
                block = far_blocks.at[a, held_at(h, j), :, halves[h]]
                source = r.give.at[:, halves[h]] if j == 0 else block
                send(source, block, sent, received, (2 * partner + core, mine))
            if some is None or 0 in some:
                later(("ag", a), far_blocks.at[a, pl.ds(0, 1 << t), :, halves[h]], sent)

    def gather_start(a):
        block = far_blocks.at[a, chip]
        dma(r.give, block, r.give_sem.at[a]).start()
        later(("ag", a), block, r.give_sem.at[a])
        gather_send(a, 0)

    def gather_wait(a, t):
        for h in range(2):
            settle(far_blocks.at[a, pl.ds(0, 1 << t), :, halves[h]], r.ag_r.at[a, h, t])

    def gather_step(a, t, some=None):
        gather_wait(a, t - 1)
        gather_send(a, t, some)

    def gather_first(a, t):
        if t < bits:
            gather_send(a, t, [0])

    def gather_rest(a):
        for t in range(1, bits):
            gather_wait(a, t - 1)
            gather_send(a, t, range(1 if t == 1 else 0, 1 << t))

    def gather_end(a):
        gather_wait(a, bits - 1)
        flush(("ag", a))

    def tiny_send(a):
        for step in range(1, chips):
            block = r.tiny.at[a, chip]
            peer = lax.rem(chip + step, chips)
            send(block, block, r.tiny_s.at[a], r.tiny_r.at[a], (2 * peer + core, mine))
        later("end", r.tiny.at[a, pl.ds(0, chips - 1)], r.tiny_s.at[a])

    def tiny_wait(a):
        settle(r.tiny.at[a, pl.ds(0, chips - 1)], r.tiny_r.at[a])

    group = min(chips, 4)
    first_tap = lax.div(2 * deep * chip, INNER)
    margin = 2 * deep * chip - first_tap * INNER

    def taps_of(kk):
        k = jnp.minimum(first_tap + kk, TAPS - 1)
        return (k, *steps_of(k))

    def fetch_fields(a, g):
        copy = dma(far_blocks.at[a, pl.ds(g * group, group)], r.taken, r.take_sem.at[2])
        copy.start()
        copy.wait()

    def image_of(i, g):
        m, s = lax.div(i, SLOTS), lax.rem(i, SLOTS)
        rows = pl.ds(pl.multiple_of(i * PIXELS, PIXELS), PIXELS)
        field = r.taken[m, pl.ds(pl.multiple_of(s * PIXELS, PIXELS), PIXELS), :].astype(BF)
        flat = r.tiny[0, g * group + m, s, 18:19, :] == 0.0
        dr = jnp.where(flat, r.geo[0, 0], r.geo[1, 0])
        dc = jnp.where(flat, r.geo[0, 1], r.geo[1, 1])
        return g * group + m, s, rows, field, dr, dc

    def group_rows(g):
        return pl.ds(g * (group * ROWS), group * ROWS)

    def columns(u, kk):
        x = 1 if u == DEF else 0
        k, down, across = taps_of(kk)
        for g in range(chips // group):
            if kk == 0 or chips > group:
                fetch_fields(0 if u == DEF else 1, g)
            if g == 0:
                flush("columns")

            def image(i, carry):
                m, s, rows, field, dr, dc = image_of(i, g)
                if u == CON:
                    hit = jnp.where((dr == down) & (dc == across), 1.0, 0.0).astype(BF)
                    r.xall[0, rows, :] = mm(hit, field, NN).astype(BF)
                    return carry
                tiny = r.tiny.at[0, m, s]
                fy, fx = tiny[pl.ds(2 * k, 1), :], tiny[pl.ds(2 * k + 1, 1), :]
                ay = jnp.where(dr == -down, 1.0 - fy, jnp.where(dr == -down - 1, fy, 0.0))
                ax = jnp.where(dc == -across, 1.0 - fx, jnp.where(dc == -across - 1, fx, 0.0))
                r.xall[0, rows, :] = mm((ay * ax).astype(BF), field, TN).astype(BF)
                return carry

            lax.fori_loop(0, group * SLOTS, image, 0)
            place = r.far_columns.at[x, kk, group_rows(g)]
            copy = dma(r.xall.at[0], place, r.x_sem.at[0])
            copy.start()
            if g + 1 < chips // group:
                copy.wait()
            else:
                later("columns", place, r.x_sem.at[0])

    def deep_make(u):
        flush("deep")
        flush("columns")
        x, back_of = (1, 3) if u == DEF else (0, 2)
        for g in range(chips // group):

            def fetch(m):
                return dma(
                    far_blocks.at[back_of, g * group + m], r.drawn.at[m % 2], r.take_sem.at[m % 2]
                )

            def draw(kk):
                slot = lax.rem(kk, 2)
                return dma(
                    r.far_columns.at[x, kk, group_rows(g)], r.xall.at[slot], r.x_sem.at[slot]
                )

            for m in range(min(2, group)):
                fetch(m).start()
            draw(0).start()
            for m in range(group):
                fetch(m).wait()

                def lower(i, carry):
                    rows = pl.ds(pl.multiple_of(m * ROWS + i * 32, 32), 32)
                    there = pl.ds(pl.multiple_of(i * 32, 32), 32)
                    r.yall[rows, :] = r.drawn[m % 2, there, :].astype(BF)
                    return carry

                lax.fori_loop(0, ROWS // 32, lower, 0)
                if m + 2 < group:
                    fetch(m + 2).start()

            def one(kk, carry):
                @pl.when(kk + 1 < taps)
                def _():
                    draw(kk + 1).start()

                draw(kk).wait()
                at = pl.ds(pl.multiple_of(kk * INNER, INNER), INNER)
                part = mm(r.xall[lax.rem(kk, 2)], r.yall[...], TN)
                if g == 0:
                    grad[at, :] = part
                else:
                    grad[at, :] += part
                return carry

            lax.fori_loop(0, taps, one, 0)
        away = pl.ds(pl.multiple_of(margin + (1 - core) * deep, 8), deep)
        send(grad.at[away], r.cored, r.core_s.at[u], r.core_r.at[u], sibling)
        later("deep", r.cored, r.core_s.at[u])

    def off_make():
        for g in range(chips // group):
            fetch_fields(0, g)

            def one(kk, carry):
                k, down, across = taps_of(kk)

                def image(i, share):
                    m, s, rows, field, dr, dc = image_of(i, g)
                    hit = jnp.where((dr == down) & (dc == across), 1.0, 0.0).astype(BF)
                    moved = mm(r.tiny[1, m, s].astype(BF), hit, NN).astype(BF)
                    return share + mm(moved, field, NN)

                at = pl.ds(pl.multiple_of(kk * INNER, INNER), INNER)
                share = lax.fori_loop(0, group * SLOTS, image, jnp.zeros((24, INNER), F32))
                if g == 0:
                    r.goff[:, at] = share
                else:
                    r.goff[:, at] += share
                return carry

            lax.fori_loop(0, taps, one, 0)
        send(r.goff, r.coreo, r.core_s.at[OFF], r.core_r.at[OFF], sibling)

    def off_core():
        settle(r.goff, r.core_s.at[OFF])
        settle(r.coreo, r.core_r.at[OFF])
        accumulate(r.goff, r.coreo)

    def deep_core(u):
        settle(r.cored, r.core_r.at[u])
        half = deep // 2
        step = math.gcd(half, 32)
        for q in range(2):
            target = r.b3.at[(2 if u == DEF else 0) + q]

            def body(i, carry):
                at = pl.multiple_of(i * step, 8)
                here = grad[pl.ds(pl.multiple_of(margin + core * deep + q * half + at, 8), step), :]
                target[pl.ds(at, step), :] = here + r.cored[pl.ds(q * half + at, step), :]
                return carry

            lax.fori_loop(0, half // step, body, 0)
    images, between, acc, up = r.images, r.between, r.acc, r.up
    ig = [r.ig[i : i + 1, :] for i in range(4)]
    ib = [r.ib[i : i + 1, :] for i in range(4)]
    bg = [r.bg[i : i + 1, :] for i in range(2)]
    bb = [r.bb[i : i + 1, :] for i in range(2)]

    def geometry():
        q = lax.broadcasted_iota(jnp.int32, (PIXELS, PIXELS), 1)
        p = lax.broadcasted_iota(jnp.int32, (PIXELS, PIXELS), 0)

        def place_of(at, kind):
            if kind:
                row = lax.shift_right_logical(at, 2)
                return row, at - row * SHORT
            row = (at >= LONG).astype(jnp.int32) + (at >= 2 * LONG).astype(jnp.int32)
            row = row + (at >= 3 * LONG).astype(jnp.int32)
            return row, at - row * LONG

        for kind in range(2):
            row_q, col_q = place_of(q, kind)
            row_p, col_p = place_of(p, kind)
            r.geo[kind, 0] = row_q - row_p
            r.geo[kind, 1] = col_q - col_p

            def hot(k, carry):
                down, across = steps_of(k)
                hit = (r.geo[kind, 0] == down) & (r.geo[kind, 1] == across)
                r.tmat[kind, k] = jnp.where(hit, 1.0, 0.0).astype(BF)
                return carry

            lax.fori_loop(0, TAPS, hot, 0)

    def shifted(s, k):
        return r.tmat[orient[s], k]

    loads.images_h.wait()
    loads.red_h.wait()
    r.a1[...] = mm(images[...], r.redwid[...], NN)
    loads.wid_h = load(7, r.wid_h, r.redwid)
    pl.semaphore_wait(barrier, everyone - 1)
    narrow_stats(r.a1, 0, geometry)
    norm_silu(r.a1, 0, ig[0], ib[0], r.inner, True)
    gather_start(0)

    loads.off_h.wait()
    inner = r.inner
    lane = lax.broadcasted_iota(jnp.int32, (PIXELS, OFFSETS), 1)
    for s in range(SLOTS):

        def gather(k, carry):
            col = mm(shifted(s, k), inner[slot_rows(s), :], NN).astype(BF)
            return carry + mm(col, offset_tap(k), NT)

        offsets = lax.fori_loop(0, TAPS, gather, jnp.zeros((PIXELS, OFFSETS), F32))
        frac = sigmoid(offsets)
        r.frac[slot_rows(s), :] = frac
        coarse = frac.astype(BF)
        fine = (frac - coarse.astype(F32)).astype(BF)
        unit = r.tmat[0, TAPS // 2]
        put = r.tiny.at[0, chip, s]
        put[...] = jnp.zeros((24, PIXELS), F32) + orient[s].astype(F32)
        put[0:OFFSETS, :] = mm(coarse, unit, TN) + mm(fine, unit, TN)
    tiny_send(0)

    def bilinear(s, k):
        down, across = steps_of(k)
        frac = r.frac[slot_rows(s), :]
        fy = jnp.sum(jnp.where(lane == 2 * k, frac, 0.0), axis=1, keepdims=True)
        fx = jnp.sum(jnp.where(lane == 2 * k + 1, frac, 0.0), axis=1, keepdims=True)
        dr, dc = r.geo[orient[s], 0], r.geo[orient[s], 1]
        in_y = (dr == down, dr == down + 1)
        in_x = (dc == across, dc == across + 1)
        ay = jnp.where(in_y[0], 1.0 - fy, jnp.where(in_y[1], fy, 0.0))
        ax = jnp.where(in_x[0], 1.0 - fx, jnp.where(in_x[1], fx, 0.0))
        return fy, fx, ay, ax, in_y, in_x

    loads.def_h.wait()
    acc[...] = jnp.zeros((ROWS, INNER), F32)

    def sample(k, carry):
        for s in range(SLOTS):
            _, _, ay, ax, _, _ = bilinear(s, k)
            weight = (ay * ax).astype(BF)
            r.wmat[s, k] = weight
            r.turned[slot_rows(s), :] = mm(weight, inner[slot_rows(s), :], NN).astype(BF)
        acc[...] += mm(r.turned[...], tap(r.dfmcon, k), NN)
        return carry

    lax.fori_loop(0, TAPS, sample, 0)
    loads.con_h = load(8, r.con_h, r.dfmcon)
    r.a2[...] = acc[...]
    narrow_stats(r.a2, 1, lambda: gather_first(0, 1))
    norm_silu(r.a2, 1, ig[1], ib[1], r.hidden, False)

    def widen(source, weight, target):
        def step(n, carry):
            rows = pl.ds(pl.multiple_of(n * 512, 512), 512)
            target[n] = mm(source[...], weight[rows, :], NT)
            return carry

        lax.fori_loop(0, CHANNELS // 512, step, 0)

    loads.exp_h.wait()
    widen(r.hidden, r.exp, r.a3)
    wide_stats(r.a3, 0, lambda: gather_rest(0))
    for n, cs in enumerate(blocks):
        mean = r.stw[0, 0:1, cs]
        steep = r.stw[0, 1:2, cs] * bg[0][:, 512 * n : 512 * n + 512]
        bias = bb[0][:, 512 * n : 512 * n + 512]

        def join(rs, lv, carry):
            z = (r.a3[n, rs, :] - mean) * steep + bias + images[rs, cs].astype(F32)
            between[rs, cs] = (z * sigmoid(z)).astype(BF)
            return carry

        sweep(join, 0)

    loads.nar_h.wait()
    r.b1[...] = mm(between[...], r.nar[...], NN)

    def work_b1():
        gather_end(0)
        tiny_wait(0)
        columns(DEF, 0)

    narrow_stats(r.b1, 2, work_b1)
    norm_silu(r.b1, 2, ig[2], ib[2], r.narrow, True)
    gather_start(1)

    loads.con_h.wait()
    acc[...] = jnp.zeros((ROWS, INNER), F32)

    def convolve(k, carry):
        for s in range(SLOTS):
            r.turned[slot_rows(s), :] = mm(
                shifted(s, k), r.narrow[slot_rows(s), :], NN
            ).astype(BF)
        acc[...] += mm(r.turned[...], tap(r.dfmcon, k), NN)
        return carry

    lax.fori_loop(0, TAPS, convolve, 0)
    r.b2[...] = acc[...]
    def work_b2():
        gather_first(1, 1)
        columns(DEF, 1)

    narrow_stats(r.b2, 3, work_b2)
    norm_silu(r.b2, 3, ig[3], ib[3], r.mixed, False)

    loads.wid_h.wait()
    widen(r.mixed, r.redwid, r.b3)

    def work_b3():
        gather_rest(1)
        for kk in range(2, taps):
            columns(DEF, kk)

    wide_stats(r.b3, 1, work_b3)

    loads.cot_h.wait()

    def last(n, rs, cs, lv, pre):
        z = pre + between[rs, cs].astype(F32)
        sg = sigmoid(z)
        r.obuf[rs, cs] = (lv * (z * sg)).astype(BF)
        return r.dwide[rs, cs].astype(F32) * (lv * (sg * (1.0 + z * (1.0 - sg))))

    def work_f():
        gather_end(1)
        columns(CON, 0)

    wide_cotangent(2, r.b3, 1, bg[1], bb[1], last, nothing, work_f)
    out_copy = dma(r.obuf, r.out_h, r.out_sem.at[0])
    out_copy.start()
    wide_begin(WID, r.dwide, r.mixed)
    acc[...] = mm(r.dwide[...], r.redwid[...], NN)
    loads.red_h = load(9, r.red_h, r.redwid)
    wide_core(WID)

    def work_e():
        wide_send(WID, 0)
        columns(CON, 1)

    narrow_cotangent(r.b2, 3, ig[3], ib[3], 4, True, work_e)

    acc[...] = jnp.zeros((ROWS, INNER), F32)

    def spread(k, carry):
        for s in range(SLOTS):
            r.turned[slot_rows(s), :] = mm(
                shifted(s, TAPS - 1 - k), r.dn[slot_rows(s), :], NN
            ).astype(BF)
        acc[...] += mm(r.turned[...], tap(r.dfmcon, k), NT)
        return carry

    lax.fori_loop(0, TAPS, spread, 0)
    loads.def_h = load(10, r.def_h, r.dfmcon)

    def work_d():
        wide_step(WID, 1)
        gather_start(2)
        for kk in range(2, taps):
            columns(CON, kk)

    narrow_cotangent(r.b1, 2, ig[2], ib[2], 5, False, work_d)
    for t in range(2, bits + 1):
        wide_step(WID, t)
    wide_begin(NAR, between, r.dn)

    def add_back(n, carry):
        rows = pl.ds(pl.multiple_of(n * 512, 512), 512)
        up[n] += mm(r.dn[...], r.nar[rows, :], NT)
        return carry

    lax.fori_loop(0, CHANNELS // 512, add_back, 0)
    wide_core(NAR)

    def first(n, rs, cs, lv, pre):
        z = pre + images[rs, cs].astype(F32)
        sg = sigmoid(z)
        return up[n, rs, :] * (sg * (1.0 + z * (1.0 - sg)))

    def work_c():
        for t in range(1, bits):
            gather_step(2, t)

    def work_more_c():
        z2(WID)

    wide_cotangent(3, r.a3, 0, bg[0], bb[0], first, work_c, work_more_c)
    wide_begin(EXP, r.dwide, r.hidden)
    acc[...] = mm(r.dwide[...], r.exp[...], NN)
    wide_core(EXP)

    def work_b():
        wide_send(NAR, 0)
        z3(WID)
        gather_end(2)
        deep_make(CON)

    narrow_cotangent(r.a2, 1, ig[1], ib[1], 6, True, work_b)
    wide_step(NAR, 1)
    gather_start(3)
    deep_core(CON)
    early, late = range(deep_parts // 2), range(deep_parts // 2, deep_parts)
    z1(CON, early)

    loads.def_h.wait()
    acc[...] = jnp.zeros((ROWS, INNER), F32)
    r.doff[...] = jnp.zeros((ROWS, OFFSETS), F32)

    def unsample(k, carry):
        r.turned[...] = mm(r.dn[...], tap(r.dfmcon, k), NT).astype(BF)
        for s in range(SLOTS):
            rs = slot_rows(s)
            back = r.turned[rs, :]
            pairs = mm(back, inner[rs, :], NT)
            fy, fx, ay, ax, in_y, in_x = bilinear(s, k)
            slope_y = jnp.where(in_y[1], ax, 0.0) - jnp.where(in_y[0], ax, 0.0)
            slope_x = jnp.where(in_x[1], ay, 0.0) - jnp.where(in_x[0], ay, 0.0)
            to_y = jnp.sum(pairs * slope_y, axis=1, keepdims=True) * (fy * (1.0 - fy))
            to_x = jnp.sum(pairs * slope_x, axis=1, keepdims=True) * (fx * (1.0 - fx))
            r.doff[rs, :] += jnp.where(lane == 2 * k, to_y, 0.0) + jnp.where(
                lane == 2 * k + 1, to_x, 0.0
            )
            acc[rs, :] += mm(r.wmat[s, k], back, TN)
        return carry

    lax.fori_loop(0, TAPS, unsample, 0)
    for s in range(SLOTS):
        put = r.tiny.at[1, chip, s]
        put[...] = jnp.zeros((24, PIXELS), F32)
        put[0:OFFSETS, :] = mm(
            r.doff[slot_rows(s), :].astype(BF), r.tmat[0, TAPS // 2], TN
        )
    tiny_send(1)

    def untap(k, carry):
        for s in range(SLOTS):
            rs = slot_rows(s)
            moved = mm(shifted(s, TAPS - 1 - k), r.doff[rs, :].astype(BF), NN).astype(BF)
            acc[rs, :] += mm(moved, offset_tap(k), NN)
        return carry

    lax.fori_loop(0, TAPS, untap, 0)

    def work_a():
        for t in range(1, bits):
            gather_step(3, t)
        wide_send(EXP, 0)
        z1(CON, late)
        for t in range(2, bits + 1):
            wide_step(NAR, t)
        z2(CON, early)
        z4(WID)

    narrow_cotangent(r.a1, 0, ig[0], ib[0], 7, False, work_a)
    wide_begin(RED, images, r.dn)

    out_copy.wait()
    loads.red_h.wait()

    def finish(n, carry):
        rows = pl.ds(pl.multiple_of(n * 512, 512), 512)
        r.obuf[:, rows] = (up[n] + mm(r.dn[...], r.redwid[rows, :], NT)).astype(BF)
        return carry

    lax.fori_loop(0, CHANNELS // 512, finish, 0)
    grad_copy = dma(r.obuf, r.grad_h, r.out_sem.at[1])
    grad_copy.start()
    wide_core(RED)
    wide_send(RED, 0)
    gather_end(3)
    deep_make(DEF)
    z2(CON, late)
    z3(CON, early)
    deep_core(DEF)
    z1(DEF)
    tiny_wait(1)
    off_make()
    wide_step(EXP, 1)
    z2(NAR)
    off_core()
    z1(OFF)
    z2(DEF, [0])
    z3(CON, late)
    wide_step(RED, 1)
    z2(DEF, [1])
    z3(DEF, [0])
    for t in range(2, bits + 1):
        wide_step(EXP, t)
    z2(DEF, [2])
    z3(NAR)
    for t in range(2, bits + 1):
        wide_step(RED, t)
    z2(DEF, [3])
    z3(DEF, [1, 2])
    z2(OFF)
    z2(EXP)
    z3(DEF, [3])
    z3(OFF)
    z2(RED)
    z3(EXP)
    z3(RED)
    z4(CON)
    z4(NAR)
    z4(DEF)
    z4(OFF)
    z4(EXP)
    z4(RED)
    for u in range(7):
        z_clear(u)
    grad_copy.wait()
    for tag in list(waiting):
        flush(tag)


MOVED = ["out", "grad", "con", "def", "wid", "nar", "exp", "red"]


def deliver(dp, names, *refs):
    r = types.SimpleNamespace(**dict(zip(names, refs)))
    _, _, _, deep, _ = layout(dp)
    place = lax.axis_index("dp")
    moves = []
    for i, name in enumerate(MOVED):
        source, target, hold = (getattr(r, kind + name) for kind in ("from_", "to_", "hold_"))
        taken = pltpu.make_async_copy(source, hold, r.sems.at[0, i])
        taken.start()
        moves.append((taken, pltpu.make_async_copy(hold, target, r.sems.at[1, i])))

    for taken, given in moves:
        taken.wait()
        given.start()

    def span(ref, start, target):
        rows, lanes = ref.shape
        moved = pltpu.roll(ref[...], lax.rem(lanes - start, lanes), 1)
        target[...] = moved[: target.shape[0], : target.shape[1]]

    span(r.g_ig, place * (INNER // dp), r.to_ig)
    span(r.g_ib, place * (INNER // dp), r.to_ib)
    span(r.g_bg, place * (CHANNELS // dp), r.to_bg)
    span(r.g_bb, place * (CHANNELS // dp), r.to_bb)
    chip, core = lax.div(place, 2), lax.rem(place, 2)
    span(r.g_off, lax.rem(2 * deep * chip, INNER) + deep * core, r.to_off)
    for taken, given in moves:
        given.wait()


def per_device(
    images,
    counts,
    orientation,
    cotangent,
    reducer,
    offseter,
    deformer,
    expander,
    narrower,
    convolver,
    widener,
    inner_gains,
    inner_biases,
    broad_gains,
    broad_biases,
):
    dp, outer = lax.axis_size("dp"), lax.axis_size("outer")
    chips, bits, wide, deep, taps = layout(dp)
    buffers = scratch(dp, outer)
    smem = pl.BlockSpec(memory_space=pltpu.SMEM)
    vmem = pl.BlockSpec(memory_space=pltpu.VMEM)
    far = pl.BlockSpec(memory_space=pl.ANY)
    shape = jax.ShapeDtypeStruct
    inputs = dict(
        counts=(smem, counts),
        orient=(smem, orientation),
        ig=(vmem, inner_gains),
        ib=(vmem, inner_biases),
        bg=(vmem, broad_gains),
        bb=(vmem, broad_biases),
        images_h=(far, images.reshape(ROWS, CHANNELS)),
        cot_h=(far, cotangent.reshape(ROWS, CHANNELS)),
        red_h=(far, reducer),
        off_h=(far, offseter.T),
        def_h=(far, deformer),
        exp_h=(far, expander),
        nar_h=(far, narrower),
        con_h=(far, convolver),
        wid_h=(far, widener),
    )
    outputs = dict(
        out_h=(far, shape((ROWS, CHANNELS), BF)),
        grad_h=(far, shape((ROWS, CHANNELS), BF)),
        g_red=(far, shape((wide, INNER), F32)),
        g_off=(far, shape((24, taps * INNER), F32)),
        g_def=(far, shape((deep, INNER), F32)),
        g_exp=(far, shape((wide, INNER), F32)),
        g_nar=(far, shape((wide, INNER), F32)),
        g_con=(far, shape((deep, INNER), F32)),
        g_wid=(far, shape((wide, INNER), F32)),
        g_ig=(vmem, shape((4, INNER), F32)),
        g_ib=(vmem, shape((4, INNER), F32)),
        g_bg=(vmem, shape((2, CHANNELS), F32)),
        g_bb=(vmem, shape((2, CHANNELS), F32)),
        far_blocks=(far, shape((4, chips, ROWS, INNER), F32)),
        far_columns=(far, shape((2, taps, chips * ROWS, INNER), BF)),
    )
    names = list(inputs) + list(outputs) + list(buffers)
    outs = pl.pallas_call(
        functools.partial(kernel, dp, outer, names),
        out_shape=[spec for _, spec in outputs.values()],
        in_specs=[space for space, _ in inputs.values()],
        out_specs=[space for space, _ in outputs.values()],
        scratch_shapes=list(buffers.values()),
        compiler_params=pltpu.CompilerParams(
            collective_id=0, has_side_effects=True, vmem_limit_bytes=63 * 1024 * 1024
        ),
        name="chain",
    )(*[value for _, value in inputs.values()])
    held = dict(zip(outputs, outs))
    big = dict(
        out=held["out_h"],
        grad=held["grad_h"],
        red=held["g_red"],
        **{"def": held["g_def"]},
        exp=held["g_exp"],
        nar=held["g_nar"],
        con=held["g_con"],
        wid=held["g_wid"],
    )
    small = {name: held[name] for name in ("g_off", "g_ig", "g_ib", "g_bg", "g_bb")}
    firsts = {"from_" + name: value for name, value in big.items()}
    finals = {"to_" + name: shape(value.shape, value.dtype) for name, value in big.items()}
    holds = {"hold_" + name: pltpu.VMEM(value.shape, value.dtype) for name, value in big.items()}
    lasts = dict(
        to_off=shape((OFFSETS, deep), F32),
        to_ig=shape((4, INNER // dp), F32),
        to_ib=shape((4, INNER // dp), F32),
        to_bg=shape((2, CHANNELS // dp), F32),
        to_bb=shape((2, CHANNELS // dp), F32),
    )
    names = [*firsts, *small, *finals, *lasts, *holds, "sems"]
    got = pl.pallas_call(
        functools.partial(deliver, dp, names),
        out_shape=[*finals.values(), *lasts.values()],
        in_specs=[far] * len(firsts) + [vmem] * len(small),
        out_specs=[far] * len(finals) + [vmem] * len(lasts),
        scratch_shapes=[*holds.values(), pltpu.SemaphoreType.DMA((2, len(big)))],
        compiler_params=pltpu.CompilerParams(vmem_limit_bytes=60 * 1024 * 1024),
        name="deliver",
    )(*firsts.values(), *small.values())
    out, grad, g_red, g_def, g_exp, g_nar, g_con, g_wid, g_off, *others = got
    return (
        out.reshape(SLOTS, PIXELS, CHANNELS),
        grad.reshape(SLOTS, PIXELS, CHANNELS),
        g_red,
        g_off.T,
        g_def,
        g_exp,
        g_nar,
        g_con,
        g_wid,
        *others,
    )


def solution(mesh):
    spread = P(("dp", "outer"), None, None)
    in_specs = (spread, P(), P(("dp", "outer")), spread) + (P(),) * 11
    out_specs = (spread, spread) + (P("dp", None),) * 7 + (P(None, "dp"),) * 4
    return jax.shard_map(
        per_device, mesh=mesh, in_specs=in_specs, out_specs=out_specs, check_vma=False
    )
```

```python
import functools
import math
import types

import jax
import jax.numpy as jnp
from jax import lax
from jax.experimental import pallas as pl
from jax.experimental.pallas import tpu as pltpu
from jax.sharding import PartitionSpec as P

CHANNELS = 2048
INNER = 512
TAPS = 9
SLOTS = 2
SHORT = 4
LONG = 36
PIXELS = 144
ROWS = SLOTS * PIXELS
OFFSETS = 2 * TAPS
EPS = 1e-05
BF = jnp.bfloat16
F32 = jnp.float32
MESH = pl.DeviceIdType.MESH
NN = (((1,), (0,)), ((), ()))
NT = (((1,), (1,)), ((), ()))
TN = (((0,), (0,)), ((), ()))


def mm(left, right, dims):
    return lax.dot_general(left, right, dims, preferred_element_type=F32)


def sigmoid(value):
    return 0.5 * jnp.tanh(0.5 * value) + 0.5


def fold(value):
    return jnp.sum(value.reshape(value.shape[0] // 8, 8, value.shape[1]), axis=0)


def total_row(value):
    return jnp.sum(value, axis=0, keepdims=True)


def layout(dp):
    chips = dp // 2
    bits = chips.bit_length() - 1
    wide = CHANNELS // dp
    deep = TAPS * INNER // dp
    taps = max(
        -(-(2 * deep * chip % INNER + 2 * deep) // INNER) for chip in range(chips)
    )
    return chips, bits, wide, deep, taps


def scratch(dp, outer):
    vmem = pltpu.VMEM
    dma = pltpu.SemaphoreType.DMA
    chips, bits, wide, deep, taps = layout(dp)
    everyone = dp * outer
    group = min(chips, 4)
    return dict(
        images=vmem((ROWS, CHANNELS), BF),
        between=vmem((ROWS, CHANNELS), BF),
        dwide=vmem((ROWS, CHANNELS), BF),
        obuf=vmem((ROWS, CHANNELS), BF),
        redwid=vmem((CHANNELS, INNER), BF),
        exp=vmem((CHANNELS, INNER), BF),
        nar=vmem((CHANNELS, INNER), BF),
        dfmcon=vmem((TAPS * INNER, INNER), BF),
        off=vmem((OFFSETS, TAPS * INNER), BF),
        a1=vmem((ROWS, INNER), F32),
        a2=vmem((ROWS, INNER), F32),
        b1=vmem((ROWS, INNER), F32),
        b2=vmem((ROWS, INNER), F32),
        acc=vmem((ROWS, INNER), F32),
        a3=vmem((CHANNELS // 512, ROWS, 512), F32),
        b3=vmem((CHANNELS // 512, ROWS, 512), F32),
        up=vmem((CHANNELS // 512, ROWS, 512), F32),
        inner=vmem((ROWS, INNER), BF),
        hidden=vmem((ROWS, INNER), BF),
        narrow=vmem((ROWS, INNER), BF),
        mixed=vmem((ROWS, INNER), BF),
        dn=vmem((ROWS, INNER), BF),
        turned=vmem((ROWS, INNER), BF),
        wmat=vmem((SLOTS, TAPS, PIXELS, PIXELS), BF),
        tmat=vmem((2, TAPS, PIXELS, PIXELS), BF),
        geo=vmem((2, 2, PIXELS, PIXELS), jnp.int32),
        frac=vmem((ROWS, OFFSETS), F32),
        doff=vmem((ROWS, OFFSETS), F32),
        stn=vmem((4, 2, INNER), F32),
        stw=vmem((2, 2, CHANNELS), F32),
        rxn=vmem((8, everyone, 2, INNER), F32),
        rxw1=vmem((4, dp, 2, CHANNELS), F32),
        rxw2=vmem((4, outer, 2, CHANNELS), F32),
        pool=vmem((3, chips, wide, INNER), F32),
        corel=vmem((chips, wide, INNER), F32),
        land=vmem((2, 2, chips - 1, wide, INNER // 2), F32),
        zwide=vmem((3, 3, wide, INNER), F32),
        tiny=vmem((2, chips, SLOTS, 24, PIXELS), F32),
        give=vmem((ROWS, INNER), F32),
        taken=vmem((group, ROWS, INNER), F32),
        drawn=vmem((ROWS, INNER), F32),
        yall=vmem((group * ROWS, INNER), BF),
        xall=vmem((2, group * ROWS, INNER), BF),
        grad=vmem((taps * INNER, INNER), F32),
        cored=vmem((deep, INNER), F32),
        zdeep=vmem((2, 2, deep // 2, INNER), F32),
        goff=vmem((24, taps * INNER), F32),
        coreo=vmem((24, taps * INNER), F32),
        zoff=vmem((2, 24, taps * INNER), F32),
        free=pltpu.SemaphoreType.REGULAR,
        credit=pltpu.SemaphoreType.REGULAR((2, bits)),
        swapped=pltpu.SemaphoreType.REGULAR,
        load_sem=dma((11,)),
        out_sem=dma((2,)),
        res_sem=dma((7, 4)),
        xn_s=dma((8,)),
        xn_r=dma((8,)),
        xw_s=dma((4, 2)),
        xw_r=dma((4, 2)),
        core_s=dma((7,)),
        core_r=dma((7,)),
        step_s=dma((4, 2, bits)),
        step_r=dma((4, 2, bits)),
        give_sem=dma((4,)),
        take_sem=dma((3,)),
        x_sem=dma((2,)),
        ag_s=dma((4, 2, bits)),
        ag_r=dma((4, 2, bits)),
        tiny_s=dma((2,)),
        tiny_r=dma((2,)),
        z_s=dma((7, 4, 3)),
        z_r=dma((7, 4, 3)),
    )


def kernel(dp, outer, names, *refs):
    assert outer == 4
    r = types.SimpleNamespace(**dict(zip(names, refs)))
    chips, bits, wide, deep, taps = layout(dp)
    everyone = dp * outer
    me = lax.axis_index("dp")
    mine = lax.axis_index("outer")
    own = me * outer + mine
    core = lax.rem(me, 2)
    chip = lax.div(me, 2)
    sibling = (me + 1 - 2 * core, mine)
    inside = (mine == 1) | (mine == 2)
    outside = (mine == 0) | (mine == 3)
    counts, orient = r.counts, r.orient
    dma = pltpu.make_async_copy

    loads = types.SimpleNamespace()

    def load(place, source, target):
        copy = dma(source, target, r.load_sem.at[place])
        copy.start()
        return copy

    loads.images_h = load(0, r.images_h, r.images)
    loads.red_h = load(1, r.red_h, r.redwid)
    loads.off_h = load(2, r.off_h, r.off)
    loads.def_h = load(3, r.def_h, r.dfmcon)
    loads.exp_h = load(4, r.exp_h, r.exp)
    loads.nar_h = load(5, r.nar_h, r.nar)
    loads.cot_h = load(6, r.cot_h, r.dwide)

    def other(step):
        target = lax.rem(own + step, everyone)
        return lax.div(target, outer), lax.rem(target, outer)

    barrier = pltpu.get_barrier_semaphore()

    def greet(step, carry):
        pl.semaphore_signal(barrier, inc=1, device_id=other(step), device_id_type=MESH)
        return carry

    lax.fori_loop(1, everyone, greet, 0)

    def size(i, carry):
        sizes, near, far = carry
        row, place = lax.div(i, outer), lax.rem(i, outer)
        held = counts[i].astype(F32)
        here = jnp.where(place == mine, held, 0.0)

        def mark(count, at, value):
            line = lax.broadcasted_iota(jnp.int32, (count, 1), 0)
            return jnp.where(line == at, value, 0.0)

        return (
            sizes + mark(everyone, i, held),
            near + mark(dp, row, here),
            far + mark(outer, place, held),
        )

    zeros = tuple(jnp.zeros((count, 1), F32) for count in (everyone, dp, outer))
    sizes, near, far = (
        value * float(PIXELS) for value in lax.fori_loop(0, everyone, size, zeros)
    )
    near_total = total_row(near)
    total = total_row(far)
    held = counts[own].astype(F32)
    live1 = held - 1.0
    local = held * float(PIXELS)

    def sweep(body, init):
        def step(i, carry):
            lv = jnp.where(i < 3, 1.0, live1)
            for j in range(3):
                carry = body(pl.ds(pl.multiple_of(i * 48 + j * 16, 16), 16), lv, carry)
            return carry

        return lax.fori_loop(0, 6, step, init)

    def send(source, target, sent, received, device):
        pltpu.make_async_remote_copy(
            src_ref=source,
            dst_ref=target,
            send_sem=sent,
            recv_sem=received,
            device_id=device,
            device_id_type=MESH,
        ).start()

    def settle(view, sem):
        dma(view, view, sem).wait()

    waiting = {}

    def later(tag, view, sem, when=None):
        waiting.setdefault(tag, []).append((when, view, sem))

    def flush(tag):
        for when, view, sem in waiting.pop(tag, []):
            if when is None:
                settle(view, sem)
            else:
                pl.when(when)(functools.partial(settle, view, sem))

    def accumulate(target, source):
        rows = target.shape[0]
        step = math.gcd(rows, 32)

        def body(i, carry):
            rs = pl.ds(pl.multiple_of(i * step, 8), step)
            target[rs, :] += source[rs, :]
            return carry

        lax.fori_loop(0, rows // step, body, 0)

    def mix(target, one, two):
        rows = target.shape[0]
        step = math.gcd(rows, 32)

        def body(i, carry):
            rs = pl.ds(pl.multiple_of(i * step, 8), step)
            target[rs, :] = one[rs, :] + two[rs, :]
            return carry

        lax.fori_loop(0, rows // step, body, 0)

    def flip(value, bit):
        weight = 1 << bit
        return value + weight - 2 * weight * lax.rem(lax.div(value, weight), 2)

    def bit_of(value, bit):
        return lax.rem(lax.div(value, 1 << bit), 2)

    orders = [
        list(range(bits)),
        list(range(bits // 2, bits)) + list(range(bits // 2)),
    ]
    halves = [pl.ds(0, INNER // 2), pl.ds(INNER // 2, INNER // 2)]

    def merge(rx, counted, size, forward):
        first = rx[:, 0, :]
        second = rx[:, 1, :]
        if forward:
            summed = total_row(first)
            apart = first / counted - summed / size
            spread = total_row(second + counted * apart * apart)
            return jnp.concatenate([summed, spread], axis=0)
        return jnp.concatenate([total_row(first), total_row(second)], axis=0)

    def nothing():
        pass

    def share_narrow(number, forward, work):
        rx = r.rxn.at[number]

        def step(i, carry):
            line, part = lax.div(i, dp), lax.rem(i, dp)
            z = jnp.where(mine < outer // 2, outer - 1 - line, line)
            peer = 0
            for bit in range(bits + 1):
                here, turn = bit_of(me, bit), 1 - bit_of(part, bit)
                peer = peer + (here + turn - 2 * here * turn) * (1 << bit)

            @pl.when(peer * outer + z != own)
            def _():
                send(rx.at[own], rx.at[own], r.xn_s.at[number], r.xn_r.at[number], (peer, z))

            return carry

        lax.fori_loop(0, everyone, step, 0)
        rest = rx.at[pl.ds(0, everyone - 1)]
        later("end", rest, r.xn_s.at[number])
        work()
        settle(rest, r.xn_r.at[number])
        return merge(rx, sizes, total, forward)

    def share_wide(number, forward, work, work_more):
        rx1, rx2 = r.rxw1.at[number], r.rxw2.at[number]
        for step in range(1, dp):
            send(
                rx1.at[me],
                rx1.at[me],
                r.xw_s.at[number, 0],
                r.xw_r.at[number, 0],
                (lax.rem(me + step, dp), mine),
            )
        rest = rx1.at[pl.ds(0, dp - 1)]
        later("end", rest, r.xw_s.at[number, 0])
        work()
        settle(rest, r.xw_r.at[number, 0])
        rx2[mine] = merge(rx1, near, near_total, forward)
        for step in range(1, outer):
            send(
                rx2.at[mine],
                rx2.at[mine],
                r.xw_s.at[number, 1],
                r.xw_r.at[number, 1],
                (me, lax.rem(mine + step, outer)),
            )
        rest = rx2.at[pl.ds(0, outer - 1)]
        later("end", rest, r.xw_s.at[number, 1])
        work_more()
        settle(rest, r.xw_r.at[number, 1])
        return merge(rx2, far, total, forward)

    def local_stats(ref, put, cs):
        zero = jnp.zeros((8, 512), F32)
        summed = total_row(sweep(lambda rs, lv, c: c + lv * fold(ref[rs, :]), zero))
        mean = summed / local

        def squares(rs, lv, carry):
            apart = ref[rs, :] - mean
            return carry + lv * fold(apart * apart)

        put[0:1, cs] = summed
        put[1:2, cs] = total_row(sweep(squares, zero))

    def keep_stats(both, st):
        st[0:1, :] = both[0:1] / total
        st[1:2, :] = lax.rsqrt(both[1:2] / total + EPS)

    def narrow_stats(ref, number, work=nothing):
        local_stats(ref, r.rxn.at[number, own], pl.ds(0, INNER))
        keep_stats(share_narrow(number, True, work), r.stn.at[number])

    blocks = [pl.ds(start, 512) for start in range(0, CHANNELS, 512)]

    def wide_stats(ref, number, work=nothing, work_more=nothing):
        for n, cs in enumerate(blocks):
            local_stats(ref.at[n], r.rxw1.at[number, me], cs)
        keep_stats(share_wide(number, True, work, work_more), r.stw.at[number])

    def norm_silu(ref, number, gain, bias, out, spread):
        st = r.stn.at[number]
        mean, scale = st[0:1, :], st[1:2, :]
        steep = scale * gain

        def body(rs, lv, carry):
            z = (ref[rs, :] - mean) * steep + bias
            value = (z * sigmoid(z)).astype(BF)
            out[rs, :] = value
            if spread:
                r.give[rs, :] = value.astype(F32)
            return carry

        sweep(body, 0)

    def narrow_cotangent(ref, place, gain, bias, number, spread, work=nothing):
        acc = r.acc
        st = r.stn.at[place]
        mean, scale = st[0:1, :], st[1:2, :]

        def body(rs, lv, carry):
            xhat = (ref[rs, :] - mean) * scale
            z = xhat * gain + bias
            sg = sigmoid(z)
            g = acc[rs, :] * (sg * (1.0 + z * (1.0 - sg)))
            acc[rs, :] = g
            return carry[0] + fold(g), carry[1] + fold(g * xhat)

        zero = jnp.zeros((8, INNER), F32)
        summed, paired = sweep(body, (zero, zero))
        put = r.rxn.at[number, own]
        put[0:1, :] = total_row(summed)
        put[1:2, :] = total_row(paired)
        both = share_narrow(number, False, work)
        r.g_ib[place : place + 1, :] = both[0:1]
        r.g_ig[place : place + 1, :] = both[1:2]
        steep = scale * gain
        lift, tilt = both[0:1] / total, both[1:2] / total

        def back(rs, lv, carry):
            xhat = (ref[rs, :] - mean) * scale
            value = (steep * (acc[rs, :] - lv * (lift + xhat * tilt))).astype(BF)
            r.dn[rs, :] = value
            if spread:
                r.give[rs, :] = value.astype(F32)
            return carry

        sweep(back, 0)

    def wide_cotangent(number, ref, place, gain, bias, cotangent, work=nothing, work_more=nothing):
        put = r.rxw1.at[number, me]
        st = r.stw.at[place]
        for n, cs in enumerate(blocks):
            mean, scale = st[0:1, cs], st[1:2, cs]
            gn, bs = gain[:, 512 * n : 512 * n + 512], bias[:, 512 * n : 512 * n + 512]

            def body(rs, lv, carry):
                xhat = (ref[n, rs, :] - mean) * scale
                g = cotangent(n, rs, cs, lv, xhat * gn + bs)
                r.up[n, rs, :] = g
                return carry[0] + fold(g), carry[1] + fold(g * xhat)

            zero = jnp.zeros((8, 512), F32)
            summed, paired = sweep(body, (zero, zero))
            put[0:1, cs] = total_row(summed)
            put[1:2, cs] = total_row(paired)
        both = share_wide(number, False, work, work_more)
        r.g_bb[place : place + 1, :] = both[0:1]
        r.g_bg[place : place + 1, :] = both[1:2]
        for n, cs in enumerate(blocks):
            mean, scale = st[0:1, cs], st[1:2, cs]
            span = slice(512 * n, 512 * n + 512)
            steep = scale * gain[:, span]
            lift, tilt = both[0:1, span] / total, both[1:2, span] / total

            def back(rs, lv, carry):
                xhat = (ref[n, rs, :] - mean) * scale
                value = steep * (r.up[n, rs, :] - lv * (lift + xhat * tilt))
                r.dwide[rs, cs] = value.astype(BF)
                return carry

            sweep(back, 0)

    def tap(ref, k):
        return ref[pl.ds(pl.multiple_of(k * INNER, INNER), INNER), :]

    def offset_tap(k):
        return r.off[:, pl.ds(pl.multiple_of(k * INNER, INNER), INNER)]

    def slot_rows(s):
        return pl.ds(s * PIXELS, PIXELS)

    def steps_of(k):
        return 2 * lax.div(k, 3) - 2, 2 * lax.rem(k, 3) - 2

    WID, CON, NAR, EXP, DEF, RED, OFF = range(7)
    nth = {WID: 0, NAR: 1, EXP: 2, RED: 3}
    result = {
        WID: r.g_wid,
        CON: r.g_con,
        NAR: r.g_nar,
        EXP: r.g_exp,
        DEF: r.g_def,
        RED: r.g_red,
        OFF: r.g_off,
    }
    pool, land, grad, far_blocks = r.pool, r.land, r.grad, r.far_blocks

    deep_parts = 4 if deep % 32 == 0 else 2
    wide_parts = {WID: 2, NAR: 2, EXP: 2, RED: 4}

    def z_hold(u):
        if u == RED:
            return [r.a3.at[i, pl.ds(0, wide)] for i in range(3)]
        return [r.zwide.at[nth[u], i] for i in range(3)]

    def z_parts(u):
        if u in nth:
            hold = z_hold(u)
            for q in range(wide_parts[u]):
                rows = wide // (wide_parts[u] // 2)
                rs, hs = pl.ds(q // 2 * rows, rows), halves[q % 2]
                yield tuple(ref.at[rs, hs] for ref in hold) + (result[u].at[rs, hs],)
        elif u == OFF:
            yield r.goff, r.zoff.at[0], r.zoff.at[1], result[u]
        else:
            for q in range(deep_parts):
                back, at = divmod(q, deep_parts // 2)
                source = r.b3.at[(2 if u == DEF else 0) + back]
                if u == DEF:
                    first, second = (r.b1, r.a2) if back == 0 else (r.b2, r.a3.at[3])
                else:
                    first, second = r.zdeep.at[0, back], r.zdeep.at[1, back]
                size = deep // deep_parts
                rows = pl.ds(at * size, size)
                out = result[u].at[pl.ds(q * size, size)]
                yield source.at[rows], first.at[rows], second.at[rows], out

    def z_sems(u, q, step):
        return r.z_s.at[u, q, step], r.z_r.at[u, q, step]

    def z1(u, some=None):
        for q, (source, first, second, out) in enumerate(z_parts(u)):
            if some is not None and q not in some:
                continue
            sent, received = z_sems(u, q, 0)

            @pl.when(outside)
            def _():
                send(source, first, sent, received, (me, flip(mine, 0)))

            later(("z", u), source, sent, outside)

    def z2(u, some=None):
        for q, (source, first, second, out) in enumerate(z_parts(u)):
            if some is not None and q not in some:
                continue
            sent, received = z_sems(u, q, 1)

            @pl.when(inside)
            def _():
                settle(first, z_sems(u, q, 0)[1])
                accumulate(source, first)
                send(source, second, sent, received, (me, 3 - mine))

            later(("z", u), source, sent, inside)

    def z3(u, some=None):
        for q, (source, first, second, out) in enumerate(z_parts(u)):
            if some is not None and q not in some:
                continue
            sent, received = z_sems(u, q, 2)

            @pl.when(inside)
            def _():
                settle(second, z_sems(u, q, 1)[1])
                accumulate(second, source)
                send(second, first, sent, received, (me, flip(mine, 0)))
                dma(second, out, r.res_sem.at[u, q]).start()

            later(("zl", u), second, sent, inside)

    def z4(u, some=None):
        for q, (source, first, second, out) in enumerate(z_parts(u)):
            if some is not None and q not in some:
                continue

            @pl.when(outside)
            def _():
                settle(first, z_sems(u, q, 2)[1])
                dma(first, out, r.res_sem.at[u, q]).start()

    def z_clear(u):
        flush(("z", u))
        flush(("zl", u))
        for q, (source, first, second, out) in enumerate(z_parts(u)):
            dma(first, out, r.res_sem.at[u, q]).wait()

    def wide_begin(u, left, right):
        p = nth[u] % 2
        flush("sib")
        flush(("keep", p))
        low = p + (2 - p) * core
        high = p + (2 - p) * (1 - core)
        if u == EXP:
            pl.semaphore_wait(r.swapped, 1)

        def step(m, carry):
            block = left[:, pl.ds(pl.multiple_of(m * (2 * wide), 2 * wide), 2 * wide)]
            pool[low, m] = mm(block[:, :wide], right[...], TN)
            pool[high, m] = mm(block[:, wide:], right[...], TN)
            send(
                pool.at[2, m], r.corel.at[m], r.core_s.at[u], r.core_r.at[u], sibling
            )
            return carry

        lax.fori_loop(0, chips, step, 0)
        later("sib", r.corel, r.core_s.at[u])

    def piece(h, t, j, toward):
        value = 0
        for i, bit in enumerate(orders[h]):
            if i < t:
                part = bit_of(chip, bit)
            elif i == t:
                part = bit_of(toward, bit)
            else:
                part = (j >> (i - t - 1)) & 1
            value = value + part * (1 << bit)
        return value

    def step_place(u, h, t):
        first, count = chips - (chips >> t), chips >> (t + 1)
        p = nth[u] % 2
        sems = r.step_s.at[nth[u], h, t], r.step_r.at[nth[u], h, t]
        return p, first, count, sems, land.at[p, h, pl.ds(first, count)]

    def wide_send(u, t):
        for h in range(2):
            p, first, count, (sent, received), region = step_place(u, h, t)
            toward = flip(chip, orders[h][t])
            if u == RED:
                pl.semaphore_wait(r.credit.at[h, t], 1)
            for j in range(count):
                send(
                    pool.at[p, piece(h, t, j, toward), :, halves[h]],
                    land.at[p, h, first + j],
                    sent,
                    received,
                    (2 * toward + core, mine),
                )
            later(("keep", p), region, sent)

    def wide_add(u, t):
        for h in range(2):
            p, first, count, (sent, received), region = step_place(u, h, t)
            settle(region, received)
            if t == bits - 1:
                mix(z_hold(u)[0].at[:, halves[h]], pool.at[p, chip, :, halves[h]], land.at[p, h, first])
            else:
                for j in range(count):
                    accumulate(
                        pool.at[p, piece(h, t, j, chip), :, halves[h]], land.at[p, h, first + j]
                    )
            if u == NAR:
                pl.semaphore_signal(
                    r.credit.at[h, t],
                    inc=1,
                    device_id=(2 * flip(chip, orders[h][t]) + core, mine),
                    device_id_type=MESH,
                )

    def wide_core(u):
        p = nth[u] % 2
        settle(r.corel, r.core_r.at[u])

        def step(m, carry):
            accumulate(pool.at[p, m], r.corel.at[m])
            return carry

        lax.fori_loop(0, chips, step, 0)
        if u == NAR:
            pl.semaphore_signal(r.swapped, inc=1, device_id=sibling, device_id_type=MESH)

    def wide_step(u, t):
        wide_add(u, t - 1)
        if t < bits:
            wide_send(u, t)
        else:
            z1(u)

    def held_at(h, j):
        value = chip
        for i in range(bits):
            if (j >> i) & 1:
                value = flip(value, orders[h][i])
        return value

    def gather_send(a, t, some=None):
        for h in range(2):
            partner = flip(chip, orders[h][t])
            sent, received = r.ag_s.at[a, h, t], r.ag_r.at[a, h, t]
            for j in range(1 << t) if some is None else some:
                block = far_blocks.at[a, held_at(h, j), :, halves[h]]
                source = r.give.at[:, halves[h]] if j == 0 else block
                send(source, block, sent, received, (2 * partner + core, mine))
            if some is None or 0 in some:
                later(("ag", a), far_blocks.at[a, pl.ds(0, 1 << t), :, halves[h]], sent)

    def gather_start(a):
        block = far_blocks.at[a, chip]
        dma(r.give, block, r.give_sem.at[a]).start()
        later(("ag", a), block, r.give_sem.at[a])
        gather_send(a, 0)

    def gather_wait(a, t):
        for h in range(2):
            settle(far_blocks.at[a, pl.ds(0, 1 << t), :, halves[h]], r.ag_r.at[a, h, t])

    def gather_step(a, t, some=None):
        gather_wait(a, t - 1)
        gather_send(a, t, some)

    def gather_first(a, t):
        if t < bits:
            gather_send(a, t, [0])

    def gather_rest(a):
        for t in range(1, bits):
            gather_wait(a, t - 1)
            gather_send(a, t, range(1 if t == 1 else 0, 1 << t))

    def gather_end(a):
        gather_wait(a, bits - 1)
        flush(("ag", a))

    def tiny_send(a):
        for step in range(1, chips):
            block = r.tiny.at[a, chip]
            peer = lax.rem(chip + step, chips)
            send(block, block, r.tiny_s.at[a], r.tiny_r.at[a], (2 * peer + core, mine))
        later("end", r.tiny.at[a, pl.ds(0, chips - 1)], r.tiny_s.at[a])

    def tiny_wait(a):
        settle(r.tiny.at[a, pl.ds(0, chips - 1)], r.tiny_r.at[a])

    group = min(chips, 4)
    first_tap = lax.div(2 * deep * chip, INNER)
    margin = 2 * deep * chip - first_tap * INNER

    def taps_of(kk):
        k = jnp.minimum(first_tap + kk, TAPS - 1)
        return (k, *steps_of(k))

    def fetch_fields(a, g):
        copy = dma(far_blocks.at[a, pl.ds(g * group, group)], r.taken, r.take_sem.at[2])
        copy.start()
        copy.wait()

    def image_of(i, g):
        m, s = lax.div(i, SLOTS), lax.rem(i, SLOTS)
        rows = pl.ds(pl.multiple_of(i * PIXELS, PIXELS), PIXELS)
        field = r.taken[m, pl.ds(pl.multiple_of(s * PIXELS, PIXELS), PIXELS), :].astype(BF)
        flat = r.tiny[0, g * group + m, s, 18:19, :] == 0.0
        dr = jnp.where(flat, r.geo[0, 0], r.geo[1, 0])
        dc = jnp.where(flat, r.geo[0, 1], r.geo[1, 1])
        return g * group + m, s, rows, field, dr, dc

    def group_rows(g):
        return pl.ds(g * (group * ROWS), group * ROWS)

    def columns(u, kk):
        x = 1 if u == DEF else 0
        k, down, across = taps_of(kk)
        for g in range(chips // group):
            if kk == 0 or chips > group:
                fetch_fields(0 if u == DEF else 1, g)
            if g == 0:
                flush("columns")

            def image(i, carry):
                m, s, rows, field, dr, dc = image_of(i, g)
                if u == CON:
                    hit = jnp.where((dr == down) & (dc == across), 1.0, 0.0).astype(BF)
                    r.xall[0, rows, :] = mm(hit, field, NN).astype(BF)
                    return carry
                tiny = r.tiny.at[0, m, s]
                fy, fx = tiny[pl.ds(2 * k, 1), :], tiny[pl.ds(2 * k + 1, 1), :]
                ay = jnp.where(dr == -down, 1.0 - fy, jnp.where(dr == -down - 1, fy, 0.0))
                ax = jnp.where(dc == -across, 1.0 - fx, jnp.where(dc == -across - 1, fx, 0.0))
                r.xall[0, rows, :] = mm((ay * ax).astype(BF), field, TN).astype(BF)
                return carry

            lax.fori_loop(0, group * SLOTS, image, 0, unroll=4)
            place = r.far_columns.at[x, kk, group_rows(g)]
            copy = dma(r.xall.at[0], place, r.x_sem.at[0])
            copy.start()
            if g + 1 < chips // group:
                copy.wait()
            else:
                later("columns", place, r.x_sem.at[0])

    def deep_make(u):
        flush("deep")
        flush("columns")
        x, back_of = (1, 3) if u == DEF else (0, 2)
        slots = (r.give, r.drawn)
        for g in range(chips // group):

            def fetch(m):
                return dma(far_blocks.at[back_of, g * group + m], slots[m % 2], r.take_sem.at[m % 2])

            def draw(kk):
                slot = lax.rem(kk, 2)
                return dma(
                    r.far_columns.at[x, kk, group_rows(g)], r.xall.at[slot], r.x_sem.at[slot]
                )

            for m in range(min(2, group)):
                fetch(m).start()
            draw(0).start()
            for m in range(group):
                fetch(m).wait()

                def lower(i, carry):
                    rows = pl.ds(pl.multiple_of(m * ROWS + i * 32, 32), 32)
                    there = pl.ds(pl.multiple_of(i * 32, 32), 32)
                    r.yall[rows, :] = slots[m % 2][there, :].astype(BF)
                    return carry

                lax.fori_loop(0, ROWS // 32, lower, 0)
                if m + 2 < group:
                    fetch(m + 2).start()

            def one(kk, carry):
                @pl.when(kk + 1 < taps)
                def _():
                    draw(kk + 1).start()

                draw(kk).wait()
                at = pl.ds(pl.multiple_of(kk * INNER, INNER), INNER)
                part = mm(r.xall[lax.rem(kk, 2)], r.yall[...], TN)
                if g == 0:
                    grad[at, :] = part
                else:
                    grad[at, :] += part
                return carry

            lax.fori_loop(0, taps, one, 0)
        away = pl.ds(pl.multiple_of(margin + (1 - core) * deep, 8), deep)
        send(grad.at[away], r.cored, r.core_s.at[u], r.core_r.at[u], sibling)
        later("deep", r.cored, r.core_s.at[u])

    def off_make():
        for g in range(chips // group):
            fetch_fields(0, g)

            def one(kk, carry):
                k, down, across = taps_of(kk)

                def image(i, share):
                    m, s, rows, field, dr, dc = image_of(i, g)
                    hit = jnp.where((dr == down) & (dc == across), 1.0, 0.0).astype(BF)
                    moved = mm(r.tiny[1, m, s].astype(BF), hit, NN).astype(BF)
                    return share + mm(moved, field, NN)

                at = pl.ds(pl.multiple_of(kk * INNER, INNER), INNER)
                share = lax.fori_loop(
                    0, group * SLOTS, image, jnp.zeros((24, INNER), F32), unroll=8
                )
                if g == 0:
                    r.goff[:, at] = share
                else:
                    r.goff[:, at] += share
                return carry

            lax.fori_loop(0, taps, one, 0)
        send(r.goff, r.coreo, r.core_s.at[OFF], r.core_r.at[OFF], sibling)

    def off_core():
        settle(r.goff, r.core_s.at[OFF])
        settle(r.coreo, r.core_r.at[OFF])
        accumulate(r.goff, r.coreo)

    def deep_core(u):
        settle(r.cored, r.core_r.at[u])
        half = deep // 2
        step = math.gcd(half, 32)
        for q in range(2):
            target = r.b3.at[(2 if u == DEF else 0) + q]

            def body(i, carry):
                at = pl.multiple_of(i * step, 8)
                here = grad[pl.ds(pl.multiple_of(margin + core * deep + q * half + at, 8), step), :]
                target[pl.ds(at, step), :] = here + r.cored[pl.ds(q * half + at, step), :]
                return carry

            lax.fori_loop(0, half // step, body, 0)
    images, between, acc, up = r.images, r.between, r.acc, r.up
    ig = [r.ig[i : i + 1, :] for i in range(4)]
    ib = [r.ib[i : i + 1, :] for i in range(4)]
    bg = [r.bg[i : i + 1, :] for i in range(2)]
    bb = [r.bb[i : i + 1, :] for i in range(2)]

    def geometry():
        q = lax.broadcasted_iota(jnp.int32, (PIXELS, PIXELS), 1)
        p = lax.broadcasted_iota(jnp.int32, (PIXELS, PIXELS), 0)

        def place_of(at, kind):
            if kind:
                row = lax.shift_right_logical(at, 2)
                return row, at - row * SHORT
            row = (at >= LONG).astype(jnp.int32) + (at >= 2 * LONG).astype(jnp.int32)
            row = row + (at >= 3 * LONG).astype(jnp.int32)
            return row, at - row * LONG

        for kind in range(2):
            row_q, col_q = place_of(q, kind)
            row_p, col_p = place_of(p, kind)
            r.geo[kind, 0] = row_q - row_p
            r.geo[kind, 1] = col_q - col_p

            def hot(k, carry):
                down, across = steps_of(k)
                hit = (r.geo[kind, 0] == down) & (r.geo[kind, 1] == across)
                r.tmat[kind, k] = jnp.where(hit, 1.0, 0.0).astype(BF)
                return carry

            lax.fori_loop(0, TAPS, hot, 0)

    def shifted(s, k):
        return r.tmat[orient[s], k]

    loads.images_h.wait()
    loads.red_h.wait()
    r.a1[...] = mm(images[...], r.redwid[...], NN)
    loads.wid_h = load(7, r.wid_h, r.redwid)
    pl.semaphore_wait(barrier, everyone - 1)
    narrow_stats(r.a1, 0, geometry)
    norm_silu(r.a1, 0, ig[0], ib[0], r.inner, True)
    gather_start(0)

    loads.off_h.wait()
    inner = r.inner
    lane = lax.broadcasted_iota(jnp.int32, (PIXELS, OFFSETS), 1)

    def gather(k, carry):
        cols = [mm(shifted(s, k), inner[slot_rows(s), :], NN).astype(BF) for s in range(SLOTS)]
        weight = offset_tap(k)
        return tuple(old + mm(col, weight, NT) for old, col in zip(carry, cols))

    zero = jnp.zeros((PIXELS, OFFSETS), F32)
    both_offsets = lax.fori_loop(0, TAPS, gather, (zero,) * SLOTS, unroll=3)
    for s in range(SLOTS):
        frac = sigmoid(both_offsets[s])
        r.frac[slot_rows(s), :] = frac
        coarse = frac.astype(BF)
        fine = (frac - coarse.astype(F32)).astype(BF)
        unit = r.tmat[0, TAPS // 2]
        put = r.tiny.at[0, chip, s]
        put[...] = jnp.zeros((24, PIXELS), F32) + orient[s].astype(F32)
        put[0:OFFSETS, :] = mm(coarse, unit, TN) + mm(fine, unit, TN)
    tiny_send(0)

    def bilinear(s, k):
        down, across = steps_of(k)
        frac = r.frac[slot_rows(s), :]
        fy = jnp.sum(jnp.where(lane == 2 * k, frac, 0.0), axis=1, keepdims=True)
        fx = jnp.sum(jnp.where(lane == 2 * k + 1, frac, 0.0), axis=1, keepdims=True)
        dr, dc = r.geo[orient[s], 0], r.geo[orient[s], 1]
        in_y = (dr == down, dr == down + 1)
        in_x = (dc == across, dc == across + 1)
        ay = jnp.where(in_y[0], 1.0 - fy, jnp.where(in_y[1], fy, 0.0))
        ax = jnp.where(in_x[0], 1.0 - fx, jnp.where(in_x[1], fx, 0.0))
        return fy, fx, ay, ax, in_y, in_x

    loads.def_h.wait()
    acc[...] = jnp.zeros((ROWS, INNER), F32)

    def sample(k, carry):
        for s in range(SLOTS):
            _, _, ay, ax, _, _ = bilinear(s, k)
            weight = (ay * ax).astype(BF)
            r.wmat[s, k] = weight
            r.turned[slot_rows(s), :] = mm(weight, inner[slot_rows(s), :], NN).astype(BF)
        acc[...] += mm(r.turned[...], tap(r.dfmcon, k), NN)
        return carry

    lax.fori_loop(0, TAPS, sample, 0, unroll=3)
    loads.con_h = load(8, r.con_h, r.dfmcon)
    r.a2[...] = acc[...]
    narrow_stats(r.a2, 1, lambda: gather_first(0, 1))
    norm_silu(r.a2, 1, ig[1], ib[1], r.hidden, False)

    def widen(source, weight, target):
        def step(n, carry):
            rows = pl.ds(pl.multiple_of(n * 512, 512), 512)
            target[n] = mm(source[...], weight[rows, :], NT)
            return carry

        lax.fori_loop(0, CHANNELS // 512, step, 0)

    loads.exp_h.wait()
    widen(r.hidden, r.exp, r.a3)
    wide_stats(r.a3, 0, lambda: gather_rest(0))
    for n, cs in enumerate(blocks):
        mean = r.stw[0, 0:1, cs]
        steep = r.stw[0, 1:2, cs] * bg[0][:, 512 * n : 512 * n + 512]
        bias = bb[0][:, 512 * n : 512 * n + 512]

        def join(rs, lv, carry):
            z = (r.a3[n, rs, :] - mean) * steep + bias + images[rs, cs].astype(F32)
            between[rs, cs] = (z * sigmoid(z)).astype(BF)
            return carry

        sweep(join, 0)

    loads.nar_h.wait()
    r.b1[...] = mm(between[...], r.nar[...], NN)

    def work_b1():
        gather_end(0)
        tiny_wait(0)
        columns(DEF, 0)

    narrow_stats(r.b1, 2, work_b1)
    norm_silu(r.b1, 2, ig[2], ib[2], r.narrow, True)
    gather_start(1)

    loads.con_h.wait()
    acc[...] = jnp.zeros((ROWS, INNER), F32)

    def convolve(k, carry):
        for s in range(SLOTS):
            r.turned[slot_rows(s), :] = mm(
                shifted(s, k), r.narrow[slot_rows(s), :], NN
            ).astype(BF)
        acc[...] += mm(r.turned[...], tap(r.dfmcon, k), NN)
        return carry

    lax.fori_loop(0, TAPS, convolve, 0, unroll=3)
    r.b2[...] = acc[...]
    def work_b2():
        gather_first(1, 1)
        columns(DEF, 1)

    narrow_stats(r.b2, 3, work_b2)
    norm_silu(r.b2, 3, ig[3], ib[3], r.mixed, False)

    loads.wid_h.wait()
    widen(r.mixed, r.redwid, r.b3)

    def work_b3():
        gather_rest(1)
        for kk in range(2, taps):
            columns(DEF, kk)

    wide_stats(r.b3, 1, work_b3)

    loads.cot_h.wait()

    def last(n, rs, cs, lv, pre):
        z = pre + between[rs, cs].astype(F32)
        sg = sigmoid(z)
        r.obuf[rs, cs] = (lv * (z * sg)).astype(BF)
        return r.dwide[rs, cs].astype(F32) * (lv * (sg * (1.0 + z * (1.0 - sg))))

    def work_f():
        gather_end(1)
        columns(CON, 0)

    wide_cotangent(2, r.b3, 1, bg[1], bb[1], last, nothing, work_f)
    out_copy = dma(r.obuf, r.out_h, r.out_sem.at[0])
    out_copy.start()
    wide_begin(WID, r.dwide, r.mixed)
    acc[...] = mm(r.dwide[...], r.redwid[...], NN)
    loads.red_h = load(9, r.red_h, r.redwid)

    def work_e():
        wide_core(WID)
        wide_send(WID, 0)
        columns(CON, 1)

    narrow_cotangent(r.b2, 3, ig[3], ib[3], 4, True, work_e)

    acc[...] = jnp.zeros((ROWS, INNER), F32)

    def spread(k, carry):
        for s in range(SLOTS):
            r.turned[slot_rows(s), :] = mm(
                shifted(s, TAPS - 1 - k), r.dn[slot_rows(s), :], NN
            ).astype(BF)
        acc[...] += mm(r.turned[...], tap(r.dfmcon, k), NT)
        return carry

    lax.fori_loop(0, TAPS, spread, 0, unroll=3)
    loads.def_h = load(10, r.def_h, r.dfmcon)

    def work_d():
        wide_step(WID, 1)
        gather_start(2)
        for kk in range(2, taps):
            columns(CON, kk)

    narrow_cotangent(r.b1, 2, ig[2], ib[2], 5, False, work_d)
    for t in range(2, bits + 1):
        wide_step(WID, t)

    def add_back(n, carry):
        rows = pl.ds(pl.multiple_of(n * 512, 512), 512)
        up[n] += mm(r.dn[...], r.nar[rows, :], NT)
        return carry

    lax.fori_loop(0, CHANNELS // 512, add_back, 0)

    def first(n, rs, cs, lv, pre):
        z = pre + images[rs, cs].astype(F32)
        sg = sigmoid(z)
        return up[n, rs, :] * (sg * (1.0 + z * (1.0 - sg)))

    def work_c():
        for t in range(1, bits):
            gather_step(2, t)
        wide_begin(NAR, between, r.dn)

    def work_more_c():
        z2(WID)
        wide_core(NAR)

    wide_cotangent(3, r.a3, 0, bg[0], bb[0], first, work_c, work_more_c)
    acc[...] = mm(r.dwide[...], r.exp[...], NN)

    def work_b():
        wide_send(NAR, 0)
        z3(WID)
        wide_begin(EXP, r.dwide, r.hidden)
        gather_end(2)
        deep_make(CON)

    narrow_cotangent(r.a2, 1, ig[1], ib[1], 6, True, work_b)
    wide_step(NAR, 1)
    gather_start(3)
    deep_core(CON)
    early, late = range(deep_parts // 2), range(deep_parts // 2, deep_parts)
    z1(CON, early)

    loads.def_h.wait()
    acc[...] = jnp.zeros((ROWS, INNER), F32)
    r.doff[...] = jnp.zeros((ROWS, OFFSETS), F32)

    def unsample(k, carry):
        r.turned[...] = mm(r.dn[...], tap(r.dfmcon, k), NT).astype(BF)
        for s in range(SLOTS):
            rs = slot_rows(s)
            back = r.turned[rs, :]
            pairs = mm(back, inner[rs, :], NT)
            fy, fx, ay, ax, in_y, in_x = bilinear(s, k)
            slope_y = jnp.where(in_y[1], ax, 0.0) - jnp.where(in_y[0], ax, 0.0)
            slope_x = jnp.where(in_x[1], ay, 0.0) - jnp.where(in_x[0], ay, 0.0)
            to_y = jnp.sum(pairs * slope_y, axis=1, keepdims=True) * (fy * (1.0 - fy))
            to_x = jnp.sum(pairs * slope_x, axis=1, keepdims=True) * (fx * (1.0 - fx))
            r.doff[rs, :] += jnp.where(lane == 2 * k, to_y, 0.0) + jnp.where(
                lane == 2 * k + 1, to_x, 0.0
            )
            acc[rs, :] += mm(r.wmat[s, k], back, TN)
        return carry

    lax.fori_loop(0, TAPS, unsample, 0, unroll=3)
    for s in range(SLOTS):
        put = r.tiny.at[1, chip, s]
        put[...] = jnp.zeros((24, PIXELS), F32)
        put[0:OFFSETS, :] = mm(
            r.doff[slot_rows(s), :].astype(BF), r.tmat[0, TAPS // 2], TN
        )
    tiny_send(1)

    def untap(k, carry):
        for s in range(SLOTS):
            rs = slot_rows(s)
            moved = mm(shifted(s, TAPS - 1 - k), r.doff[rs, :].astype(BF), NN).astype(BF)
            acc[rs, :] += mm(moved, offset_tap(k), NN)
        return carry

    lax.fori_loop(0, TAPS, untap, 0, unroll=3)

    wide_core(EXP)

    def work_a():
        for t in range(1, bits):
            gather_step(3, t)
        wide_send(EXP, 0)
        z1(CON, late)
        for t in range(2, bits + 1):
            wide_step(NAR, t)
        z2(CON, early)
        z4(WID)

    narrow_cotangent(r.a1, 0, ig[0], ib[0], 7, False, work_a)
    wide_begin(RED, images, r.dn)

    out_copy.wait()
    loads.red_h.wait()

    def finish(n, carry):
        rows = pl.ds(pl.multiple_of(n * 512, 512), 512)
        r.obuf[:, rows] = (up[n] + mm(r.dn[...], r.redwid[rows, :], NT)).astype(BF)
        return carry

    lax.fori_loop(0, CHANNELS // 512, finish, 0)
    grad_copy = dma(r.obuf, r.grad_h, r.out_sem.at[1])
    grad_copy.start()
    gather_end(3)
    deep_make(DEF)
    wide_core(RED)
    wide_send(RED, 0)
    z2(CON, late)
    z3(CON, early)
    deep_core(DEF)
    z1(DEF)
    wide_step(EXP, 1)
    z2(NAR)
    z3(CON, late)
    tiny_wait(1)
    off_make()
    z2(DEF, [0])
    off_core()
    z1(OFF)
    wide_step(RED, 1)
    z2(DEF, [1])
    z3(NAR)
    for t in range(2, bits + 1):
        wide_step(EXP, t)
    z2(DEF, [2])
    z3(DEF, [0])
    for t in range(2, bits + 1):
        wide_step(RED, t)
    z2(DEF, [3])
    z3(DEF, [1])
    z2(OFF)
    z2(EXP, [0])
    z3(DEF, [2])
    z2(EXP, [1])
    z3(DEF, [3])
    z3(OFF)
    z3(EXP, [0])
    z2(RED, [0])
    z2(RED, [1])
    z3(EXP, [1])
    z2(RED, [2])
    z3(RED, [0])
    z2(RED, [3])
    z3(RED, [1, 2, 3])
    z4(CON)
    z4(NAR)
    z4(DEF)
    z4(OFF)
    z4(EXP)
    z4(RED)
    for u in range(7):
        z_clear(u)
    grad_copy.wait()
    for tag in list(waiting):
        flush(tag)


MOVED = ["out", "grad", "con", "def", "wid", "nar", "exp", "red"]


def deliver(dp, names, *refs):
    r = types.SimpleNamespace(**dict(zip(names, refs)))
    _, _, _, deep, _ = layout(dp)
    place = lax.axis_index("dp")
    moves = []
    for i, name in enumerate(MOVED):
        source, target, hold = (getattr(r, kind + name) for kind in ("from_", "to_", "hold_"))
        taken = pltpu.make_async_copy(source, hold, r.sems.at[0, i])
        taken.start()
        moves.append((taken, pltpu.make_async_copy(hold, target, r.sems.at[1, i])))

    for taken, given in moves:
        taken.wait()
        given.start()

    def span(ref, start, target):
        rows, lanes = ref.shape
        moved = pltpu.roll(ref[...], lax.rem(lanes - start, lanes), 1)
        target[...] = moved[: target.shape[0], : target.shape[1]]

    span(r.g_ig, place * (INNER // dp), r.to_ig)
    span(r.g_ib, place * (INNER // dp), r.to_ib)
    span(r.g_bg, place * (CHANNELS // dp), r.to_bg)
    span(r.g_bb, place * (CHANNELS // dp), r.to_bb)
    chip, core = lax.div(place, 2), lax.rem(place, 2)
    span(r.g_off, lax.rem(2 * deep * chip, INNER) + deep * core, r.to_off)
    for taken, given in moves:
        given.wait()


def per_device(
    images,
    counts,
    orientation,
    cotangent,
    reducer,
    offseter,
    deformer,
    expander,
    narrower,
    convolver,
    widener,
    inner_gains,
    inner_biases,
    broad_gains,
    broad_biases,
):
    dp, outer = lax.axis_size("dp"), lax.axis_size("outer")
    chips, bits, wide, deep, taps = layout(dp)
    buffers = scratch(dp, outer)
    smem = pl.BlockSpec(memory_space=pltpu.SMEM)
    vmem = pl.BlockSpec(memory_space=pltpu.VMEM)
    far = pl.BlockSpec(memory_space=pl.ANY)
    shape = jax.ShapeDtypeStruct
    inputs = dict(
        counts=(smem, counts),
        orient=(smem, orientation),
        ig=(vmem, inner_gains),
        ib=(vmem, inner_biases),
        bg=(vmem, broad_gains),
        bb=(vmem, broad_biases),
        images_h=(far, images.reshape(ROWS, CHANNELS)),
        cot_h=(far, cotangent.reshape(ROWS, CHANNELS)),
        red_h=(far, reducer),
        off_h=(far, offseter.T),
        def_h=(far, deformer),
        exp_h=(far, expander),
        nar_h=(far, narrower),
        con_h=(far, convolver),
        wid_h=(far, widener),
    )
    outputs = dict(
        out_h=(far, shape((ROWS, CHANNELS), BF)),
        grad_h=(far, shape((ROWS, CHANNELS), BF)),
        g_red=(far, shape((wide, INNER), F32)),
        g_off=(far, shape((24, taps * INNER), F32)),
        g_def=(far, shape((deep, INNER), F32)),
        g_exp=(far, shape((wide, INNER), F32)),
        g_nar=(far, shape((wide, INNER), F32)),
        g_con=(far, shape((deep, INNER), F32)),
        g_wid=(far, shape((wide, INNER), F32)),
        g_ig=(vmem, shape((4, INNER), F32)),
        g_ib=(vmem, shape((4, INNER), F32)),
        g_bg=(vmem, shape((2, CHANNELS), F32)),
        g_bb=(vmem, shape((2, CHANNELS), F32)),
        far_blocks=(far, shape((4, chips, ROWS, INNER), F32)),
        far_columns=(far, shape((2, taps, chips * ROWS, INNER), BF)),
    )
    names = list(inputs) + list(outputs) + list(buffers)
    outs = pl.pallas_call(
        functools.partial(kernel, dp, outer, names),
        out_shape=[spec for _, spec in outputs.values()],
        in_specs=[space for space, _ in inputs.values()],
        out_specs=[space for space, _ in outputs.values()],
        scratch_shapes=list(buffers.values()),
        compiler_params=pltpu.CompilerParams(
            collective_id=0, has_side_effects=True, vmem_limit_bytes=63 * 1024 * 1024
        ),
        name="chain",
    )(*[value for _, value in inputs.values()])
    held = dict(zip(outputs, outs))
    big = dict(
        out=held["out_h"],
        grad=held["grad_h"],
        red=held["g_red"],
        **{"def": held["g_def"]},
        exp=held["g_exp"],
        nar=held["g_nar"],
        con=held["g_con"],
        wid=held["g_wid"],
    )
    small = {name: held[name] for name in ("g_off", "g_ig", "g_ib", "g_bg", "g_bb")}
    firsts = {"from_" + name: value for name, value in big.items()}
    finals = {"to_" + name: shape(value.shape, value.dtype) for name, value in big.items()}
    holds = {"hold_" + name: pltpu.VMEM(value.shape, value.dtype) for name, value in big.items()}
    lasts = dict(
        to_off=shape((OFFSETS, deep), F32),
        to_ig=shape((4, INNER // dp), F32),
        to_ib=shape((4, INNER // dp), F32),
        to_bg=shape((2, CHANNELS // dp), F32),
        to_bb=shape((2, CHANNELS // dp), F32),
    )
    names = [*firsts, *small, *finals, *lasts, *holds, "sems"]
    got = pl.pallas_call(
        functools.partial(deliver, dp, names),
        out_shape=[*finals.values(), *lasts.values()],
        in_specs=[far] * len(firsts) + [vmem] * len(small),
        out_specs=[far] * len(finals) + [vmem] * len(lasts),
        scratch_shapes=[*holds.values(), pltpu.SemaphoreType.DMA((2, len(big)))],
        compiler_params=pltpu.CompilerParams(vmem_limit_bytes=60 * 1024 * 1024),
        name="deliver",
    )(*firsts.values(), *small.values())
    out, grad, g_red, g_def, g_exp, g_nar, g_con, g_wid, g_off, *others = got
    return (
        out.reshape(SLOTS, PIXELS, CHANNELS),
        grad.reshape(SLOTS, PIXELS, CHANNELS),
        g_red,
        g_off.T,
        g_def,
        g_exp,
        g_nar,
        g_con,
        g_wid,
        *others,
    )


def solution(mesh):
    spread = P(("dp", "outer"), None, None)
    in_specs = (spread, P(), P(("dp", "outer")), spread) + (P(),) * 11
    out_specs = (spread, spread) + (P("dp", None),) * 7 + (P(None, "dp"),) * 4
    return jax.shard_map(
        per_device, mesh=mesh, in_specs=in_specs, out_specs=out_specs, check_vma=False
    )
```

```python
import functools
import math
import types

import jax
import jax.numpy as jnp
from jax import lax
from jax.experimental import pallas as pl
from jax.experimental.pallas import tpu as pltpu
from jax.sharding import PartitionSpec as P

CHANNELS = 2048
INNER = 512
TAPS = 9
SLOTS = 2
SHORT = 4
LONG = 36
PIXELS = 144
ROWS = SLOTS * PIXELS
OFFSETS = 2 * TAPS
EPS = 1e-05
BF = jnp.bfloat16
F32 = jnp.float32
MESH = pl.DeviceIdType.MESH
NN = (((1,), (0,)), ((), ()))
NT = (((1,), (1,)), ((), ()))
TN = (((0,), (0,)), ((), ()))


def mm(left, right, dims):
    return lax.dot_general(left, right, dims, preferred_element_type=F32)


def sigmoid(value):
    return 0.5 * jnp.tanh(0.5 * value) + 0.5


def fold(value):
    return jnp.sum(value.reshape(value.shape[0] // 8, 8, value.shape[1]), axis=0)


def total_row(value):
    return jnp.sum(value, axis=0, keepdims=True)


def layout(dp):
    chips = dp // 2
    bits = chips.bit_length() - 1
    wide = CHANNELS // dp
    deep = TAPS * INNER // dp
    taps = max(
        -(-(2 * deep * chip % INNER + 2 * deep) // INNER) for chip in range(chips)
    )
    return chips, bits, wide, deep, taps


def scratch(dp, outer):
    vmem = pltpu.VMEM
    dma = pltpu.SemaphoreType.DMA
    chips, bits, wide, deep, taps = layout(dp)
    everyone = dp * outer
    group = min(chips, 4)
    return dict(
        images=vmem((ROWS, CHANNELS), BF),
        between=vmem((ROWS, CHANNELS), BF),
        dwide=vmem((ROWS, CHANNELS), BF),
        obuf=vmem((ROWS, CHANNELS), BF),
        redwid=vmem((CHANNELS, INNER), BF),
        exp=vmem((CHANNELS, INNER), BF),
        nar=vmem((CHANNELS, INNER), BF),
        dfmcon=vmem((TAPS * INNER, INNER), BF),
        off=vmem((OFFSETS, TAPS * INNER), BF),
        a1=vmem((ROWS, INNER), F32),
        a2=vmem((ROWS, INNER), F32),
        b1=vmem((ROWS, INNER), F32),
        b2=vmem((ROWS, INNER), F32),
        acc=vmem((ROWS, INNER), F32),
        a3=vmem((CHANNELS // 512, ROWS, 512), F32),
        b3=vmem((CHANNELS // 512, ROWS, 512), F32),
        up=vmem((CHANNELS // 512, ROWS, 512), F32),
        inner=vmem((ROWS, INNER), BF),
        hidden=vmem((ROWS, INNER), BF),
        narrow=vmem((ROWS, INNER), BF),
        mixed=vmem((ROWS, INNER), BF),
        dn=vmem((ROWS, INNER), BF),
        turned=vmem((ROWS, INNER), BF),
        wmat=vmem((SLOTS, TAPS, PIXELS, PIXELS), BF),
        tmat=vmem((2, TAPS, PIXELS, PIXELS), BF),
        geo=vmem((2, 2, PIXELS, PIXELS), jnp.int32),
        frac=vmem((ROWS, OFFSETS), F32),
        doff=vmem((ROWS, OFFSETS), F32),
        stn=vmem((4, 2, INNER), F32),
        stw=vmem((2, 2, CHANNELS), F32),
        rxn=vmem((8, everyone, 2, INNER), F32),
        rxw1=vmem((4, dp, 2, CHANNELS), F32),
        rxw2=vmem((4, outer, 2, CHANNELS), F32),
        pool=vmem((3, chips, wide, INNER), F32),
        corel=vmem((chips, wide, INNER), F32),
        land=vmem((2, 2, chips - 1, wide, INNER // 2), F32),
        zwide=vmem((3, 3, wide, INNER), F32),
        tiny=vmem((2, chips, SLOTS, 24, PIXELS), F32),
        give=vmem((ROWS, INNER), F32),
        taken=vmem((group, ROWS, INNER), F32),
        drawn=vmem((ROWS, INNER), F32),
        yall=vmem((group * ROWS, INNER), BF),
        xall=vmem((2, group * ROWS, INNER), BF),
        grad=vmem((taps * INNER, INNER), F32),
        cored=vmem((deep, INNER), F32),
        zdeep=vmem((2, 2, deep // 2, INNER), F32),
        goff=vmem((24, taps * INNER), F32),
        coreo=vmem((24, taps * INNER), F32),
        zoff=vmem((2, 24, taps * INNER), F32),
        free=pltpu.SemaphoreType.REGULAR,
        credit=pltpu.SemaphoreType.REGULAR((2, bits)),
        swapped=pltpu.SemaphoreType.REGULAR,
        load_sem=dma((11,)),
        out_sem=dma((2,)),
        res_sem=dma((7, 4)),
        xn_s=dma((8,)),
        xn_r=dma((8,)),
        xw_s=dma((4, 2)),
        xw_r=dma((4, 2)),
        core_s=dma((7,)),
        core_r=dma((7,)),
        step_s=dma((4, 2, bits)),
        step_r=dma((4, 2, bits)),
        give_sem=dma((4,)),
        take_sem=dma((3,)),
        x_sem=dma((2,)),
        ag_s=dma((4, 2, bits)),
        ag_r=dma((4, 2, bits)),
        tiny_s=dma((2,)),
        tiny_r=dma((2,)),
        z_s=dma((7, 4, 3)),
        z_r=dma((7, 4, 3)),
    )


def kernel(dp, outer, names, *refs):
    assert outer == 4
    r = types.SimpleNamespace(**dict(zip(names, refs)))
    chips, bits, wide, deep, taps = layout(dp)
    everyone = dp * outer
    me = lax.axis_index("dp")
    mine = lax.axis_index("outer")
    own = me * outer + mine
    core = lax.rem(me, 2)
    chip = lax.div(me, 2)
    sibling = (me + 1 - 2 * core, mine)
    inside = (mine == 1) | (mine == 2)
    outside = (mine == 0) | (mine == 3)
    counts, orient = r.counts, r.orient
    dma = pltpu.make_async_copy

    loads = types.SimpleNamespace()

    def load(place, source, target):
        copy = dma(source, target, r.load_sem.at[place])
        copy.start()
        return copy

    loads.images_h = load(0, r.images_h, r.images)
    loads.red_h = load(1, r.red_h, r.redwid)
    loads.off_h = load(2, r.off_h, r.off)
    loads.def_h = load(3, r.def_h, r.dfmcon)
    loads.exp_h = load(4, r.exp_h, r.exp)
    loads.nar_h = load(5, r.nar_h, r.nar)
    loads.cot_h = load(6, r.cot_h, r.dwide)

    def other(step):
        target = lax.rem(own + step, everyone)
        return lax.div(target, outer), lax.rem(target, outer)

    barrier = pltpu.get_barrier_semaphore()

    def greet(step, carry):
        pl.semaphore_signal(barrier, inc=1, device_id=other(step), device_id_type=MESH)
        return carry

    lax.fori_loop(1, everyone, greet, 0)

    def size(i, carry):
        sizes, near, far = carry
        row, place = lax.div(i, outer), lax.rem(i, outer)
        held = counts[i].astype(F32)
        here = jnp.where(place == mine, held, 0.0)

        def mark(count, at, value):
            line = lax.broadcasted_iota(jnp.int32, (count, 1), 0)
            return jnp.where(line == at, value, 0.0)

        return (
            sizes + mark(everyone, i, held),
            near + mark(dp, row, here),
            far + mark(outer, place, held),
        )

    zeros = tuple(jnp.zeros((count, 1), F32) for count in (everyone, dp, outer))
    sizes, near, far = (
        value * float(PIXELS) for value in lax.fori_loop(0, everyone, size, zeros)
    )
    near_total = total_row(near)
    total = total_row(far)
    held = counts[own].astype(F32)
    live1 = held - 1.0
    local = held * float(PIXELS)

    def sweep(body, init):
        def step(i, carry):
            lv = jnp.where(i < 3, 1.0, live1)
            for j in range(3):
                carry = body(pl.ds(pl.multiple_of(i * 48 + j * 16, 16), 16), lv, carry)
            return carry

        return lax.fori_loop(0, 6, step, init)

    def send(source, target, sent, received, device):
        pltpu.make_async_remote_copy(
            src_ref=source,
            dst_ref=target,
            send_sem=sent,
            recv_sem=received,
            device_id=device,
            device_id_type=MESH,
        ).start()

    def settle(view, sem):
        dma(view, view, sem).wait()

    waiting = {}

    def later(tag, view, sem, when=None):
        waiting.setdefault(tag, []).append((when, view, sem))

    def flush(tag):
        for when, view, sem in waiting.pop(tag, []):
            if when is None:
                settle(view, sem)
            else:
                pl.when(when)(functools.partial(settle, view, sem))

    def accumulate(target, source):
        rows = target.shape[0]
        step = math.gcd(rows, 32)

        def body(i, carry):
            rs = pl.ds(pl.multiple_of(i * step, 8), step)
            target[rs, :] += source[rs, :]
            return carry

        lax.fori_loop(0, rows // step, body, 0)

    def mix(target, one, two):
        rows = target.shape[0]
        step = math.gcd(rows, 32)

        def body(i, carry):
            rs = pl.ds(pl.multiple_of(i * step, 8), step)
            target[rs, :] = one[rs, :] + two[rs, :]
            return carry

        lax.fori_loop(0, rows // step, body, 0)

    def flip(value, bit):
        weight = 1 << bit
        return value + weight - 2 * weight * lax.rem(lax.div(value, weight), 2)

    def bit_of(value, bit):
        return lax.rem(lax.div(value, 1 << bit), 2)

    orders = [
        list(range(bits)),
        list(range(bits // 2, bits)) + list(range(bits // 2)),
    ]
    halves = [pl.ds(0, INNER // 2), pl.ds(INNER // 2, INNER // 2)]

    def merge(rx, counted, size, forward):
        first = rx[:, 0, :]
        second = rx[:, 1, :]
        if forward:
            summed = total_row(first)
            apart = first / counted - summed / size
            spread = total_row(second + counted * apart * apart)
            return jnp.concatenate([summed, spread], axis=0)
        return jnp.concatenate([total_row(first), total_row(second)], axis=0)

    def nothing():
        pass

    def share_narrow(number, forward, work):
        rx = r.rxn.at[number]

        def step(i, carry):
            line, part = lax.div(i, dp), lax.rem(i, dp)
            z = jnp.where(mine < outer // 2, outer - 1 - line, line)
            peer = 0
            for bit in range(bits + 1):
                here, turn = bit_of(me, bit), 1 - bit_of(part, bit)
                peer = peer + (here + turn - 2 * here * turn) * (1 << bit)

            @pl.when(peer * outer + z != own)
            def _():
                send(rx.at[own], rx.at[own], r.xn_s.at[number], r.xn_r.at[number], (peer, z))

            return carry

        lax.fori_loop(0, everyone, step, 0)
        rest = rx.at[pl.ds(0, everyone - 1)]
        later("end", rest, r.xn_s.at[number])
        work()
        settle(rest, r.xn_r.at[number])
        return merge(rx, sizes, total, forward)

    def share_wide(number, forward, work, work_more):
        rx1, rx2 = r.rxw1.at[number], r.rxw2.at[number]
        for step in range(1, dp):
            send(
                rx1.at[me],
                rx1.at[me],
                r.xw_s.at[number, 0],
                r.xw_r.at[number, 0],
                (lax.rem(me + step, dp), mine),
            )
        rest = rx1.at[pl.ds(0, dp - 1)]
        later("end", rest, r.xw_s.at[number, 0])
        work()
        settle(rest, r.xw_r.at[number, 0])
        rx2[mine] = merge(rx1, near, near_total, forward)
        for step in range(1, outer):
            send(
                rx2.at[mine],
                rx2.at[mine],
                r.xw_s.at[number, 1],
                r.xw_r.at[number, 1],
                (me, lax.rem(mine + step, outer)),
            )
        rest = rx2.at[pl.ds(0, outer - 1)]
        later("end", rest, r.xw_s.at[number, 1])
        work_more()
        settle(rest, r.xw_r.at[number, 1])
        return merge(rx2, far, total, forward)

    def local_stats(ref, put, cs):
        zero = jnp.zeros((8, 512), F32)
        summed = total_row(sweep(lambda rs, lv, c: c + lv * fold(ref[rs, :]), zero))
        mean = summed / local

        def squares(rs, lv, carry):
            apart = ref[rs, :] - mean
            return carry + lv * fold(apart * apart)

        put[0:1, cs] = summed
        put[1:2, cs] = total_row(sweep(squares, zero))

    def keep_stats(both, st):
        st[0:1, :] = both[0:1] / total
        st[1:2, :] = lax.rsqrt(both[1:2] / total + EPS)

    def narrow_stats(ref, number, work=nothing):
        local_stats(ref, r.rxn.at[number, own], pl.ds(0, INNER))
        keep_stats(share_narrow(number, True, work), r.stn.at[number])

    blocks = [pl.ds(start, 512) for start in range(0, CHANNELS, 512)]

    def wide_stats(ref, number, work=nothing, work_more=nothing):
        for n, cs in enumerate(blocks):
            local_stats(ref.at[n], r.rxw1.at[number, me], cs)
        keep_stats(share_wide(number, True, work, work_more), r.stw.at[number])

    def norm_silu(ref, number, gain, bias, out, spread):
        st = r.stn.at[number]
        mean, scale = st[0:1, :], st[1:2, :]
        steep = scale * gain

        def body(rs, lv, carry):
            z = (ref[rs, :] - mean) * steep + bias
            value = (z * sigmoid(z)).astype(BF)
            out[rs, :] = value
            if spread:
                r.give[rs, :] = value.astype(F32)
            return carry

        sweep(body, 0)

    def narrow_cotangent(ref, place, gain, bias, number, spread, work=nothing):
        acc = r.acc
        st = r.stn.at[place]
        mean, scale = st[0:1, :], st[1:2, :]

        def body(rs, lv, carry):
            xhat = (ref[rs, :] - mean) * scale
            z = xhat * gain + bias
            sg = sigmoid(z)
            g = acc[rs, :] * (sg * (1.0 + z * (1.0 - sg)))
            acc[rs, :] = g
            return carry[0] + fold(g), carry[1] + fold(g * xhat)

        zero = jnp.zeros((8, INNER), F32)
        summed, paired = sweep(body, (zero, zero))
        put = r.rxn.at[number, own]
        put[0:1, :] = total_row(summed)
        put[1:2, :] = total_row(paired)
        both = share_narrow(number, False, work)
        r.g_ib[place : place + 1, :] = both[0:1]
        r.g_ig[place : place + 1, :] = both[1:2]
        steep = scale * gain
        lift, tilt = both[0:1] / total, both[1:2] / total

        def back(rs, lv, carry):
            xhat = (ref[rs, :] - mean) * scale
            value = (steep * (acc[rs, :] - lv * (lift + xhat * tilt))).astype(BF)
            r.dn[rs, :] = value
            if spread:
                r.give[rs, :] = value.astype(F32)
            return carry

        sweep(back, 0)

    def wide_cotangent(number, ref, place, gain, bias, cotangent, work=nothing, work_more=nothing):
        put = r.rxw1.at[number, me]
        st = r.stw.at[place]
        for n, cs in enumerate(blocks):
            mean, scale = st[0:1, cs], st[1:2, cs]
            gn, bs = gain[:, 512 * n : 512 * n + 512], bias[:, 512 * n : 512 * n + 512]

            def body(rs, lv, carry):
                xhat = (ref[n, rs, :] - mean) * scale
                g = cotangent(n, rs, cs, lv, xhat * gn + bs)
                r.up[n, rs, :] = g
                return carry[0] + fold(g), carry[1] + fold(g * xhat)

            zero = jnp.zeros((8, 512), F32)
            summed, paired = sweep(body, (zero, zero))
            put[0:1, cs] = total_row(summed)
            put[1:2, cs] = total_row(paired)
        both = share_wide(number, False, work, work_more)
        r.g_bb[place : place + 1, :] = both[0:1]
        r.g_bg[place : place + 1, :] = both[1:2]
        for n, cs in enumerate(blocks):
            mean, scale = st[0:1, cs], st[1:2, cs]
            span = slice(512 * n, 512 * n + 512)
            steep = scale * gain[:, span]
            lift, tilt = both[0:1, span] / total, both[1:2, span] / total

            def back(rs, lv, carry):
                xhat = (ref[n, rs, :] - mean) * scale
                value = steep * (r.up[n, rs, :] - lv * (lift + xhat * tilt))
                r.dwide[rs, cs] = value.astype(BF)
                return carry

            sweep(back, 0)

    def tap(ref, k):
        return ref[pl.ds(pl.multiple_of(k * INNER, INNER), INNER), :]

    def offset_tap(k):
        return r.off[:, pl.ds(pl.multiple_of(k * INNER, INNER), INNER)]

    def slot_rows(s):
        return pl.ds(s * PIXELS, PIXELS)

    def steps_of(k):
        return 2 * lax.div(k, 3) - 2, 2 * lax.rem(k, 3) - 2

    WID, CON, NAR, EXP, DEF, RED, OFF = range(7)
    nth = {WID: 0, NAR: 1, EXP: 2, RED: 3}
    result = {
        WID: r.g_wid,
        CON: r.g_con,
        NAR: r.g_nar,
        EXP: r.g_exp,
        DEF: r.g_def,
        RED: r.g_red,
        OFF: r.g_off,
    }
    pool, land, grad, far_blocks = r.pool, r.land, r.grad, r.far_blocks

    deep_parts = 4 if deep % 32 == 0 else 2
    wide_parts = {WID: 2, NAR: 2, EXP: 2, RED: 4}

    def z_hold(u):
        if u == RED:
            return [r.a3.at[i, pl.ds(0, wide)] for i in range(3)]
        return [r.zwide.at[nth[u], i] for i in range(3)]

    def z_parts(u):
        if u in nth:
            hold = z_hold(u)
            for q in range(wide_parts[u]):
                rows = wide // (wide_parts[u] // 2)
                rs, hs = pl.ds(q // 2 * rows, rows), halves[q % 2]
                yield tuple(ref.at[rs, hs] for ref in hold) + (result[u].at[rs, hs],)
        elif u == OFF:
            yield r.goff, r.zoff.at[0], r.zoff.at[1], result[u]
        else:
            for q in range(deep_parts):
                back, at = divmod(q, deep_parts // 2)
                source = r.b3.at[(2 if u == DEF else 0) + back]
                if u == DEF:
                    first, second = (r.b1, r.a2) if back == 0 else (r.b2, r.a3.at[3])
                else:
                    first, second = r.zdeep.at[0, back], r.zdeep.at[1, back]
                size = deep // deep_parts
                rows = pl.ds(at * size, size)
                out = result[u].at[pl.ds(q * size, size)]
                yield source.at[rows], first.at[rows], second.at[rows], out

    def z_sems(u, q, step):
        return r.z_s.at[u, q, step], r.z_r.at[u, q, step]

    def z1(u, some=None):
        for q, (source, first, second, out) in enumerate(z_parts(u)):
            if some is not None and q not in some:
                continue
            sent, received = z_sems(u, q, 0)

            @pl.when(outside)
            def _():
                send(source, first, sent, received, (me, flip(mine, 0)))

            later(("z", u), source, sent, outside)

    def z2(u, some=None):
        for q, (source, first, second, out) in enumerate(z_parts(u)):
            if some is not None and q not in some:
                continue
            sent, received = z_sems(u, q, 1)

            @pl.when(inside)
            def _():
                settle(first, z_sems(u, q, 0)[1])
                accumulate(source, first)
                send(source, second, sent, received, (me, 3 - mine))

            later(("z", u), source, sent, inside)

    def z3(u, some=None):
        for q, (source, first, second, out) in enumerate(z_parts(u)):
            if some is not None and q not in some:
                continue
            sent, received = z_sems(u, q, 2)

            @pl.when(inside)
            def _():
                settle(second, z_sems(u, q, 1)[1])
                accumulate(second, source)
                send(second, first, sent, received, (me, flip(mine, 0)))
                dma(second, out, r.res_sem.at[u, q]).start()

            later(("zl", u), second, sent, inside)

    def z4(u, some=None):
        for q, (source, first, second, out) in enumerate(z_parts(u)):
            if some is not None and q not in some:
                continue

            @pl.when(outside)
            def _():
                settle(first, z_sems(u, q, 2)[1])
                dma(first, out, r.res_sem.at[u, q]).start()

    def z_clear(u):
        flush(("z", u))
        flush(("zl", u))
        for q, (source, first, second, out) in enumerate(z_parts(u)):
            dma(first, out, r.res_sem.at[u, q]).wait()

    def wide_begin(u, left, right):
        p = nth[u] % 2
        flush("sib")
        flush(("keep", p))
        low = p + (2 - p) * core
        high = p + (2 - p) * (1 - core)
        if u == EXP:
            pl.semaphore_wait(r.swapped, 1)

        def step(m, carry):
            block = left[:, pl.ds(pl.multiple_of(m * (2 * wide), 2 * wide), 2 * wide)]
            pool[low, m] = mm(block[:, :wide], right[...], TN)
            pool[high, m] = mm(block[:, wide:], right[...], TN)
            send(
                pool.at[2, m], r.corel.at[m], r.core_s.at[u], r.core_r.at[u], sibling
            )
            return carry

        lax.fori_loop(0, chips, step, 0)
        later("sib", r.corel, r.core_s.at[u])

    def piece(h, t, j, toward):
        value = 0
        for i, bit in enumerate(orders[h]):
            if i < t:
                part = bit_of(chip, bit)
            elif i == t:
                part = bit_of(toward, bit)
            else:
                part = (j >> (i - t - 1)) & 1
            value = value + part * (1 << bit)
        return value

    def step_place(u, h, t):
        first, count = chips - (chips >> t), chips >> (t + 1)
        p = nth[u] % 2
        sems = r.step_s.at[nth[u], h, t], r.step_r.at[nth[u], h, t]
        return p, first, count, sems, land.at[p, h, pl.ds(first, count)]

    def wide_send(u, t):
        for h in range(2):
            p, first, count, (sent, received), region = step_place(u, h, t)
            toward = flip(chip, orders[h][t])
            if u == RED:
                pl.semaphore_wait(r.credit.at[h, t], 1)
            for j in range(count):
                send(
                    pool.at[p, piece(h, t, j, toward), :, halves[h]],
                    land.at[p, h, first + j],
                    sent,
                    received,
                    (2 * toward + core, mine),
                )
            later(("keep", p), region, sent)

    def wide_add(u, t):
        for h in range(2):
            p, first, count, (sent, received), region = step_place(u, h, t)
            settle(region, received)
            if t == bits - 1:
                mix(z_hold(u)[0].at[:, halves[h]], pool.at[p, chip, :, halves[h]], land.at[p, h, first])
            else:
                for j in range(count):
                    accumulate(
                        pool.at[p, piece(h, t, j, chip), :, halves[h]], land.at[p, h, first + j]
                    )
            if u == NAR:
                pl.semaphore_signal(
                    r.credit.at[h, t],
                    inc=1,
                    device_id=(2 * flip(chip, orders[h][t]) + core, mine),
                    device_id_type=MESH,
                )

    def wide_core(u):
        p = nth[u] % 2
        settle(r.corel, r.core_r.at[u])

        def step(m, carry):
            accumulate(pool.at[p, m], r.corel.at[m])
            return carry

        lax.fori_loop(0, chips, step, 0)
        if u == NAR:
            pl.semaphore_signal(r.swapped, inc=1, device_id=sibling, device_id_type=MESH)

    def wide_step(u, t):
        wide_add(u, t - 1)
        if t < bits:
            wide_send(u, t)
        else:
            z1(u)

    def held_at(h, j):
        value = chip
        for i in range(bits):
            if (j >> i) & 1:
                value = flip(value, orders[h][i])
        return value

    def gather_send(a, t, some=None):
        for h in range(2):
            partner = flip(chip, orders[h][t])
            sent, received = r.ag_s.at[a, h, t], r.ag_r.at[a, h, t]
            for j in range(1 << t) if some is None else some:
                block = far_blocks.at[a, held_at(h, j), :, halves[h]]
                source = r.give.at[:, halves[h]] if j == 0 else block
                send(source, block, sent, received, (2 * partner + core, mine))
            if some is None or 0 in some:
                later(("ag", a), far_blocks.at[a, pl.ds(0, 1 << t), :, halves[h]], sent)

    def gather_start(a):
        block = far_blocks.at[a, chip]
        dma(r.give, block, r.give_sem.at[a]).start()
        later(("ag", a), block, r.give_sem.at[a])
        gather_send(a, 0)

    def gather_wait(a, t):
        for h in range(2):
            settle(far_blocks.at[a, pl.ds(0, 1 << t), :, halves[h]], r.ag_r.at[a, h, t])

    def gather_step(a, t, some=None):
        gather_wait(a, t - 1)
        gather_send(a, t, some)

    def gather_first(a, t):
        if t < bits:
            gather_send(a, t, [0])

    def gather_rest(a):
        for t in range(1, bits):
            gather_wait(a, t - 1)
            gather_send(a, t, range(1 if t == 1 else 0, 1 << t))

    def gather_end(a):
        gather_wait(a, bits - 1)
        flush(("ag", a))

    def tiny_send(a):
        for step in range(1, chips):
            block = r.tiny.at[a, chip]
            peer = lax.rem(chip + step, chips)
            send(block, block, r.tiny_s.at[a], r.tiny_r.at[a], (2 * peer + core, mine))
        later("end", r.tiny.at[a, pl.ds(0, chips - 1)], r.tiny_s.at[a])

    def tiny_wait(a):
        settle(r.tiny.at[a, pl.ds(0, chips - 1)], r.tiny_r.at[a])

    group = min(chips, 4)
    first_tap = lax.div(2 * deep * chip, INNER)
    margin = 2 * deep * chip - first_tap * INNER

    def taps_of(kk):
        k = jnp.minimum(first_tap + kk, TAPS - 1)
        return (k, *steps_of(k))

    def fetch_fields(a, g):
        copy = dma(far_blocks.at[a, pl.ds(g * group, group)], r.taken, r.take_sem.at[2])
        copy.start()
        copy.wait()

    def image_of(i, g):
        m, s = lax.div(i, SLOTS), lax.rem(i, SLOTS)
        rows = pl.ds(pl.multiple_of(i * PIXELS, PIXELS), PIXELS)
        field = r.taken[m, pl.ds(pl.multiple_of(s * PIXELS, PIXELS), PIXELS), :].astype(BF)
        flat = r.tiny[0, g * group + m, s, 18:19, :] == 0.0
        dr = jnp.where(flat, r.geo[0, 0], r.geo[1, 0])
        dc = jnp.where(flat, r.geo[0, 1], r.geo[1, 1])
        return g * group + m, s, rows, field, dr, dc

    def group_rows(g):
        return pl.ds(g * (group * ROWS), group * ROWS)

    def columns(u, kk):
        x = 1 if u == DEF else 0
        k, down, across = taps_of(kk)
        for g in range(chips // group):
            if kk == 0 or chips > group:
                fetch_fields(0 if u == DEF else 1, g)
            if g == 0:
                flush("columns")

            def image(i, carry):
                m, s, rows, field, dr, dc = image_of(i, g)
                if u == CON:
                    hit = jnp.where((dr == down) & (dc == across), 1.0, 0.0).astype(BF)
                    r.xall[0, rows, :] = mm(hit, field, NN).astype(BF)
                    return carry
                tiny = r.tiny.at[0, m, s]
                fy, fx = tiny[pl.ds(2 * k, 1), :], tiny[pl.ds(2 * k + 1, 1), :]
                ay = jnp.where(dr == -down, 1.0 - fy, jnp.where(dr == -down - 1, fy, 0.0))
                ax = jnp.where(dc == -across, 1.0 - fx, jnp.where(dc == -across - 1, fx, 0.0))
                r.xall[0, rows, :] = mm((ay * ax).astype(BF), field, TN).astype(BF)
                return carry

            lax.fori_loop(0, group * SLOTS, image, 0, unroll=4)
            place = r.far_columns.at[x, kk, group_rows(g)]
            copy = dma(r.xall.at[0], place, r.x_sem.at[0])
            copy.start()
            if g + 1 < chips // group:
                copy.wait()
            else:
                later("columns", place, r.x_sem.at[0])

    def deep_make(u):
        flush("deep")
        flush("columns")
        x, back_of = (1, 3) if u == DEF else (0, 2)
        slots = (r.give, r.drawn)
        for g in range(chips // group):

            def fetch(m):
                return dma(far_blocks.at[back_of, g * group + m], slots[m % 2], r.take_sem.at[m % 2])

            def draw(kk):
                slot = lax.rem(kk, 2)
                return dma(
                    r.far_columns.at[x, kk, group_rows(g)], r.xall.at[slot], r.x_sem.at[slot]
                )

            for m in range(min(2, group)):
                fetch(m).start()
            draw(0).start()
            for m in range(group):
                fetch(m).wait()

                def lower(i, carry):
                    rows = pl.ds(pl.multiple_of(m * ROWS + i * 32, 32), 32)
                    there = pl.ds(pl.multiple_of(i * 32, 32), 32)
                    r.yall[rows, :] = slots[m % 2][there, :].astype(BF)
                    return carry

                lax.fori_loop(0, ROWS // 32, lower, 0)
                if m + 2 < group:
                    fetch(m + 2).start()

            def one(kk, carry):
                @pl.when(kk + 1 < taps)
                def _():
                    draw(kk + 1).start()

                draw(kk).wait()
                at = pl.ds(pl.multiple_of(kk * INNER, INNER), INNER)
                part = mm(r.xall[lax.rem(kk, 2)], r.yall[...], TN)
                if g == 0:
                    grad[at, :] = part
                else:
                    grad[at, :] += part
                return carry

            lax.fori_loop(0, taps, one, 0)
        away = pl.ds(pl.multiple_of(margin + (1 - core) * deep, 8), deep)
        send(grad.at[away], r.cored, r.core_s.at[u], r.core_r.at[u], sibling)
        later("deep", r.cored, r.core_s.at[u])

    def off_make():
        for g in range(chips // group):
            fetch_fields(0, g)

            def one(kk, carry):
                k, down, across = taps_of(kk)

                def image(i, share):
                    m, s, rows, field, dr, dc = image_of(i, g)
                    hit = jnp.where((dr == down) & (dc == across), 1.0, 0.0).astype(BF)
                    moved = mm(r.tiny[1, m, s].astype(BF), hit, NN).astype(BF)
                    return share + mm(moved, field, NN)

                at = pl.ds(pl.multiple_of(kk * INNER, INNER), INNER)
                share = lax.fori_loop(
                    0, group * SLOTS, image, jnp.zeros((24, INNER), F32), unroll=8
                )
                if g == 0:
                    r.goff[:, at] = share
                else:
                    r.goff[:, at] += share
                return carry

            lax.fori_loop(0, taps, one, 0)
        send(r.goff, r.coreo, r.core_s.at[OFF], r.core_r.at[OFF], sibling)

    def off_core():
        settle(r.goff, r.core_s.at[OFF])
        settle(r.coreo, r.core_r.at[OFF])
        accumulate(r.goff, r.coreo)

    def deep_core(u):
        settle(r.cored, r.core_r.at[u])
        half = deep // 2
        step = math.gcd(half, 32)
        for q in range(2):
            target = r.b3.at[(2 if u == DEF else 0) + q]

            def body(i, carry):
                at = pl.multiple_of(i * step, 8)
                here = grad[pl.ds(pl.multiple_of(margin + core * deep + q * half + at, 8), step), :]
                target[pl.ds(at, step), :] = here + r.cored[pl.ds(q * half + at, step), :]
                return carry

            lax.fori_loop(0, half // step, body, 0)
    images, between, acc, up = r.images, r.between, r.acc, r.up
    ig = [r.ig[i : i + 1, :] for i in range(4)]
    ib = [r.ib[i : i + 1, :] for i in range(4)]
    bg = [r.bg[i : i + 1, :] for i in range(2)]
    bb = [r.bb[i : i + 1, :] for i in range(2)]

    def geometry():
        q = lax.broadcasted_iota(jnp.int32, (PIXELS, PIXELS), 1)
        p = lax.broadcasted_iota(jnp.int32, (PIXELS, PIXELS), 0)

        def place_of(at, kind):
            if kind:
                row = lax.shift_right_logical(at, 2)
                return row, at - row * SHORT
            row = (at >= LONG).astype(jnp.int32) + (at >= 2 * LONG).astype(jnp.int32)
            row = row + (at >= 3 * LONG).astype(jnp.int32)
            return row, at - row * LONG

        for kind in range(2):
            row_q, col_q = place_of(q, kind)
            row_p, col_p = place_of(p, kind)
            r.geo[kind, 0] = row_q - row_p
            r.geo[kind, 1] = col_q - col_p

            def hot(k, carry):
                down, across = steps_of(k)
                hit = (r.geo[kind, 0] == down) & (r.geo[kind, 1] == across)
                r.tmat[kind, k] = jnp.where(hit, 1.0, 0.0).astype(BF)
                return carry

            lax.fori_loop(0, TAPS, hot, 0)

    def shifted(s, k):
        return r.tmat[orient[s], k]

    loads.images_h.wait()
    loads.red_h.wait()
    r.a1[...] = mm(images[...], r.redwid[...], NN)
    loads.wid_h = load(7, r.wid_h, r.redwid)
    pl.semaphore_wait(barrier, everyone - 1)
    narrow_stats(r.a1, 0, geometry)
    norm_silu(r.a1, 0, ig[0], ib[0], r.inner, True)
    gather_start(0)

    loads.off_h.wait()
    inner = r.inner
    lane = lax.broadcasted_iota(jnp.int32, (PIXELS, OFFSETS), 1)

    def gather(k, carry):
        cols = [mm(shifted(s, k), inner[slot_rows(s), :], NN).astype(BF) for s in range(SLOTS)]
        weight = offset_tap(k)
        return tuple(old + mm(col, weight, NT) for old, col in zip(carry, cols))

    zero = jnp.zeros((PIXELS, OFFSETS), F32)
    both_offsets = lax.fori_loop(0, TAPS, gather, (zero,) * SLOTS, unroll=3)
    for s in range(SLOTS):
        frac = sigmoid(both_offsets[s])
        r.frac[slot_rows(s), :] = frac
        coarse = frac.astype(BF)
        fine = (frac - coarse.astype(F32)).astype(BF)
        unit = r.tmat[0, TAPS // 2]
        put = r.tiny.at[0, chip, s]
        put[...] = jnp.zeros((24, PIXELS), F32) + orient[s].astype(F32)
        put[0:OFFSETS, :] = mm(coarse, unit, TN) + mm(fine, unit, TN)
    tiny_send(0)

    def bilinear(s, k):
        down, across = steps_of(k)
        frac = r.frac[slot_rows(s), :]
        fy = jnp.sum(jnp.where(lane == 2 * k, frac, 0.0), axis=1, keepdims=True)
        fx = jnp.sum(jnp.where(lane == 2 * k + 1, frac, 0.0), axis=1, keepdims=True)
        dr, dc = r.geo[orient[s], 0], r.geo[orient[s], 1]
        in_y = (dr == down, dr == down + 1)
        in_x = (dc == across, dc == across + 1)
        ay = jnp.where(in_y[0], 1.0 - fy, jnp.where(in_y[1], fy, 0.0))
        ax = jnp.where(in_x[0], 1.0 - fx, jnp.where(in_x[1], fx, 0.0))
        return fy, fx, ay, ax, in_y, in_x

    loads.def_h.wait()
    acc[...] = jnp.zeros((ROWS, INNER), F32)

    def sample(k, carry):
        for s in range(SLOTS):
            _, _, ay, ax, _, _ = bilinear(s, k)
            weight = (ay * ax).astype(BF)
            r.wmat[s, k] = weight
            r.turned[slot_rows(s), :] = mm(weight, inner[slot_rows(s), :], NN).astype(BF)
        acc[...] += mm(r.turned[...], tap(r.dfmcon, k), NN)
        return carry

    lax.fori_loop(0, TAPS, sample, 0, unroll=3)
    loads.con_h = load(8, r.con_h, r.dfmcon)
    r.a2[...] = acc[...]
    narrow_stats(r.a2, 1, lambda: gather_first(0, 1))
    norm_silu(r.a2, 1, ig[1], ib[1], r.hidden, False)

    def widen(source, weight, target):
        def step(n, carry):
            rows = pl.ds(pl.multiple_of(n * 512, 512), 512)
            target[n] = mm(source[...], weight[rows, :], NT)
            return carry

        lax.fori_loop(0, CHANNELS // 512, step, 0)

    loads.exp_h.wait()
    widen(r.hidden, r.exp, r.a3)
    wide_stats(r.a3, 0, lambda: gather_rest(0))
    for n, cs in enumerate(blocks):
        mean = r.stw[0, 0:1, cs]
        steep = r.stw[0, 1:2, cs] * bg[0][:, 512 * n : 512 * n + 512]
        bias = bb[0][:, 512 * n : 512 * n + 512]

        def join(rs, lv, carry):
            z = (r.a3[n, rs, :] - mean) * steep + bias + images[rs, cs].astype(F32)
            between[rs, cs] = (z * sigmoid(z)).astype(BF)
            return carry

        sweep(join, 0)

    loads.nar_h.wait()
    r.b1[...] = mm(between[...], r.nar[...], NN)

    def work_b1():
        gather_end(0)
        tiny_wait(0)
        columns(DEF, 0)

    narrow_stats(r.b1, 2, work_b1)
    norm_silu(r.b1, 2, ig[2], ib[2], r.narrow, True)
    gather_start(1)

    loads.con_h.wait()
    acc[...] = jnp.zeros((ROWS, INNER), F32)

    def convolve(k, carry):
        for s in range(SLOTS):
            r.turned[slot_rows(s), :] = mm(
                shifted(s, k), r.narrow[slot_rows(s), :], NN
            ).astype(BF)
        acc[...] += mm(r.turned[...], tap(r.dfmcon, k), NN)
        return carry

    lax.fori_loop(0, TAPS, convolve, 0, unroll=3)
    r.b2[...] = acc[...]
    def work_b2():
        gather_first(1, 1)
        columns(DEF, 1)

    narrow_stats(r.b2, 3, work_b2)
    norm_silu(r.b2, 3, ig[3], ib[3], r.mixed, False)

    loads.wid_h.wait()
    widen(r.mixed, r.redwid, r.b3)

    def work_b3():
        gather_rest(1)
        for kk in range(2, taps):
            columns(DEF, kk)

    wide_stats(r.b3, 1, work_b3)

    loads.cot_h.wait()

    def last(n, rs, cs, lv, pre):
        z = pre + between[rs, cs].astype(F32)
        sg = sigmoid(z)
        r.obuf[rs, cs] = (lv * (z * sg)).astype(BF)
        return r.dwide[rs, cs].astype(F32) * (lv * (sg * (1.0 + z * (1.0 - sg))))

    def work_f():
        gather_end(1)
        columns(CON, 0)

    wide_cotangent(2, r.b3, 1, bg[1], bb[1], last, nothing, work_f)
    out_copy = dma(r.obuf, r.out_h, r.out_sem.at[0])
    out_copy.start()
    wide_begin(WID, r.dwide, r.mixed)
    acc[...] = mm(r.dwide[...], r.redwid[...], NN)
    loads.red_h = load(9, r.red_h, r.redwid)

    def work_e():
        wide_core(WID)
        wide_send(WID, 0)
        columns(CON, 1)

    narrow_cotangent(r.b2, 3, ig[3], ib[3], 4, True, work_e)

    acc[...] = jnp.zeros((ROWS, INNER), F32)

    def spread(k, carry):
        for s in range(SLOTS):
            r.turned[slot_rows(s), :] = mm(
                shifted(s, TAPS - 1 - k), r.dn[slot_rows(s), :], NN
            ).astype(BF)
        acc[...] += mm(r.turned[...], tap(r.dfmcon, k), NT)
        return carry

    lax.fori_loop(0, TAPS, spread, 0, unroll=3)
    loads.def_h = load(10, r.def_h, r.dfmcon)

    def work_d():
        wide_step(WID, 1)
        gather_start(2)
        for kk in range(2, taps):
            columns(CON, kk)

    narrow_cotangent(r.b1, 2, ig[2], ib[2], 5, False, work_d)
    for t in range(2, bits + 1):
        wide_step(WID, t)

    def add_back(n, carry):
        rows = pl.ds(pl.multiple_of(n * 512, 512), 512)
        up[n] += mm(r.dn[...], r.nar[rows, :], NT)
        return carry

    lax.fori_loop(0, CHANNELS // 512, add_back, 0)

    def first(n, rs, cs, lv, pre):
        z = pre + images[rs, cs].astype(F32)
        sg = sigmoid(z)
        return up[n, rs, :] * (sg * (1.0 + z * (1.0 - sg)))

    def work_c():
        for t in range(1, bits):
            gather_step(2, t)
        wide_begin(NAR, between, r.dn)

    def work_more_c():
        z2(WID)
        wide_core(NAR)

    wide_cotangent(3, r.a3, 0, bg[0], bb[0], first, work_c, work_more_c)
    acc[...] = mm(r.dwide[...], r.exp[...], NN)

    def work_b():
        wide_send(NAR, 0)
        z3(WID)
        wide_begin(EXP, r.dwide, r.hidden)
        gather_end(2)
        deep_make(CON)

    narrow_cotangent(r.a2, 1, ig[1], ib[1], 6, True, work_b)
    wide_step(NAR, 1)
    gather_start(3)
    deep_core(CON)
    early, late = range(deep_parts // 2), range(deep_parts // 2, deep_parts)
    z1(CON, early)

    loads.def_h.wait()
    acc[...] = jnp.zeros((ROWS, INNER), F32)
    r.doff[...] = jnp.zeros((ROWS, OFFSETS), F32)

    def unsample(k, carry):
        r.turned[...] = mm(r.dn[...], tap(r.dfmcon, k), NT).astype(BF)
        for s in range(SLOTS):
            rs = slot_rows(s)
            back = r.turned[rs, :]
            pairs = mm(back, inner[rs, :], NT)
            fy, fx, ay, ax, in_y, in_x = bilinear(s, k)
            slope_y = jnp.where(in_y[1], ax, 0.0) - jnp.where(in_y[0], ax, 0.0)
            slope_x = jnp.where(in_x[1], ay, 0.0) - jnp.where(in_x[0], ay, 0.0)
            to_y = jnp.sum(pairs * slope_y, axis=1, keepdims=True) * (fy * (1.0 - fy))
            to_x = jnp.sum(pairs * slope_x, axis=1, keepdims=True) * (fx * (1.0 - fx))
            r.doff[rs, :] += jnp.where(lane == 2 * k, to_y, 0.0) + jnp.where(
                lane == 2 * k + 1, to_x, 0.0
            )
            acc[rs, :] += mm(r.wmat[s, k], back, TN)
        return carry

    lax.fori_loop(0, TAPS, unsample, 0, unroll=3)
    z2(CON, [0])
    for s in range(SLOTS):
        put = r.tiny.at[1, chip, s]
        put[...] = jnp.zeros((24, PIXELS), F32)
        put[0:OFFSETS, :] = mm(
            r.doff[slot_rows(s), :].astype(BF), r.tmat[0, TAPS // 2], TN
        )
    tiny_send(1)

    def untap(k, carry):
        for s in range(SLOTS):
            rs = slot_rows(s)
            moved = mm(shifted(s, TAPS - 1 - k), r.doff[rs, :].astype(BF), NN).astype(BF)
            acc[rs, :] += mm(moved, offset_tap(k), NN)
        return carry

    lax.fori_loop(0, TAPS, untap, 0, unroll=3)

    wide_core(EXP)

    def work_a():
        for t in range(1, bits):
            gather_step(3, t)
        wide_send(EXP, 0)
        z1(CON, late)
        for t in range(2, bits + 1):
            wide_step(NAR, t)
        z2(CON, [1])
        z4(WID)

    narrow_cotangent(r.a1, 0, ig[0], ib[0], 7, False, work_a)
    z3(CON, [0])
    wide_begin(RED, images, r.dn)
    z2(CON, [2])
    out_copy.wait()
    loads.red_h.wait()

    def finish(n, carry):
        rows = pl.ds(pl.multiple_of(n * 512, 512), 512)
        r.obuf[:, rows] = (up[n] + mm(r.dn[...], r.redwid[rows, :], NT)).astype(BF)
        return carry

    lax.fori_loop(0, CHANNELS // 512, finish, 0)
    grad_copy = dma(r.obuf, r.grad_h, r.out_sem.at[1])
    grad_copy.start()
    z2(CON, [3])
    z3(CON, [1])
    gather_end(3)
    deep_make(DEF)
    z2(NAR, [0])
    z3(CON, [2])
    wide_core(RED)
    wide_send(RED, 0)
    deep_core(DEF)
    z1(DEF)
    z2(NAR, [1])
    z3(CON, [3])
    wide_step(EXP, 1)
    tiny_wait(1)
    off_make()
    z2(DEF, [0])
    z3(NAR, [0])
    off_core()
    z1(OFF)
    wide_step(RED, 1)
    z2(DEF, [1])
    z3(NAR, [1])
    for t in range(2, bits + 1):
        wide_step(EXP, t)
    z2(DEF, [2])
    z3(DEF, [0])
    for t in range(2, bits + 1):
        wide_step(RED, t)
    z2(DEF, [3])
    z3(DEF, [1])
    z2(OFF)
    z3(DEF, [2])
    z2(EXP, [0])
    z3(DEF, [3])
    z3(OFF)
    z2(EXP, [1])
    z2(RED, [0])
    z3(EXP, [0])
    z2(RED, [1])
    z2(RED, [2])
    z3(EXP, [1])
    z2(RED, [3])
    z3(RED, [0])
    z3(RED, [1])
    z3(RED, [2])
    z3(RED, [3])
    z4(CON)
    z4(NAR)
    z4(DEF)
    z4(OFF)
    z4(EXP)
    z4(RED)
    for u in range(7):
        z_clear(u)
    grad_copy.wait()
    for tag in list(waiting):
        flush(tag)


MOVED = ["out", "grad", "con", "def", "wid", "nar", "exp", "red"]


def deliver(dp, names, *refs):
    r = types.SimpleNamespace(**dict(zip(names, refs)))
    _, _, _, deep, _ = layout(dp)
    place = lax.axis_index("dp")
    moves = []
    for i, name in enumerate(MOVED):
        source, target, hold = (getattr(r, kind + name) for kind in ("from_", "to_", "hold_"))
        taken = pltpu.make_async_copy(source, hold, r.sems.at[0, i])
        taken.start()
        moves.append((taken, pltpu.make_async_copy(hold, target, r.sems.at[1, i])))

    for taken, given in moves:
        taken.wait()
        given.start()

    def span(ref, start, target):
        rows, lanes = ref.shape
        moved = pltpu.roll(ref[...], lax.rem(lanes - start, lanes), 1)
        target[...] = moved[: target.shape[0], : target.shape[1]]

    span(r.g_ig, place * (INNER // dp), r.to_ig)
    span(r.g_ib, place * (INNER // dp), r.to_ib)
    span(r.g_bg, place * (CHANNELS // dp), r.to_bg)
    span(r.g_bb, place * (CHANNELS // dp), r.to_bb)
    chip, core = lax.div(place, 2), lax.rem(place, 2)
    span(r.g_off, lax.rem(2 * deep * chip, INNER) + deep * core, r.to_off)
    for taken, given in moves:
        given.wait()


def per_device(
    images,
    counts,
    orientation,
    cotangent,
    reducer,
    offseter,
    deformer,
    expander,
    narrower,
    convolver,
    widener,
    inner_gains,
    inner_biases,
    broad_gains,
    broad_biases,
):
    dp, outer = lax.axis_size("dp"), lax.axis_size("outer")
    chips, bits, wide, deep, taps = layout(dp)
    buffers = scratch(dp, outer)
    smem = pl.BlockSpec(memory_space=pltpu.SMEM)
    vmem = pl.BlockSpec(memory_space=pltpu.VMEM)
    far = pl.BlockSpec(memory_space=pl.ANY)
    shape = jax.ShapeDtypeStruct
    inputs = dict(
        counts=(smem, counts),
        orient=(smem, orientation),
        ig=(vmem, inner_gains),
        ib=(vmem, inner_biases),
        bg=(vmem, broad_gains),
        bb=(vmem, broad_biases),
        images_h=(far, images.reshape(ROWS, CHANNELS)),
        cot_h=(far, cotangent.reshape(ROWS, CHANNELS)),
        red_h=(far, reducer),
        off_h=(far, offseter.T),
        def_h=(far, deformer),
        exp_h=(far, expander),
        nar_h=(far, narrower),
        con_h=(far, convolver),
        wid_h=(far, widener),
    )
    outputs = dict(
        out_h=(far, shape((ROWS, CHANNELS), BF)),
        grad_h=(far, shape((ROWS, CHANNELS), BF)),
        g_red=(far, shape((wide, INNER), F32)),
        g_off=(far, shape((24, taps * INNER), F32)),
        g_def=(far, shape((deep, INNER), F32)),
        g_exp=(far, shape((wide, INNER), F32)),
        g_nar=(far, shape((wide, INNER), F32)),
        g_con=(far, shape((deep, INNER), F32)),
        g_wid=(far, shape((wide, INNER), F32)),
        g_ig=(vmem, shape((4, INNER), F32)),
        g_ib=(vmem, shape((4, INNER), F32)),
        g_bg=(vmem, shape((2, CHANNELS), F32)),
        g_bb=(vmem, shape((2, CHANNELS), F32)),
        far_blocks=(far, shape((4, chips, ROWS, INNER), F32)),
        far_columns=(far, shape((2, taps, chips * ROWS, INNER), BF)),
    )
    names = list(inputs) + list(outputs) + list(buffers)
    outs = pl.pallas_call(
        functools.partial(kernel, dp, outer, names),
        out_shape=[spec for _, spec in outputs.values()],
        in_specs=[space for space, _ in inputs.values()],
        out_specs=[space for space, _ in outputs.values()],
        scratch_shapes=list(buffers.values()),
        compiler_params=pltpu.CompilerParams(
            collective_id=0, has_side_effects=True, vmem_limit_bytes=63 * 1024 * 1024
        ),
        name="chain",
    )(*[value for _, value in inputs.values()])
    held = dict(zip(outputs, outs))
    big = dict(
        out=held["out_h"],
        grad=held["grad_h"],
        red=held["g_red"],
        **{"def": held["g_def"]},
        exp=held["g_exp"],
        nar=held["g_nar"],
        con=held["g_con"],
        wid=held["g_wid"],
    )
    small = {name: held[name] for name in ("g_off", "g_ig", "g_ib", "g_bg", "g_bb")}
    firsts = {"from_" + name: value for name, value in big.items()}
    finals = {"to_" + name: shape(value.shape, value.dtype) for name, value in big.items()}
    holds = {"hold_" + name: pltpu.VMEM(value.shape, value.dtype) for name, value in big.items()}
    lasts = dict(
        to_off=shape((OFFSETS, deep), F32),
        to_ig=shape((4, INNER // dp), F32),
        to_ib=shape((4, INNER // dp), F32),
        to_bg=shape((2, CHANNELS // dp), F32),
        to_bb=shape((2, CHANNELS // dp), F32),
    )
    names = [*firsts, *small, *finals, *lasts, *holds, "sems"]
    got = pl.pallas_call(
        functools.partial(deliver, dp, names),
        out_shape=[*finals.values(), *lasts.values()],
        in_specs=[far] * len(firsts) + [vmem] * len(small),
        out_specs=[far] * len(finals) + [vmem] * len(lasts),
        scratch_shapes=[*holds.values(), pltpu.SemaphoreType.DMA((2, len(big)))],
        compiler_params=pltpu.CompilerParams(vmem_limit_bytes=60 * 1024 * 1024),
        name="deliver",
    )(*firsts.values(), *small.values())
    out, grad, g_red, g_def, g_exp, g_nar, g_con, g_wid, g_off, *others = got
    return (
        out.reshape(SLOTS, PIXELS, CHANNELS),
        grad.reshape(SLOTS, PIXELS, CHANNELS),
        g_red,
        g_off.T,
        g_def,
        g_exp,
        g_nar,
        g_con,
        g_wid,
        *others,
    )


def solution(mesh):
    spread = P(("dp", "outer"), None, None)
    in_specs = (spread, P(), P(("dp", "outer")), spread) + (P(),) * 11
    out_specs = (spread, spread) + (P("dp", None),) * 7 + (P(None, "dp"),) * 4
    return jax.shard_map(
        per_device, mesh=mesh, in_specs=in_specs, out_specs=out_specs, check_vma=False
    )
```

```python
import functools
import math
import types

import jax
import jax.numpy as jnp
from jax import lax
from jax.experimental import pallas as pl
from jax.experimental.pallas import tpu as pltpu
from jax.sharding import PartitionSpec as P

CHANNELS = 2048
INNER = 512
TAPS = 9
SLOTS = 2
SHORT = 4
LONG = 36
PIXELS = 144
ROWS = SLOTS * PIXELS
OFFSETS = 2 * TAPS
EPS = 1e-05
BF = jnp.bfloat16
F32 = jnp.float32
MESH = pl.DeviceIdType.MESH
NN = (((1,), (0,)), ((), ()))
NT = (((1,), (1,)), ((), ()))
TN = (((0,), (0,)), ((), ()))


def mm(left, right, dims):
    return lax.dot_general(left, right, dims, preferred_element_type=F32)


def sigmoid(value):
    return 0.5 * jnp.tanh(0.5 * value) + 0.5


def fold(value):
    return jnp.sum(value.reshape(value.shape[0] // 8, 8, value.shape[1]), axis=0)


def total_row(value):
    return jnp.sum(value, axis=0, keepdims=True)


def layout(dp):
    chips = dp // 2
    bits = chips.bit_length() - 1
    wide = CHANNELS // dp
    deep = TAPS * INNER // dp
    taps = max(
        -(-(2 * deep * chip % INNER + 2 * deep) // INNER) for chip in range(chips)
    )
    return chips, bits, wide, deep, taps


def scratch(dp, outer):
    vmem = pltpu.VMEM
    dma = pltpu.SemaphoreType.DMA
    chips, bits, wide, deep, taps = layout(dp)
    everyone = dp * outer
    group = min(chips, 4)
    return dict(
        images=vmem((ROWS, CHANNELS), BF),
        between=vmem((ROWS, CHANNELS), BF),
        dwide=vmem((ROWS, CHANNELS), BF),
        obuf=vmem((ROWS, CHANNELS), BF),
        redwid=vmem((CHANNELS, INNER), BF),
        exp=vmem((CHANNELS, INNER), BF),
        nar=vmem((CHANNELS, INNER), BF),
        dfmcon=vmem((TAPS * INNER, INNER), BF),
        off=vmem((OFFSETS, TAPS * INNER), BF),
        a1=vmem((ROWS, INNER), F32),
        a2=vmem((ROWS, INNER), F32),
        b1=vmem((ROWS, INNER), F32),
        b2=vmem((ROWS, INNER), F32),
        acc=vmem((ROWS, INNER), F32),
        a3=vmem((CHANNELS // 512, ROWS, 512), F32),
        b3=vmem((CHANNELS // 512, ROWS, 512), F32),
        up=vmem((CHANNELS // 512, ROWS, 512), F32),
        inner=vmem((ROWS, INNER), BF),
        hidden=vmem((ROWS, INNER), BF),
        narrow=vmem((ROWS, INNER), BF),
        mixed=vmem((ROWS, INNER), BF),
        dn=vmem((ROWS, INNER), BF),
        turned=vmem((ROWS, INNER), BF),
        wmat=vmem((SLOTS, TAPS, PIXELS, PIXELS), BF),
        tmat=vmem((2, TAPS, PIXELS, PIXELS), BF),
        geo=vmem((2, 2, PIXELS, PIXELS), jnp.int32),
        frac=vmem((ROWS, OFFSETS), F32),
        doff=vmem((ROWS, OFFSETS), F32),
        stn=vmem((4, 2, INNER), F32),
        stw=vmem((2, 2, CHANNELS), F32),
        rxn=vmem((8, everyone, 2, INNER), F32),
        rxw1=vmem((4, dp, 2, CHANNELS), F32),
        rxw2=vmem((4, outer, 2, CHANNELS), F32),
        pool=vmem((3, chips, wide, INNER), F32),
        corel=vmem((chips, wide, INNER), F32),
        land=vmem((2, 2, chips - 1, wide, INNER // 2), F32),
        zwide=vmem((3, 3, wide, INNER), F32),
        tiny=vmem((2, chips, SLOTS, 24, PIXELS), F32),
        give=vmem((ROWS, INNER), F32),
        taken=vmem((group, ROWS, INNER), F32),
        drawn=vmem((ROWS, INNER), F32),
        yall=vmem((group * ROWS, INNER), BF),
        xall=vmem((2, group * ROWS, INNER), BF),
        grad=vmem((taps * INNER, INNER), F32),
        cored=vmem((deep, INNER), F32),
        zdeep=vmem((2, 2, deep // 2, INNER), F32),
        goff=vmem((24, taps * INNER), F32),
        coreo=vmem((24, taps * INNER), F32),
        zoff=vmem((2, 24, taps * INNER), F32),
        free=pltpu.SemaphoreType.REGULAR,
        credit=pltpu.SemaphoreType.REGULAR((2, bits)),
        swapped=pltpu.SemaphoreType.REGULAR,
        load_sem=dma((11,)),
        out_sem=dma((2,)),
        res_sem=dma((7, 4)),
        xn_s=dma((8,)),
        xn_r=dma((8,)),
        xw_s=dma((4, 2)),
        xw_r=dma((4, 2)),
        core_s=dma((7,)),
        core_r=dma((7,)),
        step_s=dma((4, 2, bits)),
        step_r=dma((4, 2, bits)),
        give_sem=dma((4,)),
        take_sem=dma((3,)),
        x_sem=dma((2,)),
        ag_s=dma((4, 2, bits)),
        ag_r=dma((4, 2, bits)),
        tiny_s=dma((2,)),
        tiny_r=dma((2,)),
        z_s=dma((7, 4, 3)),
        z_r=dma((7, 4, 3)),
    )


def kernel(dp, outer, names, *refs):
    assert outer == 4
    r = types.SimpleNamespace(**dict(zip(names, refs)))
    chips, bits, wide, deep, taps = layout(dp)
    everyone = dp * outer
    me = lax.axis_index("dp")
    mine = lax.axis_index("outer")
    own = me * outer + mine
    core = lax.rem(me, 2)
    chip = lax.div(me, 2)
    sibling = (me + 1 - 2 * core, mine)
    inside = (mine == 1) | (mine == 2)
    outside = (mine == 0) | (mine == 3)
    counts, orient = r.counts, r.orient
    dma = pltpu.make_async_copy

    loads = types.SimpleNamespace()

    def load(place, source, target):
        copy = dma(source, target, r.load_sem.at[place])
        copy.start()
        return copy

    loads.images_h = load(0, r.images_h, r.images)
    loads.red_h = load(1, r.red_h, r.redwid)
    loads.off_h = load(2, r.off_h, r.off)
    loads.def_h = load(3, r.def_h, r.dfmcon)
    loads.exp_h = load(4, r.exp_h, r.exp)
    loads.nar_h = load(5, r.nar_h, r.nar)
    loads.cot_h = load(6, r.cot_h, r.dwide)

    def other(step):
        target = lax.rem(own + step, everyone)
        return lax.div(target, outer), lax.rem(target, outer)

    barrier = pltpu.get_barrier_semaphore()

    def greet(step, carry):
        pl.semaphore_signal(barrier, inc=1, device_id=other(step), device_id_type=MESH)
        return carry

    lax.fori_loop(1, everyone, greet, 0)

    def size(i, carry):
        sizes, near, far = carry
        row, place = lax.div(i, outer), lax.rem(i, outer)
        held = counts[i].astype(F32)
        here = jnp.where(place == mine, held, 0.0)

        def mark(count, at, value):
            line = lax.broadcasted_iota(jnp.int32, (count, 1), 0)
            return jnp.where(line == at, value, 0.0)

        return (
            sizes + mark(everyone, i, held),
            near + mark(dp, row, here),
            far + mark(outer, place, held),
        )

    zeros = tuple(jnp.zeros((count, 1), F32) for count in (everyone, dp, outer))
    sizes, near, far = (
        value * float(PIXELS) for value in lax.fori_loop(0, everyone, size, zeros)
    )
    near_total = total_row(near)
    total = total_row(far)
    held = counts[own].astype(F32)
    live1 = held - 1.0
    local = held * float(PIXELS)

    def sweep(body, init):
        def step(i, carry):
            lv = jnp.where(i < 3, 1.0, live1)
            for j in range(3):
                carry = body(pl.ds(pl.multiple_of(i * 48 + j * 16, 16), 16), lv, carry)
            return carry

        return lax.fori_loop(0, 6, step, init, unroll=2)

    def send(source, target, sent, received, device):
        pltpu.make_async_remote_copy(
            src_ref=source,
            dst_ref=target,
            send_sem=sent,
            recv_sem=received,
            device_id=device,
            device_id_type=MESH,
        ).start()

    def settle(view, sem):
        dma(view, view, sem).wait()

    waiting = {}

    def later(tag, view, sem, when=None):
        waiting.setdefault(tag, []).append((when, view, sem))

    def flush(tag):
        for when, view, sem in waiting.pop(tag, []):
            if when is None:
                settle(view, sem)
            else:
                pl.when(when)(functools.partial(settle, view, sem))

    def accumulate(target, source):
        rows = target.shape[0]
        step = math.gcd(rows, 32)

        def body(i, carry):
            rs = pl.ds(pl.multiple_of(i * step, 8), step)
            target[rs, :] += source[rs, :]
            return carry

        lax.fori_loop(0, rows // step, body, 0)

    def mix(target, one, two):
        rows = target.shape[0]
        step = math.gcd(rows, 32)

        def body(i, carry):
            rs = pl.ds(pl.multiple_of(i * step, 8), step)
            target[rs, :] = one[rs, :] + two[rs, :]
            return carry

        lax.fori_loop(0, rows // step, body, 0)

    def flip(value, bit):
        weight = 1 << bit
        return value + weight - 2 * weight * lax.rem(lax.div(value, weight), 2)

    def bit_of(value, bit):
        return lax.rem(lax.div(value, 1 << bit), 2)

    orders = [
        list(range(bits)),
        list(range(bits // 2, bits)) + list(range(bits // 2)),
    ]
    halves = [pl.ds(0, INNER // 2), pl.ds(INNER // 2, INNER // 2)]

    def merge(rx, counted, size, forward):
        first = rx[:, 0, :]
        second = rx[:, 1, :]
        if forward:
            summed = total_row(first)
            apart = first / counted - summed / size
            spread = total_row(second + counted * apart * apart)
            return jnp.concatenate([summed, spread], axis=0)
        return jnp.concatenate([total_row(first), total_row(second)], axis=0)

    def nothing():
        pass

    def share_narrow(number, forward, work):
        rx = r.rxn.at[number]

        def step(i, carry):
            line, part = lax.div(i, dp), lax.rem(i, dp)
            z = jnp.where(mine < outer // 2, outer - 1 - line, line)
            peer = 0
            for bit in range(bits + 1):
                here, turn = bit_of(me, bit), 1 - bit_of(part, bit)
                peer = peer + (here + turn - 2 * here * turn) * (1 << bit)

            @pl.when(peer * outer + z != own)
            def _():
                send(rx.at[own], rx.at[own], r.xn_s.at[number], r.xn_r.at[number], (peer, z))

            return carry

        lax.fori_loop(0, everyone, step, 0)
        rest = rx.at[pl.ds(0, everyone - 1)]
        later("end", rest, r.xn_s.at[number])
        work()
        settle(rest, r.xn_r.at[number])
        return merge(rx, sizes, total, forward)

    def share_wide(number, forward, work, work_more):
        rx1, rx2 = r.rxw1.at[number], r.rxw2.at[number]
        for turn in range(dp - 1, 0, -1):
            peer = me
            for bit in range(bits + 1):
                if (turn >> bit) & 1:
                    peer = flip(peer, bit)
            send(rx1.at[me], rx1.at[me], r.xw_s.at[number, 0], r.xw_r.at[number, 0], (peer, mine))
        rest = rx1.at[pl.ds(0, dp - 1)]
        later("end", rest, r.xw_s.at[number, 0])
        work()
        settle(rest, r.xw_r.at[number, 0])
        rx2[mine] = merge(rx1, near, near_total, forward)
        for line in range(outer):
            z = jnp.where(mine < outer // 2, outer - 1 - line, line)

            @pl.when(z != mine)
            def _():
                send(
                    rx2.at[mine],
                    rx2.at[mine],
                    r.xw_s.at[number, 1],
                    r.xw_r.at[number, 1],
                    (me, z),
                )

        rest = rx2.at[pl.ds(0, outer - 1)]
        later("end", rest, r.xw_s.at[number, 1])
        work_more()
        settle(rest, r.xw_r.at[number, 1])
        return merge(rx2, far, total, forward)

    def local_stats(ref, put, cs):
        zero = jnp.zeros((8, 512), F32)
        summed = total_row(sweep(lambda rs, lv, c: c + lv * fold(ref[rs, :]), zero))
        mean = summed / local

        def squares(rs, lv, carry):
            apart = ref[rs, :] - mean
            return carry + lv * fold(apart * apart)

        put[0:1, cs] = summed
        put[1:2, cs] = total_row(sweep(squares, zero))

    def keep_stats(both, st):
        st[0:1, :] = both[0:1] / total
        st[1:2, :] = lax.rsqrt(both[1:2] / total + EPS)

    def narrow_stats(ref, number, work=nothing):
        local_stats(ref, r.rxn.at[number, own], pl.ds(0, INNER))
        keep_stats(share_narrow(number, True, work), r.stn.at[number])

    blocks = [pl.ds(start, 512) for start in range(0, CHANNELS, 512)]

    def wide_stats(ref, number, work=nothing, work_more=nothing):
        for n, cs in enumerate(blocks):
            local_stats(ref.at[n], r.rxw1.at[number, me], cs)
        keep_stats(share_wide(number, True, work, work_more), r.stw.at[number])

    def norm_silu(ref, number, gain, bias, out, spread):
        st = r.stn.at[number]
        mean, scale = st[0:1, :], st[1:2, :]
        steep = scale * gain

        def body(rs, lv, carry):
            z = (ref[rs, :] - mean) * steep + bias
            value = (z * sigmoid(z)).astype(BF)
            out[rs, :] = value
            if spread:
                r.give[rs, :] = value.astype(F32)
            return carry

        sweep(body, 0)

    def narrow_cotangent(ref, place, gain, bias, number, spread, work=nothing):
        acc = r.acc
        st = r.stn.at[place]
        mean, scale = st[0:1, :], st[1:2, :]

        def body(rs, lv, carry):
            xhat = (ref[rs, :] - mean) * scale
            z = xhat * gain + bias
            sg = sigmoid(z)
            g = acc[rs, :] * (sg * (1.0 + z * (1.0 - sg)))
            acc[rs, :] = g
            return carry[0] + fold(g), carry[1] + fold(g * xhat)

        zero = jnp.zeros((8, INNER), F32)
        summed, paired = sweep(body, (zero, zero))
        put = r.rxn.at[number, own]
        put[0:1, :] = total_row(summed)
        put[1:2, :] = total_row(paired)
        both = share_narrow(number, False, work)
        r.g_ib[place : place + 1, :] = both[0:1]
        r.g_ig[place : place + 1, :] = both[1:2]
        steep = scale * gain
        lift, tilt = both[0:1] / total, both[1:2] / total

        def back(rs, lv, carry):
            xhat = (ref[rs, :] - mean) * scale
            value = (steep * (acc[rs, :] - lv * (lift + xhat * tilt))).astype(BF)
            r.dn[rs, :] = value
            if spread:
                r.give[rs, :] = value.astype(F32)
            return carry

        sweep(back, 0)

    def wide_cotangent(number, ref, place, gain, bias, cotangent, work=nothing, work_more=nothing):
        put = r.rxw1.at[number, me]
        st = r.stw.at[place]
        for n, cs in enumerate(blocks):
            mean, scale = st[0:1, cs], st[1:2, cs]
            gn, bs = gain[:, 512 * n : 512 * n + 512], bias[:, 512 * n : 512 * n + 512]

            def body(rs, lv, carry):
                xhat = (ref[n, rs, :] - mean) * scale
                g = cotangent(n, rs, cs, lv, xhat * gn + bs)
                r.up[n, rs, :] = g
                return carry[0] + fold(g), carry[1] + fold(g * xhat)

            zero = jnp.zeros((8, 512), F32)
            summed, paired = sweep(body, (zero, zero))
            put[0:1, cs] = total_row(summed)
            put[1:2, cs] = total_row(paired)
        both = share_wide(number, False, work, work_more)
        r.g_bb[place : place + 1, :] = both[0:1]
        r.g_bg[place : place + 1, :] = both[1:2]
        for n, cs in enumerate(blocks):
            mean, scale = st[0:1, cs], st[1:2, cs]
            span = slice(512 * n, 512 * n + 512)
            steep = scale * gain[:, span]
            lift, tilt = both[0:1, span] / total, both[1:2, span] / total

            def back(rs, lv, carry):
                xhat = (ref[n, rs, :] - mean) * scale
                value = steep * (r.up[n, rs, :] - lv * (lift + xhat * tilt))
                r.dwide[rs, cs] = value.astype(BF)
                return carry

            sweep(back, 0)

    def tap(ref, k):
        return ref[pl.ds(pl.multiple_of(k * INNER, INNER), INNER), :]

    def offset_tap(k):
        return r.off[:, pl.ds(pl.multiple_of(k * INNER, INNER), INNER)]

    def slot_rows(s):
        return pl.ds(s * PIXELS, PIXELS)

    def steps_of(k):
        return 2 * lax.div(k, 3) - 2, 2 * lax.rem(k, 3) - 2

    WID, CON, NAR, EXP, DEF, RED, OFF = range(7)
    nth = {WID: 0, NAR: 1, EXP: 2, RED: 3}
    result = {
        WID: r.g_wid,
        CON: r.g_con,
        NAR: r.g_nar,
        EXP: r.g_exp,
        DEF: r.g_def,
        RED: r.g_red,
        OFF: r.g_off,
    }
    pool, land, grad, far_blocks = r.pool, r.land, r.grad, r.far_blocks

    deep_parts = 4 if deep % 32 == 0 else 2
    wide_parts = {WID: 2, NAR: 2, EXP: 2, RED: 4}

    def z_hold(u):
        if u == RED:
            return [r.a3.at[i, pl.ds(0, wide)] for i in range(3)]
        return [r.zwide.at[nth[u], i] for i in range(3)]

    def z_parts(u):
        if u in nth:
            hold = z_hold(u)
            for q in range(wide_parts[u]):
                rows = wide // (wide_parts[u] // 2)
                rs, hs = pl.ds(q // 2 * rows, rows), halves[q % 2]
                yield tuple(ref.at[rs, hs] for ref in hold) + (result[u].at[rs, hs],)
        elif u == OFF:
            yield r.goff, r.zoff.at[0], r.zoff.at[1], result[u]
        else:
            for q in range(deep_parts):
                back, at = divmod(q, deep_parts // 2)
                source = r.b3.at[(2 if u == DEF else 0) + back]
                if u == DEF:
                    first, second = (r.b1, r.a2) if back == 0 else (r.b2, r.a3.at[3])
                else:
                    first, second = r.zdeep.at[0, back], r.zdeep.at[1, back]
                size = deep // deep_parts
                rows = pl.ds(at * size, size)
                out = result[u].at[pl.ds(q * size, size)]
                yield source.at[rows], first.at[rows], second.at[rows], out

    def z_sems(u, q, step):
        return r.z_s.at[u, q, step], r.z_r.at[u, q, step]

    def z1(u, some=None):
        for q, (source, first, second, out) in enumerate(z_parts(u)):
            if some is not None and q not in some:
                continue
            sent, received = z_sems(u, q, 0)

            @pl.when(outside)
            def _():
                send(source, first, sent, received, (me, flip(mine, 0)))

            later(("z", u), source, sent, outside)

    def z2(u, some=None):
        for q, (source, first, second, out) in enumerate(z_parts(u)):
            if some is not None and q not in some:
                continue
            sent, received = z_sems(u, q, 1)

            @pl.when(inside)
            def _():
                settle(first, z_sems(u, q, 0)[1])
                accumulate(source, first)
                send(source, second, sent, received, (me, 3 - mine))

            later(("z", u), source, sent, inside)

    def z3(u, some=None):
        for q, (source, first, second, out) in enumerate(z_parts(u)):
            if some is not None and q not in some:
                continue
            sent, received = z_sems(u, q, 2)

            @pl.when(inside)
            def _():
                settle(second, z_sems(u, q, 1)[1])
                accumulate(second, source)
                send(second, first, sent, received, (me, flip(mine, 0)))
                dma(second, out, r.res_sem.at[u, q]).start()

            later(("zl", u), second, sent, inside)

    def z4(u, some=None):
        for q, (source, first, second, out) in enumerate(z_parts(u)):
            if some is not None and q not in some:
                continue

            @pl.when(outside)
            def _():
                settle(first, z_sems(u, q, 2)[1])
                dma(first, out, r.res_sem.at[u, q]).start()

    def z_clear(u):
        flush(("z", u))
        flush(("zl", u))
        for q, (source, first, second, out) in enumerate(z_parts(u)):
            dma(first, out, r.res_sem.at[u, q]).wait()

    def wide_begin(u, left, right):
        p = nth[u] % 2
        flush("sib")
        flush(("keep", p))
        low = p + (2 - p) * core
        high = p + (2 - p) * (1 - core)
        if u == EXP:
            pl.semaphore_wait(r.swapped, 1)

        def step(m, carry):
            block = left[:, pl.ds(pl.multiple_of(m * (2 * wide), 2 * wide), 2 * wide)]
            pool[low, m] = mm(block[:, :wide], right[...], TN)
            pool[high, m] = mm(block[:, wide:], right[...], TN)
            send(
                pool.at[2, m], r.corel.at[m], r.core_s.at[u], r.core_r.at[u], sibling
            )
            return carry

        lax.fori_loop(0, chips, step, 0)
        later("sib", r.corel, r.core_s.at[u])

    def piece(h, t, j, toward):
        value = 0
        for i, bit in enumerate(orders[h]):
            if i < t:
                part = bit_of(chip, bit)
            elif i == t:
                part = bit_of(toward, bit)
            else:
                part = (j >> (i - t - 1)) & 1
            value = value + part * (1 << bit)
        return value

    def step_place(u, h, t):
        first, count = chips - (chips >> t), chips >> (t + 1)
        p = nth[u] % 2
        sems = r.step_s.at[nth[u], h, t], r.step_r.at[nth[u], h, t]
        return p, first, count, sems, land.at[p, h, pl.ds(first, count)]

    def wide_send(u, t):
        for h in range(2):
            p, first, count, (sent, received), region = step_place(u, h, t)
            toward = flip(chip, orders[h][t])
            if u == RED:
                pl.semaphore_wait(r.credit.at[h, t], 1)
            for j in range(count):
                send(
                    pool.at[p, piece(h, t, j, toward), :, halves[h]],
                    land.at[p, h, first + j],
                    sent,
                    received,
                    (2 * toward + core, mine),
                )
            later(("keep", p), region, sent)

    def wide_add(u, t):
        for h in range(2):
            p, first, count, (sent, received), region = step_place(u, h, t)
            settle(region, received)
            if t == bits - 1:
                mix(z_hold(u)[0].at[:, halves[h]], pool.at[p, chip, :, halves[h]], land.at[p, h, first])
            else:
                for j in range(count):
                    accumulate(
                        pool.at[p, piece(h, t, j, chip), :, halves[h]], land.at[p, h, first + j]
                    )
            if u == NAR:
                pl.semaphore_signal(
                    r.credit.at[h, t],
                    inc=1,
                    device_id=(2 * flip(chip, orders[h][t]) + core, mine),
                    device_id_type=MESH,
                )

    def wide_core(u):
        p = nth[u] % 2
        settle(r.corel, r.core_r.at[u])

        def step(m, carry):
            accumulate(pool.at[p, m], r.corel.at[m])
            return carry

        lax.fori_loop(0, chips, step, 0)
        if u == NAR:
            pl.semaphore_signal(r.swapped, inc=1, device_id=sibling, device_id_type=MESH)

    def wide_step(u, t):
        wide_add(u, t - 1)
        if t < bits:
            wide_send(u, t)
        else:
            z1(u)

    def held_at(h, j):
        value = chip
        for i in range(bits):
            if (j >> i) & 1:
                value = flip(value, orders[h][i])
        return value

    def gather_send(a, t, some=None):
        for h in range(2):
            partner = flip(chip, orders[h][t])
            sent, received = r.ag_s.at[a, h, t], r.ag_r.at[a, h, t]
            for j in range(1 << t) if some is None else some:
                block = far_blocks.at[a, held_at(h, j), :, halves[h]]
                source = r.give.at[:, halves[h]] if j == 0 else block
                send(source, block, sent, received, (2 * partner + core, mine))
            if some is None or 0 in some:
                later(("ag", a), far_blocks.at[a, pl.ds(0, 1 << t), :, halves[h]], sent)

    def gather_start(a):
        block = far_blocks.at[a, chip]
        dma(r.give, block, r.give_sem.at[a]).start()
        later(("ag", a), block, r.give_sem.at[a])
        gather_send(a, 0)

    def gather_wait(a, t):
        for h in range(2):
            settle(far_blocks.at[a, pl.ds(0, 1 << t), :, halves[h]], r.ag_r.at[a, h, t])

    def gather_step(a, t, some=None):
        gather_wait(a, t - 1)
        gather_send(a, t, some)

    def gather_first(a, t):
        if t < bits:
            gather_send(a, t, [0])

    def gather_rest(a):
        for t in range(1, bits):
            gather_wait(a, t - 1)
            gather_send(a, t, range(1 if t == 1 else 0, 1 << t))

    def gather_end(a):
        gather_wait(a, bits - 1)
        flush(("ag", a))

    def tiny_send(a):
        for step in range(1, chips):
            block = r.tiny.at[a, chip]
            peer = lax.rem(chip + step, chips)
            send(block, block, r.tiny_s.at[a], r.tiny_r.at[a], (2 * peer + core, mine))
        later("end", r.tiny.at[a, pl.ds(0, chips - 1)], r.tiny_s.at[a])

    def tiny_wait(a):
        settle(r.tiny.at[a, pl.ds(0, chips - 1)], r.tiny_r.at[a])

    group = min(chips, 4)
    first_tap = lax.div(2 * deep * chip, INNER)
    margin = 2 * deep * chip - first_tap * INNER

    def taps_of(kk):
        k = jnp.minimum(first_tap + kk, TAPS - 1)
        return (k, *steps_of(k))

    def fetch_fields(a, g):
        copy = dma(far_blocks.at[a, pl.ds(g * group, group)], r.taken, r.take_sem.at[2])
        copy.start()
        copy.wait()

    def image_of(i, g):
        m, s = lax.div(i, SLOTS), lax.rem(i, SLOTS)
        rows = pl.ds(pl.multiple_of(i * PIXELS, PIXELS), PIXELS)
        field = r.taken[m, pl.ds(pl.multiple_of(s * PIXELS, PIXELS), PIXELS), :].astype(BF)
        flat = r.tiny[0, g * group + m, s, 18:19, :] == 0.0
        dr = jnp.where(flat, r.geo[0, 0], r.geo[1, 0])
        dc = jnp.where(flat, r.geo[0, 1], r.geo[1, 1])
        return g * group + m, s, rows, field, dr, dc

    def group_rows(g):
        return pl.ds(g * (group * ROWS), group * ROWS)

    def columns(u, kk):
        x = 1 if u == DEF else 0
        k, down, across = taps_of(kk)
        for g in range(chips // group):
            if kk == 0 or chips > group:
                fetch_fields(0 if u == DEF else 1, g)
            if g == 0:
                flush("columns")

            def image(i, carry):
                m, s, rows, field, dr, dc = image_of(i, g)
                if u == CON:
                    hit = jnp.where((dr == down) & (dc == across), 1.0, 0.0).astype(BF)
                    r.xall[0, rows, :] = mm(hit, field, NN).astype(BF)
                    return carry
                tiny = r.tiny.at[0, m, s]
                fy, fx = tiny[pl.ds(2 * k, 1), :], tiny[pl.ds(2 * k + 1, 1), :]
                ay = jnp.where(dr == -down, 1.0 - fy, jnp.where(dr == -down - 1, fy, 0.0))
                ax = jnp.where(dc == -across, 1.0 - fx, jnp.where(dc == -across - 1, fx, 0.0))
                r.xall[0, rows, :] = mm((ay * ax).astype(BF), field, TN).astype(BF)
                return carry

            lax.fori_loop(0, group * SLOTS, image, 0, unroll=4)
            place = r.far_columns.at[x, kk, group_rows(g)]
            copy = dma(r.xall.at[0], place, r.x_sem.at[0])
            copy.start()
            if g + 1 < chips // group:
                copy.wait()
            else:
                later("columns", place, r.x_sem.at[0])

    def deep_make(u):
        flush("deep")
        flush("columns")
        x, back_of = (1, 3) if u == DEF else (0, 2)
        slots = (r.give, r.drawn)
        for g in range(chips // group):

            def fetch(m):
                return dma(far_blocks.at[back_of, g * group + m], slots[m % 2], r.take_sem.at[m % 2])

            def draw(kk):
                slot = lax.rem(kk, 2)
                return dma(
                    r.far_columns.at[x, kk, group_rows(g)], r.xall.at[slot], r.x_sem.at[slot]
                )

            for m in range(min(2, group)):
                fetch(m).start()
            draw(0).start()
            for m in range(group):
                fetch(m).wait()

                def lower(i, carry):
                    rows = pl.ds(pl.multiple_of(m * ROWS + i * 32, 32), 32)
                    there = pl.ds(pl.multiple_of(i * 32, 32), 32)
                    r.yall[rows, :] = slots[m % 2][there, :].astype(BF)
                    return carry

                lax.fori_loop(0, ROWS // 32, lower, 0)
                if m + 2 < group:
                    fetch(m + 2).start()

            def one(kk, carry):
                @pl.when(kk + 1 < taps)
                def _():
                    draw(kk + 1).start()

                draw(kk).wait()
                at = pl.ds(pl.multiple_of(kk * INNER, INNER), INNER)
                part = mm(r.xall[lax.rem(kk, 2)], r.yall[...], TN)
                if g == 0:
                    grad[at, :] = part
                else:
                    grad[at, :] += part
                return carry

            lax.fori_loop(0, taps, one, 0)
        away = pl.ds(pl.multiple_of(margin + (1 - core) * deep, 8), deep)
        send(grad.at[away], r.cored, r.core_s.at[u], r.core_r.at[u], sibling)
        later("deep", r.cored, r.core_s.at[u])

    def off_make():
        for g in range(chips // group):
            fetch_fields(0, g)

            def one(kk, carry):
                k, down, across = taps_of(kk)

                def image(i, share):
                    m, s, rows, field, dr, dc = image_of(i, g)
                    hit = jnp.where((dr == down) & (dc == across), 1.0, 0.0).astype(BF)
                    moved = mm(r.tiny[1, m, s].astype(BF), hit, NN).astype(BF)
                    return share + mm(moved, field, NN)

                at = pl.ds(pl.multiple_of(kk * INNER, INNER), INNER)
                share = lax.fori_loop(
                    0, group * SLOTS, image, jnp.zeros((24, INNER), F32), unroll=8
                )
                if g == 0:
                    r.goff[:, at] = share
                else:
                    r.goff[:, at] += share
                return carry

            lax.fori_loop(0, taps, one, 0)
        send(r.goff, r.coreo, r.core_s.at[OFF], r.core_r.at[OFF], sibling)

    def off_core():
        settle(r.goff, r.core_s.at[OFF])
        settle(r.coreo, r.core_r.at[OFF])
        accumulate(r.goff, r.coreo)

    def deep_core(u):
        settle(r.cored, r.core_r.at[u])
        half = deep // 2
        step = math.gcd(half, 32)
        for q in range(2):
            target = r.b3.at[(2 if u == DEF else 0) + q]

            def body(i, carry):
                at = pl.multiple_of(i * step, 8)
                here = grad[pl.ds(pl.multiple_of(margin + core * deep + q * half + at, 8), step), :]
                target[pl.ds(at, step), :] = here + r.cored[pl.ds(q * half + at, step), :]
                return carry

            lax.fori_loop(0, half // step, body, 0)
    images, between, acc, up = r.images, r.between, r.acc, r.up
    ig = [r.ig[i : i + 1, :] for i in range(4)]
    ib = [r.ib[i : i + 1, :] for i in range(4)]
    bg = [r.bg[i : i + 1, :] for i in range(2)]
    bb = [r.bb[i : i + 1, :] for i in range(2)]

    def geometry():
        q = lax.broadcasted_iota(jnp.int32, (PIXELS, PIXELS), 1)
        p = lax.broadcasted_iota(jnp.int32, (PIXELS, PIXELS), 0)

        def place_of(at, kind):
            if kind:
                row = lax.shift_right_logical(at, 2)
                return row, at - row * SHORT
            row = (at >= LONG).astype(jnp.int32) + (at >= 2 * LONG).astype(jnp.int32)
            row = row + (at >= 3 * LONG).astype(jnp.int32)
            return row, at - row * LONG

        for kind in range(2):
            row_q, col_q = place_of(q, kind)
            row_p, col_p = place_of(p, kind)
            r.geo[kind, 0] = row_q - row_p
            r.geo[kind, 1] = col_q - col_p

            def hot(k, carry):
                down, across = steps_of(k)
                hit = (r.geo[kind, 0] == down) & (r.geo[kind, 1] == across)
                r.tmat[kind, k] = jnp.where(hit, 1.0, 0.0).astype(BF)
                return carry

            lax.fori_loop(0, TAPS, hot, 0)

    def shifted(s, k):
        return r.tmat[orient[s], k]

    loads.images_h.wait()
    loads.red_h.wait()
    r.a1[...] = mm(images[...], r.redwid[...], NN)
    loads.wid_h = load(7, r.wid_h, r.redwid)
    pl.semaphore_wait(barrier, everyone - 1)
    narrow_stats(r.a1, 0, geometry)
    norm_silu(r.a1, 0, ig[0], ib[0], r.inner, True)
    gather_start(0)

    loads.off_h.wait()
    inner = r.inner
    lane = lax.broadcasted_iota(jnp.int32, (PIXELS, OFFSETS), 1)

    def gather(k, carry):
        cols = [mm(shifted(s, k), inner[slot_rows(s), :], NN).astype(BF) for s in range(SLOTS)]
        weight = offset_tap(k)
        return tuple(old + mm(col, weight, NT) for old, col in zip(carry, cols))

    zero = jnp.zeros((PIXELS, OFFSETS), F32)
    both_offsets = lax.fori_loop(0, TAPS, gather, (zero,) * SLOTS, unroll=3)
    for s in range(SLOTS):
        frac = sigmoid(both_offsets[s])
        r.frac[slot_rows(s), :] = frac
        coarse = frac.astype(BF)
        fine = (frac - coarse.astype(F32)).astype(BF)
        unit = r.tmat[0, TAPS // 2]
        put = r.tiny.at[0, chip, s]
        put[...] = jnp.zeros((24, PIXELS), F32) + orient[s].astype(F32)
        put[0:OFFSETS, :] = mm(coarse, unit, TN) + mm(fine, unit, TN)
    tiny_send(0)

    def bilinear(s, k):
        down, across = steps_of(k)
        frac = r.frac[slot_rows(s), :]
        fy = jnp.sum(jnp.where(lane == 2 * k, frac, 0.0), axis=1, keepdims=True)
        fx = jnp.sum(jnp.where(lane == 2 * k + 1, frac, 0.0), axis=1, keepdims=True)
        dr, dc = r.geo[orient[s], 0], r.geo[orient[s], 1]
        in_y = (dr == down, dr == down + 1)
        in_x = (dc == across, dc == across + 1)
        ay = jnp.where(in_y[0], 1.0 - fy, jnp.where(in_y[1], fy, 0.0))
        ax = jnp.where(in_x[0], 1.0 - fx, jnp.where(in_x[1], fx, 0.0))
        return fy, fx, ay, ax, in_y, in_x

    loads.def_h.wait()
    acc[...] = jnp.zeros((ROWS, INNER), F32)

    def sample(k, carry):
        for s in range(SLOTS):
            _, _, ay, ax, _, _ = bilinear(s, k)
            weight = (ay * ax).astype(BF)
            r.wmat[s, k] = weight
            r.turned[slot_rows(s), :] = mm(weight, inner[slot_rows(s), :], NN).astype(BF)
        acc[...] += mm(r.turned[...], tap(r.dfmcon, k), NN)
        return carry

    lax.fori_loop(0, TAPS, sample, 0, unroll=3)
    loads.con_h = load(8, r.con_h, r.dfmcon)
    r.a2[...] = acc[...]
    narrow_stats(r.a2, 1, lambda: gather_first(0, 1))
    norm_silu(r.a2, 1, ig[1], ib[1], r.hidden, False)

    def widen(source, weight, target):
        def step(n, carry):
            rows = pl.ds(pl.multiple_of(n * 512, 512), 512)
            target[n] = mm(source[...], weight[rows, :], NT)
            return carry

        lax.fori_loop(0, CHANNELS // 512, step, 0, unroll=2)

    loads.exp_h.wait()
    widen(r.hidden, r.exp, r.a3)
    wide_stats(r.a3, 0, lambda: gather_rest(0))
    for n, cs in enumerate(blocks):
        mean = r.stw[0, 0:1, cs]
        steep = r.stw[0, 1:2, cs] * bg[0][:, 512 * n : 512 * n + 512]
        bias = bb[0][:, 512 * n : 512 * n + 512]

        def join(rs, lv, carry):
            z = (r.a3[n, rs, :] - mean) * steep + bias + images[rs, cs].astype(F32)
            between[rs, cs] = (z * sigmoid(z)).astype(BF)
            return carry

        sweep(join, 0)

    loads.nar_h.wait()
    r.b1[...] = mm(between[...], r.nar[...], NN)

    def work_b1():
        gather_end(0)
        tiny_wait(0)
        columns(DEF, 0)

    narrow_stats(r.b1, 2, work_b1)
    norm_silu(r.b1, 2, ig[2], ib[2], r.narrow, True)
    gather_start(1)

    loads.con_h.wait()
    acc[...] = jnp.zeros((ROWS, INNER), F32)

    def convolve(k, carry):
        for s in range(SLOTS):
            r.turned[slot_rows(s), :] = mm(
                shifted(s, k), r.narrow[slot_rows(s), :], NN
            ).astype(BF)
        acc[...] += mm(r.turned[...], tap(r.dfmcon, k), NN)
        return carry

    lax.fori_loop(0, TAPS, convolve, 0, unroll=3)
    r.b2[...] = acc[...]
    def work_b2():
        gather_first(1, 1)
        columns(DEF, 1)

    narrow_stats(r.b2, 3, work_b2)
    norm_silu(r.b2, 3, ig[3], ib[3], r.mixed, False)

    loads.wid_h.wait()
    widen(r.mixed, r.redwid, r.b3)

    def work_b3():
        gather_rest(1)
        for kk in range(2, taps):
            columns(DEF, kk)

    wide_stats(r.b3, 1, work_b3)

    loads.cot_h.wait()

    def last(n, rs, cs, lv, pre):
        z = pre + between[rs, cs].astype(F32)
        sg = sigmoid(z)
        r.obuf[rs, cs] = (lv * (z * sg)).astype(BF)
        return r.dwide[rs, cs].astype(F32) * (lv * (sg * (1.0 + z * (1.0 - sg))))

    def work_f():
        gather_end(1)
        columns(CON, 0)

    wide_cotangent(2, r.b3, 1, bg[1], bb[1], last, nothing, work_f)
    out_copy = dma(r.obuf, r.out_h, r.out_sem.at[0])
    out_copy.start()
    wide_begin(WID, r.dwide, r.mixed)
    acc[...] = mm(r.dwide[...], r.redwid[...], NN)
    loads.red_h = load(9, r.red_h, r.redwid)

    def work_e():
        wide_core(WID)
        wide_send(WID, 0)
        columns(CON, 1)

    narrow_cotangent(r.b2, 3, ig[3], ib[3], 4, True, work_e)

    acc[...] = jnp.zeros((ROWS, INNER), F32)

    def spread(k, carry):
        for s in range(SLOTS):
            r.turned[slot_rows(s), :] = mm(
                shifted(s, TAPS - 1 - k), r.dn[slot_rows(s), :], NN
            ).astype(BF)
        acc[...] += mm(r.turned[...], tap(r.dfmcon, k), NT)
        return carry

    lax.fori_loop(0, TAPS, spread, 0, unroll=3)
    loads.def_h = load(10, r.def_h, r.dfmcon)

    def work_d():
        wide_step(WID, 1)
        gather_start(2)
        for kk in range(2, taps):
            columns(CON, kk)

    narrow_cotangent(r.b1, 2, ig[2], ib[2], 5, False, work_d)
    for t in range(2, bits + 1):
        wide_step(WID, t)

    def add_back(n, carry):
        rows = pl.ds(pl.multiple_of(n * 512, 512), 512)
        up[n] += mm(r.dn[...], r.nar[rows, :], NT)
        return carry

    lax.fori_loop(0, CHANNELS // 512, add_back, 0, unroll=2)

    def first(n, rs, cs, lv, pre):
        z = pre + images[rs, cs].astype(F32)
        sg = sigmoid(z)
        return up[n, rs, :] * (sg * (1.0 + z * (1.0 - sg)))

    def work_c():
        for t in range(1, bits):
            gather_step(2, t)
        wide_begin(NAR, between, r.dn)

    def work_more_c():
        z2(WID)
        wide_core(NAR)

    wide_cotangent(3, r.a3, 0, bg[0], bb[0], first, work_c, work_more_c)
    acc[...] = mm(r.dwide[...], r.exp[...], NN)

    def work_b():
        wide_send(NAR, 0)
        z3(WID)
        wide_begin(EXP, r.dwide, r.hidden)
        gather_end(2)
        deep_make(CON)

    narrow_cotangent(r.a2, 1, ig[1], ib[1], 6, True, work_b)
    wide_step(NAR, 1)
    gather_start(3)
    deep_core(CON)
    early, late = range(deep_parts // 2), range(deep_parts // 2, deep_parts)
    z1(CON, early)

    loads.def_h.wait()
    acc[...] = jnp.zeros((ROWS, INNER), F32)
    r.doff[...] = jnp.zeros((ROWS, OFFSETS), F32)

    def unsample(k, carry):
        r.turned[...] = mm(r.dn[...], tap(r.dfmcon, k), NT).astype(BF)
        for s in range(SLOTS):
            rs = slot_rows(s)
            back = r.turned[rs, :]
            pairs = mm(back, inner[rs, :], NT)
            fy, fx, ay, ax, in_y, in_x = bilinear(s, k)
            slope_y = jnp.where(in_y[1], ax, 0.0) - jnp.where(in_y[0], ax, 0.0)
            slope_x = jnp.where(in_x[1], ay, 0.0) - jnp.where(in_x[0], ay, 0.0)
            to_y = jnp.sum(pairs * slope_y, axis=1, keepdims=True) * (fy * (1.0 - fy))
            to_x = jnp.sum(pairs * slope_x, axis=1, keepdims=True) * (fx * (1.0 - fx))
            r.doff[rs, :] += jnp.where(lane == 2 * k, to_y, 0.0) + jnp.where(
                lane == 2 * k + 1, to_x, 0.0
            )
            acc[rs, :] += mm(r.wmat[s, k], back, TN)
        return carry

    lax.fori_loop(0, TAPS, unsample, 0, unroll=3)
    z2(CON, [0])
    for s in range(SLOTS):
        put = r.tiny.at[1, chip, s]
        put[...] = jnp.zeros((24, PIXELS), F32)
        put[0:OFFSETS, :] = mm(
            r.doff[slot_rows(s), :].astype(BF), r.tmat[0, TAPS // 2], TN
        )
    tiny_send(1)

    def untap(k, carry):
        for s in range(SLOTS):
            rs = slot_rows(s)
            moved = mm(shifted(s, TAPS - 1 - k), r.doff[rs, :].astype(BF), NN).astype(BF)
            acc[rs, :] += mm(moved, offset_tap(k), NN)
        return carry

    lax.fori_loop(0, TAPS, untap, 0, unroll=3)

    wide_core(EXP)

    def work_a():
        for t in range(1, bits):
            gather_step(3, t)
        wide_send(EXP, 0)
        z1(CON, late)
        for t in range(2, bits + 1):
            wide_step(NAR, t)
        z2(CON, [1])
        z4(WID)

    narrow_cotangent(r.a1, 0, ig[0], ib[0], 7, False, work_a)
    z3(CON, [0])
    wide_begin(RED, images, r.dn)
    z2(CON, [2])
    out_copy.wait()
    loads.red_h.wait()

    def finish(n, carry):
        rows = pl.ds(pl.multiple_of(n * 512, 512), 512)
        r.obuf[:, rows] = (up[n] + mm(r.dn[...], r.redwid[rows, :], NT)).astype(BF)
        return carry

    lax.fori_loop(0, CHANNELS // 512, finish, 0, unroll=2)
    grad_copy = dma(r.obuf, r.grad_h, r.out_sem.at[1])
    grad_copy.start()
    z2(CON, [3])
    z3(CON, [1])
    gather_end(3)
    deep_make(DEF)
    z2(NAR, [0])
    z3(CON, [2])
    wide_core(RED)
    wide_send(RED, 0)
    deep_core(DEF)
    z1(DEF)
    z2(NAR, [1])
    z3(CON, [3])
    wide_step(EXP, 1)
    tiny_wait(1)
    off_make()
    z2(DEF, [0])
    z3(NAR, [0])
    off_core()
    z1(OFF)
    wide_step(RED, 1)
    z2(DEF, [1])
    z3(NAR, [1])
    for t in range(2, bits + 1):
        wide_step(EXP, t)
    z2(DEF, [2])
    z3(DEF, [0])
    for t in range(2, bits + 1):
        wide_step(RED, t)
    z2(DEF, [3])
    z3(DEF, [1])
    z2(OFF)
    z3(DEF, [2])
    z2(EXP, [0])
    z3(DEF, [3])
    z3(OFF)
    z2(EXP, [1])
    z2(RED, [0])
    z3(EXP, [0])
    z2(RED, [1])
    z2(RED, [2])
    z3(EXP, [1])
    z2(RED, [3])
    z3(RED, [0])
    z3(RED, [1])
    z3(RED, [2])
    z3(RED, [3])
    z4(CON)
    z4(NAR)
    z4(DEF)
    z4(OFF)
    z4(EXP)
    z4(RED)
    for u in range(7):
        z_clear(u)
    grad_copy.wait()
    for tag in list(waiting):
        flush(tag)


MOVED = ["out", "grad", "con", "def", "wid", "nar", "exp", "red"]


def deliver(dp, names, *refs):
    r = types.SimpleNamespace(**dict(zip(names, refs)))
    _, _, _, deep, _ = layout(dp)
    place = lax.axis_index("dp")
    moves = []
    for i, name in enumerate(MOVED):
        source, target, hold = (getattr(r, kind + name) for kind in ("from_", "to_", "hold_"))
        taken = pltpu.make_async_copy(source, hold, r.sems.at[0, i])
        taken.start()
        moves.append((taken, pltpu.make_async_copy(hold, target, r.sems.at[1, i])))

    for taken, given in moves:
        taken.wait()
        given.start()

    def span(ref, start, target):
        rows, lanes = ref.shape
        moved = pltpu.roll(ref[...], lax.rem(lanes - start, lanes), 1)
        target[...] = moved[: target.shape[0], : target.shape[1]]

    span(r.g_ig, place * (INNER // dp), r.to_ig)
    span(r.g_ib, place * (INNER // dp), r.to_ib)
    span(r.g_bg, place * (CHANNELS // dp), r.to_bg)
    span(r.g_bb, place * (CHANNELS // dp), r.to_bb)
    chip, core = lax.div(place, 2), lax.rem(place, 2)
    span(r.g_off, lax.rem(2 * deep * chip, INNER) + deep * core, r.to_off)
    for taken, given in moves:
        given.wait()


def per_device(
    images,
    counts,
    orientation,
    cotangent,
    reducer,
    offseter,
    deformer,
    expander,
    narrower,
    convolver,
    widener,
    inner_gains,
    inner_biases,
    broad_gains,
    broad_biases,
):
    dp, outer = lax.axis_size("dp"), lax.axis_size("outer")
    chips, bits, wide, deep, taps = layout(dp)
    buffers = scratch(dp, outer)
    smem = pl.BlockSpec(memory_space=pltpu.SMEM)
    vmem = pl.BlockSpec(memory_space=pltpu.VMEM)
    far = pl.BlockSpec(memory_space=pl.ANY)
    shape = jax.ShapeDtypeStruct
    inputs = dict(
        counts=(smem, counts),
        orient=(smem, orientation),
        ig=(vmem, inner_gains),
        ib=(vmem, inner_biases),
        bg=(vmem, broad_gains),
        bb=(vmem, broad_biases),
        images_h=(far, images.reshape(ROWS, CHANNELS)),
        cot_h=(far, cotangent.reshape(ROWS, CHANNELS)),
        red_h=(far, reducer),
        off_h=(far, offseter.T),
        def_h=(far, deformer),
        exp_h=(far, expander),
        nar_h=(far, narrower),
        con_h=(far, convolver),
        wid_h=(far, widener),
    )
    outputs = dict(
        out_h=(far, shape((ROWS, CHANNELS), BF)),
        grad_h=(far, shape((ROWS, CHANNELS), BF)),
        g_red=(far, shape((wide, INNER), F32)),
        g_off=(far, shape((24, taps * INNER), F32)),
        g_def=(far, shape((deep, INNER), F32)),
        g_exp=(far, shape((wide, INNER), F32)),
        g_nar=(far, shape((wide, INNER), F32)),
        g_con=(far, shape((deep, INNER), F32)),
        g_wid=(far, shape((wide, INNER), F32)),
        g_ig=(vmem, shape((4, INNER), F32)),
        g_ib=(vmem, shape((4, INNER), F32)),
        g_bg=(vmem, shape((2, CHANNELS), F32)),
        g_bb=(vmem, shape((2, CHANNELS), F32)),
        far_blocks=(far, shape((4, chips, ROWS, INNER), F32)),
        far_columns=(far, shape((2, taps, chips * ROWS, INNER), BF)),
    )
    names = list(inputs) + list(outputs) + list(buffers)
    outs = pl.pallas_call(
        functools.partial(kernel, dp, outer, names),
        out_shape=[spec for _, spec in outputs.values()],
        in_specs=[space for space, _ in inputs.values()],
        out_specs=[space for space, _ in outputs.values()],
        scratch_shapes=list(buffers.values()),
        compiler_params=pltpu.CompilerParams(
            collective_id=0, has_side_effects=True, vmem_limit_bytes=63 * 1024 * 1024
        ),
        name="chain",
    )(*[value for _, value in inputs.values()])
    held = dict(zip(outputs, outs))
    big = dict(
        out=held["out_h"],
        grad=held["grad_h"],
        red=held["g_red"],
        **{"def": held["g_def"]},
        exp=held["g_exp"],
        nar=held["g_nar"],
        con=held["g_con"],
        wid=held["g_wid"],
    )
    small = {name: held[name] for name in ("g_off", "g_ig", "g_ib", "g_bg", "g_bb")}
    firsts = {"from_" + name: value for name, value in big.items()}
    finals = {"to_" + name: shape(value.shape, value.dtype) for name, value in big.items()}
    holds = {"hold_" + name: pltpu.VMEM(value.shape, value.dtype) for name, value in big.items()}
    lasts = dict(
        to_off=shape((OFFSETS, deep), F32),
        to_ig=shape((4, INNER // dp), F32),
        to_ib=shape((4, INNER // dp), F32),
        to_bg=shape((2, CHANNELS // dp), F32),
        to_bb=shape((2, CHANNELS // dp), F32),
    )
    names = [*firsts, *small, *finals, *lasts, *holds, "sems"]
    got = pl.pallas_call(
        functools.partial(deliver, dp, names),
        out_shape=[*finals.values(), *lasts.values()],
        in_specs=[far] * len(firsts) + [vmem] * len(small),
        out_specs=[far] * len(finals) + [vmem] * len(lasts),
        scratch_shapes=[*holds.values(), pltpu.SemaphoreType.DMA((2, len(big)))],
        compiler_params=pltpu.CompilerParams(vmem_limit_bytes=60 * 1024 * 1024),
        name="deliver",
    )(*firsts.values(), *small.values())
    out, grad, g_red, g_def, g_exp, g_nar, g_con, g_wid, g_off, *others = got
    return (
        out.reshape(SLOTS, PIXELS, CHANNELS),
        grad.reshape(SLOTS, PIXELS, CHANNELS),
        g_red,
        g_off.T,
        g_def,
        g_exp,
        g_nar,
        g_con,
        g_wid,
        *others,
    )


def solution(mesh):
    spread = P(("dp", "outer"), None, None)
    in_specs = (spread, P(), P(("dp", "outer")), spread) + (P(),) * 11
    out_specs = (spread, spread) + (P("dp", None),) * 7 + (P(None, "dp"),) * 4
    return jax.shard_map(
        per_device, mesh=mesh, in_specs=in_specs, out_specs=out_specs, check_vma=False
    )
```

```python
import functools
import math
import types

import jax
import jax.numpy as jnp
from jax import lax
from jax.experimental import pallas as pl
from jax.experimental.pallas import tpu as pltpu
from jax.sharding import PartitionSpec as P

CHANNELS = 2048
INNER = 512
TAPS = 9
SLOTS = 2
SHORT = 4
LONG = 36
PIXELS = 144
ROWS = SLOTS * PIXELS
OFFSETS = 2 * TAPS
EPS = 1e-05
BF = jnp.bfloat16
F32 = jnp.float32
MESH = pl.DeviceIdType.MESH
NN = (((1,), (0,)), ((), ()))
NT = (((1,), (1,)), ((), ()))
TN = (((0,), (0,)), ((), ()))


def mm(left, right, dims):
    return lax.dot_general(left, right, dims, preferred_element_type=F32)


def sigmoid(value):
    return 0.5 * jnp.tanh(0.5 * value) + 0.5


def fold(value):
    return jnp.sum(value.reshape(value.shape[0] // 8, 8, value.shape[1]), axis=0)


def total_row(value):
    return jnp.sum(value, axis=0, keepdims=True)


def layout(dp):
    chips = dp // 2
    bits = chips.bit_length() - 1
    wide = CHANNELS // dp
    deep = TAPS * INNER // dp
    taps = max(
        -(-(2 * deep * chip % INNER + 2 * deep) // INNER) for chip in range(chips)
    )
    return chips, bits, wide, deep, taps


def scratch(dp, outer):
    vmem = pltpu.VMEM
    dma = pltpu.SemaphoreType.DMA
    chips, bits, wide, deep, taps = layout(dp)
    everyone = dp * outer
    group = min(chips, 4)
    return dict(
        images=vmem((ROWS, CHANNELS), BF),
        between=vmem((ROWS, CHANNELS), BF),
        dwide=vmem((ROWS, CHANNELS), BF),
        obuf=vmem((ROWS, CHANNELS), BF),
        redwid=vmem((CHANNELS, INNER), BF),
        exp=vmem((CHANNELS, INNER), BF),
        nar=vmem((CHANNELS, INNER), BF),
        dfmcon=vmem((TAPS * INNER, INNER), BF),
        off=vmem((OFFSETS, TAPS * INNER), BF),
        a1=vmem((ROWS, INNER), F32),
        a2=vmem((ROWS, INNER), F32),
        b1=vmem((ROWS, INNER), F32),
        b2=vmem((ROWS, INNER), F32),
        acc=vmem((ROWS, INNER), F32),
        a3=vmem((CHANNELS // 512, ROWS, 512), F32),
        b3=vmem((CHANNELS // 512, ROWS, 512), F32),
        up=vmem((CHANNELS // 512, ROWS, 512), F32),
        inner=vmem((ROWS, INNER), BF),
        hidden=vmem((ROWS, INNER), BF),
        narrow=vmem((ROWS, INNER), BF),
        mixed=vmem((ROWS, INNER), BF),
        dn=vmem((ROWS, INNER), BF),
        turned=vmem((ROWS, INNER), BF),
        wmat=vmem((SLOTS, TAPS, PIXELS, PIXELS), BF),
        tmat=vmem((2, TAPS, PIXELS, PIXELS), BF),
        geo=vmem((2, 2, PIXELS, PIXELS), jnp.int32),
        frac=vmem((ROWS, OFFSETS), F32),
        doff=vmem((ROWS, OFFSETS), F32),
        stn=vmem((4, 2, INNER), F32),
        stw=vmem((2, 2, CHANNELS), F32),
        rxn=vmem((8, everyone, 2, INNER), F32),
        rxw1=vmem((4, dp, 2, CHANNELS), F32),
        rxw2=vmem((4, outer, 2, CHANNELS), F32),
        pool=vmem((3, chips, wide, INNER), F32),
        corel=vmem((chips, wide, INNER), F32),
        land=vmem((2, 2, chips - 1, wide, INNER // 2), F32),
        zwide=vmem((3, 3, wide, INNER), F32),
        tiny=vmem((2, chips, SLOTS, 24, PIXELS), F32),
        give=vmem((ROWS, INNER), F32),
        taken=vmem((group, ROWS, INNER), F32),
        drawn=vmem((ROWS, INNER), F32),
        yall=vmem((group * ROWS, INNER), BF),
        xall=vmem((2, group * ROWS, INNER), BF),
        grad=vmem((taps * INNER, INNER), F32),
        cored=vmem((deep, INNER), F32),
        zdeep=vmem((2, 2, deep // 2, INNER), F32),
        goff=vmem((24, taps * INNER), F32),
        coreo=vmem((24, taps * INNER), F32),
        zoff=vmem((2, 24, taps * INNER), F32),
        free=pltpu.SemaphoreType.REGULAR,
        credit=pltpu.SemaphoreType.REGULAR((2, bits)),
        swapped=pltpu.SemaphoreType.REGULAR,
        load_sem=dma((11,)),
        out_sem=dma((2,)),
        res_sem=dma((7, 4)),
        xn_s=dma((8,)),
        xn_r=dma((8,)),
        xw_s=dma((4, 2)),
        xw_r=dma((4, 2)),
        core_s=dma((7,)),
        core_r=dma((7,)),
        step_s=dma((4, 2, bits)),
        step_r=dma((4, 2, bits)),
        give_sem=dma((4,)),
        take_sem=dma((3,)),
        x_sem=dma((2,)),
        ag_s=dma((4, 2, bits)),
        ag_r=dma((4, 2, bits)),
        tiny_s=dma((2,)),
        tiny_r=dma((2,)),
        z_s=dma((7, 4, 3)),
        z_r=dma((7, 4, 3)),
    )


def kernel(dp, outer, names, *refs):
    assert outer == 4
    r = types.SimpleNamespace(**dict(zip(names, refs)))
    chips, bits, wide, deep, taps = layout(dp)
    everyone = dp * outer
    me = lax.axis_index("dp")
    mine = lax.axis_index("outer")
    own = me * outer + mine
    core = lax.rem(me, 2)
    chip = lax.div(me, 2)
    sibling = (me + 1 - 2 * core, mine)
    inside = (mine == 1) | (mine == 2)
    outside = (mine == 0) | (mine == 3)
    counts, orient = r.counts, r.orient
    dma = pltpu.make_async_copy

    loads = types.SimpleNamespace()

    def load(place, source, target):
        copy = dma(source, target, r.load_sem.at[place])
        copy.start()
        return copy

    loads.images_h = load(0, r.images_h, r.images)
    loads.red_h = load(1, r.red_h, r.redwid)
    loads.off_h = load(2, r.off_h, r.off)
    loads.def_h = load(3, r.def_h, r.dfmcon)
    loads.exp_h = load(4, r.exp_h, r.exp)
    loads.nar_h = load(5, r.nar_h, r.nar)
    loads.cot_h = load(6, r.cot_h, r.dwide)

    def other(step):
        target = lax.rem(own + step, everyone)
        return lax.div(target, outer), lax.rem(target, outer)

    barrier = pltpu.get_barrier_semaphore()

    def greet(step, carry):
        pl.semaphore_signal(barrier, inc=1, device_id=other(step), device_id_type=MESH)
        return carry

    lax.fori_loop(1, everyone, greet, 0)

    def size(i, carry):
        sizes, near, far = carry
        row, place = lax.div(i, outer), lax.rem(i, outer)
        held = counts[i].astype(F32)
        here = jnp.where(place == mine, held, 0.0)

        def mark(count, at, value):
            line = lax.broadcasted_iota(jnp.int32, (count, 1), 0)
            return jnp.where(line == at, value, 0.0)

        return (
            sizes + mark(everyone, i, held),
            near + mark(dp, row, here),
            far + mark(outer, place, held),
        )

    zeros = tuple(jnp.zeros((count, 1), F32) for count in (everyone, dp, outer))
    sizes, near, far = (
        value * float(PIXELS) for value in lax.fori_loop(0, everyone, size, zeros)
    )
    near_total = total_row(near)
    total = total_row(far)
    held = counts[own].astype(F32)
    live1 = held - 1.0
    local = held * float(PIXELS)

    def sweep(body, init):
        def step(i, carry):
            lv = jnp.where(i < 3, 1.0, live1)
            for j in range(3):
                carry = body(pl.ds(pl.multiple_of(i * 48 + j * 16, 16), 16), lv, carry)
            return carry

        return lax.fori_loop(0, 6, step, init, unroll=2)

    def send(source, target, sent, received, device):
        pltpu.make_async_remote_copy(
            src_ref=source,
            dst_ref=target,
            send_sem=sent,
            recv_sem=received,
            device_id=device,
            device_id_type=MESH,
        ).start()

    def settle(view, sem):
        dma(view, view, sem).wait()

    waiting = {}

    def later(tag, view, sem, when=None):
        waiting.setdefault(tag, []).append((when, view, sem))

    def flush(tag):
        for when, view, sem in waiting.pop(tag, []):
            if when is None:
                settle(view, sem)
            else:
                pl.when(when)(functools.partial(settle, view, sem))

    def accumulate(target, source):
        rows = target.shape[0]
        step = math.gcd(rows, 32)

        def body(i, carry):
            rs = pl.ds(pl.multiple_of(i * step, 8), step)
            target[rs, :] += source[rs, :]
            return carry

        count = rows // step
        lax.fori_loop(0, count, body, 0, unroll=math.gcd(count, 3) if count % 2 else 2)

    def mix(target, one, two):
        rows = target.shape[0]
        step = math.gcd(rows, 32)

        def body(i, carry):
            rs = pl.ds(pl.multiple_of(i * step, 8), step)
            target[rs, :] = one[rs, :] + two[rs, :]
            return carry

        count = rows // step
        lax.fori_loop(0, count, body, 0, unroll=math.gcd(count, 3) if count % 2 else 2)

    def flip(value, bit):
        weight = 1 << bit
        return value + weight - 2 * weight * lax.rem(lax.div(value, weight), 2)

    def bit_of(value, bit):
        return lax.rem(lax.div(value, 1 << bit), 2)

    orders = [
        list(range(bits)),
        list(range(bits // 2, bits)) + list(range(bits // 2)),
    ]
    halves = [pl.ds(0, INNER // 2), pl.ds(INNER // 2, INNER // 2)]

    def merge(rx, counted, size, forward):
        first = rx[:, 0, :]
        second = rx[:, 1, :]
        if forward:
            summed = total_row(first)
            apart = first / counted - summed / size
            spread = total_row(second + counted * apart * apart)
            return jnp.concatenate([summed, spread], axis=0)
        return jnp.concatenate([total_row(first), total_row(second)], axis=0)

    def nothing():
        pass

    def share_narrow(number, forward, work):
        rx = r.rxn.at[number]

        def step(i, carry):
            line, part = lax.div(i, dp), lax.rem(i, dp)
            z = jnp.where(mine < outer // 2, outer - 1 - line, line)
            peer = 0
            for bit in range(bits + 1):
                here, turn = bit_of(me, bit), 1 - bit_of(part, bit)
                peer = peer + (here + turn - 2 * here * turn) * (1 << bit)

            @pl.when(peer * outer + z != own)
            def _():
                send(rx.at[own], rx.at[own], r.xn_s.at[number], r.xn_r.at[number], (peer, z))

            return carry

        lax.fori_loop(0, everyone, step, 0)
        rest = rx.at[pl.ds(0, everyone - 1)]
        later("end", rest, r.xn_s.at[number])
        work()
        settle(rest, r.xn_r.at[number])
        return merge(rx, sizes, total, forward)

    def share_wide(number, forward, work, work_more):
        rx1, rx2 = r.rxw1.at[number], r.rxw2.at[number]
        for turn in range(dp - 1, 0, -1):
            peer = me
            for bit in range(bits + 1):
                if (turn >> bit) & 1:
                    peer = flip(peer, bit)
            send(rx1.at[me], rx1.at[me], r.xw_s.at[number, 0], r.xw_r.at[number, 0], (peer, mine))
        rest = rx1.at[pl.ds(0, dp - 1)]
        later("end", rest, r.xw_s.at[number, 0])
        work()
        settle(rest, r.xw_r.at[number, 0])
        rx2[mine] = merge(rx1, near, near_total, forward)
        for line in range(outer):
            z = jnp.where(mine < outer // 2, outer - 1 - line, line)

            @pl.when(z != mine)
            def _():
                send(
                    rx2.at[mine],
                    rx2.at[mine],
                    r.xw_s.at[number, 1],
                    r.xw_r.at[number, 1],
                    (me, z),
                )

        rest = rx2.at[pl.ds(0, outer - 1)]
        later("end", rest, r.xw_s.at[number, 1])
        work_more()
        settle(rest, r.xw_r.at[number, 1])
        return merge(rx2, far, total, forward)

    def local_stats(ref, put, cs):
        zero = jnp.zeros((8, 512), F32)
        summed = total_row(sweep(lambda rs, lv, c: c + lv * fold(ref[rs, :]), zero))
        mean = summed / local

        def squares(rs, lv, carry):
            apart = ref[rs, :] - mean
            return carry + lv * fold(apart * apart)

        put[0:1, cs] = summed
        put[1:2, cs] = total_row(sweep(squares, zero))

    def keep_stats(both, st):
        st[0:1, :] = both[0:1] / total
        st[1:2, :] = lax.rsqrt(both[1:2] / total + EPS)

    def narrow_stats(ref, number, work=nothing):
        local_stats(ref, r.rxn.at[number, own], pl.ds(0, INNER))
        keep_stats(share_narrow(number, True, work), r.stn.at[number])

    blocks = [pl.ds(start, 512) for start in range(0, CHANNELS, 512)]

    def wide_stats(ref, number, work=nothing, work_more=nothing):
        for n, cs in enumerate(blocks):
            local_stats(ref.at[n], r.rxw1.at[number, me], cs)
        keep_stats(share_wide(number, True, work, work_more), r.stw.at[number])

    def norm_silu(ref, number, gain, bias, out, spread):
        st = r.stn.at[number]
        mean, scale = st[0:1, :], st[1:2, :]
        steep = scale * gain

        def body(rs, lv, carry):
            z = (ref[rs, :] - mean) * steep + bias
            value = (z * sigmoid(z)).astype(BF)
            out[rs, :] = value
            if spread:
                r.give[rs, :] = value.astype(F32)
            return carry

        sweep(body, 0)

    def narrow_cotangent(ref, place, gain, bias, number, spread, work=nothing):
        acc = r.acc
        st = r.stn.at[place]
        mean, scale = st[0:1, :], st[1:2, :]

        def body(rs, lv, carry):
            xhat = (ref[rs, :] - mean) * scale
            z = xhat * gain + bias
            sg = sigmoid(z)
            g = acc[rs, :] * (sg * (1.0 + z * (1.0 - sg)))
            acc[rs, :] = g
            return carry[0] + fold(g), carry[1] + fold(g * xhat)

        zero = jnp.zeros((8, INNER), F32)
        summed, paired = sweep(body, (zero, zero))
        put = r.rxn.at[number, own]
        put[0:1, :] = total_row(summed)
        put[1:2, :] = total_row(paired)
        both = share_narrow(number, False, work)
        r.g_ib[place : place + 1, :] = both[0:1]
        r.g_ig[place : place + 1, :] = both[1:2]
        steep = scale * gain
        lift, tilt = both[0:1] / total, both[1:2] / total

        def back(rs, lv, carry):
            xhat = (ref[rs, :] - mean) * scale
            value = (steep * (acc[rs, :] - lv * (lift + xhat * tilt))).astype(BF)
            r.dn[rs, :] = value
            if spread:
                r.give[rs, :] = value.astype(F32)
            return carry

        sweep(back, 0)

    def wide_cotangent(number, ref, place, gain, bias, cotangent, work=nothing, work_more=nothing):
        put = r.rxw1.at[number, me]
        st = r.stw.at[place]
        for n, cs in enumerate(blocks):
            mean, scale = st[0:1, cs], st[1:2, cs]
            gn, bs = gain[:, 512 * n : 512 * n + 512], bias[:, 512 * n : 512 * n + 512]

            def body(rs, lv, carry):
                xhat = (ref[n, rs, :] - mean) * scale
                g = cotangent(n, rs, cs, lv, xhat * gn + bs)
                r.up[n, rs, :] = g
                return carry[0] + fold(g), carry[1] + fold(g * xhat)

            zero = jnp.zeros((8, 512), F32)
            summed, paired = sweep(body, (zero, zero))
            put[0:1, cs] = total_row(summed)
            put[1:2, cs] = total_row(paired)
        both = share_wide(number, False, work, work_more)
        r.g_bb[place : place + 1, :] = both[0:1]
        r.g_bg[place : place + 1, :] = both[1:2]
        for n, cs in enumerate(blocks):
            mean, scale = st[0:1, cs], st[1:2, cs]
            span = slice(512 * n, 512 * n + 512)
            steep = scale * gain[:, span]
            lift, tilt = both[0:1, span] / total, both[1:2, span] / total

            def back(rs, lv, carry):
                xhat = (ref[n, rs, :] - mean) * scale
                value = steep * (r.up[n, rs, :] - lv * (lift + xhat * tilt))
                r.dwide[rs, cs] = value.astype(BF)
                return carry

            sweep(back, 0)

    def tap(ref, k):
        return ref[pl.ds(pl.multiple_of(k * INNER, INNER), INNER), :]

    def offset_tap(k):
        return r.off[:, pl.ds(pl.multiple_of(k * INNER, INNER), INNER)]

    def slot_rows(s):
        return pl.ds(s * PIXELS, PIXELS)

    def steps_of(k):
        return 2 * lax.div(k, 3) - 2, 2 * lax.rem(k, 3) - 2

    WID, CON, NAR, EXP, DEF, RED, OFF = range(7)
    nth = {WID: 0, NAR: 1, EXP: 2, RED: 3}
    result = {
        WID: r.g_wid,
        CON: r.g_con,
        NAR: r.g_nar,
        EXP: r.g_exp,
        DEF: r.g_def,
        RED: r.g_red,
        OFF: r.g_off,
    }
    pool, land, grad, far_blocks = r.pool, r.land, r.grad, r.far_blocks

    deep_parts = 4 if deep % 32 == 0 else 2
    wide_parts = {WID: 2, NAR: 2, EXP: 2, RED: 4}

    def z_hold(u):
        if u == RED:
            return [r.a3.at[i, pl.ds(0, wide)] for i in range(3)]
        return [r.zwide.at[nth[u], i] for i in range(3)]

    def z_parts(u):
        if u in nth:
            hold = z_hold(u)
            for q in range(wide_parts[u]):
                rows = wide // (wide_parts[u] // 2)
                rs, hs = pl.ds(q // 2 * rows, rows), halves[q % 2]
                yield tuple(ref.at[rs, hs] for ref in hold) + (result[u].at[rs, hs],)
        elif u == OFF:
            yield r.goff, r.zoff.at[0], r.zoff.at[1], result[u]
        else:
            for q in range(deep_parts):
                back, at = divmod(q, deep_parts // 2)
                source = r.b3.at[(2 if u == DEF else 0) + back]
                if u == DEF:
                    first, second = (r.b1, r.a2) if back == 0 else (r.b2, r.a3.at[3])
                else:
                    first, second = r.zdeep.at[0, back], r.zdeep.at[1, back]
                size = deep // deep_parts
                rows = pl.ds(at * size, size)
                out = result[u].at[pl.ds(q * size, size)]
                yield source.at[rows], first.at[rows], second.at[rows], out

    def z_sems(u, q, step):
        return r.z_s.at[u, q, step], r.z_r.at[u, q, step]

    def z1(u, some=None):
        for q, (source, first, second, out) in enumerate(z_parts(u)):
            if some is not None and q not in some:
                continue
            sent, received = z_sems(u, q, 0)

            @pl.when(outside)
            def _():
                send(source, first, sent, received, (me, flip(mine, 0)))

            later(("z", u), source, sent, outside)

    def z2(u, some=None):
        for q, (source, first, second, out) in enumerate(z_parts(u)):
            if some is not None and q not in some:
                continue
            sent, received = z_sems(u, q, 1)

            @pl.when(inside)
            def _():
                settle(first, z_sems(u, q, 0)[1])
                accumulate(source, first)
                send(source, second, sent, received, (me, 3 - mine))

            later(("z", u), source, sent, inside)

    def z3(u, some=None):
        for q, (source, first, second, out) in enumerate(z_parts(u)):
            if some is not None and q not in some:
                continue
            sent, received = z_sems(u, q, 2)

            @pl.when(inside)
            def _():
                settle(second, z_sems(u, q, 1)[1])
                accumulate(second, source)
                send(second, first, sent, received, (me, flip(mine, 0)))
                dma(second, out, r.res_sem.at[u, q]).start()

            later(("zl", u), second, sent, inside)

    def z4(u, some=None):
        for q, (source, first, second, out) in enumerate(z_parts(u)):
            if some is not None and q not in some:
                continue

            @pl.when(outside)
            def _():
                settle(first, z_sems(u, q, 2)[1])
                dma(first, out, r.res_sem.at[u, q]).start()

    def z_clear(u):
        flush(("z", u))
        flush(("zl", u))
        for q, (source, first, second, out) in enumerate(z_parts(u)):
            dma(first, out, r.res_sem.at[u, q]).wait()

    def wide_begin(u, left, right):
        p = nth[u] % 2
        flush("sib")
        flush(("keep", p))
        low = p + (2 - p) * core
        high = p + (2 - p) * (1 - core)
        if u == EXP:
            pl.semaphore_wait(r.swapped, 1)

        def step(m, carry):
            block = left[:, pl.ds(pl.multiple_of(m * (2 * wide), 2 * wide), 2 * wide)]
            pool[low, m] = mm(block[:, :wide], right[...], TN)
            pool[high, m] = mm(block[:, wide:], right[...], TN)
            send(
                pool.at[2, m], r.corel.at[m], r.core_s.at[u], r.core_r.at[u], sibling
            )
            return carry

        lax.fori_loop(0, chips, step, 0)
        later("sib", r.corel, r.core_s.at[u])

    def piece(h, t, j, toward):
        value = 0
        for i, bit in enumerate(orders[h]):
            if i < t:
                part = bit_of(chip, bit)
            elif i == t:
                part = bit_of(toward, bit)
            else:
                part = (j >> (i - t - 1)) & 1
            value = value + part * (1 << bit)
        return value

    def step_place(u, h, t):
        first, count = chips - (chips >> t), chips >> (t + 1)
        p = nth[u] % 2
        sems = r.step_s.at[nth[u], h, t], r.step_r.at[nth[u], h, t]
        return p, first, count, sems, land.at[p, h, pl.ds(first, count)]

    def wide_send(u, t):
        for h in range(2):
            p, first, count, (sent, received), region = step_place(u, h, t)
            toward = flip(chip, orders[h][t])
            if u == RED:
                pl.semaphore_wait(r.credit.at[h, t], 1)
            for j in range(count):
                send(
                    pool.at[p, piece(h, t, j, toward), :, halves[h]],
                    land.at[p, h, first + j],
                    sent,
                    received,
                    (2 * toward + core, mine),
                )
            later(("keep", p), region, sent)

    def wide_add(u, t):
        for h in range(2):
            p, first, count, (sent, received), region = step_place(u, h, t)
            settle(region, received)
            if t == bits - 1:
                mix(z_hold(u)[0].at[:, halves[h]], pool.at[p, chip, :, halves[h]], land.at[p, h, first])
            else:
                for j in range(count):
                    accumulate(
                        pool.at[p, piece(h, t, j, chip), :, halves[h]], land.at[p, h, first + j]
                    )
            if u == NAR:
                pl.semaphore_signal(
                    r.credit.at[h, t],
                    inc=1,
                    device_id=(2 * flip(chip, orders[h][t]) + core, mine),
                    device_id_type=MESH,
                )

    def wide_core(u):
        p = nth[u] % 2
        settle(r.corel, r.core_r.at[u])

        def step(m, carry):
            accumulate(pool.at[p, m], r.corel.at[m])
            return carry

        lax.fori_loop(0, chips, step, 0)
        if u == NAR:
            pl.semaphore_signal(r.swapped, inc=1, device_id=sibling, device_id_type=MESH)

    def wide_step(u, t):
        wide_add(u, t - 1)
        if t < bits:
            wide_send(u, t)
        else:
            z1(u)

    def held_at(h, j):
        value = chip
        for i in range(bits):
            if (j >> i) & 1:
                value = flip(value, orders[h][i])
        return value

    def gather_send(a, t, some=None):
        for h in range(2):
            partner = flip(chip, orders[h][t])
            sent, received = r.ag_s.at[a, h, t], r.ag_r.at[a, h, t]
            for j in range(1 << t) if some is None else some:
                block = far_blocks.at[a, held_at(h, j), :, halves[h]]
                source = r.give.at[:, halves[h]] if j == 0 else block
                send(source, block, sent, received, (2 * partner + core, mine))
            if some is None or 0 in some:
                later(("ag", a), far_blocks.at[a, pl.ds(0, 1 << t), :, halves[h]], sent)

    def gather_start(a):
        block = far_blocks.at[a, chip]
        dma(r.give, block, r.give_sem.at[a]).start()
        later(("ag", a), block, r.give_sem.at[a])
        gather_send(a, 0)

    def gather_wait(a, t):
        for h in range(2):
            settle(far_blocks.at[a, pl.ds(0, 1 << t), :, halves[h]], r.ag_r.at[a, h, t])

    def gather_step(a, t, some=None):
        gather_wait(a, t - 1)
        gather_send(a, t, some)

    def gather_first(a, t):
        if t < bits:
            gather_send(a, t, [0])

    def gather_rest(a):
        for t in range(1, bits):
            gather_wait(a, t - 1)
            gather_send(a, t, range(1 if t == 1 else 0, 1 << t))

    def gather_end(a):
        gather_wait(a, bits - 1)
        flush(("ag", a))

    def tiny_send(a):
        for step in range(1, chips):
            block = r.tiny.at[a, chip]
            peer = lax.rem(chip + step, chips)
            send(block, block, r.tiny_s.at[a], r.tiny_r.at[a], (2 * peer + core, mine))
        later("end", r.tiny.at[a, pl.ds(0, chips - 1)], r.tiny_s.at[a])

    def tiny_wait(a):
        settle(r.tiny.at[a, pl.ds(0, chips - 1)], r.tiny_r.at[a])

    group = min(chips, 4)
    first_tap = lax.div(2 * deep * chip, INNER)
    margin = 2 * deep * chip - first_tap * INNER

    def taps_of(kk):
        k = jnp.minimum(first_tap + kk, TAPS - 1)
        return (k, *steps_of(k))

    def fetch_fields(a, g):
        copy = dma(far_blocks.at[a, pl.ds(g * group, group)], r.taken, r.take_sem.at[2])
        copy.start()
        copy.wait()

    def image_of(i, g):
        m, s = lax.div(i, SLOTS), lax.rem(i, SLOTS)
        rows = pl.ds(pl.multiple_of(i * PIXELS, PIXELS), PIXELS)
        field = r.taken[m, pl.ds(pl.multiple_of(s * PIXELS, PIXELS), PIXELS), :].astype(BF)
        flat = r.tiny[0, g * group + m, s, 18:19, :] == 0.0
        dr = jnp.where(flat, r.geo[0, 0], r.geo[1, 0])
        dc = jnp.where(flat, r.geo[0, 1], r.geo[1, 1])
        return g * group + m, s, rows, field, dr, dc

    def group_rows(g):
        return pl.ds(g * (group * ROWS), group * ROWS)

    def columns(u, kk):
        x = 1 if u == DEF else 0
        k, down, across = taps_of(kk)
        for g in range(chips // group):
            if kk == 0 or chips > group:
                fetch_fields(0 if u == DEF else 1, g)
            if g == 0:
                flush("columns")

            def image(i, carry):
                m, s, rows, field, dr, dc = image_of(i, g)
                if u == CON:
                    hit = jnp.where((dr == down) & (dc == across), 1.0, 0.0).astype(BF)
                    r.xall[0, rows, :] = mm(hit, field, NN).astype(BF)
                    return carry
                tiny = r.tiny.at[0, m, s]
                fy, fx = tiny[pl.ds(2 * k, 1), :], tiny[pl.ds(2 * k + 1, 1), :]
                ay = jnp.where(dr == -down, 1.0 - fy, jnp.where(dr == -down - 1, fy, 0.0))
                ax = jnp.where(dc == -across, 1.0 - fx, jnp.where(dc == -across - 1, fx, 0.0))
                r.xall[0, rows, :] = mm((ay * ax).astype(BF), field, TN).astype(BF)
                return carry

            lax.fori_loop(0, group * SLOTS, image, 0, unroll=4)
            place = r.far_columns.at[x, kk, group_rows(g)]
            copy = dma(r.xall.at[0], place, r.x_sem.at[0])
            copy.start()
            if g + 1 < chips // group:
                copy.wait()
            else:
                later("columns", place, r.x_sem.at[0])

    def deep_make(u):
        flush("deep")
        flush("columns")
        x, back_of = (1, 3) if u == DEF else (0, 2)
        slots = (r.give, r.drawn)
        for g in range(chips // group):

            def fetch(m):
                return dma(far_blocks.at[back_of, g * group + m], slots[m % 2], r.take_sem.at[m % 2])

            def draw(kk):
                slot = lax.rem(kk, 2)
                return dma(
                    r.far_columns.at[x, kk, group_rows(g)], r.xall.at[slot], r.x_sem.at[slot]
                )

            for m in range(min(2, group)):
                fetch(m).start()
            draw(0).start()
            for m in range(group):
                fetch(m).wait()

                def lower(i, carry):
                    rows = pl.ds(pl.multiple_of(m * ROWS + i * 32, 32), 32)
                    there = pl.ds(pl.multiple_of(i * 32, 32), 32)
                    r.yall[rows, :] = slots[m % 2][there, :].astype(BF)
                    return carry

                lax.fori_loop(0, ROWS // 32, lower, 0, unroll=3)
                if m + 2 < group:
                    fetch(m + 2).start()

            def one(kk, carry):
                @pl.when(kk + 1 < taps)
                def _():
                    draw(kk + 1).start()

                draw(kk).wait()
                at = pl.ds(pl.multiple_of(kk * INNER, INNER), INNER)
                part = mm(r.xall[lax.rem(kk, 2)], r.yall[...], TN)
                if g == 0:
                    grad[at, :] = part
                else:
                    grad[at, :] += part
                return carry

            lax.fori_loop(0, taps, one, 0)
        away = pl.ds(pl.multiple_of(margin + (1 - core) * deep, 8), deep)
        send(grad.at[away], r.cored, r.core_s.at[u], r.core_r.at[u], sibling)
        later("deep", r.cored, r.core_s.at[u])

    def off_make():
        for g in range(chips // group):
            fetch_fields(0, g)

            def one(kk, carry):
                k, down, across = taps_of(kk)

                def image(i, share):
                    m, s, rows, field, dr, dc = image_of(i, g)
                    hit = jnp.where((dr == down) & (dc == across), 1.0, 0.0).astype(BF)
                    moved = mm(r.tiny[1, m, s].astype(BF), hit, NN).astype(BF)
                    return share + mm(moved, field, NN)

                at = pl.ds(pl.multiple_of(kk * INNER, INNER), INNER)
                share = lax.fori_loop(
                    0, group * SLOTS, image, jnp.zeros((24, INNER), F32), unroll=8
                )
                if g == 0:
                    r.goff[:, at] = share
                else:
                    r.goff[:, at] += share
                return carry

            lax.fori_loop(0, taps, one, 0)
        send(r.goff, r.coreo, r.core_s.at[OFF], r.core_r.at[OFF], sibling)

    def off_core():
        settle(r.goff, r.core_s.at[OFF])
        settle(r.coreo, r.core_r.at[OFF])
        accumulate(r.goff, r.coreo)

    def deep_core(u):
        settle(r.cored, r.core_r.at[u])
        half = deep // 2
        step = math.gcd(half, 32)
        for q in range(2):
            target = r.b3.at[(2 if u == DEF else 0) + q]

            def body(i, carry):
                at = pl.multiple_of(i * step, 8)
                here = grad[pl.ds(pl.multiple_of(margin + core * deep + q * half + at, 8), step), :]
                target[pl.ds(at, step), :] = here + r.cored[pl.ds(q * half + at, step), :]
                return carry

            lax.fori_loop(0, half // step, body, 0)
    images, between, acc, up = r.images, r.between, r.acc, r.up
    ig = [r.ig[i : i + 1, :] for i in range(4)]
    ib = [r.ib[i : i + 1, :] for i in range(4)]
    bg = [r.bg[i : i + 1, :] for i in range(2)]
    bb = [r.bb[i : i + 1, :] for i in range(2)]

    def geometry():
        q = lax.broadcasted_iota(jnp.int32, (PIXELS, PIXELS), 1)
        p = lax.broadcasted_iota(jnp.int32, (PIXELS, PIXELS), 0)

        def place_of(at, kind):
            if kind:
                row = lax.shift_right_logical(at, 2)
                return row, at - row * SHORT
            row = (at >= LONG).astype(jnp.int32) + (at >= 2 * LONG).astype(jnp.int32)
            row = row + (at >= 3 * LONG).astype(jnp.int32)
            return row, at - row * LONG

        for kind in range(2):
            row_q, col_q = place_of(q, kind)
            row_p, col_p = place_of(p, kind)
            r.geo[kind, 0] = row_q - row_p
            r.geo[kind, 1] = col_q - col_p

            def hot(k, carry):
                down, across = steps_of(k)
                hit = (r.geo[kind, 0] == down) & (r.geo[kind, 1] == across)
                r.tmat[kind, k] = jnp.where(hit, 1.0, 0.0).astype(BF)
                return carry

            lax.fori_loop(0, TAPS, hot, 0)

    def shifted(s, k):
        return r.tmat[orient[s], k]

    loads.images_h.wait()
    loads.red_h.wait()
    r.a1[...] = mm(images[...], r.redwid[...], NN)
    loads.wid_h = load(7, r.wid_h, r.redwid)
    pl.semaphore_wait(barrier, everyone - 1)
    narrow_stats(r.a1, 0, geometry)
    norm_silu(r.a1, 0, ig[0], ib[0], r.inner, True)
    gather_start(0)

    loads.off_h.wait()
    inner = r.inner
    lane = lax.broadcasted_iota(jnp.int32, (PIXELS, OFFSETS), 1)

    def gather(k, carry):
        cols = [mm(shifted(s, k), inner[slot_rows(s), :], NN).astype(BF) for s in range(SLOTS)]
        weight = offset_tap(k)
        return tuple(old + mm(col, weight, NT) for old, col in zip(carry, cols))

    zero = jnp.zeros((PIXELS, OFFSETS), F32)
    both_offsets = lax.fori_loop(0, TAPS, gather, (zero,) * SLOTS, unroll=3)
    for s in range(SLOTS):
        frac = sigmoid(both_offsets[s])
        r.frac[slot_rows(s), :] = frac
        coarse = frac.astype(BF)
        fine = (frac - coarse.astype(F32)).astype(BF)
        unit = r.tmat[0, TAPS // 2]
        put = r.tiny.at[0, chip, s]
        put[...] = jnp.zeros((24, PIXELS), F32) + orient[s].astype(F32)
        put[0:OFFSETS, :] = mm(coarse, unit, TN) + mm(fine, unit, TN)
    tiny_send(0)

    def bilinear(s, k):
        down, across = steps_of(k)
        frac = r.frac[slot_rows(s), :]
        fy = jnp.sum(jnp.where(lane == 2 * k, frac, 0.0), axis=1, keepdims=True)
        fx = jnp.sum(jnp.where(lane == 2 * k + 1, frac, 0.0), axis=1, keepdims=True)
        dr, dc = r.geo[orient[s], 0], r.geo[orient[s], 1]
        in_y = (dr == down, dr == down + 1)
        in_x = (dc == across, dc == across + 1)
        ay = jnp.where(in_y[0], 1.0 - fy, jnp.where(in_y[1], fy, 0.0))
        ax = jnp.where(in_x[0], 1.0 - fx, jnp.where(in_x[1], fx, 0.0))
        return fy, fx, ay, ax, in_y, in_x

    loads.def_h.wait()
    acc[...] = jnp.zeros((ROWS, INNER), F32)

    def sample(k, carry):
        for s in range(SLOTS):
            _, _, ay, ax, _, _ = bilinear(s, k)
            weight = (ay * ax).astype(BF)
            r.wmat[s, k] = weight
            r.turned[slot_rows(s), :] = mm(weight, inner[slot_rows(s), :], NN).astype(BF)
        acc[...] += mm(r.turned[...], tap(r.dfmcon, k), NN)
        return carry

    lax.fori_loop(0, TAPS, sample, 0, unroll=3)
    loads.con_h = load(8, r.con_h, r.dfmcon)
    r.a2[...] = acc[...]
    narrow_stats(r.a2, 1, lambda: gather_first(0, 1))
    norm_silu(r.a2, 1, ig[1], ib[1], r.hidden, False)

    def widen(source, weight, target):
        def step(n, carry):
            rows = pl.ds(pl.multiple_of(n * 512, 512), 512)
            target[n] = mm(source[...], weight[rows, :], NT)
            return carry

        lax.fori_loop(0, CHANNELS // 512, step, 0, unroll=2)

    loads.exp_h.wait()
    widen(r.hidden, r.exp, r.a3)
    wide_stats(r.a3, 0, lambda: gather_rest(0))
    for n, cs in enumerate(blocks):
        mean = r.stw[0, 0:1, cs]
        steep = r.stw[0, 1:2, cs] * bg[0][:, 512 * n : 512 * n + 512]
        bias = bb[0][:, 512 * n : 512 * n + 512]

        def join(rs, lv, carry):
            z = (r.a3[n, rs, :] - mean) * steep + bias + images[rs, cs].astype(F32)
            between[rs, cs] = (z * sigmoid(z)).astype(BF)
            return carry

        sweep(join, 0)

    loads.nar_h.wait()
    r.b1[...] = mm(between[...], r.nar[...], NN)

    def work_b1():
        gather_end(0)
        tiny_wait(0)
        columns(DEF, 0)

    narrow_stats(r.b1, 2, work_b1)
    norm_silu(r.b1, 2, ig[2], ib[2], r.narrow, True)
    gather_start(1)

    loads.con_h.wait()
    acc[...] = jnp.zeros((ROWS, INNER), F32)

    def convolve(k, carry):
        for s in range(SLOTS):
            r.turned[slot_rows(s), :] = mm(
                shifted(s, k), r.narrow[slot_rows(s), :], NN
            ).astype(BF)
        acc[...] += mm(r.turned[...], tap(r.dfmcon, k), NN)
        return carry

    lax.fori_loop(0, TAPS, convolve, 0, unroll=3)
    r.b2[...] = acc[...]
    def work_b2():
        gather_first(1, 1)
        columns(DEF, 1)

    narrow_stats(r.b2, 3, work_b2)
    norm_silu(r.b2, 3, ig[3], ib[3], r.mixed, False)

    loads.wid_h.wait()
    widen(r.mixed, r.redwid, r.b3)

    def work_b3():
        gather_rest(1)
        for kk in range(2, taps):
            columns(DEF, kk)

    wide_stats(r.b3, 1, work_b3)

    loads.cot_h.wait()

    def last(n, rs, cs, lv, pre):
        z = pre + between[rs, cs].astype(F32)
        sg = sigmoid(z)
        r.obuf[rs, cs] = (lv * (z * sg)).astype(BF)
        return r.dwide[rs, cs].astype(F32) * (lv * (sg * (1.0 + z * (1.0 - sg))))

    def work_f():
        gather_end(1)
        columns(CON, 0)

    wide_cotangent(2, r.b3, 1, bg[1], bb[1], last, nothing, work_f)
    out_copy = dma(r.obuf, r.out_h, r.out_sem.at[0])
    out_copy.start()
    wide_begin(WID, r.dwide, r.mixed)
    acc[...] = mm(r.dwide[...], r.redwid[...], NN)
    loads.red_h = load(9, r.red_h, r.redwid)

    def work_e():
        wide_core(WID)
        wide_send(WID, 0)
        columns(CON, 1)

    narrow_cotangent(r.b2, 3, ig[3], ib[3], 4, True, work_e)

    acc[...] = jnp.zeros((ROWS, INNER), F32)

    def spread(k, carry):
        for s in range(SLOTS):
            r.turned[slot_rows(s), :] = mm(
                shifted(s, TAPS - 1 - k), r.dn[slot_rows(s), :], NN
            ).astype(BF)
        acc[...] += mm(r.turned[...], tap(r.dfmcon, k), NT)
        return carry

    lax.fori_loop(0, TAPS, spread, 0, unroll=3)
    loads.def_h = load(10, r.def_h, r.dfmcon)

    def work_d():
        wide_step(WID, 1)
        gather_start(2)
        for kk in range(2, taps):
            columns(CON, kk)

    narrow_cotangent(r.b1, 2, ig[2], ib[2], 5, False, work_d)
    for t in range(2, bits + 1):
        wide_step(WID, t)

    def add_back(n, carry):
        rows = pl.ds(pl.multiple_of(n * 512, 512), 512)
        up[n] += mm(r.dn[...], r.nar[rows, :], NT)
        return carry

    lax.fori_loop(0, CHANNELS // 512, add_back, 0, unroll=2)

    def first(n, rs, cs, lv, pre):
        z = pre + images[rs, cs].astype(F32)
        sg = sigmoid(z)
        return up[n, rs, :] * (sg * (1.0 + z * (1.0 - sg)))

    def work_c():
        for t in range(1, bits):
            gather_step(2, t)
        wide_begin(NAR, between, r.dn)

    def work_more_c():
        z2(WID)
        wide_core(NAR)

    wide_cotangent(3, r.a3, 0, bg[0], bb[0], first, work_c, work_more_c)
    acc[...] = mm(r.dwide[...], r.exp[...], NN)

    def work_b():
        wide_send(NAR, 0)
        z3(WID)
        wide_begin(EXP, r.dwide, r.hidden)
        gather_end(2)
        deep_make(CON)

    narrow_cotangent(r.a2, 1, ig[1], ib[1], 6, True, work_b)
    gather_start(3)
    deep_core(CON)
    early, late = range(deep_parts // 2), range(deep_parts // 2, deep_parts)
    z1(CON, early)

    loads.def_h.wait()
    acc[...] = jnp.zeros((ROWS, INNER), F32)
    r.doff[...] = jnp.zeros((ROWS, OFFSETS), F32)

    def unsample(k, carry):
        r.turned[...] = mm(r.dn[...], tap(r.dfmcon, k), NT).astype(BF)
        for s in range(SLOTS):
            rs = slot_rows(s)
            back = r.turned[rs, :]
            pairs = mm(back, inner[rs, :], NT)
            fy, fx, ay, ax, in_y, in_x = bilinear(s, k)
            slope_y = jnp.where(in_y[1], ax, 0.0) - jnp.where(in_y[0], ax, 0.0)
            slope_x = jnp.where(in_x[1], ay, 0.0) - jnp.where(in_x[0], ay, 0.0)
            to_y = jnp.sum(pairs * slope_y, axis=1, keepdims=True) * (fy * (1.0 - fy))
            to_x = jnp.sum(pairs * slope_x, axis=1, keepdims=True) * (fx * (1.0 - fx))
            r.doff[rs, :] += jnp.where(lane == 2 * k, to_y, 0.0) + jnp.where(
                lane == 2 * k + 1, to_x, 0.0
            )
            acc[rs, :] += mm(r.wmat[s, k], back, TN)
        return carry

    lax.fori_loop(0, TAPS, unsample, 0, unroll=3)
    wide_step(NAR, 1)
    z2(CON, [0])
    for s in range(SLOTS):
        put = r.tiny.at[1, chip, s]
        put[...] = jnp.zeros((24, PIXELS), F32)
        put[0:OFFSETS, :] = mm(
            r.doff[slot_rows(s), :].astype(BF), r.tmat[0, TAPS // 2], TN
        )
    tiny_send(1)

    def untap(k, carry):
        for s in range(SLOTS):
            rs = slot_rows(s)
            moved = mm(shifted(s, TAPS - 1 - k), r.doff[rs, :].astype(BF), NN).astype(BF)
            acc[rs, :] += mm(moved, offset_tap(k), NN)
        return carry

    lax.fori_loop(0, TAPS, untap, 0, unroll=3)

    wide_core(EXP)

    def work_a():
        for t in range(1, bits):
            gather_step(3, t)
        wide_send(EXP, 0)
        z1(CON, late)
        for t in range(2, bits + 1):
            wide_step(NAR, t)
        z2(CON, [1])
        z4(WID)

    narrow_cotangent(r.a1, 0, ig[0], ib[0], 7, False, work_a)
    z3(CON, [0])
    wide_begin(RED, images, r.dn)
    z2(CON, [2])
    out_copy.wait()
    loads.red_h.wait()

    def finish(n, carry):
        rows = pl.ds(pl.multiple_of(n * 512, 512), 512)
        r.obuf[:, rows] = (up[n] + mm(r.dn[...], r.redwid[rows, :], NT)).astype(BF)
        return carry

    lax.fori_loop(0, CHANNELS // 512, finish, 0, unroll=2)
    grad_copy = dma(r.obuf, r.grad_h, r.out_sem.at[1])
    grad_copy.start()
    z2(CON, [3])
    z3(CON, [1])
    gather_end(3)
    deep_make(DEF)
    z2(NAR, [0])
    z3(CON, [2])
    wide_core(RED)
    wide_send(RED, 0)
    deep_core(DEF)
    z1(DEF)
    z2(NAR, [1])
    z3(CON, [3])
    wide_step(EXP, 1)
    tiny_wait(1)
    off_make()
    z2(DEF, [0])
    z3(NAR, [0])
    off_core()
    z1(OFF)
    wide_step(RED, 1)
    z2(DEF, [1])
    z3(NAR, [1])
    for t in range(2, bits + 1):
        wide_step(EXP, t)
    z2(DEF, [2])
    z3(DEF, [0])
    for t in range(2, bits + 1):
        wide_step(RED, t)
    z2(DEF, [3])
    z3(DEF, [1])
    z2(OFF)
    z3(DEF, [2])
    z2(EXP, [0])
    z3(DEF, [3])
    z3(OFF)
    z2(EXP, [1])
    z2(RED, [0])
    z3(EXP, [0])
    z2(RED, [1])
    z2(RED, [2])
    z3(EXP, [1])
    z2(RED, [3])
    z3(RED, [0])
    z3(RED, [1])
    z3(RED, [2])
    z3(RED, [3])
    z4(CON)
    z4(NAR)
    z4(DEF)
    z4(OFF)
    z4(EXP)
    z4(RED)
    for u in range(7):
        z_clear(u)
    grad_copy.wait()
    for tag in list(waiting):
        flush(tag)


MOVED = ["out", "grad", "con", "def", "wid", "nar", "exp", "red"]


def deliver(dp, names, *refs):
    r = types.SimpleNamespace(**dict(zip(names, refs)))
    _, _, _, deep, _ = layout(dp)
    place = lax.axis_index("dp")
    moves = []
    for i, name in enumerate(MOVED):
        source, target, hold = (getattr(r, kind + name) for kind in ("from_", "to_", "hold_"))
        taken = pltpu.make_async_copy(source, hold, r.sems.at[0, i])
        taken.start()
        moves.append((taken, pltpu.make_async_copy(hold, target, r.sems.at[1, i])))

    for taken, given in moves:
        taken.wait()
        given.start()

    def span(ref, start, target):
        rows, lanes = ref.shape
        moved = pltpu.roll(ref[...], lax.rem(lanes - start, lanes), 1)
        target[...] = moved[: target.shape[0], : target.shape[1]]

    span(r.g_ig, place * (INNER // dp), r.to_ig)
    span(r.g_ib, place * (INNER // dp), r.to_ib)
    span(r.g_bg, place * (CHANNELS // dp), r.to_bg)
    span(r.g_bb, place * (CHANNELS // dp), r.to_bb)
    chip, core = lax.div(place, 2), lax.rem(place, 2)
    span(r.g_off, lax.rem(2 * deep * chip, INNER) + deep * core, r.to_off)
    for taken, given in moves:
        given.wait()


def per_device(
    images,
    counts,
    orientation,
    cotangent,
    reducer,
    offseter,
    deformer,
    expander,
    narrower,
    convolver,
    widener,
    inner_gains,
    inner_biases,
    broad_gains,
    broad_biases,
):
    dp, outer = lax.axis_size("dp"), lax.axis_size("outer")
    chips, bits, wide, deep, taps = layout(dp)
    buffers = scratch(dp, outer)
    smem = pl.BlockSpec(memory_space=pltpu.SMEM)
    vmem = pl.BlockSpec(memory_space=pltpu.VMEM)
    far = pl.BlockSpec(memory_space=pl.ANY)
    shape = jax.ShapeDtypeStruct
    inputs = dict(
        counts=(smem, counts),
        orient=(smem, orientation),
        ig=(vmem, inner_gains),
        ib=(vmem, inner_biases),
        bg=(vmem, broad_gains),
        bb=(vmem, broad_biases),
        images_h=(far, images.reshape(ROWS, CHANNELS)),
        cot_h=(far, cotangent.reshape(ROWS, CHANNELS)),
        red_h=(far, reducer),
        off_h=(far, offseter.T),
        def_h=(far, deformer),
        exp_h=(far, expander),
        nar_h=(far, narrower),
        con_h=(far, convolver),
        wid_h=(far, widener),
    )
    outputs = dict(
        out_h=(far, shape((ROWS, CHANNELS), BF)),
        grad_h=(far, shape((ROWS, CHANNELS), BF)),
        g_red=(far, shape((wide, INNER), F32)),
        g_off=(far, shape((24, taps * INNER), F32)),
        g_def=(far, shape((deep, INNER), F32)),
        g_exp=(far, shape((wide, INNER), F32)),
        g_nar=(far, shape((wide, INNER), F32)),
        g_con=(far, shape((deep, INNER), F32)),
        g_wid=(far, shape((wide, INNER), F32)),
        g_ig=(vmem, shape((4, INNER), F32)),
        g_ib=(vmem, shape((4, INNER), F32)),
        g_bg=(vmem, shape((2, CHANNELS), F32)),
        g_bb=(vmem, shape((2, CHANNELS), F32)),
        far_blocks=(far, shape((4, chips, ROWS, INNER), F32)),
        far_columns=(far, shape((2, taps, chips * ROWS, INNER), BF)),
    )
    names = list(inputs) + list(outputs) + list(buffers)
    outs = pl.pallas_call(
        functools.partial(kernel, dp, outer, names),
        out_shape=[spec for _, spec in outputs.values()],
        in_specs=[space for space, _ in inputs.values()],
        out_specs=[space for space, _ in outputs.values()],
        scratch_shapes=list(buffers.values()),
        compiler_params=pltpu.CompilerParams(
            collective_id=0, has_side_effects=True, vmem_limit_bytes=63 * 1024 * 1024
        ),
        name="chain",
    )(*[value for _, value in inputs.values()])
    held = dict(zip(outputs, outs))
    big = dict(
        out=held["out_h"],
        grad=held["grad_h"],
        red=held["g_red"],
        **{"def": held["g_def"]},
        exp=held["g_exp"],
        nar=held["g_nar"],
        con=held["g_con"],
        wid=held["g_wid"],
    )
    small = {name: held[name] for name in ("g_off", "g_ig", "g_ib", "g_bg", "g_bb")}
    firsts = {"from_" + name: value for name, value in big.items()}
    finals = {"to_" + name: shape(value.shape, value.dtype) for name, value in big.items()}
    holds = {"hold_" + name: pltpu.VMEM(value.shape, value.dtype) for name, value in big.items()}
    lasts = dict(
        to_off=shape((OFFSETS, deep), F32),
        to_ig=shape((4, INNER // dp), F32),
        to_ib=shape((4, INNER // dp), F32),
        to_bg=shape((2, CHANNELS // dp), F32),
        to_bb=shape((2, CHANNELS // dp), F32),
    )
    names = [*firsts, *small, *finals, *lasts, *holds, "sems"]
    got = pl.pallas_call(
        functools.partial(deliver, dp, names),
        out_shape=[*finals.values(), *lasts.values()],
        in_specs=[far] * len(firsts) + [vmem] * len(small),
        out_specs=[far] * len(finals) + [vmem] * len(lasts),
        scratch_shapes=[*holds.values(), pltpu.SemaphoreType.DMA((2, len(big)))],
        compiler_params=pltpu.CompilerParams(vmem_limit_bytes=60 * 1024 * 1024),
        name="deliver",
    )(*firsts.values(), *small.values())
    out, grad, g_red, g_def, g_exp, g_nar, g_con, g_wid, g_off, *others = got
    return (
        out.reshape(SLOTS, PIXELS, CHANNELS),
        grad.reshape(SLOTS, PIXELS, CHANNELS),
        g_red,
        g_off.T,
        g_def,
        g_exp,
        g_nar,
        g_con,
        g_wid,
        *others,
    )


def solution(mesh):
    spread = P(("dp", "outer"), None, None)
    in_specs = (spread, P(), P(("dp", "outer")), spread) + (P(),) * 11
    out_specs = (spread, spread) + (P("dp", None),) * 7 + (P(None, "dp"),) * 4
    return jax.shard_map(
        per_device, mesh=mesh, in_specs=in_specs, out_specs=out_specs, check_vma=False
    )
```

```python
import functools
import math
import types

import jax
import jax.numpy as jnp
from jax import lax
from jax.experimental import pallas as pl
from jax.experimental.pallas import tpu as pltpu
from jax.sharding import PartitionSpec as P

CHANNELS = 2048
INNER = 512
TAPS = 9
SLOTS = 2
SHORT = 4
LONG = 36
PIXELS = 144
ROWS = SLOTS * PIXELS
OFFSETS = 2 * TAPS
EPS = 1e-05
BF = jnp.bfloat16
F32 = jnp.float32
MESH = pl.DeviceIdType.MESH
NN = (((1,), (0,)), ((), ()))
NT = (((1,), (1,)), ((), ()))
TN = (((0,), (0,)), ((), ()))


def mm(left, right, dims):
    return lax.dot_general(left, right, dims, preferred_element_type=F32)


def sigmoid(value):
    return 0.5 * jnp.tanh(0.5 * value) + 0.5


def fold(value):
    return jnp.sum(value.reshape(value.shape[0] // 8, 8, value.shape[1]), axis=0)


def total_row(value):
    return jnp.sum(value, axis=0, keepdims=True)


def layout(dp):
    chips = dp // 2
    bits = chips.bit_length() - 1
    wide = CHANNELS // dp
    deep = TAPS * INNER // dp
    taps = max(
        -(-(2 * deep * chip % INNER + 2 * deep) // INNER) for chip in range(chips)
    )
    return chips, bits, wide, deep, taps


def scratch(dp, outer):
    vmem = pltpu.VMEM
    dma = pltpu.SemaphoreType.DMA
    chips, bits, wide, deep, taps = layout(dp)
    everyone = dp * outer
    group = min(chips, 4)
    return dict(
        images=vmem((ROWS, CHANNELS), BF),
        between=vmem((ROWS, CHANNELS), BF),
        dwide=vmem((ROWS, CHANNELS), BF),
        obuf=vmem((ROWS, CHANNELS), BF),
        redwid=vmem((CHANNELS, INNER), BF),
        exp=vmem((CHANNELS, INNER), BF),
        nar=vmem((CHANNELS, INNER), BF),
        dfmcon=vmem((TAPS * INNER, INNER), BF),
        off=vmem((OFFSETS, TAPS * INNER), BF),
        a1=vmem((ROWS, INNER), F32),
        a2=vmem((ROWS, INNER), F32),
        b1=vmem((ROWS, INNER), F32),
        b2=vmem((ROWS, INNER), F32),
        acc=vmem((ROWS, INNER), F32),
        a3=vmem((CHANNELS // 512, ROWS, 512), F32),
        b3=vmem((CHANNELS // 512, ROWS, 512), F32),
        up=vmem((CHANNELS // 512, ROWS, 512), F32),
        inner=vmem((ROWS, INNER), BF),
        hidden=vmem((ROWS, INNER), BF),
        narrow=vmem((ROWS, INNER), BF),
        mixed=vmem((ROWS, INNER), BF),
        dn=vmem((ROWS, INNER), BF),
        turned=vmem((ROWS, INNER), BF),
        wmat=vmem((SLOTS, TAPS, PIXELS, PIXELS), BF),
        tmat=vmem((2, TAPS, PIXELS, PIXELS), BF),
        geo=vmem((2, 2, PIXELS, PIXELS), jnp.int32),
        frac=vmem((ROWS, OFFSETS), F32),
        doff=vmem((ROWS, OFFSETS), F32),
        stn=vmem((4, 2, INNER), F32),
        stw=vmem((2, 2, CHANNELS), F32),
        rxn=vmem((8, everyone, 2, INNER), F32),
        rxw1=vmem((4, dp, 2, CHANNELS), F32),
        rxw2=vmem((4, outer, 2, CHANNELS), F32),
        pool=vmem((3, chips, wide, INNER), F32),
        corel=vmem((chips, wide, INNER), F32),
        land=vmem((2, 2, chips - 1, wide, INNER // 2), F32),
        zwide=vmem((3, 3, wide, INNER), F32),
        tiny=vmem((2, chips, SLOTS, 24, PIXELS), F32),
        give=vmem((ROWS, INNER), F32),
        taken=vmem((group, ROWS, INNER), F32),
        drawn=vmem((ROWS, INNER), F32),
        yall=vmem((group * ROWS, INNER), BF),
        xall=vmem((2, group * ROWS, INNER), BF),
        grad=vmem((taps * INNER, INNER), F32),
        cored=vmem((deep, INNER), F32),
        zdeep=vmem((2, 2, deep // 2, INNER), F32),
        goff=vmem((24, taps * INNER), F32),
        coreo=vmem((24, taps * INNER), F32),
        zoff=vmem((2, 24, taps * INNER), F32),
        free=pltpu.SemaphoreType.REGULAR,
        credit=pltpu.SemaphoreType.REGULAR((2, bits)),
        swapped=pltpu.SemaphoreType.REGULAR,
        load_sem=dma((11,)),
        out_sem=dma((2,)),
        res_sem=dma((7, 4)),
        xn_s=dma((8,)),
        xn_r=dma((8,)),
        xw_s=dma((4, 2)),
        xw_r=dma((4, 2)),
        core_s=dma((7,)),
        core_r=dma((7,)),
        step_s=dma((4, 2, bits)),
        step_r=dma((4, 2, bits)),
        give_sem=dma((4,)),
        take_sem=dma((3,)),
        x_sem=dma((2,)),
        ag_s=dma((4, 2, bits)),
        ag_r=dma((4, 2, bits)),
        tiny_s=dma((2,)),
        tiny_r=dma((2,)),
        z_s=dma((7, 4, 3)),
        z_r=dma((7, 4, 3)),
    )


def kernel(dp, outer, names, *refs):
    assert outer == 4
    r = types.SimpleNamespace(**dict(zip(names, refs)))
    chips, bits, wide, deep, taps = layout(dp)
    everyone = dp * outer
    me = lax.axis_index("dp")
    mine = lax.axis_index("outer")
    own = me * outer + mine
    core = lax.rem(me, 2)
    chip = lax.div(me, 2)
    sibling = (me + 1 - 2 * core, mine)
    inside = (mine == 1) | (mine == 2)
    outside = (mine == 0) | (mine == 3)
    counts, orient = r.counts, r.orient
    dma = pltpu.make_async_copy

    loads = types.SimpleNamespace()

    def load(place, source, target):
        copy = dma(source, target, r.load_sem.at[place])
        copy.start()
        return copy

    loads.images_h = load(0, r.images_h, r.images)
    loads.red_h = load(1, r.red_h, r.redwid)
    loads.off_h = load(2, r.off_h, r.off)
    loads.def_h = load(3, r.def_h, r.dfmcon)
    loads.exp_h = load(4, r.exp_h, r.exp)
    loads.nar_h = load(5, r.nar_h, r.nar)
    loads.cot_h = load(6, r.cot_h, r.dwide)

    def other(step):
        target = lax.rem(own + step, everyone)
        return lax.div(target, outer), lax.rem(target, outer)

    barrier = pltpu.get_barrier_semaphore()

    def greet(step, carry):
        pl.semaphore_signal(barrier, inc=1, device_id=other(step), device_id_type=MESH)
        return carry

    lax.fori_loop(1, everyone, greet, 0)

    def size(i, carry):
        sizes, near, far = carry
        row, place = lax.div(i, outer), lax.rem(i, outer)
        held = counts[i].astype(F32)
        here = jnp.where(place == mine, held, 0.0)

        def mark(count, at, value):
            line = lax.broadcasted_iota(jnp.int32, (count, 1), 0)
            return jnp.where(line == at, value, 0.0)

        return (
            sizes + mark(everyone, i, held),
            near + mark(dp, row, here),
            far + mark(outer, place, held),
        )

    zeros = tuple(jnp.zeros((count, 1), F32) for count in (everyone, dp, outer))
    sizes, near, far = (
        value * float(PIXELS) for value in lax.fori_loop(0, everyone, size, zeros)
    )
    near_total = total_row(near)
    total = total_row(far)
    held = counts[own].astype(F32)
    live1 = held - 1.0
    local = held * float(PIXELS)

    def sweep(body, init):
        def step(i, carry):
            lv = jnp.where(i < 3, 1.0, live1)
            for j in range(3):
                carry = body(pl.ds(pl.multiple_of(i * 48 + j * 16, 16), 16), lv, carry)
            return carry

        return lax.fori_loop(0, 6, step, init, unroll=2)

    def send(source, target, sent, received, device):
        pltpu.make_async_remote_copy(
            src_ref=source,
            dst_ref=target,
            send_sem=sent,
            recv_sem=received,
            device_id=device,
            device_id_type=MESH,
        ).start()

    def settle(view, sem):
        dma(view, view, sem).wait()

    waiting = {}

    def later(tag, view, sem, when=None):
        waiting.setdefault(tag, []).append((when, view, sem))

    def flush(tag):
        for when, view, sem in waiting.pop(tag, []):
            if when is None:
                settle(view, sem)
            else:
                pl.when(when)(functools.partial(settle, view, sem))

    def accumulate(target, source):
        rows = target.shape[0]
        step = math.gcd(rows, 32)

        def body(i, carry):
            rs = pl.ds(pl.multiple_of(i * step, 8), step)
            target[rs, :] += source[rs, :]
            return carry

        count = rows // step
        lax.fori_loop(0, count, body, 0, unroll=math.gcd(count, 3) if count % 2 else 2)

    def mix(target, one, two):
        rows = target.shape[0]
        step = math.gcd(rows, 32)

        def body(i, carry):
            rs = pl.ds(pl.multiple_of(i * step, 8), step)
            target[rs, :] = one[rs, :] + two[rs, :]
            return carry

        count = rows // step
        lax.fori_loop(0, count, body, 0, unroll=math.gcd(count, 3) if count % 2 else 2)

    def flip(value, bit):
        weight = 1 << bit
        return value + weight - 2 * weight * lax.rem(lax.div(value, weight), 2)

    def bit_of(value, bit):
        return lax.rem(lax.div(value, 1 << bit), 2)

    orders = [
        list(range(bits)),
        list(range(bits // 2, bits)) + list(range(bits // 2)),
    ]
    halves = [pl.ds(0, INNER // 2), pl.ds(INNER // 2, INNER // 2)]

    def merge(rx, counted, size, forward):
        first = rx[:, 0, :]
        second = rx[:, 1, :]
        if forward:
            summed = total_row(first)
            apart = first / counted - summed / size
            spread = total_row(second + counted * apart * apart)
            return jnp.concatenate([summed, spread], axis=0)
        return jnp.concatenate([total_row(first), total_row(second)], axis=0)

    def nothing():
        pass

    def share_narrow(number, forward, work):
        rx = r.rxn.at[number]

        def step(i, carry):
            line, part = lax.div(i, dp), lax.rem(i, dp)
            z = jnp.where(mine < outer // 2, outer - 1 - line, line)
            peer = 0
            for bit in range(bits + 1):
                here, turn = bit_of(me, bit), 1 - bit_of(part, bit)
                peer = peer + (here + turn - 2 * here * turn) * (1 << bit)

            @pl.when(peer * outer + z != own)
            def _():
                send(rx.at[own], rx.at[own], r.xn_s.at[number], r.xn_r.at[number], (peer, z))

            return carry

        lax.fori_loop(0, everyone, step, 0)
        rest = rx.at[pl.ds(0, everyone - 1)]
        later("end", rest, r.xn_s.at[number])
        work()
        settle(rest, r.xn_r.at[number])
        return merge(rx, sizes, total, forward)

    def share_wide(number, forward, work, work_more):
        rx1, rx2 = r.rxw1.at[number], r.rxw2.at[number]
        for turn in range(dp - 1, 0, -1):
            peer = me
            for bit in range(bits + 1):
                if (turn >> bit) & 1:
                    peer = flip(peer, bit)
            send(rx1.at[me], rx1.at[me], r.xw_s.at[number, 0], r.xw_r.at[number, 0], (peer, mine))
        rest = rx1.at[pl.ds(0, dp - 1)]
        later("end", rest, r.xw_s.at[number, 0])
        work()
        settle(rest, r.xw_r.at[number, 0])
        rx2[mine] = merge(rx1, near, near_total, forward)
        for line in range(outer):
            z = jnp.where(mine < outer // 2, outer - 1 - line, line)

            @pl.when(z != mine)
            def _():
                send(
                    rx2.at[mine],
                    rx2.at[mine],
                    r.xw_s.at[number, 1],
                    r.xw_r.at[number, 1],
                    (me, z),
                )

        rest = rx2.at[pl.ds(0, outer - 1)]
        later("end", rest, r.xw_s.at[number, 1])
        work_more()
        settle(rest, r.xw_r.at[number, 1])
        return merge(rx2, far, total, forward)

    def local_stats(ref, put, cs):
        zero = jnp.zeros((8, 512), F32)
        summed = total_row(sweep(lambda rs, lv, c: c + lv * fold(ref[rs, :]), zero))
        mean = summed / local

        def squares(rs, lv, carry):
            apart = ref[rs, :] - mean
            return carry + lv * fold(apart * apart)

        put[0:1, cs] = summed
        put[1:2, cs] = total_row(sweep(squares, zero))

    def keep_stats(both, st):
        st[0:1, :] = both[0:1] / total
        st[1:2, :] = lax.rsqrt(both[1:2] / total + EPS)

    def narrow_stats(ref, number, work=nothing):
        local_stats(ref, r.rxn.at[number, own], pl.ds(0, INNER))
        keep_stats(share_narrow(number, True, work), r.stn.at[number])

    blocks = [pl.ds(start, 512) for start in range(0, CHANNELS, 512)]

    def wide_stats(ref, number, work=nothing, work_more=nothing):
        for n, cs in enumerate(blocks):
            local_stats(ref.at[n], r.rxw1.at[number, me], cs)
        keep_stats(share_wide(number, True, work, work_more), r.stw.at[number])

    def norm_silu(ref, number, gain, bias, out, spread):
        st = r.stn.at[number]
        mean, scale = st[0:1, :], st[1:2, :]
        steep = scale * gain

        def body(rs, lv, carry):
            z = (ref[rs, :] - mean) * steep + bias
            value = (z * sigmoid(z)).astype(BF)
            out[rs, :] = value
            if spread:
                r.give[rs, :] = value.astype(F32)
            return carry

        sweep(body, 0)

    def narrow_cotangent(ref, place, gain, bias, number, spread, work=nothing):
        acc = r.acc
        st = r.stn.at[place]
        mean, scale = st[0:1, :], st[1:2, :]

        def body(rs, lv, carry):
            xhat = (ref[rs, :] - mean) * scale
            z = xhat * gain + bias
            sg = sigmoid(z)
            g = acc[rs, :] * (sg * (1.0 + z * (1.0 - sg)))
            acc[rs, :] = g
            return carry[0] + fold(g), carry[1] + fold(g * xhat)

        zero = jnp.zeros((8, INNER), F32)
        summed, paired = sweep(body, (zero, zero))
        put = r.rxn.at[number, own]
        put[0:1, :] = total_row(summed)
        put[1:2, :] = total_row(paired)
        both = share_narrow(number, False, work)
        r.g_ib[place : place + 1, :] = both[0:1]
        r.g_ig[place : place + 1, :] = both[1:2]
        steep = scale * gain
        lift, tilt = both[0:1] / total, both[1:2] / total

        def back(rs, lv, carry):
            xhat = (ref[rs, :] - mean) * scale
            value = (steep * (acc[rs, :] - lv * (lift + xhat * tilt))).astype(BF)
            r.dn[rs, :] = value
            if spread:
                r.give[rs, :] = value.astype(F32)
            return carry

        sweep(back, 0)

    def wide_cotangent(number, ref, place, gain, bias, cotangent, work=nothing, work_more=nothing):
        put = r.rxw1.at[number, me]
        st = r.stw.at[place]
        for n, cs in enumerate(blocks):
            mean, scale = st[0:1, cs], st[1:2, cs]
            gn, bs = gain[:, 512 * n : 512 * n + 512], bias[:, 512 * n : 512 * n + 512]

            def body(rs, lv, carry):
                xhat = (ref[n, rs, :] - mean) * scale
                g = cotangent(n, rs, cs, lv, xhat * gn + bs)
                r.up[n, rs, :] = g
                return carry[0] + fold(g), carry[1] + fold(g * xhat)

            zero = jnp.zeros((8, 512), F32)
            summed, paired = sweep(body, (zero, zero))
            put[0:1, cs] = total_row(summed)
            put[1:2, cs] = total_row(paired)
        both = share_wide(number, False, work, work_more)
        r.g_bb[place : place + 1, :] = both[0:1]
        r.g_bg[place : place + 1, :] = both[1:2]
        for n, cs in enumerate(blocks):
            mean, scale = st[0:1, cs], st[1:2, cs]
            span = slice(512 * n, 512 * n + 512)
            steep = scale * gain[:, span]
            lift, tilt = both[0:1, span] / total, both[1:2, span] / total

            def back(rs, lv, carry):
                xhat = (ref[n, rs, :] - mean) * scale
                value = steep * (r.up[n, rs, :] - lv * (lift + xhat * tilt))
                r.dwide[rs, cs] = value.astype(BF)
                return carry

            sweep(back, 0)

    def tap(ref, k):
        return ref[pl.ds(pl.multiple_of(k * INNER, INNER), INNER), :]

    def offset_tap(k):
        return r.off[:, pl.ds(pl.multiple_of(k * INNER, INNER), INNER)]

    def slot_rows(s):
        return pl.ds(s * PIXELS, PIXELS)

    def steps_of(k):
        return 2 * lax.div(k, 3) - 2, 2 * lax.rem(k, 3) - 2

    WID, CON, NAR, EXP, DEF, RED, OFF = range(7)
    nth = {WID: 0, NAR: 1, EXP: 2, RED: 3}
    result = {
        WID: r.g_wid,
        CON: r.g_con,
        NAR: r.g_nar,
        EXP: r.g_exp,
        DEF: r.g_def,
        RED: r.g_red,
        OFF: r.g_off,
    }
    pool, land, grad, far_blocks = r.pool, r.land, r.grad, r.far_blocks

    deep_parts = 4 if deep % 32 == 0 else 2
    wide_parts = {WID: 2, NAR: 2, EXP: 2, RED: 4}

    def z_hold(u):
        if u == RED:
            return [r.a3.at[i, pl.ds(0, wide)] for i in range(3)]
        return [r.zwide.at[nth[u], i] for i in range(3)]

    def z_parts(u):
        if u in nth:
            hold = z_hold(u)
            for q in range(wide_parts[u]):
                rows = wide // (wide_parts[u] // 2)
                rs, hs = pl.ds(q // 2 * rows, rows), halves[q % 2]
                yield tuple(ref.at[rs, hs] for ref in hold) + (result[u].at[rs, hs],)
        elif u == OFF:
            yield r.goff, r.zoff.at[0], r.zoff.at[1], result[u]
        else:
            for q in range(deep_parts):
                back, at = divmod(q, deep_parts // 2)
                source = r.b3.at[(2 if u == DEF else 0) + back]
                if u == DEF:
                    first, second = (r.b1, r.a2) if back == 0 else (r.b2, r.a3.at[3])
                else:
                    first, second = r.zdeep.at[0, back], r.zdeep.at[1, back]
                size = deep // deep_parts
                rows = pl.ds(at * size, size)
                out = result[u].at[pl.ds(q * size, size)]
                yield source.at[rows], first.at[rows], second.at[rows], out

    def z_sems(u, q, step):
        return r.z_s.at[u, q, step], r.z_r.at[u, q, step]

    def z1(u, some=None):
        for q, (source, first, second, out) in enumerate(z_parts(u)):
            if some is not None and q not in some:
                continue
            sent, received = z_sems(u, q, 0)

            @pl.when(outside)
            def _():
                send(source, first, sent, received, (me, flip(mine, 0)))

            later(("z", u), source, sent, outside)

    def z2(u, some=None):
        for q, (source, first, second, out) in enumerate(z_parts(u)):
            if some is not None and q not in some:
                continue
            sent, received = z_sems(u, q, 1)

            @pl.when(inside)
            def _():
                settle(first, z_sems(u, q, 0)[1])
                accumulate(source, first)
                send(source, second, sent, received, (me, 3 - mine))

            later(("z", u), source, sent, inside)

    def z3(u, some=None):
        for q, (source, first, second, out) in enumerate(z_parts(u)):
            if some is not None and q not in some:
                continue
            sent, received = z_sems(u, q, 2)

            @pl.when(inside)
            def _():
                settle(second, z_sems(u, q, 1)[1])
                accumulate(second, source)
                send(second, first, sent, received, (me, flip(mine, 0)))
                dma(second, out, r.res_sem.at[u, q]).start()

            later(("zl", u), second, sent, inside)

    def z4(u, some=None):
        for q, (source, first, second, out) in enumerate(z_parts(u)):
            if some is not None and q not in some:
                continue

            @pl.when(outside)
            def _():
                settle(first, z_sems(u, q, 2)[1])
                dma(first, out, r.res_sem.at[u, q]).start()

    def z_clear(u):
        flush(("z", u))
        flush(("zl", u))
        for q, (source, first, second, out) in enumerate(z_parts(u)):
            dma(first, out, r.res_sem.at[u, q]).wait()

    def wide_begin(u, left, right):
        p = nth[u] % 2
        flush("sib")
        flush(("keep", p))
        low = p + (2 - p) * core
        high = p + (2 - p) * (1 - core)
        if u == EXP:
            pl.semaphore_wait(r.swapped, 1)

        def step(m, carry):
            block = left[:, pl.ds(pl.multiple_of(m * (2 * wide), 2 * wide), 2 * wide)]
            pool[low, m] = mm(block[:, :wide], right[...], TN)
            pool[high, m] = mm(block[:, wide:], right[...], TN)
            send(
                pool.at[2, m], r.corel.at[m], r.core_s.at[u], r.core_r.at[u], sibling
            )
            return carry

        lax.fori_loop(0, chips, step, 0)
        later("sib", r.corel, r.core_s.at[u])

    def piece(h, t, j, toward):
        value = 0
        for i, bit in enumerate(orders[h]):
            if i < t:
                part = bit_of(chip, bit)
            elif i == t:
                part = bit_of(toward, bit)
            else:
                part = (j >> (i - t - 1)) & 1
            value = value + part * (1 << bit)
        return value

    def step_place(u, h, t):
        first, count = chips - (chips >> t), chips >> (t + 1)
        p = nth[u] % 2
        sems = r.step_s.at[nth[u], h, t], r.step_r.at[nth[u], h, t]
        return p, first, count, sems, land.at[p, h, pl.ds(first, count)]

    def wide_send(u, t):
        for h in range(2):
            p, first, count, (sent, received), region = step_place(u, h, t)
            toward = flip(chip, orders[h][t])
            if u == RED:
                pl.semaphore_wait(r.credit.at[h, t], 1)
            for j in range(count):
                send(
                    pool.at[p, piece(h, t, j, toward), :, halves[h]],
                    land.at[p, h, first + j],
                    sent,
                    received,
                    (2 * toward + core, mine),
                )
            later(("keep", p), region, sent)

    def wide_add(u, t):
        for h in range(2):
            p, first, count, (sent, received), region = step_place(u, h, t)
            settle(region, received)
            if t == bits - 1:
                mix(z_hold(u)[0].at[:, halves[h]], pool.at[p, chip, :, halves[h]], land.at[p, h, first])
            else:
                for j in range(count):
                    accumulate(
                        pool.at[p, piece(h, t, j, chip), :, halves[h]], land.at[p, h, first + j]
                    )
            if u == NAR:
                pl.semaphore_signal(
                    r.credit.at[h, t],
                    inc=1,
                    device_id=(2 * flip(chip, orders[h][t]) + core, mine),
                    device_id_type=MESH,
                )

    def wide_core(u):
        p = nth[u] % 2
        settle(r.corel, r.core_r.at[u])

        def step(m, carry):
            accumulate(pool.at[p, m], r.corel.at[m])
            return carry

        lax.fori_loop(0, chips, step, 0)
        if u == NAR:
            pl.semaphore_signal(r.swapped, inc=1, device_id=sibling, device_id_type=MESH)

    def wide_step(u, t):
        wide_add(u, t - 1)
        if t < bits:
            wide_send(u, t)
        else:
            z1(u)

    def held_at(h, j):
        value = chip
        for i in range(bits):
            if (j >> i) & 1:
                value = flip(value, orders[h][i])
        return value

    def gather_send(a, t, some=None):
        for h in range(2):
            partner = flip(chip, orders[h][t])
            sent, received = r.ag_s.at[a, h, t], r.ag_r.at[a, h, t]
            for j in range(1 << t) if some is None else some:
                block = far_blocks.at[a, held_at(h, j), :, halves[h]]
                source = r.give.at[:, halves[h]] if j == 0 else block
                send(source, block, sent, received, (2 * partner + core, mine))
            if some is None or 0 in some:
                later(("ag", a), far_blocks.at[a, pl.ds(0, 1 << t), :, halves[h]], sent)

    def gather_start(a):
        block = far_blocks.at[a, chip]
        dma(r.give, block, r.give_sem.at[a]).start()
        later(("ag", a), block, r.give_sem.at[a])
        gather_send(a, 0)

    def gather_wait(a, t):
        for h in range(2):
            settle(far_blocks.at[a, pl.ds(0, 1 << t), :, halves[h]], r.ag_r.at[a, h, t])

    def gather_step(a, t, some=None):
        gather_wait(a, t - 1)
        gather_send(a, t, some)

    def gather_first(a, t):
        if t < bits:
            gather_send(a, t, [0])

    def gather_rest(a):
        for t in range(1, bits):
            gather_wait(a, t - 1)
            gather_send(a, t, range(1 if t == 1 else 0, 1 << t))

    def gather_end(a):
        gather_wait(a, bits - 1)
        flush(("ag", a))

    def tiny_send(a):
        for step in range(1, chips):
            block = r.tiny.at[a, chip]
            peer = lax.rem(chip + step, chips)
            send(block, block, r.tiny_s.at[a], r.tiny_r.at[a], (2 * peer + core, mine))
        later("end", r.tiny.at[a, pl.ds(0, chips - 1)], r.tiny_s.at[a])

    def tiny_wait(a):
        settle(r.tiny.at[a, pl.ds(0, chips - 1)], r.tiny_r.at[a])

    group = min(chips, 4)
    first_tap = lax.div(2 * deep * chip, INNER)
    margin = 2 * deep * chip - first_tap * INNER

    def taps_of(kk):
        k = jnp.minimum(first_tap + kk, TAPS - 1)
        return (k, *steps_of(k))

    def fetch_fields(a, g):
        copy = dma(far_blocks.at[a, pl.ds(g * group, group)], r.taken, r.take_sem.at[2])
        copy.start()
        copy.wait()

    def image_of(i, g):
        m, s = lax.div(i, SLOTS), lax.rem(i, SLOTS)
        rows = pl.ds(pl.multiple_of(i * PIXELS, PIXELS), PIXELS)
        field = r.taken[m, pl.ds(pl.multiple_of(s * PIXELS, PIXELS), PIXELS), :].astype(BF)
        flat = r.tiny[0, g * group + m, s, 18:19, :] == 0.0
        dr = jnp.where(flat, r.geo[0, 0], r.geo[1, 0])
        dc = jnp.where(flat, r.geo[0, 1], r.geo[1, 1])
        return g * group + m, s, rows, field, dr, dc

    def group_rows(g):
        return pl.ds(g * (group * ROWS), group * ROWS)

    def columns(u, kk):
        x = 1 if u == DEF else 0
        k, down, across = taps_of(kk)
        for g in range(chips // group):
            if kk == 0 or chips > group:
                fetch_fields(0 if u == DEF else 1, g)
            if g == 0:
                flush("columns")

            def image(i, carry):
                m, s, rows, field, dr, dc = image_of(i, g)
                if u == CON:
                    hit = jnp.where((dr == down) & (dc == across), 1.0, 0.0).astype(BF)
                    r.xall[0, rows, :] = mm(hit, field, NN).astype(BF)
                    return carry
                tiny = r.tiny.at[0, m, s]
                fy, fx = tiny[pl.ds(2 * k, 1), :], tiny[pl.ds(2 * k + 1, 1), :]
                ay = jnp.where(dr == -down, 1.0 - fy, jnp.where(dr == -down - 1, fy, 0.0))
                ax = jnp.where(dc == -across, 1.0 - fx, jnp.where(dc == -across - 1, fx, 0.0))
                r.xall[0, rows, :] = mm((ay * ax).astype(BF), field, TN).astype(BF)
                return carry

            lax.fori_loop(0, group * SLOTS, image, 0, unroll=4)
            place = r.far_columns.at[x, kk, group_rows(g)]
            copy = dma(r.xall.at[0], place, r.x_sem.at[0])
            copy.start()
            if g + 1 < chips // group:
                copy.wait()
            else:
                later("columns", place, r.x_sem.at[0])

    def deep_make(u):
        flush("deep")
        flush("columns")
        x, back_of = (1, 3) if u == DEF else (0, 2)
        slots = (r.give, r.drawn)
        for g in range(chips // group):

            def fetch(m):
                return dma(far_blocks.at[back_of, g * group + m], slots[m % 2], r.take_sem.at[m % 2])

            def draw(kk):
                slot = lax.rem(kk, 2)
                return dma(
                    r.far_columns.at[x, kk, group_rows(g)], r.xall.at[slot], r.x_sem.at[slot]
                )

            for m in range(min(2, group)):
                fetch(m).start()
            draw(0).start()
            for m in range(group):
                fetch(m).wait()

                def lower(i, carry):
                    rows = pl.ds(pl.multiple_of(m * ROWS + i * 32, 32), 32)
                    there = pl.ds(pl.multiple_of(i * 32, 32), 32)
                    r.yall[rows, :] = slots[m % 2][there, :].astype(BF)
                    return carry

                lax.fori_loop(0, ROWS // 32, lower, 0, unroll=3)
                if m + 2 < group:
                    fetch(m + 2).start()

            def one(kk, carry):
                @pl.when(kk + 1 < taps)
                def _():
                    draw(kk + 1).start()

                draw(kk).wait()
                at = pl.ds(pl.multiple_of(kk * INNER, INNER), INNER)
                part = mm(r.xall[lax.rem(kk, 2)], r.yall[...], TN)
                if g == 0:
                    grad[at, :] = part
                else:
                    grad[at, :] += part
                return carry

            lax.fori_loop(0, taps, one, 0)
        away = pl.ds(pl.multiple_of(margin + (1 - core) * deep, 8), deep)
        send(grad.at[away], r.cored, r.core_s.at[u], r.core_r.at[u], sibling)
        later("deep", r.cored, r.core_s.at[u])

    def off_make():
        for g in range(chips // group):
            fetch_fields(0, g)

            def one(kk, carry):
                k, down, across = taps_of(kk)

                def image(i, share):
                    m, s, rows, field, dr, dc = image_of(i, g)
                    hit = jnp.where((dr == down) & (dc == across), 1.0, 0.0).astype(BF)
                    moved = mm(r.tiny[1, m, s].astype(BF), hit, NN).astype(BF)
                    return share + mm(moved, field, NN)

                at = pl.ds(pl.multiple_of(kk * INNER, INNER), INNER)
                share = lax.fori_loop(
                    0, group * SLOTS, image, jnp.zeros((24, INNER), F32), unroll=8
                )
                if g == 0:
                    r.goff[:, at] = share
                else:
                    r.goff[:, at] += share
                return carry

            lax.fori_loop(0, taps, one, 0)
        send(r.goff, r.coreo, r.core_s.at[OFF], r.core_r.at[OFF], sibling)

    def off_core():
        settle(r.goff, r.core_s.at[OFF])
        settle(r.coreo, r.core_r.at[OFF])
        accumulate(r.goff, r.coreo)

    def deep_core(u):
        settle(r.cored, r.core_r.at[u])
        half = deep // 2
        step = math.gcd(half, 32)
        for q in range(2):
            target = r.b3.at[(2 if u == DEF else 0) + q]

            def body(i, carry):
                at = pl.multiple_of(i * step, 8)
                here = grad[pl.ds(pl.multiple_of(margin + core * deep + q * half + at, 8), step), :]
                target[pl.ds(at, step), :] = here + r.cored[pl.ds(q * half + at, step), :]
                return carry

            lax.fori_loop(0, half // step, body, 0)
    images, between, acc, up = r.images, r.between, r.acc, r.up
    ig = [r.ig[i : i + 1, :] for i in range(4)]
    ib = [r.ib[i : i + 1, :] for i in range(4)]
    bg = [r.bg[i : i + 1, :] for i in range(2)]
    bb = [r.bb[i : i + 1, :] for i in range(2)]

    def geometry():
        q = lax.broadcasted_iota(jnp.int32, (PIXELS, PIXELS), 1)
        p = lax.broadcasted_iota(jnp.int32, (PIXELS, PIXELS), 0)

        def place_of(at, kind):
            if kind:
                row = lax.shift_right_logical(at, 2)
                return row, at - row * SHORT
            row = (at >= LONG).astype(jnp.int32) + (at >= 2 * LONG).astype(jnp.int32)
            row = row + (at >= 3 * LONG).astype(jnp.int32)
            return row, at - row * LONG

        for kind in range(2):
            row_q, col_q = place_of(q, kind)
            row_p, col_p = place_of(p, kind)
            r.geo[kind, 0] = row_q - row_p
            r.geo[kind, 1] = col_q - col_p

            def hot(k, carry):
                down, across = steps_of(k)
                hit = (r.geo[kind, 0] == down) & (r.geo[kind, 1] == across)
                r.tmat[kind, k] = jnp.where(hit, 1.0, 0.0).astype(BF)
                return carry

            lax.fori_loop(0, TAPS, hot, 0)

    def shifted(s, k):
        return r.tmat[orient[s], k]

    loads.images_h.wait()
    loads.red_h.wait()
    r.a1[...] = mm(images[...], r.redwid[...], NN)
    loads.wid_h = load(7, r.wid_h, r.redwid)
    pl.semaphore_wait(barrier, everyone - 1)
    narrow_stats(r.a1, 0, geometry)
    norm_silu(r.a1, 0, ig[0], ib[0], r.inner, True)
    gather_start(0)

    loads.off_h.wait()
    inner = r.inner
    lane = lax.broadcasted_iota(jnp.int32, (PIXELS, OFFSETS), 1)

    def gather(k, carry):
        cols = [mm(shifted(s, k), inner[slot_rows(s), :], NN).astype(BF) for s in range(SLOTS)]
        weight = offset_tap(k)
        return tuple(old + mm(col, weight, NT) for old, col in zip(carry, cols))

    zero = jnp.zeros((PIXELS, OFFSETS), F32)
    both_offsets = lax.fori_loop(0, TAPS, gather, (zero,) * SLOTS, unroll=3)
    for s in range(SLOTS):
        frac = sigmoid(both_offsets[s])
        r.frac[slot_rows(s), :] = frac
        coarse = frac.astype(BF)
        fine = (frac - coarse.astype(F32)).astype(BF)
        unit = r.tmat[0, TAPS // 2]
        put = r.tiny.at[0, chip, s]
        put[...] = jnp.zeros((24, PIXELS), F32) + orient[s].astype(F32)
        put[0:OFFSETS, :] = mm(coarse, unit, TN) + mm(fine, unit, TN)
    tiny_send(0)

    def bilinear(s, k):
        down, across = steps_of(k)
        frac = r.frac[slot_rows(s), :]
        fy = jnp.sum(jnp.where(lane == 2 * k, frac, 0.0), axis=1, keepdims=True)
        fx = jnp.sum(jnp.where(lane == 2 * k + 1, frac, 0.0), axis=1, keepdims=True)
        dr, dc = r.geo[orient[s], 0], r.geo[orient[s], 1]
        in_y = (dr == down, dr == down + 1)
        in_x = (dc == across, dc == across + 1)
        ay = jnp.where(in_y[0], 1.0 - fy, jnp.where(in_y[1], fy, 0.0))
        ax = jnp.where(in_x[0], 1.0 - fx, jnp.where(in_x[1], fx, 0.0))
        return fy, fx, ay, ax, in_y, in_x

    loads.def_h.wait()
    acc[...] = jnp.zeros((ROWS, INNER), F32)

    def sample(k, carry):
        for s in range(SLOTS):
            _, _, ay, ax, _, _ = bilinear(s, k)
            weight = (ay * ax).astype(BF)
            r.wmat[s, k] = weight
            r.turned[slot_rows(s), :] = mm(weight, inner[slot_rows(s), :], NN).astype(BF)
        acc[...] += mm(r.turned[...], tap(r.dfmcon, k), NN)
        return carry

    lax.fori_loop(0, TAPS, sample, 0, unroll=3)
    loads.con_h = load(8, r.con_h, r.dfmcon)
    r.a2[...] = acc[...]
    narrow_stats(r.a2, 1, lambda: gather_first(0, 1))
    norm_silu(r.a2, 1, ig[1], ib[1], r.hidden, False)

    def widen(source, weight, target):
        def step(n, carry):
            rows = pl.ds(pl.multiple_of(n * 512, 512), 512)
            target[n] = mm(source[...], weight[rows, :], NT)
            return carry

        lax.fori_loop(0, CHANNELS // 512, step, 0, unroll=2)

    loads.exp_h.wait()
    widen(r.hidden, r.exp, r.a3)
    wide_stats(r.a3, 0, lambda: gather_rest(0))
    for n, cs in enumerate(blocks):
        mean = r.stw[0, 0:1, cs]
        steep = r.stw[0, 1:2, cs] * bg[0][:, 512 * n : 512 * n + 512]
        bias = bb[0][:, 512 * n : 512 * n + 512]

        def join(rs, lv, carry):
            z = (r.a3[n, rs, :] - mean) * steep + bias + images[rs, cs].astype(F32)
            between[rs, cs] = (z * sigmoid(z)).astype(BF)
            return carry

        sweep(join, 0)

    loads.nar_h.wait()
    r.b1[...] = mm(between[...], r.nar[...], NN)

    def work_b1():
        gather_end(0)
        tiny_wait(0)
        columns(DEF, 0)

    narrow_stats(r.b1, 2, work_b1)
    norm_silu(r.b1, 2, ig[2], ib[2], r.narrow, True)
    gather_start(1)

    loads.con_h.wait()
    acc[...] = jnp.zeros((ROWS, INNER), F32)

    def convolve(k, carry):
        for s in range(SLOTS):
            r.turned[slot_rows(s), :] = mm(
                shifted(s, k), r.narrow[slot_rows(s), :], NN
            ).astype(BF)
        acc[...] += mm(r.turned[...], tap(r.dfmcon, k), NN)
        return carry

    lax.fori_loop(0, TAPS, convolve, 0, unroll=3)
    r.b2[...] = acc[...]
    def work_b2():
        gather_first(1, 1)
        columns(DEF, 1)

    narrow_stats(r.b2, 3, work_b2)
    norm_silu(r.b2, 3, ig[3], ib[3], r.mixed, False)

    loads.wid_h.wait()
    widen(r.mixed, r.redwid, r.b3)

    def work_b3():
        gather_rest(1)
        for kk in range(2, taps):
            columns(DEF, kk)

    wide_stats(r.b3, 1, work_b3)

    loads.cot_h.wait()

    def last(n, rs, cs, lv, pre):
        z = pre + between[rs, cs].astype(F32)
        sg = sigmoid(z)
        r.obuf[rs, cs] = (lv * (z * sg)).astype(BF)
        return r.dwide[rs, cs].astype(F32) * (lv * (sg * (1.0 + z * (1.0 - sg))))

    def work_f():
        gather_end(1)
        columns(CON, 0)

    wide_cotangent(2, r.b3, 1, bg[1], bb[1], last, nothing, work_f)
    out_copy = dma(r.obuf, r.out_h, r.out_sem.at[0])
    out_copy.start()
    wide_begin(WID, r.dwide, r.mixed)
    acc[...] = mm(r.dwide[...], r.redwid[...], NN)
    loads.red_h = load(9, r.red_h, r.redwid)

    def work_e():
        wide_core(WID)
        wide_send(WID, 0)
        columns(CON, 1)

    narrow_cotangent(r.b2, 3, ig[3], ib[3], 4, True, work_e)

    acc[...] = jnp.zeros((ROWS, INNER), F32)

    def spread(k, carry):
        for s in range(SLOTS):
            r.turned[slot_rows(s), :] = mm(
                shifted(s, TAPS - 1 - k), r.dn[slot_rows(s), :], NN
            ).astype(BF)
        acc[...] += mm(r.turned[...], tap(r.dfmcon, k), NT)
        return carry

    lax.fori_loop(0, TAPS, spread, 0, unroll=3)
    loads.def_h = load(10, r.def_h, r.dfmcon)

    def work_d():
        wide_step(WID, 1)
        gather_start(2)
        for kk in range(2, taps):
            columns(CON, kk)

    narrow_cotangent(r.b1, 2, ig[2], ib[2], 5, False, work_d)
    for t in range(2, bits + 1):
        wide_step(WID, t)

    def add_back(n, carry):
        rows = pl.ds(pl.multiple_of(n * 512, 512), 512)
        up[n] += mm(r.dn[...], r.nar[rows, :], NT)
        return carry

    lax.fori_loop(0, CHANNELS // 512, add_back, 0, unroll=2)

    def first(n, rs, cs, lv, pre):
        z = pre + images[rs, cs].astype(F32)
        sg = sigmoid(z)
        return up[n, rs, :] * (sg * (1.0 + z * (1.0 - sg)))

    def work_c():
        for t in range(1, bits):
            gather_step(2, t)
        wide_begin(NAR, between, r.dn)

    def work_more_c():
        z2(WID)
        wide_core(NAR)

    wide_cotangent(3, r.a3, 0, bg[0], bb[0], first, work_c, work_more_c)
    acc[...] = mm(r.dwide[...], r.exp[...], NN)

    def work_b():
        wide_send(NAR, 0)
        wide_begin(EXP, r.dwide, r.hidden)
        gather_end(2)
        deep_make(CON)
        z3(WID)

    narrow_cotangent(r.a2, 1, ig[1], ib[1], 6, True, work_b)
    gather_start(3)
    deep_core(CON)
    early, late = range(deep_parts // 2), range(deep_parts // 2, deep_parts)
    z1(CON, early)

    loads.def_h.wait()
    acc[...] = jnp.zeros((ROWS, INNER), F32)
    r.doff[...] = jnp.zeros((ROWS, OFFSETS), F32)

    def unsample(k, carry):
        r.turned[...] = mm(r.dn[...], tap(r.dfmcon, k), NT).astype(BF)
        for s in range(SLOTS):
            rs = slot_rows(s)
            back = r.turned[rs, :]
            pairs = mm(back, inner[rs, :], NT)
            fy, fx, ay, ax, in_y, in_x = bilinear(s, k)
            slope_y = jnp.where(in_y[1], ax, 0.0) - jnp.where(in_y[0], ax, 0.0)
            slope_x = jnp.where(in_x[1], ay, 0.0) - jnp.where(in_x[0], ay, 0.0)
            to_y = jnp.sum(pairs * slope_y, axis=1, keepdims=True) * (fy * (1.0 - fy))
            to_x = jnp.sum(pairs * slope_x, axis=1, keepdims=True) * (fx * (1.0 - fx))
            r.doff[rs, :] += jnp.where(lane == 2 * k, to_y, 0.0) + jnp.where(
                lane == 2 * k + 1, to_x, 0.0
            )
            acc[rs, :] += mm(r.wmat[s, k], back, TN)
        return carry

    lax.fori_loop(0, TAPS, unsample, 0, unroll=3)
    wide_step(NAR, 1)
    z2(CON, [0])
    for s in range(SLOTS):
        put = r.tiny.at[1, chip, s]
        put[...] = jnp.zeros((24, PIXELS), F32)
        put[0:OFFSETS, :] = mm(
            r.doff[slot_rows(s), :].astype(BF), r.tmat[0, TAPS // 2], TN
        )
    tiny_send(1)

    def untap(k, carry):
        for s in range(SLOTS):
            rs = slot_rows(s)
            moved = mm(shifted(s, TAPS - 1 - k), r.doff[rs, :].astype(BF), NN).astype(BF)
            acc[rs, :] += mm(moved, offset_tap(k), NN)
        return carry

    lax.fori_loop(0, TAPS, untap, 0, unroll=3)

    wide_core(EXP)

    def work_a():
        for t in range(1, bits):
            gather_step(3, t)
        wide_send(EXP, 0)
        z1(CON, late)
        for t in range(2, bits + 1):
            wide_step(NAR, t)
        z2(CON, [1])
        z4(WID)

    narrow_cotangent(r.a1, 0, ig[0], ib[0], 7, False, work_a)
    z3(CON, [0])
    wide_begin(RED, images, r.dn)
    z2(CON, [2])
    out_copy.wait()
    loads.red_h.wait()

    def finish(n, carry):
        rows = pl.ds(pl.multiple_of(n * 512, 512), 512)
        r.obuf[:, rows] = (up[n] + mm(r.dn[...], r.redwid[rows, :], NT)).astype(BF)
        return carry

    lax.fori_loop(0, CHANNELS // 512, finish, 0, unroll=2)
    grad_copy = dma(r.obuf, r.grad_h, r.out_sem.at[1])
    grad_copy.start()
    z2(CON, [3])
    z3(CON, [1])
    gather_end(3)
    deep_make(DEF)
    z2(NAR, [0])
    z3(CON, [2])
    wide_core(RED)
    wide_send(RED, 0)
    deep_core(DEF)
    z1(DEF)
    z2(NAR, [1])
    z3(CON, [3])
    wide_step(EXP, 1)
    tiny_wait(1)
    off_make()
    z2(DEF, [0])
    z3(NAR, [0])
    off_core()
    z1(OFF)
    wide_step(RED, 1)
    z2(DEF, [1])
    z3(NAR, [1])
    for t in range(2, bits + 1):
        wide_step(EXP, t)
    z2(DEF, [2])
    z3(DEF, [0])
    for t in range(2, bits + 1):
        wide_step(RED, t)
    z2(DEF, [3])
    z3(DEF, [1])
    z2(OFF)
    z3(DEF, [2])
    z2(EXP, [0])
    z3(DEF, [3])
    z3(OFF)
    z2(EXP, [1])
    z2(RED, [0])
    z3(EXP, [0])
    z2(RED, [1])
    z2(RED, [2])
    z3(EXP, [1])
    z2(RED, [3])
    z3(RED, [0])
    z3(RED, [1])
    z3(RED, [2])
    z3(RED, [3])
    z4(CON)
    z4(NAR)
    z4(DEF)
    z4(OFF)
    z4(EXP)
    z4(RED)
    for u in range(7):
        z_clear(u)
    grad_copy.wait()
    for tag in list(waiting):
        flush(tag)


MOVED = ["out", "grad", "con", "def", "wid", "nar", "exp", "red"]


def deliver(dp, names, *refs):
    r = types.SimpleNamespace(**dict(zip(names, refs)))
    _, _, _, deep, _ = layout(dp)
    place = lax.axis_index("dp")
    moves = []
    for i, name in enumerate(MOVED):
        source, target, hold = (getattr(r, kind + name) for kind in ("from_", "to_", "hold_"))
        taken = pltpu.make_async_copy(source, hold, r.sems.at[0, i])
        taken.start()
        moves.append((taken, pltpu.make_async_copy(hold, target, r.sems.at[1, i])))

    for taken, given in moves:
        taken.wait()
        given.start()

    def span(ref, start, target):
        rows, lanes = ref.shape
        moved = pltpu.roll(ref[...], lax.rem(lanes - start, lanes), 1)
        target[...] = moved[: target.shape[0], : target.shape[1]]

    span(r.g_ig, place * (INNER // dp), r.to_ig)
    span(r.g_ib, place * (INNER // dp), r.to_ib)
    span(r.g_bg, place * (CHANNELS // dp), r.to_bg)
    span(r.g_bb, place * (CHANNELS // dp), r.to_bb)
    chip, core = lax.div(place, 2), lax.rem(place, 2)
    span(r.g_off, lax.rem(2 * deep * chip, INNER) + deep * core, r.to_off)
    for taken, given in moves:
        given.wait()


def per_device(
    images,
    counts,
    orientation,
    cotangent,
    reducer,
    offseter,
    deformer,
    expander,
    narrower,
    convolver,
    widener,
    inner_gains,
    inner_biases,
    broad_gains,
    broad_biases,
):
    dp, outer = lax.axis_size("dp"), lax.axis_size("outer")
    chips, bits, wide, deep, taps = layout(dp)
    buffers = scratch(dp, outer)
    smem = pl.BlockSpec(memory_space=pltpu.SMEM)
    vmem = pl.BlockSpec(memory_space=pltpu.VMEM)
    far = pl.BlockSpec(memory_space=pl.ANY)
    shape = jax.ShapeDtypeStruct
    inputs = dict(
        counts=(smem, counts),
        orient=(smem, orientation),
        ig=(vmem, inner_gains),
        ib=(vmem, inner_biases),
        bg=(vmem, broad_gains),
        bb=(vmem, broad_biases),
        images_h=(far, images.reshape(ROWS, CHANNELS)),
        cot_h=(far, cotangent.reshape(ROWS, CHANNELS)),
        red_h=(far, reducer),
        off_h=(far, offseter.T),
        def_h=(far, deformer),
        exp_h=(far, expander),
        nar_h=(far, narrower),
        con_h=(far, convolver),
        wid_h=(far, widener),
    )
    outputs = dict(
        out_h=(far, shape((ROWS, CHANNELS), BF)),
        grad_h=(far, shape((ROWS, CHANNELS), BF)),
        g_red=(far, shape((wide, INNER), F32)),
        g_off=(far, shape((24, taps * INNER), F32)),
        g_def=(far, shape((deep, INNER), F32)),
        g_exp=(far, shape((wide, INNER), F32)),
        g_nar=(far, shape((wide, INNER), F32)),
        g_con=(far, shape((deep, INNER), F32)),
        g_wid=(far, shape((wide, INNER), F32)),
        g_ig=(vmem, shape((4, INNER), F32)),
        g_ib=(vmem, shape((4, INNER), F32)),
        g_bg=(vmem, shape((2, CHANNELS), F32)),
        g_bb=(vmem, shape((2, CHANNELS), F32)),
        far_blocks=(far, shape((4, chips, ROWS, INNER), F32)),
        far_columns=(far, shape((2, taps, chips * ROWS, INNER), BF)),
    )
    names = list(inputs) + list(outputs) + list(buffers)
    outs = pl.pallas_call(
        functools.partial(kernel, dp, outer, names),
        out_shape=[spec for _, spec in outputs.values()],
        in_specs=[space for space, _ in inputs.values()],
        out_specs=[space for space, _ in outputs.values()],
        scratch_shapes=list(buffers.values()),
        compiler_params=pltpu.CompilerParams(
            collective_id=0, has_side_effects=True, vmem_limit_bytes=63 * 1024 * 1024
        ),
        name="chain",
    )(*[value for _, value in inputs.values()])
    held = dict(zip(outputs, outs))
    big = dict(
        out=held["out_h"],
        grad=held["grad_h"],
        red=held["g_red"],
        **{"def": held["g_def"]},
        exp=held["g_exp"],
        nar=held["g_nar"],
        con=held["g_con"],
        wid=held["g_wid"],
    )
    small = {name: held[name] for name in ("g_off", "g_ig", "g_ib", "g_bg", "g_bb")}
    firsts = {"from_" + name: value for name, value in big.items()}
    finals = {"to_" + name: shape(value.shape, value.dtype) for name, value in big.items()}
    holds = {"hold_" + name: pltpu.VMEM(value.shape, value.dtype) for name, value in big.items()}
    lasts = dict(
        to_off=shape((OFFSETS, deep), F32),
        to_ig=shape((4, INNER // dp), F32),
        to_ib=shape((4, INNER // dp), F32),
        to_bg=shape((2, CHANNELS // dp), F32),
        to_bb=shape((2, CHANNELS // dp), F32),
    )
    names = [*firsts, *small, *finals, *lasts, *holds, "sems"]
    got = pl.pallas_call(
        functools.partial(deliver, dp, names),
        out_shape=[*finals.values(), *lasts.values()],
        in_specs=[far] * len(firsts) + [vmem] * len(small),
        out_specs=[far] * len(finals) + [vmem] * len(lasts),
        scratch_shapes=[*holds.values(), pltpu.SemaphoreType.DMA((2, len(big)))],
        compiler_params=pltpu.CompilerParams(vmem_limit_bytes=60 * 1024 * 1024),
        name="deliver",
    )(*firsts.values(), *small.values())
    out, grad, g_red, g_def, g_exp, g_nar, g_con, g_wid, g_off, *others = got
    return (
        out.reshape(SLOTS, PIXELS, CHANNELS),
        grad.reshape(SLOTS, PIXELS, CHANNELS),
        g_red,
        g_off.T,
        g_def,
        g_exp,
        g_nar,
        g_con,
        g_wid,
        *others,
    )


def solution(mesh):
    spread = P(("dp", "outer"), None, None)
    in_specs = (spread, P(), P(("dp", "outer")), spread) + (P(),) * 11
    out_specs = (spread, spread) + (P("dp", None),) * 7 + (P(None, "dp"),) * 4
    return jax.shard_map(
        per_device, mesh=mesh, in_specs=in_specs, out_specs=out_specs, check_vma=False
    )
```
